32 devices in a mesh: fsdp: 8 (over y, x, core), seq: 4 (over z).
Axes of the slice: x: 2, y: 2, z: 4, core: 2. Of those that a mesh axis runs over, the one named last changes fastest.
Arguments:
- tokens: bfloat16 [64, 256, 768], P('fsdp', 'seq'), may hold values from -6 to 6
- ln1_gain: bfloat16 [768], P('fsdp'), may hold values from 0.5 to 1.5
- ln1_bias: bfloat16 [768], P('fsdp'), may hold values from -1.5 to 1.5
- w_qkv: bfloat16 [768, 2304], P('fsdp'), may hold values from -0.21875 to 0.21875
- w_out: bfloat16 [768, 768], P('fsdp'), may hold values from -1.75 to 1.75
- ln2_gain: bfloat16 [768], P('fsdp'), may hold values from 0.5 to 1.5
- ln2_bias: bfloat16 [768], P('fsdp'), may hold values from -1.5 to 1.5
- w_router: bfloat16 [768, 4], P('fsdp'), may hold values from -0.14941406 to 0.14941406
- w_in: bfloat16 [4, 3072, 768], P(None, 'fsdp'), may hold values from -0.21875 to 0.21875
- w_down: bfloat16 [4, 3072, 768], P(None, 'fsdp'), may hold values from -0.875 to 0.875
- padding: int32 [64, 256], P('fsdp'), may hold values from 0 to 1, as said below
- routes: int32 [64, 256, 2], P('fsdp', 'seq'), may hold values from 0 to 3, all different within a row
- priority: int32 [64, 256], P('fsdp', 'seq'), may hold values from 0 to 16383, as said below
- cotangent: bfloat16 [64, 256, 768], P('fsdp', 'seq'), may hold values from -6 to 6
Outputs:
- outputs: bfloat16 [64, 256, 768], P('fsdp', 'seq')
- grad_tokens: bfloat16 [64, 256, 768], P('fsdp', 'seq')
- grad_ln1_gain: float32 [768], P('fsdp')
- grad_ln1_bias: float32 [768], P('fsdp')
- grad_w_qkv: float32 [768, 2304], P('fsdp')
- grad_w_out: float32 [768, 768], P('fsdp')
- grad_ln2_gain: float32 [768], P('fsdp')
- grad_ln2_bias: float32 [768], P('fsdp')
- grad_w_router: float32 [768, 4], P('fsdp')
- grad_w_in: float32 [4, 3072, 768], P(None, 'fsdp')
- grad_w_down: float32 [4, 3072, 768], P(None, 'fsdp')
The draws below stay inside these ranges and needn't reach their ends.
Inputs may be any that keep to these rules, and one draw needn't show every extreme that they name: `padding`: an image's ones are a prefix of 128 or more positions, and some image has ones at all 256 positions. `routes`: a token's two experts differ, and every expert is named by some token. `priority`: all values are different.
All inputs are finite; a program needn't handle non-finite values.
Results may differ from the reference program's by a relative error of at most 0.018.
Values may be sent and summed in bfloat16 or wider, within the bound.
No kernel may reach another device: no remote copies, remote signals or barrier semaphores. Data moves between devices by JAX's collectives and lax.ppermute only.
A program may use at most 192 MiB of HBM per device.

```python
from functools import partial
import jax
import jax.numpy as jnp
from jax import lax

D = 768
HEADS = 12
HEAD_DIM = 64
FF = 3072
EXPERTS = 4
LEN = 256
IMG_DEV = 8
IMAGES = 64
POS = 64
TOK_DEV = 512
CAP = 256
N_FSDP = 8
N_SEQ = 4


def draw_padding(key, part):
    key = jax.random.fold_in(key, 11)
    key_counts, key_full = jax.random.split(key)
    counts = jax.random.randint(key_counts, (IMAGES,), LEN // 2, LEN + 1)
    chosen = jax.random.randint(key_full, (), 0, IMAGES)
    counts = jnp.where(jnp.arange(IMAGES) == chosen, LEN, counts)
    return (jnp.arange(LEN)[None, :] < counts[:, None]).astype(jnp.int32)


def draw_priority(key, part):
    key = jax.random.fold_in(key, 23)
    return jax.random.permutation(key, IMAGES * LEN).reshape(IMAGES, LEN).astype(jnp.int32)


def levels(stream_key, extent, shards, least, top_value):
    loudness, own = 1.0, jax.random.fold_in(stream_key, 6)
    for position, blocks in shards:
        draws = jnp.exp(jax.random.uniform(jax.random.fold_in(own, position), (blocks,), jnp.float32, least / len(shards), top_value / len(shards)))
        loudness = loudness * jnp.repeat(draws, extent[position] // blocks).reshape([-1 if axis == position else 1 for axis in range(len(extent))])
    return loudness


def different_ones(rng, rows, number_of, top, lift):
    sequence = jax.random.permutation(jax.random.fold_in(rng, 1), number_of)
    pull = sequence
    for power in range(3):
        pull = pull * pull // number_of
    pull = pull * lift // number_of
    tickets = jax.random.randint(jax.random.fold_in(rng, 2), (rows, number_of), 0, 4096) + pull
    holders = jax.random.permutation(jax.random.fold_in(rng, 3), rows)[jnp.arange(number_of) % rows]
    tickets = jnp.where(jnp.arange(rows)[:, None] == holders[None, :], 1 << 14, tickets)
    score = tickets * number_of + jnp.arange(number_of)
    return lax.top_k(score.astype(jnp.int32), top)[1].astype(jnp.int32)


def noise(key, extent, scale, limit, cuts=(), kind=jnp.bfloat16):
    drawn = scale * jax.random.normal(key, extent, jnp.float32)
    if cuts:
        drawn = drawn * levels(key, extent, cuts, -0.22, 0.18)
    return jnp.clip(drawn, -limit, limit).astype(kind)


def setup_inputs(seed: int = 0) -> dict:
    streams_of = jax.random.split(jax.random.key(seed), 15)
    return {
        "tokens": noise(streams_of[0], (IMAGES, LEN, D), 1.0, 6.0, ((0, 8), (1, 4))),
        "ln1_gain": jnp.clip(1.0 + 0.1 * jax.random.normal(streams_of[1], (D,), jnp.float32), 0.5, 1.5).astype(jnp.bfloat16),
        "ln1_bias": noise(streams_of[2], (D,), 0.3, 1.5, ((0, 8),)),
        "w_qkv": noise(streams_of[3], (D, 3 * D), D ** -0.5, 0.21875, ((0, 8),)),
        "w_out": noise(streams_of[4], (D, D), (D // 64) ** -0.5, 1.75, ((0, 8),)),
        "ln2_gain": jnp.clip(1.0 + 0.1 * jax.random.normal(streams_of[5], (D,), jnp.float32), 0.5, 1.5).astype(jnp.bfloat16),
        "ln2_bias": noise(streams_of[6], (D,), 0.3, 1.5, ((0, 8),)),
        "w_router": noise(streams_of[7], (D, EXPERTS), 0.025, 0.14941406, ((0, 8),)),
        "w_in": noise(streams_of[8], (EXPERTS, FF, D), D ** -0.5, 0.21875, ((1, 8),)),
        "w_down": noise(streams_of[9], (EXPERTS, FF, D), (FF // 64) ** -0.5, 0.875, ((1, 8),)),
        "padding": draw_padding(jax.random.fold_in(streams_of[14], 71), 0),
        "routes": different_ones(streams_of[11], IMAGES * LEN, EXPERTS, 2, 4096).reshape((IMAGES, LEN, 2)),
        "priority": draw_priority(jax.random.fold_in(streams_of[14], 71), 0),
        "cotangent": noise(streams_of[13], (IMAGES, LEN, D), 1.0, 6.0, ((0, 8), (1, 4))),
    }


exact_prec = lax.Precision.HIGHEST
norm_eps = 1e-06
neg_fill = -1e+30

@jax.custom_vjp
def low(v):
    return lax.optimization_barrier(v.astype(jnp.bfloat16)).astype(jnp.float32)

@jax.custom_vjp
def low_back(v):
    return v

def low_keep(v):
    return (low(v), None)

def low_pass(kept, grad):
    return (grad,)

def back_keep(v):
    return (v, None)

def back_low(kept, grad):
    return (low(grad),)
low.defvjp(low_keep, low_pass)
low_back.defvjp(back_keep, back_low)

def layer_norm(inputs, gain_vec, bias_vec):
    average = lax.optimization_barrier(jnp.mean(inputs, -1, keepdims=True))
    centred = inputs - average
    spread = lax.optimization_barrier(jnp.mean(centred * centred, -1, keepdims=True))
    return centred * lax.rsqrt(spread + norm_eps) * gain_vec + bias_vec

def attend(pieces):
    queries, key_rows, values, visible = pieces
    scores = low_back(jnp.einsum('qhd,khd->hqk', queries, key_rows, precision=exact_prec) * HEAD_DIM ** (-0.5))
    scores = jnp.where(visible[None, None, :] > 0, scores, neg_fill)
    row_max = lax.optimization_barrier(jnp.max(scores, -1, keepdims=True))
    shifted = jnp.exp(scores - row_max)
    weights = low(shifted / lax.optimization_barrier(jnp.sum(shifted, -1, keepdims=True)))
    return jnp.einsum('hqk,khd->qhd', weights, values, precision=exact_prec)

def to_groups(group_array):
    trailing = group_array.shape[2:]
    group_array = group_array.reshape((N_FSDP, IMG_DEV, N_SEQ, POS) + trailing)
    group_array = jnp.moveaxis(group_array, 2, 1)
    return group_array.reshape((N_FSDP * N_SEQ, TOK_DEV) + trailing)

def from_groups(group_array):
    trailing = group_array.shape[2:]
    group_array = group_array.reshape((N_FSDP, N_SEQ, IMG_DEV, POS) + trailing)
    group_array = jnp.moveaxis(group_array, 1, 2)
    return group_array.reshape((IMAGES, LEN) + trailing)

def assign_slots(pieces):
    route_g, live_g, order_g = pieces
    alive = live_g > 0
    earlier = order_g[None, :] < order_g[:, None]
    route_first = route_g[:, 0]
    route_second = route_g[:, 1]
    same_first = (route_first[None, :] == route_first[:, None]) & alive[None, :]
    same_second = (route_second[None, :] == route_second[:, None]) & alive[None, :]
    cross = (route_first[None, :] == route_second[:, None]) & alive[None, :]
    slot_first = lax.optimization_barrier(jnp.sum((earlier & same_first).astype(jnp.int32), 1))
    slot_second = lax.optimization_barrier(jnp.sum((earlier & same_second).astype(jnp.int32), 1)) + lax.optimization_barrier(jnp.sum(cross.astype(jnp.int32), 1))
    dest_first = jnp.where(alive & (slot_first < CAP), route_first * CAP + slot_first, EXPERTS * CAP)
    dest_second = jnp.where(alive & (slot_second < CAP), route_second * CAP + slot_second, EXPERTS * CAP)
    return (dest_first.astype(jnp.int32), dest_second.astype(jnp.int32))

def experts_group(pieces, w_in, w_down):
    normed, dest_first, dest_second, gate_first, gate_second = pieces
    slots = jnp.zeros((EXPERTS * CAP + 1, D), normed.dtype)
    slots = slots.at[dest_first].add(normed).at[dest_second].add(normed)
    slots = slots[:EXPERTS * CAP].reshape(EXPERTS, CAP, D)
    pre_act = low_back(jnp.einsum('ecd,efd->ecf', slots, w_in, precision=exact_prec))
    hidden = low(jax.nn.gelu(pre_act, approximate=False))
    result = low_back(jnp.einsum('ecf,efd->ecd', hidden, w_down, precision=exact_prec))
    result = jnp.concatenate([result.reshape(EXPERTS * CAP, D), jnp.zeros((1, D), result.dtype)])
    return gate_first[:, None] * result[dest_first] + gate_second[:, None] * result[dest_second]

def reference(tokens, ln1_gain, ln1_bias, w_qkv, w_out, ln2_gain, ln2_bias, w_router, w_in, w_down, padding, routes, priority, cotangent):
    visible = padding
    dest_first, dest_second = lax.map(assign_slots, (to_groups(routes), to_groups(padding), to_groups(priority)))
    labels = jnp.arange(EXPERTS, dtype=jnp.int32)
    first_hot = (routes[..., 0:1] == labels).astype(jnp.float32)
    second_hot = (routes[..., 1:2] == labels).astype(jnp.float32)
    token_live = padding.astype(jnp.float32)[..., None]

    def forward(inputs, gain_one, bias_one, qkv_weight, out_weight, gain_two, bias_two, router_weight, in_weight, down_weight):
        normed_one = low(layer_norm(inputs, gain_one, bias_one))
        projected = low(low_back(jnp.einsum('isd,de->ise', normed_one, qkv_weight, precision=exact_prec)))
        projected = projected.reshape(IMAGES, LEN, HEADS, 3, HEAD_DIM)
        attended = lax.map(jax.checkpoint(attend), (projected[:, :, :, 0], projected[:, :, :, 1], projected[:, :, :, 2], visible))
        attended = low(low_back(attended.reshape(IMAGES, LEN, D)))
        middle = inputs + low_back(jnp.einsum('isd,de->ise', attended, out_weight, precision=exact_prec))
        normed_two = low(layer_norm(middle, gain_two, bias_two))
        logits = low_back(jnp.einsum('isd,de->ise', normed_two, router_weight, precision=exact_prec))
        shifted = jnp.exp(logits - lax.optimization_barrier(jnp.max(logits, -1, keepdims=True)))
        router_probs = shifted / lax.optimization_barrier(jnp.sum(shifted, -1, keepdims=True))
        gate_first = lax.optimization_barrier(jnp.sum(router_probs * first_hot, -1))
        gate_second = lax.optimization_barrier(jnp.sum(router_probs * second_hot, -1))
        expert_fn = jax.checkpoint(partial(experts_group, w_in=in_weight, w_down=down_weight))
        combined = lax.map(expert_fn, (to_groups(normed_two), dest_first, dest_second, to_groups(gate_first), to_groups(gate_second)))
        return token_live * (middle + from_groups(combined))
    floats = [tokens.astype(jnp.float32), ln1_gain.astype(jnp.float32), ln1_bias.astype(jnp.float32), w_qkv.astype(jnp.float32), w_out.astype(jnp.float32), ln2_gain.astype(jnp.float32), ln2_bias.astype(jnp.float32), w_router.astype(jnp.float32), w_in.astype(jnp.float32), w_down.astype(jnp.float32)]
    result, pullback = jax.vjp(forward, *floats)
    gradients = pullback(cotangent.astype(jnp.float32))
    return (result.astype(jnp.bfloat16), gradients[0].astype(jnp.bfloat16), gradients[1], gradients[2], gradients[3], gradients[4], gradients[5], gradients[6], gradients[7], gradients[8], gradients[9])
```

```python
import functools
import math

import jax
import jax.numpy as jnp
from jax import lax
from jax.experimental import pallas as pl
from jax.experimental.pallas import tpu as pltpu
from jax.sharding import PartitionSpec as P

HEAD_DIM = 64
LANES = 128
MASK_ROWS = 16
SMALL = 8
norm_eps = 1e-06
neg_fill = -1e30
f32 = jnp.float32
bf16 = jnp.bfloat16
VMEM_BYTES = 60 * 1024 * 1024


def mm(left, right, left_dim=1, right_dim=0):
    return lax.dot_general(
        left, right, (((left_dim,), (right_dim,)), ((), ())), preferred_element_type=f32
    )


def unit_norm(rows):
    centred = rows - jnp.mean(rows, -1, keepdims=True)
    inverse = lax.rsqrt(jnp.mean(centred * centred, -1, keepdims=True) + norm_eps)
    return centred * inverse, inverse


def norm_back(scaled, unit, inverse):
    return inverse * (
        scaled
        - jnp.mean(scaled, -1, keepdims=True)
        - unit * jnp.mean(scaled * unit, -1, keepdims=True)
    )


def half_turn(tile):
    return pltpu.roll(tile.astype(f32), HEAD_DIM, axis=1).astype(bf16)


def front_kernel(tok_ref, wall_ref, small_ref, vis_ref, mid_ref, two_ref, proj_ref, att_ref, prob_ref):
    blocks, _, span, width = tok_ref.shape
    length = blocks * span
    rows = tok_ref[...].reshape(length, width).astype(f32)
    unit, _ = unit_norm(rows)
    one = (unit * small_ref[4:5] + small_ref[5:6]).astype(bf16)
    proj_ref[0] = mm(one, wall_ref[:, : 3 * width]).astype(bf16)
    lower = lax.broadcasted_iota(jnp.int32, (length, LANES), 1) < HEAD_DIM
    zero = jnp.zeros((length, LANES), bf16)
    bias = vis_ref[0]

    def soften(index, queries, keys):
        scores = mm(queries, keys, 1, 1) * (HEAD_DIM**-0.5) + bias
        shifted = jnp.exp(scores - jnp.max(scores, -1, keepdims=True))
        weights = (shifted / jnp.sum(shifted, -1, keepdims=True)).astype(bf16)
        prob_ref[0, index] = weights
        return weights

    for pair in range(width // LANES):
        first, second, third = (
            proj_ref[0, :, (3 * pair + n) * LANES : (3 * pair + n + 1) * LANES] for n in range(3)
        )
        weights_a = soften(2 * pair, jnp.where(lower, first, zero), half_turn(first))
        weights_b = soften(2 * pair + 1, jnp.where(lower, zero, second), half_turn(third))
        both = jnp.where(lower, mm(weights_a, second), mm(weights_b, third))
        att_ref[0, :, pair * LANES : (pair + 1) * LANES] = both.astype(bf16)
    middle = rows + mm(att_ref[0], wall_ref[:, 3 * width : 4 * width])
    mid_ref[...] = middle.reshape(mid_ref.shape)
    unit, _ = unit_norm(middle)
    two_ref[...] = (unit * small_ref[6:7] + small_ref[7:8]).astype(bf16).reshape(two_ref.shape)


def front(tok, wall, small, vis):
    blocks, images, span, width = tok.shape
    length = blocks * span
    heads = width // HEAD_DIM
    split = pl.BlockSpec((blocks, 1, span, width), lambda i: (0, i, 0, 0))
    return pl.pallas_call(
        front_kernel,
        grid=(images,),
        in_specs=[
            split,
            pl.BlockSpec(wall.shape, lambda i: (0, 0)),
            pl.BlockSpec(small.shape, lambda i: (0, 0)),
            pl.BlockSpec((1, 1, length), lambda i: (i, 0, 0)),
        ],
        out_specs=[
            split,
            split,
            pl.BlockSpec((1, length, 3 * width), lambda i: (i, 0, 0)),
            pl.BlockSpec((1, length, width), lambda i: (i, 0, 0)),
            pl.BlockSpec((1, heads, length, length), lambda i: (i, 0, 0, 0)),
        ],
        out_shape=[
            jax.ShapeDtypeStruct(tok.shape, f32),
            jax.ShapeDtypeStruct(tok.shape, bf16),
            jax.ShapeDtypeStruct((images, length, 3 * width), bf16),
            jax.ShapeDtypeStruct((images, length, width), bf16),
            jax.ShapeDtypeStruct((images, heads, length, length), bf16),
        ],
        compiler_params=pltpu.CompilerParams(vmem_limit_bytes=VMEM_BYTES),
        cost_estimate=pl.CostEstimate(
            flops=2 * images * length * width * (4 * width + 2 * length),
            bytes_accessed=16 * 1024 * 1024,
            transcendentals=images * heads * length * length,
        ),
        name="front",
    )(tok, wall, small, vis)


def gelu_parts(pre):
    bell = jnp.exp(-0.5 * pre * pre)
    size = jnp.abs(pre) * 0.7071067811865476
    frac = 1.0 / (1.0 + 0.3275911 * size)
    poly = frac * (
        0.254829592
        + frac * (-0.284496736 + frac * (1.421413741 + frac * (-1.453152027 + frac * 1.061405429)))
    )
    tail = 0.5 * poly * bell
    cumulative = jnp.where(pre >= 0, 1.0 - tail, tail)
    return pre * cumulative, cumulative + pre * bell * 0.3989422804014327


def expert_kernel(
    experts, two_ref, cot_ref, win_ref, wdn_ref, wr_ref,
    out_ref, gin_ref, dwin_ref, dwdn_ref, dwr_ref, acc_in, acc_dn, acc_r,
):
    _, blocks, span, width = two_ref.shape
    count = blocks * span
    hidden_all = win_ref.shape[0]
    share = hidden_all // experts
    step = pl.program_id(0) * pl.num_programs(1) + pl.program_id(1)
    last = pl.num_programs(0) * pl.num_programs(1) - 1

    @pl.when(step == 0)
    def _():
        acc_in[...] = jnp.zeros_like(acc_in)
        acc_dn[...] = jnp.zeros_like(acc_dn)
        acc_r[...] = jnp.zeros_like(acc_r)

    two = two_ref[0].reshape(count, width)
    cot = cot_ref[0, :, :span, :].reshape(count, width)
    lane = lax.broadcasted_iota(jnp.int32, (count, LANES), 1)
    chosen = (
        lax.broadcasted_iota(jnp.int32, (MASK_ROWS, LANES), 0)
        == lax.broadcasted_iota(jnp.int32, (MASK_ROWS, LANES), 1)
    ).astype(bf16)
    kept = jnp.concatenate(
        [mm(cot_ref[0, b, span : span + MASK_ROWS, :span], chosen, 0, 0) for b in range(blocks)], 0
    )
    wr = wr_ref[...]
    logits = jnp.where(lane < experts, mm(two, wr), neg_fill)
    shifted = jnp.exp(logits - jnp.max(logits, -1, keepdims=True))
    probs = shifted / jnp.sum(shifted, -1, keepdims=True)
    gates = probs * kept

    out_sum = None
    gin_sum = None
    grad_gate = jnp.zeros((count, LANES), f32)
    per_chunk = 2 if experts % 2 == 0 else 1
    for chunk in range(experts // per_chunk):
        at = slice(chunk * per_chunk * share, (chunk + 1) * per_chunk * share)
        win, wdn = win_ref[at], wdn_ref[at]
        pre = mm(two, win, 1, 1)
        back = mm(cot, wdn, 1, 1)
        hidden, slope = gelu_parts(pre)
        product = hidden * back
        slope = slope * back
        gated, grad_pre = [], []
        for n in range(per_chunk):
            expert = chunk * per_chunk + n
            here = slice(n * share, (n + 1) * share)
            gate = gates[:, expert : expert + 1]
            gated.append(hidden[:, here] * gate)
            grad_pre.append(slope[:, here] * gate)
            grad_gate = jnp.where(
                lane == expert, jnp.sum(product[:, here], -1, keepdims=True), grad_gate
            )
        gated = jnp.concatenate(gated, 1).astype(bf16)
        grad_pre = jnp.concatenate(grad_pre, 1).astype(bf16)
        out_part = mm(gated, wdn)
        gin_part = mm(grad_pre, win)
        out_sum = out_part if out_sum is None else out_sum + out_part
        gin_sum = gin_part if gin_sum is None else gin_sum + gin_part
        acc_in[at] += mm(grad_pre, two, 0, 0)
        acc_dn[at] += mm(gated, cot, 0, 0)
    grad_gate = grad_gate * kept
    grad_logits = probs * (grad_gate - jnp.sum(probs * grad_gate, -1, keepdims=True))
    grad_logits = grad_logits.astype(bf16)
    gin_sum = gin_sum + mm(grad_logits, wr, 1, 1)
    acc_r[...] += mm(grad_logits, two, 0, 0)
    out_ref[0] = out_sum.astype(bf16).reshape(blocks, span, width)
    gin_ref[0] = gin_sum.astype(bf16).reshape(blocks, span, width)

    @pl.when(step == last)
    def _():
        dwin_ref[...] = acc_in[...].astype(bf16)
        dwdn_ref[...] = acc_dn[...].astype(bf16)
        dwr_ref[...] = acc_r[:SMALL]


def experts_all(two, cot, win, wdn, wr, experts):
    groups, blocks, span, width = two.shape
    hidden = win.shape[0]
    per = math.gcd(blocks, max(1, 512 // span))
    token_block = pl.BlockSpec((1, per, span, width), lambda g, b: (g, b, 0, 0))
    whole = lambda a: pl.BlockSpec(a.shape, lambda g, b: (0,) * len(a.shape))
    tokens = groups * blocks * span
    outs = [
        jax.ShapeDtypeStruct(two.shape, bf16),
        jax.ShapeDtypeStruct(two.shape, bf16),
        jax.ShapeDtypeStruct((hidden, width), bf16),
        jax.ShapeDtypeStruct((hidden, width), bf16),
        jax.ShapeDtypeStruct((SMALL, width), f32),
    ]
    return pl.pallas_call(
        functools.partial(expert_kernel, experts),
        grid=(groups, blocks // per),
        in_specs=[
            token_block,
            pl.BlockSpec((1, per, span + MASK_ROWS, width), lambda g, b: (g, b, 0, 0)),
            whole(win),
            whole(wdn),
            whole(wr),
        ],
        out_specs=[token_block, token_block, whole(outs[2]), whole(outs[3]), whole(outs[4])],
        out_shape=outs,
        scratch_shapes=[
            pltpu.VMEM((hidden, width), f32),
            pltpu.VMEM((hidden, width), f32),
            pltpu.VMEM((LANES, width), f32),
        ],
        compiler_params=pltpu.CompilerParams(vmem_limit_bytes=VMEM_BYTES),
        cost_estimate=pl.CostEstimate(
            flops=12 * tokens * width * hidden,
            bytes_accessed=8 * tokens * width + 8 * hidden * width,
            transcendentals=tokens * hidden,
        ),
        name="experts",
    )(two, cot, win, wdn, wr)


def back_kernel(
    gin_ref, mid_ref, cot_ref, tok_ref, att_ref, proj_ref, prob_ref, wall_ref, small_ref, dwr_ref,
    gtok_ref, dwall_ref, acc, acc_small, gatt, gproj,
):
    blocks, _, span, width = tok_ref.shape
    length = blocks * span
    step = pl.program_id(0)

    @pl.when(step == 0)
    def _():
        acc[...] = jnp.zeros_like(acc)
        acc_small[...] = jnp.zeros_like(acc_small)
        acc_small[:SMALL] = dwr_ref[...]

    gin = gin_ref[...].reshape(length, width).astype(f32)
    unit_two, inverse_two = unit_norm(mid_ref[...].reshape(length, width))
    acc_small[6:7] += jnp.sum(gin * unit_two, 0, keepdims=True)
    acc_small[7:8] += jnp.sum(gin, 0, keepdims=True)
    grad_middle = cot_ref[...].reshape(length, width).astype(f32) + norm_back(
        gin * small_ref[6:7], unit_two, inverse_two
    )
    branch = grad_middle.astype(bf16)
    acc[:, 3 * width : 4 * width] += mm(att_ref[0], branch, 0, 0)
    gatt[...] = mm(branch, wall_ref[:, 3 * width : 4 * width], 1, 1).astype(bf16)
    lower = lax.broadcasted_iota(jnp.int32, (length, LANES), 1) < HEAD_DIM
    zero = jnp.zeros((length, LANES), bf16)
    scale = HEAD_DIM**-0.5

    def score_grad(weights, grad_weights):
        weights = weights.astype(f32)
        product = weights * grad_weights
        return (product - weights * jnp.sum(product, -1, keepdims=True)).astype(bf16)

    for pair in range(width // LANES):
        places = [slice((3 * pair + n) * LANES, (3 * pair + n + 1) * LANES) for n in range(3)]
        first, second, third = (proj_ref[0, :, place] for place in places)
        first_r, second_r, third_r = half_turn(first), half_turn(second), half_turn(third)
        grad = gatt[:, pair * LANES : (pair + 1) * LANES]
        weights_a, weights_b = prob_ref[0, 2 * pair], prob_ref[0, 2 * pair + 1]
        ds_a = score_grad(weights_a, mm(jnp.where(lower, grad, zero), second, 1, 1))
        ds_b = score_grad(weights_b, mm(jnp.where(lower, zero, grad), third, 1, 1))
        gproj[:, places[0]] = (
            jnp.where(lower, mm(ds_a, first_r), mm(ds_a, first_r, 0, 0)) * scale
        ).astype(bf16)
        gproj[:, places[1]] = jnp.where(
            lower, mm(weights_a, grad, 0, 0), mm(ds_b, third_r) * scale
        ).astype(bf16)
        gproj[:, places[2]] = jnp.where(
            lower, mm(ds_b, second_r, 0, 0) * scale, mm(weights_b, grad, 0, 0)
        ).astype(bf16)
    unit_one, inverse_one = unit_norm(tok_ref[...].reshape(length, width).astype(f32))
    one = (unit_one * small_ref[4:5] + small_ref[5:6]).astype(bf16)
    grad_one = mm(gproj[...], wall_ref[:, : 3 * width], 1, 1)
    acc_small[4:5] += jnp.sum(grad_one * unit_one, 0, keepdims=True)
    acc_small[5:6] += jnp.sum(grad_one, 0, keepdims=True)
    grad_tok = grad_middle + norm_back(grad_one * small_ref[4:5], unit_one, inverse_one)
    gtok_ref[...] = grad_tok.astype(bf16).reshape(gtok_ref.shape)
    acc[:, : 3 * width] += mm(one, gproj[...], 0, 0)

    @pl.when(step == pl.num_programs(0) - 1)
    def _():
        dwall_ref[:, : 4 * width] = acc[...].astype(bf16)
        dwall_ref[:, 4 * width :] = acc_small[...].T.astype(bf16)


def back(gin, middle, cot, tok, att, proj, prob, wall, small, dwr):
    blocks, images, span, width = tok.shape
    length = blocks * span
    heads = width // HEAD_DIM
    split = pl.BlockSpec((blocks, 1, span, width), lambda i: (0, i, 0, 0))
    whole = lambda a: pl.BlockSpec(a.shape, lambda i: (0,) * len(a.shape))
    return pl.pallas_call(
        back_kernel,
        grid=(images,),
        in_specs=[
            split,
            split,
            split,
            split,
            pl.BlockSpec((1, length, width), lambda i: (i, 0, 0)),
            pl.BlockSpec((1, length, 3 * width), lambda i: (i, 0, 0)),
            pl.BlockSpec((1, heads, length, length), lambda i: (i, 0, 0, 0)),
            whole(wall),
            whole(small),
            whole(dwr),
        ],
        out_specs=[split, whole(wall)],
        out_shape=[
            jax.ShapeDtypeStruct(tok.shape, bf16),
            jax.ShapeDtypeStruct(wall.shape, bf16),
        ],
        scratch_shapes=[
            pltpu.VMEM((width, 4 * width), f32),
            pltpu.VMEM((LANES, width), f32),
            pltpu.VMEM((length, width), bf16),
            pltpu.VMEM((length, 3 * width), bf16),
        ],
        compiler_params=pltpu.CompilerParams(vmem_limit_bytes=VMEM_BYTES),
        cost_estimate=pl.CostEstimate(
            flops=4 * images * length * width * (4 * width + 3 * length),
            bytes_accessed=32 * 1024 * 1024,
            transcendentals=0,
        ),
        name="back",
    )(gin, middle, cot, tok, att, proj, prob, wall, small, dwr)


def kept_pairs(route_rows, token_live, order_rows, expert_count, capacity):
    labels = jnp.arange(expert_count, dtype=jnp.int32)
    alive = token_live > 0
    first_hot = ((route_rows[:, 0:1] == labels) & alive[:, None]).astype(bf16)
    second_hot = ((route_rows[:, 1:2] == labels) & alive[:, None]).astype(bf16)
    earlier = (order_rows[None, :] < order_rows[:, None]).astype(bf16)
    ahead = mm(earlier, jnp.concatenate([first_hot, second_hot], 1))
    ahead_first = ahead[:, :expert_count]
    ahead_second = ahead[:, expert_count:] + jnp.sum(first_hot.astype(f32), 0)
    return jnp.where(ahead_first < capacity, first_hot, 0) + jnp.where(
        ahead_second < capacity, second_hot, 0
    )


def local(
    fsdp,
    seq,
    tokens,
    ln1_gain,
    ln1_bias,
    w_qkv,
    w_out,
    ln2_gain,
    ln2_bias,
    w_router,
    w_in,
    w_down,
    padding,
    routes,
    priority,
    cotangent,
):
    images, span, width = tokens.shape
    expert_count, shard_rows = w_in.shape[0], w_in.shape[1]
    rows = images * span
    own = images // seq
    length = seq * span
    capacity = (2 * rows + expert_count - 1) // expert_count
    inner = math.gcd(fsdp, 8)
    outer = fsdp // inner
    if outer > 1:
        inner_groups = [[o * inner + n for n in range(inner)] for o in range(outer)]
        outer_groups = [[o * inner + n for o in range(outer)] for n in range(inner)]
    else:
        inner_groups = outer_groups = None
    seq_index = lax.axis_index("seq")

    columns = jnp.concatenate(
        [w_router] + [v[:, None] for v in (ln1_gain, ln1_bias, ln2_gain, ln2_bias)], 1
    )
    columns = jnp.pad(columns, ((0, 0), (0, LANES - columns.shape[1])))
    wall = lax.all_gather(
        jnp.concatenate([w_qkv, w_out, columns], 1), "fsdp", axis=0, tiled=True
    )
    wr = wall[:, 4 * width :]
    small = wr[:, :SMALL].astype(f32).T

    tok = lax.all_to_all(
        tokens.reshape(seq, own * span, width), "seq", split_axis=0, concat_axis=0, tiled=True
    ).reshape(seq, own, span, width)

    live = lax.dynamic_slice_in_dim(padding, seq_index * span, span, 1)
    kept = kept_pairs(
        routes.reshape(rows, 2), live.reshape(rows), priority.reshape(rows), expert_count, capacity
    )
    kept = jnp.swapaxes(kept.reshape(seq, own * span, expert_count), 1, 2)
    kept = jnp.pad(
        kept, ((0, 0), (0, MASK_ROWS - expert_count), (0, width - own * span))
    ).astype(bf16)
    cot = cotangent * live[:, :, None].astype(bf16)
    packed = jnp.concatenate([cot.reshape(seq, own * span, width), kept], 1)
    packed = lax.all_to_all(packed, "seq", split_axis=0, concat_axis=0, tiled=True)
    packed_all = lax.all_gather(
        packed, "fsdp", axis=0, tiled=False, axis_index_groups=inner_groups
    )

    mine = lax.dynamic_slice_in_dim(padding, seq_index * own, own, 0)
    vis = jnp.where(mine > 0, 0.0, neg_fill).astype(f32).reshape(own, 1, length)
    middle, two, proj, att, prob = front(tok, wall, small, vis)

    two_all = lax.all_gather(
        two.reshape(seq, own * span, width),
        "fsdp",
        axis=0,
        tiled=False,
        axis_index_groups=inner_groups,
    )
    win, wdn = w_in, w_down
    if outer > 1:
        win = lax.all_gather(win, "fsdp", axis=1, tiled=True, axis_index_groups=outer_groups)
        wdn = lax.all_gather(wdn, "fsdp", axis=1, tiled=True, axis_index_groups=outer_groups)
    hidden = expert_count * outer * shard_rows
    out_part, gin_part, dwin, dwdn, dwr = experts_all(
        two_all,
        packed_all,
        win.reshape(hidden, width),
        wdn.reshape(hidden, width),
        wr,
        expert_count,
    )
    gin = lax.psum_scatter(
        gin_part, "fsdp", scatter_dimension=0, tiled=False, axis_index_groups=inner_groups
    )
    combined = lax.psum_scatter(
        out_part, "fsdp", scatter_dimension=0, tiled=False, axis_index_groups=inner_groups
    )

    expert_grads = jnp.stack([dwin, dwdn]).reshape(2, expert_count, outer * shard_rows, width)
    if outer > 1:
        expert_grads = lax.psum_scatter(
            expert_grads, "fsdp", scatter_dimension=2, tiled=True, axis_index_groups=outer_groups
        )
    expert_grads = lax.psum(expert_grads, "seq").astype(f32)

    shape4 = (seq, own, span, width)
    alive = jnp.swapaxes(mine.reshape(own, seq, span), 0, 1)[:, :, :, None].astype(f32)
    outputs = (alive * (middle + combined.reshape(shape4).astype(f32))).astype(bf16)
    outputs = lax.all_to_all(
        outputs.reshape(seq, own * span, width), "seq", split_axis=0, concat_axis=0, tiled=True
    ).reshape(images, span, width)

    grad_tok, dwall = back(
        gin.reshape(shape4),
        middle,
        packed[:, : own * span].reshape(shape4),
        tok,
        att,
        proj,
        prob,
        wall,
        small,
        dwr,
    )
    grad_tokens = lax.all_to_all(
        grad_tok.reshape(seq, own * span, width), "seq", split_axis=0, concat_axis=0, tiled=True
    ).reshape(images, span, width)
    dense = lax.psum_scatter(dwall, "fsdp", scatter_dimension=0, tiled=True)
    dense = lax.psum(dense, "seq").astype(f32)
    tail = dense[:, 4 * width :]
    return (
        outputs,
        grad_tokens,
        tail[:, 4],
        tail[:, 5],
        dense[:, : 3 * width],
        dense[:, 3 * width : 4 * width],
        tail[:, 6],
        tail[:, 7],
        tail[:, :expert_count],
        expert_grads[0],
        expert_grads[1],
    )


def solution(mesh):
    rows = P("fsdp", "seq", None)
    in_specs = (
        rows,
        P("fsdp"),
        P("fsdp"),
        P("fsdp", None),
        P("fsdp", None),
        P("fsdp"),
        P("fsdp"),
        P("fsdp", None),
        P(None, "fsdp", None),
        P(None, "fsdp", None),
        P("fsdp", None),
        rows,
        P("fsdp", "seq"),
        rows,
    )
    out_specs = (
        rows,
        rows,
        P("fsdp"),
        P("fsdp"),
        P("fsdp", None),
        P("fsdp", None),
        P("fsdp"),
        P("fsdp"),
        P("fsdp", None),
        P(None, "fsdp", None),
        P(None, "fsdp", None),
    )
    return jax.shard_map(
        functools.partial(local, mesh.shape["fsdp"], mesh.shape["seq"]),
        mesh=mesh,
        in_specs=in_specs,
        out_specs=out_specs,
        check_vma=False,
    )
```

```python
import functools
import math

import jax
import jax.numpy as jnp
from jax import lax
from jax.experimental import pallas as pl
from jax.experimental.pallas import tpu as pltpu
from jax.sharding import PartitionSpec as P

HEAD_DIM = 64
LANES = 128
MASK_ROWS = 16
SMALL = 8
norm_eps = 1e-06
neg_fill = -1e30
f32 = jnp.float32
bf16 = jnp.bfloat16
VMEM_BYTES = 60 * 1024 * 1024


def mm(left, right, left_dim=1, right_dim=0):
    return lax.dot_general(
        left, right, (((left_dim,), (right_dim,)), ((), ())), preferred_element_type=f32
    )


def unit_norm(rows):
    centred = rows - jnp.mean(rows, -1, keepdims=True)
    inverse = lax.rsqrt(jnp.mean(centred * centred, -1, keepdims=True) + norm_eps)
    return centred * inverse, inverse


def norm_back(scaled, unit, inverse):
    return inverse * (
        scaled
        - jnp.mean(scaled, -1, keepdims=True)
        - unit * jnp.mean(scaled * unit, -1, keepdims=True)
    )


def half_turn(tile):
    return pltpu.roll(tile.astype(f32), HEAD_DIM, axis=1).astype(bf16)


def front_kernel(tok_ref, wall_ref, small_ref, vis_ref, mid_ref, two_first, two_second, proj_ref, att_ref, prob_ref):
    blocks, _, span, width = tok_ref.shape
    length = blocks * span
    rows = tok_ref[...].reshape(length, width).astype(f32)
    unit, _ = unit_norm(rows)
    one = (unit * small_ref[4:5] + small_ref[5:6]).astype(bf16)
    proj_ref[0] = mm(one, wall_ref[:, : 3 * width]).astype(bf16)
    lower = lax.broadcasted_iota(jnp.int32, (length, LANES), 1) < HEAD_DIM
    zero = jnp.zeros((length, LANES), bf16)
    bias = vis_ref[0]

    def soften(index, queries, keys):
        scores = mm(queries, keys, 1, 1) * (HEAD_DIM**-0.5) + bias
        shifted = jnp.exp(scores - jnp.max(scores, -1, keepdims=True))
        weights = (shifted / jnp.sum(shifted, -1, keepdims=True)).astype(bf16)
        prob_ref[0, index] = weights
        return weights

    for pair in range(width // LANES):
        first, second, third = (
            proj_ref[0, :, (3 * pair + n) * LANES : (3 * pair + n + 1) * LANES] for n in range(3)
        )
        weights_a = soften(2 * pair, jnp.where(lower, first, zero), half_turn(first))
        weights_b = soften(2 * pair + 1, jnp.where(lower, zero, second), half_turn(third))
        both = jnp.where(lower, mm(weights_a, second), mm(weights_b, third))
        att_ref[0, :, pair * LANES : (pair + 1) * LANES] = both.astype(bf16)
    middle = rows + mm(att_ref[0], wall_ref[:, 3 * width : 4 * width])
    mid_ref[...] = middle.reshape(mid_ref.shape)
    unit, _ = unit_norm(middle)
    two = (unit * small_ref[6:7] + small_ref[7:8]).astype(bf16)
    two_first[...] = two[: length // 2].reshape(two_first.shape)
    two_second[...] = two[length // 2 :].reshape(two_second.shape)


def front(tok, wall, small, vis):
    blocks, images, span, width = tok.shape
    length = blocks * span
    heads = width // HEAD_DIM
    split = pl.BlockSpec((blocks, 1, span, width), lambda i: (0, i, 0, 0))
    half = pl.BlockSpec((blocks // 2, 1, span, width), lambda i: (0, i, 0, 0))
    return pl.pallas_call(
        front_kernel,
        grid=(images,),
        in_specs=[
            split,
            pl.BlockSpec(wall.shape, lambda i: (0, 0)),
            pl.BlockSpec(small.shape, lambda i: (0, 0)),
            pl.BlockSpec((1, 1, length), lambda i: (i, 0, 0)),
        ],
        out_specs=[
            split,
            half,
            half,
            pl.BlockSpec((1, length, 3 * width), lambda i: (i, 0, 0)),
            pl.BlockSpec((1, length, width), lambda i: (i, 0, 0)),
            pl.BlockSpec((1, heads, length, length), lambda i: (i, 0, 0, 0)),
        ],
        out_shape=[
            jax.ShapeDtypeStruct(tok.shape, f32),
            jax.ShapeDtypeStruct((blocks // 2, images, span, width), bf16),
            jax.ShapeDtypeStruct((blocks // 2, images, span, width), bf16),
            jax.ShapeDtypeStruct((images, length, 3 * width), bf16),
            jax.ShapeDtypeStruct((images, length, width), bf16),
            jax.ShapeDtypeStruct((images, heads, length, length), bf16),
        ],
        compiler_params=pltpu.CompilerParams(vmem_limit_bytes=VMEM_BYTES),
        cost_estimate=pl.CostEstimate(
            flops=2 * images * length * width * (4 * width + 2 * length),
            bytes_accessed=16 * 1024 * 1024,
            transcendentals=images * heads * length * length,
        ),
        name="front",
    )(tok, wall, small, vis)


def gelu_parts(pre):
    bell = jnp.exp(-0.5 * pre * pre)
    size = jnp.abs(pre) * 0.7071067811865476
    frac = 1.0 / (1.0 + 0.3275911 * size)
    poly = frac * (
        0.254829592
        + frac * (-0.284496736 + frac * (1.421413741 + frac * (-1.453152027 + frac * 1.061405429)))
    )
    tail = 0.5 * poly * bell
    cumulative = jnp.where(pre >= 0, 1.0 - tail, tail)
    return pre * cumulative, cumulative + pre * bell * 0.3989422804014327


def expert_kernel(experts, roles, opening, *refs):
    refs = list(refs)
    count = len(roles)

    def take(number):
        taken, refs[:] = refs[:number], refs[number:]
        return taken

    two_parts, cot_parts = take(2 * count), take(2 * count)
    win_ref, wdn_ref, wr_ref = take(3)
    carried = [] if opening else take(3)
    out_even, out_odd, gin_even, gin_odd = take(4)
    if opening:
        acc_in, acc_dn, acc_r = take(3)
        two_buf, cot_buf, sems = take(3)
    else:
        dw_refs = take(2 * experts)
        (dwr_ref,) = take(1)
        two_buf, cot_buf, sems, acc_in, acc_dn, acc_r, acc_sems = take(7)
    _, blocks, span, width = two_buf.shape
    half = blocks // 2
    rows = blocks * span
    share = win_ref.shape[0] // experts
    step = pl.program_id(0)
    copies = []
    for k in range(count):
        group = []
        for h in range(2):
            at = pl.ds(h * half, half)
            group.append(
                pltpu.make_async_copy(two_parts[2 * k + h], two_buf.at[k, at], sems.at[k, h])
            )
            group.append(
                pltpu.make_async_copy(cot_parts[2 * k + h], cot_buf.at[k, at], sems.at[k, 2 + h])
            )
        copies.append(group)
    loads = [
        pltpu.make_async_copy(source, target, acc_sems.at[n])
        for n, (source, target) in enumerate(zip(carried, (acc_in, acc_dn, acc_r)))
    ]

    @pl.when(step == 0)
    def _():
        for k, group in enumerate(copies):
            for copy in group:
                copy.start()
            if k == 0:
                for load in loads:
                    load.start()
        if opening:
            acc_in[...] = jnp.zeros_like(acc_in)
            acc_dn[...] = jnp.zeros_like(acc_dn)
            acc_r[...] = jnp.zeros_like(acc_r)
        for load in loads:
            load.wait()

    for k, group in enumerate(copies):

        @pl.when(step == k)
        def _(group=group):
            for copy in group:
                copy.wait()

    two = two_buf[step].reshape(rows, width)
    cot = cot_buf[step, :, :span, :].reshape(rows, width)
    lane = lax.broadcasted_iota(jnp.int32, (rows, LANES), 1)
    chosen = (
        lax.broadcasted_iota(jnp.int32, (MASK_ROWS, LANES), 0)
        == lax.broadcasted_iota(jnp.int32, (MASK_ROWS, LANES), 1)
    ).astype(bf16)
    kept = jnp.concatenate(
        [mm(cot_buf[step, b, span : span + MASK_ROWS, :span], chosen, 0, 0) for b in range(blocks)],
        0,
    )
    wr = wr_ref[...]
    logits = jnp.where(lane < experts, mm(two, wr), neg_fill)
    shifted = jnp.exp(logits - jnp.max(logits, -1, keepdims=True))
    probs = shifted / jnp.sum(shifted, -1, keepdims=True)
    gates = probs * kept

    out_sum = None
    gin_sum = None
    grad_gate = jnp.zeros((rows, LANES), f32)
    per_chunk = 2 if experts % 2 == 0 else 1
    for chunk in range(experts // per_chunk):
        at = slice(chunk * per_chunk * share, (chunk + 1) * per_chunk * share)
        win, wdn = win_ref[at], wdn_ref[at]
        pre = mm(two, win, 1, 1)
        back_rows = mm(cot, wdn, 1, 1)
        hidden, slope = gelu_parts(pre)
        product = hidden * back_rows
        slope = slope * back_rows
        gated, grad_pre = [], []
        for n in range(per_chunk):
            expert = chunk * per_chunk + n
            here = slice(n * share, (n + 1) * share)
            gate = gates[:, expert : expert + 1]
            gated.append(hidden[:, here] * gate)
            grad_pre.append(slope[:, here] * gate)
            grad_gate = jnp.where(
                lane == expert, jnp.sum(product[:, here], -1, keepdims=True), grad_gate
            )
        gated = jnp.concatenate(gated, 1).astype(bf16)
        grad_pre = jnp.concatenate(grad_pre, 1).astype(bf16)
        out_part = mm(gated, wdn)
        gin_part = mm(grad_pre, win)
        out_sum = out_part if out_sum is None else out_sum + out_part
        gin_sum = gin_part if gin_sum is None else gin_sum + gin_part
        acc_in[at] += mm(grad_pre, two, 0, 0)
        acc_dn[at] += mm(gated, cot, 0, 0)
    grad_gate = grad_gate * kept
    grad_logits = probs * (grad_gate - jnp.sum(probs * grad_gate, -1, keepdims=True))
    grad_logits = grad_logits.astype(bf16)
    gin_sum = gin_sum + mm(grad_logits, wr, 1, 1)
    acc_r[...] += mm(grad_logits, two, 0, 0)[:SMALL]
    out_rows = out_sum.astype(bf16).reshape(blocks, span, width)
    gin_rows = gin_sum.astype(bf16).reshape(blocks, span, width)
    odd = functools.reduce(jnp.logical_or, [step == k for k, r in enumerate(roles) if r % 2])

    @pl.when(odd)
    def _():
        out_odd[0] = out_rows
        gin_odd[0] = gin_rows

    @pl.when(jnp.logical_not(odd))
    def _():
        out_even[0] = out_rows
        gin_even[0] = gin_rows

    if not opening:

        @pl.when(step == count - 1)
        def _():
            for expert in range(experts):
                at = slice(expert * share, (expert + 1) * share)
                dw_refs[expert][...] = acc_in[at].astype(bf16)
                dw_refs[experts + expert][...] = acc_dn[at].astype(bf16)
            dwr_ref[...] = acc_r[...]


PLACE = {0: 0, 1: 0, 2: 0, 3: 0, 6: 1, 7: 1, 4: 2, 5: 2}


def experts_call(two, cot, roles, win, wdn, wr, experts, carried):
    opening = carried is None
    count = len(roles)
    half, span, width = two[roles[0]][0].shape
    hidden = win.shape[0]
    share = hidden // experts
    anywhere = pl.BlockSpec(memory_space=pl.ANY)
    whole = lambda a: pl.BlockSpec(a.shape, lambda k: (0,) * len(a.shape), pipeline_mode=pl.Buffered(1))

    def held(parity):
        own = [k for k, r in enumerate(roles) if r % 2 == parity]
        places = [PLACE[roles[max([o for o in own if o <= k] or own[:1])]] for k in range(count)]

        def index(k):
            place = places[0]
            for n in range(1, count):
                if places[n] != places[n - 1]:
                    place = jnp.where(k >= n, places[n], place)
            return (place, 0, 0, 0)

        return pl.BlockSpec((1, 2 * half, span, width), index)

    pile = jax.ShapeDtypeStruct((max(PLACE[r] for r in roles) + 1, 2 * half, span, width), bf16)
    big = jax.ShapeDtypeStruct((hidden, width), f32)
    little = jax.ShapeDtypeStruct((SMALL, width), f32)
    if opening:
        extra = [big, big, little]
    else:
        extra = [jax.ShapeDtypeStruct((share, width), bf16)] * (2 * experts) + [little]
    scratch = [
        pltpu.VMEM((count, 2 * half, span, width), bf16),
        pltpu.VMEM((count, 2 * half, span + MASK_ROWS, width), bf16),
        pltpu.SemaphoreType.DMA((count, 4)),
    ]
    if not opening:
        scratch += [pltpu.VMEM(a.shape, f32) for a in (big, big, little)]
        scratch += [pltpu.SemaphoreType.DMA((3,))]
    tokens = count * 2 * half * span
    return pl.pallas_call(
        functools.partial(expert_kernel, experts, roles, opening),
        grid=(count,),
        in_specs=[anywhere] * (4 * count)
        + [whole(win), whole(wdn), whole(wr)]
        + [anywhere] * (0 if opening else 3),
        out_specs=[held(0), held(1), held(0), held(1)] + [whole(a) for a in extra],
        out_shape=[pile] * 4 + extra,
        scratch_shapes=scratch,
        compiler_params=pltpu.CompilerParams(vmem_limit_bytes=VMEM_BYTES),
        cost_estimate=pl.CostEstimate(
            flops=12 * tokens * width * hidden,
            bytes_accessed=8 * tokens * width + 8 * hidden * width,
            transcendentals=tokens * hidden,
        ),
        name="experts_own" if opening else "experts_rest",
    )(
        *[part for r in roles for part in two[r]],
        *[part for r in roles for part in cot[r]],
        win,
        wdn,
        wr,
        *([] if opening else carried),
    )


def flip(array, fsdp, bit):
    return lax.ppermute(array, "fsdp", [(n, n ^ bit) for n in range(fsdp)])


def gather_halves(first, second, fsdp):
    send = lambda array, bit: flip(array, fsdp, bit)
    parts = {0: (first, second)}
    parts[2] = (send(first, 2), send(second, 2))
    parts[4] = (send(first, 4), send(second, 4))
    parts[1] = (send(first, 1), send(second, 1))
    parts[6] = (send(parts[2][0], 4), send(parts[4][1], 2))
    for r in (2, 4, 6):
        parts[r + 1] = (send(parts[r][0], 1), send(parts[r][1], 1))
    return parts


def plus(*arrays):
    return sum(a.astype(f32) for a in arrays).astype(bf16)


def scatter_sum(own, partner, evens, odds, fsdp):
    half = own.shape[1] // 2
    send = lambda array, bit: flip(array, fsdp, bit)
    merged = plus(evens, send(odds, 1))
    got_x = send(merged[0:2, :half], 2)
    got_y = send(merged[1:3, half:], 4)
    last_y = send(plus(merged[2, :half], got_x[1]), 4)
    last_x = send(plus(merged[0, half:], got_y[0]), 2)
    own = (own[0], send(partner, 1)[0])
    return jnp.concatenate(
        [
            plus(own[0][:half], own[1][:half], got_x[0], last_y),
            plus(own[0][half:], own[1][half:], got_y[1], last_x),
        ],
        0,
    )


def line_sum(chunks, seq):
    index = lax.axis_index("seq")
    if seq != 4:
        return [lax.psum(c, "seq") for c in chunks]
    outer = (index == 0) | (index == 3)
    totals = []
    previous = None
    for chunk in chunks:
        if previous is not None:
            chunk, previous = lax.optimization_barrier((chunk, previous))
        previous = lax.ppermute(chunk, "seq", [(0, 1), (3, 2)])
        pair = plus(chunk, previous)
        total = plus(pair, lax.ppermute(pair, "seq", [(1, 2), (2, 1)]))
        back_total = lax.ppermute(total, "seq", [(1, 0), (2, 3)])
        totals.append(jnp.where(outer, back_total, total))
    return totals


def back_kernel(
    gin_ref, mid_ref, cot_ref, tok_ref, att_ref, proj_ref, prob_ref, wall_ref, small_ref, dwr_ref,
    gtok_ref, dwall_ref, acc, acc_small, gatt, gproj,
):
    blocks, _, span, width = tok_ref.shape
    length = blocks * span
    step = pl.program_id(0)

    @pl.when(step == 0)
    def _():
        acc[...] = jnp.zeros_like(acc)
        acc_small[...] = jnp.zeros_like(acc_small)
        acc_small[:SMALL] = dwr_ref[...]

    gin = gin_ref[...].reshape(length, width).astype(f32)
    unit_two, inverse_two = unit_norm(mid_ref[...].reshape(length, width))
    acc_small[6:7] += jnp.sum(gin * unit_two, 0, keepdims=True)
    acc_small[7:8] += jnp.sum(gin, 0, keepdims=True)
    grad_middle = cot_ref[...].reshape(length, width).astype(f32) + norm_back(
        gin * small_ref[6:7], unit_two, inverse_two
    )
    branch = grad_middle.astype(bf16)
    acc[:, 3 * width : 4 * width] += mm(att_ref[0], branch, 0, 0)
    gatt[...] = mm(branch, wall_ref[:, 3 * width : 4 * width], 1, 1).astype(bf16)
    lower = lax.broadcasted_iota(jnp.int32, (length, LANES), 1) < HEAD_DIM
    zero = jnp.zeros((length, LANES), bf16)
    scale = HEAD_DIM**-0.5

    def score_grad(weights, grad_weights):
        weights = weights.astype(f32)
        product = weights * grad_weights
        return (product - weights * jnp.sum(product, -1, keepdims=True)).astype(bf16)

    for pair in range(width // LANES):
        places = [slice((3 * pair + n) * LANES, (3 * pair + n + 1) * LANES) for n in range(3)]
        first, second, third = (proj_ref[0, :, place] for place in places)
        first_r, second_r, third_r = half_turn(first), half_turn(second), half_turn(third)
        grad = gatt[:, pair * LANES : (pair + 1) * LANES]
        weights_a, weights_b = prob_ref[0, 2 * pair], prob_ref[0, 2 * pair + 1]
        ds_a = score_grad(weights_a, mm(jnp.where(lower, grad, zero), second, 1, 1))
        ds_b = score_grad(weights_b, mm(jnp.where(lower, zero, grad), third, 1, 1))
        gproj[:, places[0]] = (
            jnp.where(lower, mm(ds_a, first_r), mm(ds_a, first_r, 0, 0)) * scale
        ).astype(bf16)
        gproj[:, places[1]] = jnp.where(
            lower, mm(weights_a, grad, 0, 0), mm(ds_b, third_r) * scale
        ).astype(bf16)
        gproj[:, places[2]] = jnp.where(
            lower, mm(ds_b, second_r, 0, 0) * scale, mm(weights_b, grad, 0, 0)
        ).astype(bf16)
    unit_one, inverse_one = unit_norm(tok_ref[...].reshape(length, width).astype(f32))
    one = (unit_one * small_ref[4:5] + small_ref[5:6]).astype(bf16)
    grad_one = mm(gproj[...], wall_ref[:, : 3 * width], 1, 1)
    acc_small[4:5] += jnp.sum(grad_one * unit_one, 0, keepdims=True)
    acc_small[5:6] += jnp.sum(grad_one, 0, keepdims=True)
    grad_tok = grad_middle + norm_back(grad_one * small_ref[4:5], unit_one, inverse_one)
    gtok_ref[...] = grad_tok.astype(bf16).reshape(gtok_ref.shape)
    acc[:, : 3 * width] += mm(one, gproj[...], 0, 0)

    @pl.when(step == pl.num_programs(0) - 1)
    def _():
        dwall_ref[:, : 4 * width] = acc[...].astype(bf16)
        dwall_ref[:, 4 * width :] = acc_small[...].T.astype(bf16)


def back(gin, middle, cot, tok, att, proj, prob, wall, small, dwr):
    blocks, images, span, width = tok.shape
    length = blocks * span
    heads = width // HEAD_DIM
    split = pl.BlockSpec((blocks, 1, span, width), lambda i: (0, i, 0, 0))
    whole = lambda a: pl.BlockSpec(a.shape, lambda i: (0,) * len(a.shape))
    return pl.pallas_call(
        back_kernel,
        grid=(images,),
        in_specs=[
            split,
            split,
            split,
            split,
            pl.BlockSpec((1, length, width), lambda i: (i, 0, 0)),
            pl.BlockSpec((1, length, 3 * width), lambda i: (i, 0, 0)),
            pl.BlockSpec((1, heads, length, length), lambda i: (i, 0, 0, 0)),
            whole(wall),
            whole(small),
            whole(dwr),
        ],
        out_specs=[split, whole(wall)],
        out_shape=[
            jax.ShapeDtypeStruct(tok.shape, bf16),
            jax.ShapeDtypeStruct(wall.shape, bf16),
        ],
        scratch_shapes=[
            pltpu.VMEM((width, 4 * width), f32),
            pltpu.VMEM((LANES, width), f32),
            pltpu.VMEM((length, width), bf16),
            pltpu.VMEM((length, 3 * width), bf16),
        ],
        compiler_params=pltpu.CompilerParams(vmem_limit_bytes=VMEM_BYTES),
        cost_estimate=pl.CostEstimate(
            flops=4 * images * length * width * (4 * width + 3 * length),
            bytes_accessed=32 * 1024 * 1024,
            transcendentals=0,
        ),
        name="back",
    )(gin, middle, cot, tok, att, proj, prob, wall, small, dwr)


def kept_pairs(route_rows, token_live, order_rows, expert_count, capacity):
    labels = jnp.arange(expert_count, dtype=jnp.int32)
    alive = token_live > 0
    first_hot = ((route_rows[:, 0:1] == labels) & alive[:, None]).astype(bf16)
    second_hot = ((route_rows[:, 1:2] == labels) & alive[:, None]).astype(bf16)
    earlier = (order_rows[None, :] < order_rows[:, None]).astype(bf16)
    ahead = mm(earlier, jnp.concatenate([first_hot, second_hot], 1))
    ahead_first = ahead[:, :expert_count]
    ahead_second = ahead[:, expert_count:] + jnp.sum(first_hot.astype(f32), 0)
    return jnp.where(ahead_first < capacity, first_hot, 0) + jnp.where(
        ahead_second < capacity, second_hot, 0
    )


def local(
    fsdp,
    seq,
    tokens,
    ln1_gain,
    ln1_bias,
    w_qkv,
    w_out,
    ln2_gain,
    ln2_bias,
    w_router,
    w_in,
    w_down,
    padding,
    routes,
    priority,
    cotangent,
):
    images, span, width = tokens.shape
    expert_count, shard_rows = w_in.shape[0], w_in.shape[1]
    rows = images * span
    own = images // seq
    length = seq * span
    capacity = (2 * rows + expert_count - 1) // expert_count
    inner = math.gcd(fsdp, 8)
    outer = fsdp // inner
    if outer > 1:
        outer_groups = [[o * inner + n for o in range(outer)] for n in range(inner)]
    else:
        outer_groups = None
    seq_index = lax.axis_index("seq")

    columns = jnp.concatenate(
        [w_router] + [v[:, None] for v in (ln1_gain, ln1_bias, ln2_gain, ln2_bias)], 1
    )
    columns = jnp.pad(columns, ((0, 0), (0, LANES - columns.shape[1])))
    wall = lax.all_gather(
        jnp.concatenate([w_qkv, w_out, columns], 1), "fsdp", axis=0, tiled=True
    )
    wr = wall[:, 4 * width :]
    small = wr[:, :SMALL].astype(f32).T

    tok = lax.all_to_all(
        tokens.reshape(seq, own * span, width), "seq", split_axis=0, concat_axis=0, tiled=True
    ).reshape(seq, own, span, width)

    live = lax.dynamic_slice_in_dim(padding, seq_index * span, span, 1)
    kept = kept_pairs(
        routes.reshape(rows, 2), live.reshape(rows), priority.reshape(rows), expert_count, capacity
    )
    kept = jnp.swapaxes(kept.reshape(seq, own * span, expert_count), 1, 2)
    kept = jnp.pad(
        kept, ((0, 0), (0, MASK_ROWS - expert_count), (0, width - own * span))
    ).astype(bf16)
    cot = cotangent * live[:, :, None].astype(bf16)
    packed = jnp.concatenate([cot.reshape(seq, own * span, width), kept], 1)
    packed = lax.all_to_all(packed, "seq", split_axis=0, concat_axis=0, tiled=True)
    cot_parts = gather_halves(packed[: seq // 2], packed[seq // 2 :], fsdp)

    mine = lax.dynamic_slice_in_dim(padding, seq_index * own, own, 0)
    vis = jnp.where(mine > 0, 0.0, neg_fill).astype(f32).reshape(own, 1, length)
    middle, two_first, two_second, proj, att, prob = front(tok, wall, small, vis)
    half_shape = (seq // 2, own * span, width)
    two_parts = gather_halves(two_first.reshape(half_shape), two_second.reshape(half_shape), fsdp)

    win, wdn = w_in, w_down
    if outer > 1:
        win = lax.all_gather(win, "fsdp", axis=1, tiled=True, axis_index_groups=outer_groups)
        wdn = lax.all_gather(wdn, "fsdp", axis=1, tiled=True, axis_index_groups=outer_groups)
    hidden = expert_count * outer * shard_rows
    win, wdn = win.reshape(hidden, width), wdn.reshape(hidden, width)
    out_0, out_1, gin_0, gin_1, *carried = experts_call(
        two_parts, cot_parts, (0, 1), win, wdn, wr, expert_count, None
    )
    out_even, out_odd, gin_even, gin_odd, *grads = experts_call(
        two_parts, cot_parts, (2, 4, 3, 5, 6, 7), win, wdn, wr, expert_count, carried
    )
    dwr = grads.pop()
    gin = scatter_sum(gin_0, gin_1, gin_even, gin_odd, fsdp)
    combined = scatter_sum(out_0, out_1, out_even, out_odd, fsdp)

    if outer > 1:
        grads = [
            lax.psum_scatter(
                g, "fsdp", scatter_dimension=0, tiled=True, axis_index_groups=outer_groups
            )
            for g in grads
        ]
    grads = [g.astype(f32) for g in line_sum(grads, seq)]
    expert_grads = (jnp.stack(grads[:expert_count]), jnp.stack(grads[expert_count:]))

    shape4 = (seq, own, span, width)
    alive = jnp.swapaxes(mine.reshape(own, seq, span), 0, 1)[:, :, :, None].astype(f32)
    outputs = (alive * (middle + combined.reshape(shape4).astype(f32))).astype(bf16)
    outputs = lax.all_to_all(
        outputs.reshape(seq, own * span, width), "seq", split_axis=0, concat_axis=0, tiled=True
    ).reshape(images, span, width)

    grad_tok, dwall = back(
        gin.reshape(shape4),
        middle,
        packed[:, : own * span].reshape(shape4),
        tok,
        att,
        proj,
        prob,
        wall,
        small,
        dwr,
    )
    grad_tokens = lax.all_to_all(
        grad_tok.reshape(seq, own * span, width), "seq", split_axis=0, concat_axis=0, tiled=True
    ).reshape(images, span, width)
    dense = lax.psum_scatter(dwall, "fsdp", scatter_dimension=0, tiled=True)
    dense = lax.psum(dense, "seq").astype(f32)
    tail = dense[:, 4 * width :]
    return (
        outputs,
        grad_tokens,
        tail[:, 4],
        tail[:, 5],
        dense[:, : 3 * width],
        dense[:, 3 * width : 4 * width],
        tail[:, 6],
        tail[:, 7],
        tail[:, :expert_count],
        expert_grads[0],
        expert_grads[1],
    )


def solution(mesh):
    rows = P("fsdp", "seq", None)
    in_specs = (
        rows,
        P("fsdp"),
        P("fsdp"),
        P("fsdp", None),
        P("fsdp", None),
        P("fsdp"),
        P("fsdp"),
        P("fsdp", None),
        P(None, "fsdp", None),
        P(None, "fsdp", None),
        P("fsdp", None),
        rows,
        P("fsdp", "seq"),
        rows,
    )
    out_specs = (
        rows,
        rows,
        P("fsdp"),
        P("fsdp"),
        P("fsdp", None),
        P("fsdp", None),
        P("fsdp"),
        P("fsdp"),
        P("fsdp", None),
        P(None, "fsdp", None),
        P(None, "fsdp", None),
    )
    return jax.shard_map(
        functools.partial(local, mesh.shape["fsdp"], mesh.shape["seq"]),
        mesh=mesh,
        in_specs=in_specs,
        out_specs=out_specs,
        check_vma=False,
    )
```

```python
import functools
import math

import jax
import jax.numpy as jnp
from jax import lax
from jax.experimental import pallas as pl
from jax.experimental.pallas import tpu as pltpu
from jax.sharding import PartitionSpec as P

HEAD_DIM = 64
LANES = 128
MASK_ROWS = 16
SMALL = 8
norm_eps = 1e-06
neg_fill = -1e30
f32 = jnp.float32
bf16 = jnp.bfloat16
VMEM_BYTES = 60 * 1024 * 1024
SHORT = pl.CostEstimate(flops=1000, bytes_accessed=1000, transcendentals=0)


def mm(left, right, left_dim=1, right_dim=0):
    return lax.dot_general(
        left, right, (((left_dim,), (right_dim,)), ((), ())), preferred_element_type=f32
    )


def unit_norm(rows):
    centred = rows - jnp.mean(rows, -1, keepdims=True)
    inverse = lax.rsqrt(jnp.mean(centred * centred, -1, keepdims=True) + norm_eps)
    return centred * inverse, inverse


def norm_back(scaled, unit, inverse):
    return inverse * (
        scaled
        - jnp.mean(scaled, -1, keepdims=True)
        - unit * jnp.mean(scaled * unit, -1, keepdims=True)
    )


def half_turn(tile):
    return pltpu.roll(tile.astype(f32), HEAD_DIM, axis=1).astype(bf16)


def wall_copies(pieces, offsets, place_ref, wall_ref, sems):
    copies = []
    for n, (piece, (r, skip)) in enumerate(zip(pieces, offsets)):
        rows = piece.shape[0]
        shard = wall_ref.shape[0] // 8
        start = pl.multiple_of((place_ref[0] ^ r) * shard + skip, 16)
        copies.append(pltpu.make_async_copy(piece, wall_ref.at[pl.ds(start, rows)], sems.at[n]))
    return copies


def front_kernel(offsets, *refs):
    pieces = refs[: len(offsets)]
    tok_ref, vis_ref, place_ref = refs[len(offsets) : len(offsets) + 3]
    mid_ref, two_ref, proj_ref, att_ref, prob_ref, full_ref, wr_ref, small_ref = refs[
        len(offsets) + 3 : len(offsets) + 11
    ]
    wall_ref, sems, full_sem = refs[len(offsets) + 11 :]
    blocks, _, span, width = tok_ref.shape
    length = blocks * span
    save = pltpu.make_async_copy(wall_ref, full_ref, full_sem)

    @pl.when(pl.program_id(0) == 0)
    def _():
        copies = wall_copies(pieces, offsets, place_ref, wall_ref, sems)
        for copy in copies:
            copy.start()
        for copy in copies:
            copy.wait()
        save.start()
        columns = wall_ref[:, 4 * width :]
        wr_ref[...] = columns
        small_ref[...] = columns.astype(f32).T[:SMALL]

    rows = tok_ref[...].reshape(length, width).astype(f32)
    unit, _ = unit_norm(rows)
    one = (unit * small_ref[4:5] + small_ref[5:6]).astype(bf16)
    proj_ref[0] = mm(one, wall_ref[:, : 3 * width]).astype(bf16)
    lower = lax.broadcasted_iota(jnp.int32, (length, LANES), 1) < HEAD_DIM
    zero = jnp.zeros((length, LANES), bf16)
    bias = vis_ref[0]

    def soften(index, queries, keys):
        scores = mm(queries, keys, 1, 1) * (HEAD_DIM**-0.5) + bias
        shifted = jnp.exp(scores - jnp.max(scores, -1, keepdims=True))
        weights = (shifted / jnp.sum(shifted, -1, keepdims=True)).astype(bf16)
        prob_ref[0, index] = weights
        return weights

    for pair in range(width // LANES):
        first, second, third = (
            proj_ref[0, :, (3 * pair + n) * LANES : (3 * pair + n + 1) * LANES] for n in range(3)
        )
        weights_a = soften(2 * pair, jnp.where(lower, first, zero), half_turn(first))
        weights_b = soften(2 * pair + 1, jnp.where(lower, zero, second), half_turn(third))
        both = jnp.where(lower, mm(weights_a, second), mm(weights_b, third))
        att_ref[0, :, pair * LANES : (pair + 1) * LANES] = both.astype(bf16)
    middle = rows + mm(att_ref[0], wall_ref[:, 3 * width : 4 * width])
    mid_ref[...] = middle.reshape(mid_ref.shape)
    unit, _ = unit_norm(middle)
    two_ref[...] = (unit * small_ref[6:7] + small_ref[7:8]).astype(bf16).reshape(two_ref.shape)

    @pl.when(pl.program_id(0) == pl.num_programs(0) - 1)
    def _():
        save.wait()


def front(tok, pieces, offsets, vis, place):
    blocks, images, span, width = tok.shape
    length = blocks * span
    heads = width // HEAD_DIM
    split = pl.BlockSpec((blocks, 1, span, width), lambda i: (0, i, 0, 0))
    anywhere = pl.BlockSpec(memory_space=pl.ANY)
    columns = pieces[0].shape[1]
    return pl.pallas_call(
        functools.partial(front_kernel, offsets),
        grid=(images,),
        in_specs=[anywhere] * len(pieces)
        + [
            split,
            pl.BlockSpec((1, 1, length), lambda i: (i, 0, 0)),
            pl.BlockSpec(memory_space=pltpu.SMEM),
        ],
        out_specs=[
            split,
            split,
            pl.BlockSpec((1, length, 3 * width), lambda i: (i, 0, 0)),
            pl.BlockSpec((1, length, width), lambda i: (i, 0, 0)),
            pl.BlockSpec((1, heads, length, length), lambda i: (i, 0, 0, 0)),
            anywhere,
            pl.BlockSpec((width, LANES), lambda i: (0, 0)),
            pl.BlockSpec((SMALL, width), lambda i: (0, 0)),
        ],
        out_shape=[
            jax.ShapeDtypeStruct(tok.shape, f32),
            jax.ShapeDtypeStruct(tok.shape, bf16),
            jax.ShapeDtypeStruct((images, length, 3 * width), bf16),
            jax.ShapeDtypeStruct((images, length, width), bf16),
            jax.ShapeDtypeStruct((images, heads, length, length), bf16),
            jax.ShapeDtypeStruct((width, columns), bf16),
            jax.ShapeDtypeStruct((width, LANES), bf16),
            jax.ShapeDtypeStruct((SMALL, width), f32),
        ],
        scratch_shapes=[
            pltpu.VMEM((width, columns), bf16),
            pltpu.SemaphoreType.DMA((len(pieces),)),
            pltpu.SemaphoreType.DMA(()),
        ],
        compiler_params=pltpu.CompilerParams(vmem_limit_bytes=VMEM_BYTES),
        cost_estimate=SHORT,
        name="front",
    )(*pieces, tok, vis, place)


def gelu_parts(pre):
    bell = jnp.exp(-0.5 * pre * pre)
    size = jnp.abs(pre) * 0.7071067811865476
    frac = 1.0 / (1.0 + 0.3275911 * size)
    poly = frac * (
        0.254829592
        + frac * (-0.284496736 + frac * (1.421413741 + frac * (-1.453152027 + frac * 1.061405429)))
    )
    tail = 0.5 * poly * bell
    cumulative = jnp.where(pre >= 0, 1.0 - tail, tail)
    return pre * cumulative, cumulative + pre * bell * 0.3989422804014327


def expert_kernel(plan, *refs):
    refs = list(refs)

    def take(number):
        taken, refs[:] = refs[:number], refs[number:]
        return taken

    groups = len(plan["two"])
    two_parts = [take(n) for n in plan["two"]]
    cot_parts = [take(n) for n in plan["cot"]]
    win_ref, wdn_ref, wr_ref = take(3)
    dw_carried = take(2) if plan["carried"] else None
    sums_carried = take(2 * groups) if plan["sums"] else None
    dw_refs = take(plan["halves"])
    (dwr_ref,) = take(1)
    out_refs, gin_refs = take(groups), take(groups)
    two_buf, cot_buf, sems, out_acc, gin_acc, gate_acc, probs_buf, kept_buf, acc_in, acc_dn = refs
    _, blocks, span, width = two_buf.shape
    rows = blocks * span
    experts = plan["experts"]
    expert, group = pl.program_id(0), pl.program_id(1)
    last = pl.num_programs(0) - 1
    lane = lax.broadcasted_iota(jnp.int32, (rows, LANES), 1)

    copies = []
    for k in range(groups):
        some = []
        for parts, buffer in ((two_parts[k], two_buf), (cot_parts[k], cot_buf)):
            at = 0
            for part in parts:
                size = part.shape[0]
                some.append((part, buffer.at[k, pl.ds(at, size)]))
                at += size
        copies.append(
            [pltpu.make_async_copy(s, t, sems.at[k, n]) for n, (s, t) in enumerate(some)]
        )

    @pl.when((expert == 0) & (group == 0))
    def _():
        for some in copies:
            for copy in some:
                copy.start()
        dwr_ref[...] = dw_carried[1][...] if plan["carried"] else jnp.zeros_like(dwr_ref)

    for k, some in enumerate(copies):

        @pl.when((expert == 0) & (group == k))
        def _(k=k, some=some):
            for copy in some:
                copy.wait()
            if plan["sums"]:
                out_acc[k] = sums_carried[k][...].reshape(rows, width).astype(f32)
                gin_acc[k] = sums_carried[groups + k][...].reshape(rows, width).astype(f32)

    @pl.when(expert == 0)
    def _():
        chosen = (
            lax.broadcasted_iota(jnp.int32, (MASK_ROWS, LANES), 0)
            == lax.broadcasted_iota(jnp.int32, (MASK_ROWS, LANES), 1)
        ).astype(bf16)
        kept = jnp.concatenate(
            [
                mm(cot_buf[group, b, span : span + MASK_ROWS, :span], chosen, 0, 0)
                for b in range(blocks)
            ],
            0,
        )
        logits = mm(two_buf[group].reshape(rows, width), wr_ref[...])
        logits = jnp.where(lane < experts, logits, neg_fill)
        shifted = jnp.exp(logits - jnp.max(logits, -1, keepdims=True))
        probs_buf[group] = shifted / jnp.sum(shifted, -1, keepdims=True)
        kept_buf[group] = kept
        if not plan["sums"]:
            out_acc[group] = jnp.zeros((rows, width), f32)
            gin_acc[group] = jnp.zeros((rows, width), f32)
        gate_acc[group] = jnp.zeros((rows, LANES), f32)

    @pl.when(group == 0)
    def _():
        if plan["carried"]:
            acc_in[...] = dw_carried[0][0, 0].astype(f32)
            acc_dn[...] = dw_carried[0][0, 1].astype(f32)
        else:
            acc_in[...] = jnp.zeros_like(acc_in)
            acc_dn[...] = jnp.zeros_like(acc_dn)

    two = two_buf[group].reshape(rows, width)
    cot = cot_buf[group, :, :span, :].reshape(rows, width)
    here = lane == expert + plan["first"]
    gate = jnp.sum(
        jnp.where(here, probs_buf[group] * kept_buf[group], 0.0), -1, keepdims=True
    )
    pre = mm(two, win_ref[0], 1, 1)
    back_rows = mm(cot, wdn_ref[0], 1, 1)
    hidden, slope = gelu_parts(pre)
    product = jnp.sum(hidden * back_rows, -1, keepdims=True)
    gate_acc[group] += jnp.where(here, product, 0.0)
    gated = (hidden * gate).astype(bf16)
    grad_pre = (slope * back_rows * gate).astype(bf16)
    out_acc[group] += mm(gated, wdn_ref[0])
    gin_acc[group] += mm(grad_pre, win_ref[0])
    acc_in[...] += mm(grad_pre, two, 0, 0)
    acc_dn[...] += mm(gated, cot, 0, 0)

    @pl.when(group == groups - 1)
    def _():
        size = acc_in.shape[0] // plan["halves"]
        for n in range(plan["halves"]):
            dw_refs[n][0, 0] = acc_in[n * size : (n + 1) * size].astype(bf16)
            dw_refs[n][0, 1] = acc_dn[n * size : (n + 1) * size].astype(bf16)

    for k in range(groups):

        @pl.when((expert == last) & (group == k))
        def _(k=k):
            probs = probs_buf[k]
            grad_gate = gate_acc[k] * kept_buf[k]
            grad_logits = probs * (grad_gate - jnp.sum(probs * grad_gate, -1, keepdims=True))
            grad_logits = grad_logits.astype(bf16)
            dwr_ref[...] += mm(grad_logits, two_buf[k].reshape(rows, width), 0, 0)[:SMALL]
            gin = gin_acc[k] + mm(grad_logits, wr_ref[...], 1, 1)
            out_refs[k][...] = out_acc[k].astype(bf16).reshape(blocks, span, width)
            gin_refs[k][...] = gin.astype(bf16).reshape(blocks, span, width)


def experts_call(two, cot, win, wdn, wr, span_of, carried, sums, name):
    groups = len(two)
    experts, hidden, width = win.shape
    first, many = span_of
    blocks = sum(a.shape[0] for a in two[0])
    span = two[0][0].shape[1]
    rows = blocks * span
    plan = dict(
        two=[len(parts) for parts in two],
        cot=[len(parts) for parts in cot],
        experts=experts,
        first=first,
        carried=carried is not None,
        sums=sums is not None,
        halves=1 if carried is None else 2,
    )
    halves = plan["halves"]
    anywhere = pl.BlockSpec(memory_space=pl.ANY)
    once = lambda a: pl.BlockSpec(
        a.shape, lambda e, g: (0,) * len(a.shape), pipeline_mode=pl.Buffered(1)
    )
    per_expert = pl.BlockSpec((1, hidden, width), lambda e, g: (e + first, 0, 0))
    result = jax.ShapeDtypeStruct((blocks, span, width), bf16)
    little = jax.ShapeDtypeStruct((SMALL, width), f32)
    part = jax.ShapeDtypeStruct((many, 2, hidden // halves, width), bf16)
    part_spec = pl.BlockSpec((1, 2, hidden // halves, width), lambda e, g: (e, 0, 0, 0))
    carried_spec = pl.BlockSpec((1, 2, hidden, width), lambda e, g: (e + first, 0, 0, 0))
    pieces = [a for parts in two for a in parts] + [a for parts in cot for a in parts]
    tokens = groups * rows
    outs = pl.pallas_call(
        functools.partial(expert_kernel, plan),
        grid=(many, groups),
        in_specs=[anywhere] * len(pieces)
        + [per_expert, per_expert, once(wr)]
        + ([carried_spec, once(little)] if carried is not None else [])
        + [once(result)] * len(sums or []),
        out_specs=[part_spec] * halves + [once(little)] + [once(result)] * (2 * groups),
        out_shape=[part] * halves + [little] + [result] * (2 * groups),
        scratch_shapes=[
            pltpu.VMEM((groups, blocks, span, width), bf16),
            pltpu.VMEM((groups, blocks, span + MASK_ROWS, width), bf16),
            pltpu.SemaphoreType.DMA((groups, 4)),
            pltpu.VMEM((groups, rows, width), f32),
            pltpu.VMEM((groups, rows, width), f32),
            pltpu.VMEM((groups, rows, LANES), f32),
            pltpu.VMEM((groups, rows, LANES), f32),
            pltpu.VMEM((groups, rows, LANES), f32),
            pltpu.VMEM((hidden, width), f32),
            pltpu.VMEM((hidden, width), f32),
        ],
        compiler_params=pltpu.CompilerParams(vmem_limit_bytes=VMEM_BYTES),
        cost_estimate=SHORT,
        name=name,
    )(*pieces, win, wdn, wr, *(carried or []), *(sums or []))
    dw, outs = outs[:halves], outs[halves:]
    return dw, outs[0], list(outs[1 : 1 + groups]), list(outs[1 + groups :])


def flip(array, fsdp, bits):
    return lax.ppermute(array, "fsdp", [(n, n ^ bits) for n in range(fsdp)])


def tie(value, *others):
    return lax.optimization_barrier((value, others))[0]


def plus(*arrays):
    return sum(a.astype(f32) for a in arrays).astype(bf16)


def line_sum(arrays, seq):
    if seq != 4:
        return [a for array in arrays for a in lax.psum(array, "seq").astype(f32)]
    index = lax.axis_index("seq")
    outer = (index == 0) | (index == 3)
    totals = []
    for array in arrays:
        inward = lax.ppermute(array, "seq", [(0, 1), (3, 2)])
        for n in range(array.shape[0]):
            pair = plus(array[n], inward[n])
            total = plus(pair, lax.ppermute(pair, "seq", [(1, 2), (2, 1)]))
            back_total = lax.ppermute(total, "seq", [(1, 0), (2, 3)])
            totals.append(jnp.where(outer, back_total, total).astype(f32))
    return totals


def back_kernel(
    gin_0, gin_2, gin_4, gin_6, mid_ref, cot_ref, tok_ref, att_ref, proj_ref, prob_ref, wall_ref,
    small_ref, dwr_ref, place_ref, gtok_ref, even_ref, odd_ref, acc, acc_small, gatt, gproj,
):
    blocks, _, span, width = tok_ref.shape
    length = blocks * span
    step = pl.program_id(0)

    @pl.when(step == 0)
    def _():
        acc[...] = jnp.zeros_like(acc)
        acc_small[...] = jnp.zeros_like(acc_small)
        acc_small[:SMALL] = dwr_ref[...]

    gin = sum(ref[...].reshape(length, width).astype(f32) for ref in (gin_0, gin_2, gin_4, gin_6))
    unit_two, inverse_two = unit_norm(mid_ref[...].reshape(length, width))
    acc_small[6:7] += jnp.sum(gin * unit_two, 0, keepdims=True)
    acc_small[7:8] += jnp.sum(gin, 0, keepdims=True)
    grad_middle = cot_ref[...].reshape(length, width).astype(f32) + norm_back(
        gin * small_ref[6:7], unit_two, inverse_two
    )
    branch = grad_middle.astype(bf16)
    acc[:, 3 * width : 4 * width] += mm(att_ref[0], branch, 0, 0)
    gatt[...] = mm(branch, wall_ref[:, 3 * width : 4 * width], 1, 1).astype(bf16)
    lower = lax.broadcasted_iota(jnp.int32, (length, LANES), 1) < HEAD_DIM
    zero = jnp.zeros((length, LANES), bf16)
    scale = HEAD_DIM**-0.5

    def score_grad(weights, grad_weights):
        weights = weights.astype(f32)
        product = weights * grad_weights
        return (product - weights * jnp.sum(product, -1, keepdims=True)).astype(bf16)

    for pair in range(width // LANES):
        places = [slice((3 * pair + n) * LANES, (3 * pair + n + 1) * LANES) for n in range(3)]
        first, second, third = (proj_ref[0, :, place] for place in places)
        first_r, second_r, third_r = half_turn(first), half_turn(second), half_turn(third)
        grad = gatt[:, pair * LANES : (pair + 1) * LANES]
        weights_a, weights_b = prob_ref[0, 2 * pair], prob_ref[0, 2 * pair + 1]
        ds_a = score_grad(weights_a, mm(jnp.where(lower, grad, zero), second, 1, 1))
        ds_b = score_grad(weights_b, mm(jnp.where(lower, zero, grad), third, 1, 1))
        gproj[:, places[0]] = (
            jnp.where(lower, mm(ds_a, first_r), mm(ds_a, first_r, 0, 0)) * scale
        ).astype(bf16)
        gproj[:, places[1]] = jnp.where(
            lower, mm(weights_a, grad, 0, 0), mm(ds_b, third_r) * scale
        ).astype(bf16)
        gproj[:, places[2]] = jnp.where(
            lower, mm(ds_b, second_r, 0, 0) * scale, mm(weights_b, grad, 0, 0)
        ).astype(bf16)
    unit_one, inverse_one = unit_norm(tok_ref[...].reshape(length, width).astype(f32))
    one = (unit_one * small_ref[4:5] + small_ref[5:6]).astype(bf16)
    grad_one = mm(gproj[...], wall_ref[:, : 3 * width], 1, 1)
    acc_small[4:5] += jnp.sum(grad_one * unit_one, 0, keepdims=True)
    acc_small[5:6] += jnp.sum(grad_one, 0, keepdims=True)
    grad_tok = grad_middle + norm_back(grad_one * small_ref[4:5], unit_one, inverse_one)
    gtok_ref[...] = grad_tok.astype(bf16).reshape(gtok_ref.shape)
    acc[:, : 3 * width] += mm(one, gproj[...], 0, 0)

    @pl.when(step == pl.num_programs(0) - 1)
    def _():
        acc[:, 4 * width :] = acc_small[...].T
        shard = width // 8
        for r in range(8):
            start = pl.multiple_of((place_ref[0] ^ r) * shard, 8)
            target = odd_ref if r % 2 else even_ref
            target[r // 2] = acc[pl.ds(start, shard)].astype(bf16)


def back(gins, middle, cot, tok, att, proj, prob, wall, small, dwr, place):
    blocks, images, span, width = tok.shape
    length = blocks * span
    heads = width // HEAD_DIM
    split = pl.BlockSpec((blocks, 1, span, width), lambda i: (0, i, 0, 0))
    whole = lambda a: pl.BlockSpec(a.shape, lambda i: (0,) * len(a.shape))
    parts = jax.ShapeDtypeStruct((4, width // 8, wall.shape[1]), bf16)
    return pl.pallas_call(
        back_kernel,
        grid=(images,),
        in_specs=[split] * 7
        + [
            pl.BlockSpec((1, length, width), lambda i: (i, 0, 0)),
            pl.BlockSpec((1, length, 3 * width), lambda i: (i, 0, 0)),
            pl.BlockSpec((1, heads, length, length), lambda i: (i, 0, 0, 0)),
            whole(wall),
            whole(small),
            whole(dwr),
            pl.BlockSpec(memory_space=pltpu.SMEM),
        ],
        out_specs=[split, whole(parts), whole(parts)],
        out_shape=[jax.ShapeDtypeStruct(tok.shape, bf16), parts, parts],
        scratch_shapes=[
            pltpu.VMEM(wall.shape, f32),
            pltpu.VMEM((LANES, width), f32),
            pltpu.VMEM((length, width), bf16),
            pltpu.VMEM((length, 3 * width), bf16),
        ],
        compiler_params=pltpu.CompilerParams(vmem_limit_bytes=VMEM_BYTES),
        cost_estimate=SHORT,
        name="back",
    )(*gins, middle, cot, tok, att, proj, prob, wall, small, dwr, place)


def kept_pairs(route_rows, token_live, order_rows, expert_count, capacity):
    labels = jnp.arange(expert_count, dtype=jnp.int32)
    alive = token_live > 0
    first_hot = ((route_rows[:, 0:1] == labels) & alive[:, None]).astype(bf16)
    second_hot = ((route_rows[:, 1:2] == labels) & alive[:, None]).astype(bf16)
    earlier = (order_rows[None, :] < order_rows[:, None]).astype(bf16)
    ahead = mm(earlier, jnp.concatenate([first_hot, second_hot], 1))
    ahead_first = ahead[:, :expert_count]
    ahead_second = ahead[:, expert_count:] + jnp.sum(first_hot.astype(f32), 0)
    return jnp.where(ahead_first < capacity, first_hot, 0) + jnp.where(
        ahead_second < capacity, second_hot, 0
    )


def local(
    fsdp,
    seq,
    tokens,
    ln1_gain,
    ln1_bias,
    w_qkv,
    w_out,
    ln2_gain,
    ln2_bias,
    w_router,
    w_in,
    w_down,
    padding,
    routes,
    priority,
    cotangent,
):
    images, span, width = tokens.shape
    expert_count, shard_rows = w_in.shape[0], w_in.shape[1]
    rows = images * span
    own = images // seq
    length = seq * span
    capacity = (2 * rows + expert_count - 1) // expert_count
    outer = fsdp // 8
    if outer > 1:
        outer_groups = [[o * 8 + n for o in range(outer)] for n in range(8)]
    spread = functools.partial(flip, fsdp=fsdp)
    seq_index = lax.axis_index("seq")
    place = lax.axis_index("fsdp") if outer == 1 else jnp.int32(0)
    place = place.astype(jnp.int32).reshape(1)

    columns = jnp.concatenate(
        [w_router] + [v[:, None] for v in (ln1_gain, ln1_bias, ln2_gain, ln2_bias)], 1
    )
    columns = jnp.pad(columns, ((0, 0), (0, LANES - columns.shape[1])))
    shard = jnp.concatenate([w_qkv, w_out, columns], 1)
    if outer == 1:
        cut = width // 16
        from_x, from_y = spread(shard, bits=2), spread(shard, bits=4)
        even = [
            (0, 0, shard),
            (2, 0, from_x),
            (4, 0, from_y),
            (6, 0, spread(from_x[:cut], bits=4)),
            (6, cut, spread(from_y[cut:], bits=2)),
        ]
        pieces = even + [(r + 1, skip, spread(a, bits=1)) for r, skip, a in even]
        offsets = [(r, skip) for r, skip, _ in pieces]
        pieces = [a for _, _, a in pieces]
    else:
        full = lax.all_gather(shard, "fsdp", axis=0, tiled=True)
        offsets = [(n, 0) for n in range(8)]
        pieces = list(full.reshape(8, width // 8, -1))

    tokens, shard = lax.optimization_barrier((tokens, shard))
    tok = lax.all_to_all(
        tokens.reshape(seq, own * span, width), "seq", split_axis=0, concat_axis=0, tiled=True
    ).reshape(seq, own, span, width)

    live = lax.dynamic_slice_in_dim(padding, seq_index * span, span, 1)
    kept = kept_pairs(
        routes.reshape(rows, 2), live.reshape(rows), priority.reshape(rows), expert_count, capacity
    )
    kept = jnp.swapaxes(kept.reshape(seq, own * span, expert_count), 1, 2)
    kept = jnp.pad(
        kept, ((0, 0), (0, MASK_ROWS - expert_count), (0, width - own * span))
    ).astype(bf16)
    cot = cotangent * live[:, :, None].astype(bf16)
    packed = jnp.concatenate([cot.reshape(seq, own * span, width), kept], 1)
    packed, tok = lax.optimization_barrier((packed, tok))
    packed = lax.all_to_all(packed, "seq", split_axis=0, concat_axis=0, tiled=True)
    cot_x, cot_y = spread(packed, bits=2), spread(packed, bits=4)
    half = seq // 2
    cot_far = [spread(cot_x[:half], bits=4), spread(cot_y[half:], bits=2)]

    win, wdn = w_in, w_down
    if outer > 1:
        win = lax.all_gather(win, "fsdp", axis=1, tiled=True, axis_index_groups=outer_groups)
        wdn = lax.all_gather(wdn, "fsdp", axis=1, tiled=True, axis_index_groups=outer_groups)
    win = jnp.concatenate([win, spread(win, bits=1)], 1)
    wdn = jnp.concatenate([wdn, spread(wdn, bits=1)], 1)

    mine = lax.dynamic_slice_in_dim(padding, seq_index * own, own, 0)
    vis = jnp.where(mine > 0, 0.0, neg_fill).astype(f32).reshape(own, 1, length)
    middle, two, proj, att, prob, wall, wr, small = front(tok, pieces, offsets, vis, place)
    two = two.reshape(seq, own * span, width)
    two_far = [[spread(two, bits=bits)] for bits in (2, 4, 6)]

    (dw,), dwr, out_0, gin_0 = experts_call(
        [[two]], [[packed]], win, wdn, wr, (0, expert_count), None, None, "experts_own"
    )
    cots = [[cot_x], [cot_y], cot_far]
    half = expert_count // 2
    raws = []
    outs = gins = None
    for first, many, name in ((0, half, "experts_far"), (half, expert_count - half, "experts_last")):
        sums = None if outs is None else outs + gins
        (dw_kept, dw_sent), dwr, outs, gins = experts_call(
            two_far, cots, win, wdn, wr, (first, many), [dw, dwr], sums, name
        )
        raw = plus(dw_kept, spread(dw_sent, bits=1))
        if outer > 1:
            raw = lax.psum_scatter(
                raw, "fsdp", scatter_dimension=2, tiled=True, axis_index_groups=outer_groups
            )
        raws.append(raw)
    gins = gin_0 + [spread(a, bits=bits) for a, bits in zip(gins, (2, 4, 6))]
    gins = tie(gins, raws)
    grads = line_sum(raws, seq)
    expert_grads = tuple(jnp.stack([g[n] for g in grads]) for n in range(2))

    shape4 = (seq, own, span, width)
    grad_tok, dense_even, dense_odd = back(
        [a.reshape(shape4) for a in gins],
        middle,
        packed[:, : own * span].reshape(shape4),
        tok,
        att,
        proj,
        prob,
        wall,
        small,
        dwr,
        place,
    )
    alive = jnp.swapaxes(mine.reshape(own, seq, span), 0, 1)[:, :, :, None].astype(f32)
    outs, grad_tok = lax.optimization_barrier((outs, grad_tok))
    outs = out_0 + [spread(a, bits=bits) for a, bits in zip(outs, (2, 4, 6))]
    combined = sum(a.reshape(shape4).astype(f32) for a in outs)
    outputs = (alive * (middle + combined)).astype(bf16)
    outputs = lax.all_to_all(
        outputs.reshape(seq, own * span, width), "seq", split_axis=0, concat_axis=0, tiled=True
    ).reshape(images, span, width)

    grad_tokens = lax.all_to_all(
        grad_tok.reshape(seq, own * span, width), "seq", split_axis=0, concat_axis=0, tiled=True
    ).reshape(images, span, width)
    if outer == 1:
        received = spread(dense_odd, bits=1)
        merged = [plus(dense_even[n], received[n]) for n in range(4)]
        dense = plus(merged[0], *[spread(merged[n], bits=2 * n) for n in (1, 2, 3)])
    else:
        dense = jnp.stack([dense_even, dense_odd], 1).reshape(width, -1)
        dense = lax.psum_scatter(dense, "fsdp", scatter_dimension=0, tiled=True)
    (dense,) = line_sum([dense[None]], seq)
    tail = dense[:, 4 * width :]
    return (
        outputs,
        grad_tokens,
        tail[:, 4],
        tail[:, 5],
        dense[:, : 3 * width],
        dense[:, 3 * width : 4 * width],
        tail[:, 6],
        tail[:, 7],
        tail[:, :expert_count],
        expert_grads[0],
        expert_grads[1],
    )


def solution(mesh):
    rows = P("fsdp", "seq", None)
    in_specs = (
        rows,
        P("fsdp"),
        P("fsdp"),
        P("fsdp", None),
        P("fsdp", None),
        P("fsdp"),
        P("fsdp"),
        P("fsdp", None),
        P(None, "fsdp", None),
        P(None, "fsdp", None),
        P("fsdp", None),
        rows,
        P("fsdp", "seq"),
        rows,
    )
    out_specs = (
        rows,
        rows,
        P("fsdp"),
        P("fsdp"),
        P("fsdp", None),
        P("fsdp", None),
        P("fsdp"),
        P("fsdp"),
        P("fsdp", None),
        P(None, "fsdp", None),
        P(None, "fsdp", None),
    )
    return jax.shard_map(
        functools.partial(local, mesh.shape["fsdp"], mesh.shape["seq"]),
        mesh=mesh,
        in_specs=in_specs,
        out_specs=out_specs,
        check_vma=False,
    )
```

```python
import functools
import math

import jax
import jax.numpy as jnp
from jax import lax
from jax.experimental import pallas as pl
from jax.experimental.pallas import tpu as pltpu
from jax.sharding import PartitionSpec as P

HEAD_DIM = 64
LANES = 128
MASK_ROWS = 16
SMALL = 8
norm_eps = 1e-06
neg_fill = -1e30
f32 = jnp.float32
bf16 = jnp.bfloat16
VMEM_BYTES = 60 * 1024 * 1024
SHORT = pl.CostEstimate(flops=1000, bytes_accessed=1000, transcendentals=0)


def mm(left, right, left_dim=1, right_dim=0):
    return lax.dot_general(
        left, right, (((left_dim,), (right_dim,)), ((), ())), preferred_element_type=f32
    )


def unit_norm(rows):
    centred = rows - jnp.mean(rows, -1, keepdims=True)
    inverse = lax.rsqrt(jnp.mean(centred * centred, -1, keepdims=True) + norm_eps)
    return centred * inverse, inverse


def norm_back(scaled, unit, inverse):
    return inverse * (
        scaled
        - jnp.mean(scaled, -1, keepdims=True)
        - unit * jnp.mean(scaled * unit, -1, keepdims=True)
    )


def half_turn(tile):
    return pltpu.roll(tile.astype(f32), HEAD_DIM, axis=1).astype(bf16)


def wall_copies(pieces, offsets, place_ref, wall_ref, sems):
    copies = []
    for n, (piece, (r, skip)) in enumerate(zip(pieces, offsets)):
        rows = piece.shape[0]
        shard = wall_ref.shape[0] // 8
        start = pl.multiple_of((place_ref[0] ^ r) * shard + skip, 16)
        copies.append(pltpu.make_async_copy(piece, wall_ref.at[pl.ds(start, rows)], sems.at[n]))
    return copies


def front_kernel(offsets, *refs):
    pieces = refs[: len(offsets)]
    tok_ref, vis_ref, place_ref = refs[len(offsets) : len(offsets) + 3]
    mid_ref, two_ref, proj_ref, att_ref, prob_ref, full_ref, wr_ref, small_ref = refs[
        len(offsets) + 3 : len(offsets) + 11
    ]
    wall_ref, sems, full_sem = refs[len(offsets) + 11 :]
    blocks, _, span, width = tok_ref.shape
    length = blocks * span
    save = pltpu.make_async_copy(wall_ref, full_ref, full_sem)

    @pl.when(pl.program_id(0) == 0)
    def _():
        copies = wall_copies(pieces, offsets, place_ref, wall_ref, sems)
        for copy in copies:
            copy.start()
        for copy in copies:
            copy.wait()
        save.start()
        columns = wall_ref[:, 4 * width :]
        wr_ref[...] = columns
        small_ref[...] = columns.astype(f32).T[:SMALL]

    rows = tok_ref[...].reshape(length, width).astype(f32)
    unit, _ = unit_norm(rows)
    one = (unit * small_ref[4:5] + small_ref[5:6]).astype(bf16)
    proj_ref[0] = mm(one, wall_ref[:, : 3 * width]).astype(bf16)
    lower = lax.broadcasted_iota(jnp.int32, (length, LANES), 1) < HEAD_DIM
    zero = jnp.zeros((length, LANES), bf16)
    bias = vis_ref[0]

    def soften(index, queries, keys):
        scores = mm(queries, keys, 1, 1) * (HEAD_DIM**-0.5) + bias
        shifted = jnp.exp(scores - jnp.max(scores, -1, keepdims=True))
        weights = (shifted / jnp.sum(shifted, -1, keepdims=True)).astype(bf16)
        prob_ref[0, index] = weights
        return weights

    for pair in range(width // LANES):
        first, second, third = (
            proj_ref[0, :, (3 * pair + n) * LANES : (3 * pair + n + 1) * LANES] for n in range(3)
        )
        weights_a = soften(2 * pair, jnp.where(lower, first, zero), half_turn(first))
        weights_b = soften(2 * pair + 1, jnp.where(lower, zero, second), half_turn(third))
        both = jnp.where(lower, mm(weights_a, second), mm(weights_b, third))
        att_ref[0, :, pair * LANES : (pair + 1) * LANES] = both.astype(bf16)
    middle = rows + mm(att_ref[0], wall_ref[:, 3 * width : 4 * width])
    mid_ref[...] = middle.reshape(mid_ref.shape)
    unit, _ = unit_norm(middle)
    two_ref[...] = (unit * small_ref[6:7] + small_ref[7:8]).astype(bf16).reshape(two_ref.shape)

    @pl.when(pl.program_id(0) == pl.num_programs(0) - 1)
    def _():
        save.wait()


def front(tok, pieces, offsets, vis, place):
    blocks, images, span, width = tok.shape
    length = blocks * span
    heads = width // HEAD_DIM
    split = pl.BlockSpec((blocks, 1, span, width), lambda i: (0, i, 0, 0))
    anywhere = pl.BlockSpec(memory_space=pl.ANY)
    columns = pieces[0].shape[1]
    return pl.pallas_call(
        functools.partial(front_kernel, offsets),
        grid=(images,),
        in_specs=[anywhere] * len(pieces)
        + [
            split,
            pl.BlockSpec((1, 1, length), lambda i: (i, 0, 0)),
            pl.BlockSpec(memory_space=pltpu.SMEM),
        ],
        out_specs=[
            split,
            split,
            pl.BlockSpec((1, length, 3 * width), lambda i: (i, 0, 0)),
            pl.BlockSpec((1, length, width), lambda i: (i, 0, 0)),
            pl.BlockSpec((1, heads, length, length), lambda i: (i, 0, 0, 0)),
            anywhere,
            pl.BlockSpec((width, LANES), lambda i: (0, 0)),
            pl.BlockSpec((SMALL, width), lambda i: (0, 0)),
        ],
        out_shape=[
            jax.ShapeDtypeStruct(tok.shape, f32),
            jax.ShapeDtypeStruct(tok.shape, bf16),
            jax.ShapeDtypeStruct((images, length, 3 * width), bf16),
            jax.ShapeDtypeStruct((images, length, width), bf16),
            jax.ShapeDtypeStruct((images, heads, length, length), bf16),
            jax.ShapeDtypeStruct((width, columns), bf16),
            jax.ShapeDtypeStruct((width, LANES), bf16),
            jax.ShapeDtypeStruct((SMALL, width), f32),
        ],
        scratch_shapes=[
            pltpu.VMEM((width, columns), bf16),
            pltpu.SemaphoreType.DMA((len(pieces),)),
            pltpu.SemaphoreType.DMA(()),
        ],
        compiler_params=pltpu.CompilerParams(vmem_limit_bytes=VMEM_BYTES),
        cost_estimate=SHORT,
        name="front",
    )(*pieces, tok, vis, place)


def gelu_parts(pre):
    bell = jnp.exp(-0.5 * pre * pre)
    size = jnp.abs(pre) * 0.7071067811865476
    frac = 1.0 / (1.0 + 0.3275911 * size)
    poly = frac * (
        0.254829592
        + frac * (-0.284496736 + frac * (1.421413741 + frac * (-1.453152027 + frac * 1.061405429)))
    )
    tail = 0.5 * poly * bell
    cumulative = jnp.where(pre >= 0, 1.0 - tail, tail)
    return pre * cumulative, cumulative + pre * bell * 0.3989422804014327


def expert_kernel(plan, *refs):
    refs = list(refs)

    def take(number):
        taken, refs[:] = refs[:number], refs[number:]
        return taken

    groups = len(plan["two"])
    two_parts = [take(n) for n in plan["two"]]
    cot_parts = [take(n) for n in plan["cot"]]
    win_ref, wdn_ref, wr_ref = take(3)
    dw_carried = take(2) if plan["carried"] else None
    sums_carried = take(2 * groups) if plan["sums"] else []
    dw_refs = take(plan["halves"])
    (dwr_ref,) = take(1)
    results = take(2 * groups)
    two_buf, cot_buf, sems, out_acc, gin_acc, gate_acc, probs_buf, kept_buf, acc_in, acc_dn = take(10)
    stage, stage_sems = take(2)
    dw_buf, dw_sem = take(2) if plan["carried"] else (None, None)
    _, blocks, span, width = two_buf.shape
    rows = blocks * span
    experts = plan["experts"]
    expert, group = pl.program_id(0), pl.program_id(1)
    last = pl.num_programs(0) - 1
    lane = lax.broadcasted_iota(jnp.int32, (rows, LANES), 1)

    copies = []
    for k in range(groups):
        some = []
        for parts, buffer in ((two_parts[k], two_buf), (cot_parts[k], cot_buf)):
            at = 0
            for part in parts:
                size = part.shape[0]
                some.append((part, buffer.at[k, pl.ds(at, size)]))
                at += size
        copies.append(
            [pltpu.make_async_copy(s, t, sems.at[k, n]) for n, (s, t) in enumerate(some)]
        )

    loads = [
        pltpu.make_async_copy(ref, stage.at[n], stage_sems.at[n])
        for n, ref in enumerate(sums_carried)
    ]
    stores = [
        pltpu.make_async_copy(stage.at[n], ref, stage_sems.at[n]) for n, ref in enumerate(results)
    ]
    if plan["carried"]:
        dw_load = pltpu.make_async_copy(dw_carried[0].at[plan["first"]], dw_buf, dw_sem)

    @pl.when((expert == 0) & (group == 0))
    def _():
        for k, some in enumerate(copies):
            for copy in some:
                copy.start()
        for load in loads:
            load.start()
        if plan["carried"]:
            dw_load.start()
        dwr_ref[...] = dw_carried[1][...] if plan["carried"] else jnp.zeros_like(dwr_ref)

    for k, some in enumerate(copies):

        @pl.when((expert == 0) & (group == k))
        def _(some=some):
            for copy in some:
                copy.wait()

    @pl.when(expert == 0)
    def _():
        chosen = (
            lax.broadcasted_iota(jnp.int32, (MASK_ROWS, LANES), 0)
            == lax.broadcasted_iota(jnp.int32, (MASK_ROWS, LANES), 1)
        ).astype(bf16)
        kept = jnp.concatenate(
            [
                mm(cot_buf[group, b, span : span + MASK_ROWS, :span], chosen, 0, 0)
                for b in range(blocks)
            ],
            0,
        )
        logits = mm(two_buf[group].reshape(rows, width), wr_ref[...])
        logits = jnp.where(lane < experts, logits, neg_fill)
        shifted = jnp.exp(logits - jnp.max(logits, -1, keepdims=True))
        probs_buf[group] = shifted / jnp.sum(shifted, -1, keepdims=True)
        kept_buf[group] = kept
        out_acc[group] = jnp.zeros((rows, width), f32)
        gin_acc[group] = jnp.zeros((rows, width), f32)
        gate_acc[group] = jnp.zeros((rows, LANES), f32)

    @pl.when(group == 0)
    def _():
        acc_in[...] = jnp.zeros_like(acc_in)
        acc_dn[...] = jnp.zeros_like(acc_dn)

    two = two_buf[group].reshape(rows, width)
    cot = cot_buf[group, :, :span, :].reshape(rows, width)
    here = lane == expert + plan["first"]
    gate = jnp.sum(
        jnp.where(here, probs_buf[group] * kept_buf[group], 0.0), -1, keepdims=True
    )
    pre = mm(two, win_ref[0], 1, 1)
    back_rows = mm(cot, wdn_ref[0], 1, 1)
    hidden, slope = gelu_parts(pre)
    product = jnp.sum(hidden * back_rows, -1, keepdims=True)
    gate_acc[group] += jnp.where(here, product, 0.0)
    gated = (hidden * gate).astype(bf16)
    grad_pre = (slope * back_rows * gate).astype(bf16)
    out_acc[group] += mm(gated, wdn_ref[0])
    gin_acc[group] += mm(grad_pre, win_ref[0])
    acc_in[...] += mm(grad_pre, two, 0, 0)
    acc_dn[...] += mm(gated, cot, 0, 0)

    @pl.when(group == groups - 1)
    def _():
        size = acc_in.shape[0] // plan["halves"]
        if plan["carried"]:
            dw_load.wait()
        for n in range(plan["halves"]):
            at = slice(n * size, (n + 1) * size)
            for m, acc in enumerate((acc_in, acc_dn)):
                total = acc[at]
                if plan["carried"]:
                    total = total + dw_buf[m, at].astype(f32)
                dw_refs[n][0, m] = total.astype(bf16)

    for k in range(groups):

        @pl.when((expert == last) & (group == k))
        def _(k=k):
            probs = probs_buf[k]
            grad_gate = gate_acc[k] * kept_buf[k]
            grad_logits = probs * (grad_gate - jnp.sum(probs * grad_gate, -1, keepdims=True))
            grad_logits = grad_logits.astype(bf16)
            dwr_ref[...] += mm(grad_logits, two_buf[k].reshape(rows, width), 0, 0)[:SMALL]
            both = out_acc[k], gin_acc[k] + mm(grad_logits, wr_ref[...], 1, 1)
            for n, value in zip((k, groups + k), both):
                if plan["sums"]:
                    loads[n].wait()
                    value = value + stage[n].reshape(rows, width).astype(f32)
                stage[n] = value.astype(bf16).reshape(blocks, span, width)
                stores[n].start()

    @pl.when((expert == last) & (group == groups - 1))
    def _():
        for store in stores:
            store.wait()


def experts_call(two, cot, win, wdn, wr, span_of, carried, sums, name):
    groups = len(two)
    experts, hidden, width = win.shape
    first, many = span_of
    blocks = sum(a.shape[0] for a in two[0])
    span = two[0][0].shape[1]
    rows = blocks * span
    plan = dict(
        two=[len(parts) for parts in two],
        cot=[len(parts) for parts in cot],
        experts=experts,
        first=first,
        carried=carried is not None,
        sums=sums is not None,
        halves=1 if carried is None else 2,
    )
    halves = plan["halves"]
    anywhere = pl.BlockSpec(memory_space=pl.ANY)
    once = lambda a: pl.BlockSpec(
        a.shape, lambda e, g: (0,) * len(a.shape), pipeline_mode=pl.Buffered(1)
    )
    per_expert = pl.BlockSpec((1, hidden, width), lambda e, g: (e + first, 0, 0))
    result = jax.ShapeDtypeStruct((blocks, span, width), bf16)
    little = jax.ShapeDtypeStruct((SMALL, width), f32)
    part = jax.ShapeDtypeStruct((many, 2, hidden // halves, width), bf16)
    part_spec = pl.BlockSpec((1, 2, hidden // halves, width), lambda e, g: (e, 0, 0, 0))
    pieces = [a for parts in two for a in parts] + [a for parts in cot for a in parts]
    tokens = groups * rows
    outs = pl.pallas_call(
        functools.partial(expert_kernel, plan),
        grid=(many, groups),
        in_specs=[anywhere] * len(pieces)
        + [per_expert, per_expert, once(wr)]
        + ([anywhere, once(little)] if carried is not None else [])
        + [anywhere] * len(sums or []),
        out_specs=[part_spec] * halves + [once(little)] + [anywhere] * (2 * groups),
        out_shape=[part] * halves + [little] + [result] * (2 * groups),
        scratch_shapes=[
            pltpu.VMEM((groups, blocks, span, width), bf16),
            pltpu.VMEM((groups, blocks, span + MASK_ROWS, width), bf16),
            pltpu.SemaphoreType.DMA((groups, 4)),
            pltpu.VMEM((groups, rows, width), f32),
            pltpu.VMEM((groups, rows, width), f32),
            pltpu.VMEM((groups, rows, LANES), f32),
            pltpu.VMEM((groups, rows, LANES), f32),
            pltpu.VMEM((groups, rows, LANES), f32),
            pltpu.VMEM((hidden, width), f32),
            pltpu.VMEM((hidden, width), f32),
            pltpu.VMEM((2 * groups, blocks, span, width), bf16),
            pltpu.SemaphoreType.DMA((2 * groups,)),
        ]
        + (
            [pltpu.VMEM((2, hidden, width), bf16), pltpu.SemaphoreType.DMA(())]
            if carried is not None
            else []
        ),
        compiler_params=pltpu.CompilerParams(vmem_limit_bytes=VMEM_BYTES),
        cost_estimate=SHORT,
        name=name,
    )(*pieces, win, wdn, wr, *(carried or []), *(sums or []))
    dw, outs = outs[:halves], outs[halves:]
    return dw, outs[0], list(outs[1 : 1 + groups]), list(outs[1 + groups :])


def flip(array, fsdp, bits):
    return lax.ppermute(array, "fsdp", [(n, n ^ bits) for n in range(fsdp)])


def tie(value, *others):
    return lax.optimization_barrier((value, others))[0]


def plus(*arrays):
    return sum(a.astype(f32) for a in arrays).astype(bf16)


class LineSum:
    def __init__(self, seq):
        self.seq = seq
        self.index = lax.axis_index("seq")
        self.outer = (self.index == 0) | (self.index == seq - 1)
        self.inward = self.exchanged = self.total = None
        self.raw = self.pair = None
        self.ready = []
        self.done = []

    def step(self, raw=None):
        if self.seq != 4:
            self.done += [] if raw is None else [lax.psum(raw, "seq")]
            return
        total = None if self.pair is None else plus(self.pair, self.exchanged)
        pair = None if self.raw is None else plus(self.raw, self.inward)
        if self.total is not None:
            self.done.append(jnp.where(self.outer, self.inward, self.total))
        self.raw, self.pair, self.total = raw, pair, total
        self.ready = [a for a in (raw, pair, total) if a is not None]
        if raw is not None or total is not None:
            if total is None:
                both = raw
            elif raw is None:
                both = total
            else:
                both = jnp.where(self.outer, raw, total)
            self.inward = lax.ppermute(both, "seq", [(0, 1), (1, 0), (2, 3), (3, 2)])
        if pair is not None:
            self.exchanged = lax.ppermute(pair, "seq", [(1, 2), (2, 1)])

    def finish(self, count):
        while len(self.done) < count:
            self.step()
        return self.done


def back_kernel(
    gin_0, gin_2, gin_4, gin_6, mid_ref, cot_ref, tok_ref, att_ref, proj_ref, prob_ref, wall_ref,
    small_ref, dwr_ref, place_ref, gtok_ref, even_ref, odd_ref, acc, acc_small, gatt, gproj,
):
    blocks, _, span, width = tok_ref.shape
    length = blocks * span
    step = pl.program_id(0)

    @pl.when(step == 0)
    def _():
        acc[...] = jnp.zeros_like(acc)
        acc_small[...] = jnp.zeros_like(acc_small)
        acc_small[:SMALL] = dwr_ref[...]

    gin = sum(ref[...].reshape(length, width).astype(f32) for ref in (gin_0, gin_2, gin_4, gin_6))
    unit_two, inverse_two = unit_norm(mid_ref[...].reshape(length, width))
    acc_small[6:7] += jnp.sum(gin * unit_two, 0, keepdims=True)
    acc_small[7:8] += jnp.sum(gin, 0, keepdims=True)
    grad_middle = cot_ref[...].reshape(length, width).astype(f32) + norm_back(
        gin * small_ref[6:7], unit_two, inverse_two
    )
    branch = grad_middle.astype(bf16)
    acc[:, 3 * width : 4 * width] += mm(att_ref[0], branch, 0, 0)
    gatt[...] = mm(branch, wall_ref[:, 3 * width : 4 * width], 1, 1).astype(bf16)
    lower = lax.broadcasted_iota(jnp.int32, (length, LANES), 1) < HEAD_DIM
    zero = jnp.zeros((length, LANES), bf16)
    scale = HEAD_DIM**-0.5

    def score_grad(weights, grad_weights):
        weights = weights.astype(f32)
        product = weights * grad_weights
        return (product - weights * jnp.sum(product, -1, keepdims=True)).astype(bf16)

    for pair in range(width // LANES):
        places = [slice((3 * pair + n) * LANES, (3 * pair + n + 1) * LANES) for n in range(3)]
        first, second, third = (proj_ref[0, :, place] for place in places)
        first_r, second_r, third_r = half_turn(first), half_turn(second), half_turn(third)
        grad = gatt[:, pair * LANES : (pair + 1) * LANES]
        weights_a, weights_b = prob_ref[0, 2 * pair], prob_ref[0, 2 * pair + 1]
        ds_a = score_grad(weights_a, mm(jnp.where(lower, grad, zero), second, 1, 1))
        ds_b = score_grad(weights_b, mm(jnp.where(lower, zero, grad), third, 1, 1))
        gproj[:, places[0]] = (
            jnp.where(lower, mm(ds_a, first_r), mm(ds_a, first_r, 0, 0)) * scale
        ).astype(bf16)
        gproj[:, places[1]] = jnp.where(
            lower, mm(weights_a, grad, 0, 0), mm(ds_b, third_r) * scale
        ).astype(bf16)
        gproj[:, places[2]] = jnp.where(
            lower, mm(ds_b, second_r, 0, 0) * scale, mm(weights_b, grad, 0, 0)
        ).astype(bf16)
    unit_one, inverse_one = unit_norm(tok_ref[...].reshape(length, width).astype(f32))
    one = (unit_one * small_ref[4:5] + small_ref[5:6]).astype(bf16)
    grad_one = mm(gproj[...], wall_ref[:, : 3 * width], 1, 1)
    acc_small[4:5] += jnp.sum(grad_one * unit_one, 0, keepdims=True)
    acc_small[5:6] += jnp.sum(grad_one, 0, keepdims=True)
    grad_tok = grad_middle + norm_back(grad_one * small_ref[4:5], unit_one, inverse_one)
    gtok_ref[...] = grad_tok.astype(bf16).reshape(gtok_ref.shape)
    acc[:, : 3 * width] += mm(one, gproj[...], 0, 0)

    @pl.when(step == pl.num_programs(0) - 1)
    def _():
        acc[:, 4 * width :] = acc_small[...].T
        shard = width // 8
        for r in range(8):
            start = pl.multiple_of((place_ref[0] ^ r) * shard, 8)
            target = odd_ref if r % 2 else even_ref
            target[r // 2] = acc[pl.ds(start, shard)].astype(bf16)


def back(gins, middle, cot, tok, att, proj, prob, wall, small, dwr, place):
    blocks, images, span, width = tok.shape
    length = blocks * span
    heads = width // HEAD_DIM
    split = pl.BlockSpec((blocks, 1, span, width), lambda i: (0, i, 0, 0))
    whole = lambda a: pl.BlockSpec(a.shape, lambda i: (0,) * len(a.shape))
    parts = jax.ShapeDtypeStruct((4, width // 8, wall.shape[1]), bf16)
    return pl.pallas_call(
        back_kernel,
        grid=(images,),
        in_specs=[split] * 7
        + [
            pl.BlockSpec((1, length, width), lambda i: (i, 0, 0)),
            pl.BlockSpec((1, length, 3 * width), lambda i: (i, 0, 0)),
            pl.BlockSpec((1, heads, length, length), lambda i: (i, 0, 0, 0)),
            whole(wall),
            whole(small),
            whole(dwr),
            pl.BlockSpec(memory_space=pltpu.SMEM),
        ],
        out_specs=[split, whole(parts), whole(parts)],
        out_shape=[jax.ShapeDtypeStruct(tok.shape, bf16), parts, parts],
        scratch_shapes=[
            pltpu.VMEM(wall.shape, f32),
            pltpu.VMEM((LANES, width), f32),
            pltpu.VMEM((length, width), bf16),
            pltpu.VMEM((length, 3 * width), bf16),
        ],
        compiler_params=pltpu.CompilerParams(vmem_limit_bytes=VMEM_BYTES),
        cost_estimate=SHORT,
        name="back",
    )(*gins, middle, cot, tok, att, proj, prob, wall, small, dwr, place)


def kept_pairs(route_rows, token_live, order_rows, expert_count, capacity):
    labels = jnp.arange(expert_count, dtype=jnp.int32)
    alive = token_live > 0
    first_hot = ((route_rows[:, 0:1] == labels) & alive[:, None]).astype(bf16)
    second_hot = ((route_rows[:, 1:2] == labels) & alive[:, None]).astype(bf16)
    earlier = (order_rows[None, :] < order_rows[:, None]).astype(bf16)
    ahead = mm(earlier, jnp.concatenate([first_hot, second_hot], 1))
    ahead_first = ahead[:, :expert_count]
    ahead_second = ahead[:, expert_count:] + jnp.sum(first_hot.astype(f32), 0)
    return jnp.where(ahead_first < capacity, first_hot, 0) + jnp.where(
        ahead_second < capacity, second_hot, 0
    )


def local(
    fsdp,
    seq,
    tokens,
    ln1_gain,
    ln1_bias,
    w_qkv,
    w_out,
    ln2_gain,
    ln2_bias,
    w_router,
    w_in,
    w_down,
    padding,
    routes,
    priority,
    cotangent,
):
    images, span, width = tokens.shape
    expert_count, shard_rows = w_in.shape[0], w_in.shape[1]
    rows = images * span
    own = images // seq
    length = seq * span
    capacity = (2 * rows + expert_count - 1) // expert_count
    outer = fsdp // 8
    if outer > 1:
        outer_groups = [[o * 8 + n for o in range(outer)] for n in range(8)]
    spread = functools.partial(flip, fsdp=fsdp)
    seq_index = lax.axis_index("seq")
    place = lax.axis_index("fsdp") if outer == 1 else jnp.int32(0)
    place = place.astype(jnp.int32).reshape(1)

    columns = jnp.concatenate(
        [w_router] + [v[:, None] for v in (ln1_gain, ln1_bias, ln2_gain, ln2_bias)], 1
    )
    columns = jnp.pad(columns, ((0, 0), (0, LANES - columns.shape[1])))
    shard = jnp.concatenate([w_qkv, w_out, columns], 1)
    if outer == 1:
        cut = width // 16
        from_x, from_y = spread(shard, bits=2), spread(shard, bits=4)
        even = [
            (0, 0, shard),
            (2, 0, from_x),
            (4, 0, from_y),
            (6, 0, spread(from_x[:cut], bits=4)),
            (6, cut, spread(from_y[cut:], bits=2)),
        ]
        pieces = even + [(r + 1, skip, spread(a, bits=1)) for r, skip, a in even]
        offsets = [(r, skip) for r, skip, _ in pieces]
        pieces = [a for _, _, a in pieces]
    else:
        full = lax.all_gather(shard, "fsdp", axis=0, tiled=True)
        offsets = [(n, 0) for n in range(8)]
        pieces = list(full.reshape(8, width // 8, -1))

    tokens, shard = lax.optimization_barrier((tokens, shard))
    tok = lax.all_to_all(
        tokens.reshape(seq, own * span, width), "seq", split_axis=0, concat_axis=0, tiled=True
    ).reshape(seq, own, span, width)

    live = lax.dynamic_slice_in_dim(padding, seq_index * span, span, 1)
    kept = kept_pairs(
        routes.reshape(rows, 2), live.reshape(rows), priority.reshape(rows), expert_count, capacity
    )
    kept = jnp.swapaxes(kept.reshape(seq, own * span, expert_count), 1, 2)
    kept = jnp.pad(
        kept, ((0, 0), (0, MASK_ROWS - expert_count), (0, width - own * span))
    ).astype(bf16)
    cot = cotangent * live[:, :, None].astype(bf16)
    packed = jnp.concatenate([cot.reshape(seq, own * span, width), kept], 1)
    packed = tie(packed, tok, pieces if outer > 1 else (from_x, from_y))
    packed = lax.all_to_all(packed, "seq", split_axis=0, concat_axis=0, tiled=True)
    cot_x, cot_y = spread(packed, bits=2), spread(packed, bits=4)
    half = seq // 2
    cot_far = [spread(cot_x[:half], bits=4), spread(cot_y[half:], bits=2)]

    win, wdn = w_in, w_down
    if outer > 1:
        win = lax.all_gather(win, "fsdp", axis=1, tiled=True, axis_index_groups=outer_groups)
        wdn = lax.all_gather(wdn, "fsdp", axis=1, tiled=True, axis_index_groups=outer_groups)
    win = jnp.concatenate([win, spread(win, bits=1)], 1)
    wdn = jnp.concatenate([wdn, spread(wdn, bits=1)], 1)

    mine = lax.dynamic_slice_in_dim(padding, seq_index * own, own, 0)
    vis = jnp.where(mine > 0, 0.0, neg_fill).astype(f32).reshape(own, 1, length)
    tok = tie(tok, win, wdn)
    middle, two, proj, att, prob, wall, wr, small = front(tok, pieces, offsets, vis, place)
    two = two.reshape(seq, own * span, width)
    two_far = [[spread(two, bits=bits)] for bits in (2, 4, 6)]

    (dw,), dwr, out_0, gin_0 = experts_call(
        [[two]], [[packed]], win, wdn, wr, (0, expert_count), None, None, "experts_own"
    )
    cots = [[cot_x], [cot_y], cot_far]
    line = LineSum(seq)
    outs = gins = previous = None
    for e in range(expert_count):
        sums = None if outs is None else tie(outs + gins, line.ready)
        (dw_kept, dw_sent), dwr, outs, gins = experts_call(
            two_far, cots, win, wdn, wr, (e, 1), [dw, dwr], sums, "experts_far"
        )
        if previous is not None:
            line.step(previous())

        def previous(dw_kept=dw_kept, received=spread(dw_sent, bits=1)):
            raw = plus(dw_kept, received)
            if outer > 1:
                raw = lax.psum_scatter(
                    raw, "fsdp", scatter_dimension=2, tiled=True, axis_index_groups=outer_groups
                )
            return raw

    arrived = [spread(a, bits=bits) for a, bits in zip(gins, (2, 4, 6))]
    line.step(previous())
    gins = gin_0 + tie(arrived, line.ready)
    outs = out_0 + [spread(a, bits=bits) for a, bits in zip(tie(outs, arrived), (2, 4, 6))]

    shape4 = (seq, own, span, width)
    grad_tok, dense_even, dense_odd = back(
        [a.reshape(shape4) for a in gins],
        middle,
        packed[:, : own * span].reshape(shape4),
        tok,
        att,
        proj,
        prob,
        wall,
        small,
        dwr,
        place,
    )
    line.step()
    grad_tok, dense_even, dense_odd = tie((grad_tok, dense_even, dense_odd), line.ready)
    grad_tokens = lax.all_to_all(
        grad_tok.reshape(seq, own * span, width), "seq", split_axis=0, concat_axis=0, tiled=True
    ).reshape(images, span, width)
    if outer == 1:
        received = spread(dense_odd, bits=1)
        merged = [plus(dense_even[n], received[n]) for n in range(4)]
        dense = plus(merged[0], *[spread(merged[n], bits=2 * n) for n in (1, 2, 3)])
    else:
        dense = jnp.stack([dense_even, dense_odd], 1).reshape(width, -1)
        dense = lax.psum_scatter(dense, "fsdp", scatter_dimension=0, tiled=True)
    alive = jnp.swapaxes(mine.reshape(own, seq, span), 0, 1)[:, :, :, None].astype(f32)
    combined = sum(a.reshape(shape4).astype(f32) for a in outs)
    outputs = (alive * (middle + combined)).astype(bf16)
    outputs = lax.all_to_all(
        outputs.reshape(seq, own * span, width), "seq", split_axis=0, concat_axis=0, tiled=True
    ).reshape(images, span, width)
    dense_line = LineSum(seq)
    dense_line.step(dense)
    (dense,) = dense_line.finish(1)
    dense = dense.astype(f32)
    grads = line.finish(expert_count)
    expert_grads = [jnp.concatenate([g[:, n] for g in grads], 0).astype(f32) for n in range(2)]
    tail = dense[:, 4 * width :]
    return (
        outputs,
        grad_tokens,
        tail[:, 4],
        tail[:, 5],
        dense[:, : 3 * width],
        dense[:, 3 * width : 4 * width],
        tail[:, 6],
        tail[:, 7],
        tail[:, :expert_count],
        expert_grads[0],
        expert_grads[1],
    )


def solution(mesh):
    rows = P("fsdp", "seq", None)
    in_specs = (
        rows,
        P("fsdp"),
        P("fsdp"),
        P("fsdp", None),
        P("fsdp", None),
        P("fsdp"),
        P("fsdp"),
        P("fsdp", None),
        P(None, "fsdp", None),
        P(None, "fsdp", None),
        P("fsdp", None),
        rows,
        P("fsdp", "seq"),
        rows,
    )
    out_specs = (
        rows,
        rows,
        P("fsdp"),
        P("fsdp"),
        P("fsdp", None),
        P("fsdp", None),
        P("fsdp"),
        P("fsdp"),
        P("fsdp", None),
        P(None, "fsdp", None),
        P(None, "fsdp", None),
    )
    return jax.shard_map(
        functools.partial(local, mesh.shape["fsdp"], mesh.shape["seq"]),
        mesh=mesh,
        in_specs=in_specs,
        out_specs=out_specs,
        check_vma=False,
    )
```

```python
import functools
import math

import jax
import jax.numpy as jnp
from jax import lax
from jax.experimental import pallas as pl
from jax.experimental.pallas import tpu as pltpu
from jax.sharding import PartitionSpec as P

HEAD_DIM = 64
LANES = 128
MASK_ROWS = 16
SMALL = 8
norm_eps = 1e-06
neg_fill = -1e30
f32 = jnp.float32
bf16 = jnp.bfloat16
VMEM_BYTES = 60 * 1024 * 1024
SHORT = pl.CostEstimate(flops=1000, bytes_accessed=1000, transcendentals=0)


def true_cost(flops):
    return pl.CostEstimate(flops=2 * flops, bytes_accessed=16 * 1024 * 1024, transcendentals=0)


def mm(left, right, left_dim=1, right_dim=0):
    return lax.dot_general(
        left, right, (((left_dim,), (right_dim,)), ((), ())), preferred_element_type=f32
    )


def unit_norm(rows):
    centred = rows - jnp.mean(rows, -1, keepdims=True)
    inverse = lax.rsqrt(jnp.mean(centred * centred, -1, keepdims=True) + norm_eps)
    return centred * inverse, inverse


def norm_back(scaled, unit, inverse):
    return inverse * (
        scaled
        - jnp.mean(scaled, -1, keepdims=True)
        - unit * jnp.mean(scaled * unit, -1, keepdims=True)
    )


def half_turn(tile):
    return pltpu.roll(tile.astype(f32), HEAD_DIM, axis=1).astype(bf16)


def wall_copies(pieces, offsets, place_ref, wall_ref, sems):
    copies = []
    for n, (piece, (r, skip)) in enumerate(zip(pieces, offsets)):
        rows = piece.shape[0]
        shard = wall_ref.shape[0] // 8
        start = pl.multiple_of((place_ref[0] ^ r) * shard + skip, 16)
        copies.append(pltpu.make_async_copy(piece, wall_ref.at[pl.ds(start, rows)], sems.at[n]))
    return copies


def front_kernel(offsets, *refs):
    pieces = refs[: len(offsets)]
    tok_ref, vis_ref, place_ref = refs[len(offsets) : len(offsets) + 3]
    mid_ref, two_ref, proj_ref, att_ref, prob_ref, full_ref, wr_ref, small_ref = refs[
        len(offsets) + 3 : len(offsets) + 11
    ]
    wall_ref, sems, full_sem = refs[len(offsets) + 11 :]
    blocks, _, span, width = tok_ref.shape
    length = blocks * span
    save = pltpu.make_async_copy(wall_ref, full_ref, full_sem)

    @pl.when(pl.program_id(0) == 0)
    def _():
        copies = wall_copies(pieces, offsets, place_ref, wall_ref, sems)
        for copy in copies:
            copy.start()
        for copy in copies:
            copy.wait()
        save.start()
        columns = wall_ref[:, 4 * width :]
        wr_ref[...] = columns
        small_ref[...] = columns.astype(f32).T[:SMALL]

    rows = tok_ref[...].reshape(length, width).astype(f32)
    unit, _ = unit_norm(rows)
    one = (unit * small_ref[4:5] + small_ref[5:6]).astype(bf16)
    proj_ref[0] = mm(one, wall_ref[:, : 3 * width]).astype(bf16)
    lower = lax.broadcasted_iota(jnp.int32, (length, LANES), 1) < HEAD_DIM
    zero = jnp.zeros((length, LANES), bf16)
    bias = vis_ref[0]

    def soften(index, queries, keys):
        scores = mm(queries, keys, 1, 1) * (HEAD_DIM**-0.5) + bias
        shifted = jnp.exp(scores - jnp.max(scores, -1, keepdims=True))
        weights = (shifted / jnp.sum(shifted, -1, keepdims=True)).astype(bf16)
        prob_ref[0, index] = weights
        return weights

    for pair in range(width // LANES):
        first, second, third = (
            proj_ref[0, :, (3 * pair + n) * LANES : (3 * pair + n + 1) * LANES] for n in range(3)
        )
        weights_a = soften(2 * pair, jnp.where(lower, first, zero), half_turn(first))
        weights_b = soften(2 * pair + 1, jnp.where(lower, zero, second), half_turn(third))
        both = jnp.where(lower, mm(weights_a, second), mm(weights_b, third))
        att_ref[0, :, pair * LANES : (pair + 1) * LANES] = both.astype(bf16)
    middle = rows + mm(att_ref[0], wall_ref[:, 3 * width : 4 * width])
    mid_ref[...] = middle.reshape(mid_ref.shape)
    unit, _ = unit_norm(middle)
    two_ref[...] = (unit * small_ref[6:7] + small_ref[7:8]).astype(bf16).reshape(two_ref.shape)

    @pl.when(pl.program_id(0) == pl.num_programs(0) - 1)
    def _():
        save.wait()


def front(tok, pieces, offsets, vis, place):
    blocks, images, span, width = tok.shape
    length = blocks * span
    heads = width // HEAD_DIM
    split = pl.BlockSpec((blocks, 1, span, width), lambda i: (0, i, 0, 0))
    anywhere = pl.BlockSpec(memory_space=pl.ANY)
    columns = pieces[0].shape[1]
    return pl.pallas_call(
        functools.partial(front_kernel, offsets),
        grid=(images,),
        in_specs=[anywhere] * len(pieces)
        + [
            split,
            pl.BlockSpec((1, 1, length), lambda i: (i, 0, 0)),
            pl.BlockSpec(memory_space=pltpu.SMEM),
        ],
        out_specs=[
            split,
            split,
            pl.BlockSpec((1, length, 3 * width), lambda i: (i, 0, 0)),
            pl.BlockSpec((1, length, width), lambda i: (i, 0, 0)),
            pl.BlockSpec((1, heads, length, length), lambda i: (i, 0, 0, 0)),
            anywhere,
            pl.BlockSpec((width, LANES), lambda i: (0, 0)),
            pl.BlockSpec((SMALL, width), lambda i: (0, 0)),
        ],
        out_shape=[
            jax.ShapeDtypeStruct(tok.shape, f32),
            jax.ShapeDtypeStruct(tok.shape, bf16),
            jax.ShapeDtypeStruct((images, length, 3 * width), bf16),
            jax.ShapeDtypeStruct((images, length, width), bf16),
            jax.ShapeDtypeStruct((images, heads, length, length), bf16),
            jax.ShapeDtypeStruct((width, columns), bf16),
            jax.ShapeDtypeStruct((width, LANES), bf16),
            jax.ShapeDtypeStruct((SMALL, width), f32),
        ],
        scratch_shapes=[
            pltpu.VMEM((width, columns), bf16),
            pltpu.SemaphoreType.DMA((len(pieces),)),
            pltpu.SemaphoreType.DMA(()),
        ],
        compiler_params=pltpu.CompilerParams(vmem_limit_bytes=VMEM_BYTES),
        cost_estimate=SHORT,
        name="front",
    )(*pieces, tok, vis, place)


def gelu_parts(pre):
    bell = jnp.exp(-0.5 * pre * pre)
    size = jnp.abs(pre) * 0.7071067811865476
    frac = 1.0 / (1.0 + 0.3275911 * size)
    poly = frac * (
        0.254829592
        + frac * (-0.284496736 + frac * (1.421413741 + frac * (-1.453152027 + frac * 1.061405429)))
    )
    tail = 0.5 * poly * bell
    cumulative = jnp.where(pre >= 0, 1.0 - tail, tail)
    return pre * cumulative, cumulative + pre * bell * 0.3989422804014327


def expert_kernel(plan, *refs):
    refs = list(refs)

    def take(number):
        taken, refs[:] = refs[:number], refs[number:]
        return taken

    groups, many, first, experts = plan["groups"], plan["many"], plan["first"], plan["experts"]
    two_parts = [take(n) for n in plan["two"]]
    cot_parts = [take(n) for n in plan["cot"]]
    weights = take(4)
    (wr_ref,) = take(1)
    dw_carried = take(2) if plan["dw"] else None
    sums_carried = take(2 * groups) if plan["resume"] else []
    (state_in,) = take(1) if plan["resume"] else (None,)
    dw_refs = take(plan["halves"])
    (dwr_ref,) = take(1)
    results = take(2 * groups)
    (state_out,) = take(1) if not plan["final"] else (None,)
    two_buf, cot_buf, sems, win_buf, wdn_buf, weight_sems, acc_in, acc_dn = take(8)
    stage, stage_sems = take(2)
    out_acc, gin_acc = take(2) if many > 1 else (None, None)
    dw_buf, dw_sem = take(2) if plan["dw"] else (None, None)
    gate_buf = take(1)[0] if plan["final"] else None
    (fresh,) = take(1) if plan["final"] and not plan["resume"] else (None,)
    _, blocks, span, width = two_buf.shape
    rows = blocks * span
    hidden_rows = win_buf.shape[1]
    shard = hidden_rows // 2
    expert, group = pl.program_id(0), pl.program_id(1)
    lane = lax.broadcasted_iota(jnp.int32, (rows, LANES), 1)
    fixed = state_in if plan["resume"] else (fresh if plan["final"] else state_out)

    def gate_at(k):
        return gate_buf.at[k] if plan["final"] else state_out.at[2, k]

    copies = []
    for k in range(groups):
        some = []
        for parts, buffer in ((two_parts[k], two_buf), (cot_parts[k], cot_buf)):
            at = 0
            for part in parts:
                size = part.shape[0]
                some.append((part, buffer.at[k, pl.ds(at, size)]))
                at += size
        copies.append(
            [pltpu.make_async_copy(s, t, sems.at[k, n]) for n, (s, t) in enumerate(some)]
        )
    fetches = [
        [
            pltpu.make_async_copy(
                ref.at[first + e],
                (win_buf, wdn_buf)[n // 2].at[e, pl.ds((n % 2) * shard, shard)],
                weight_sems.at[e, n],
            )
            for n, ref in enumerate(weights)
        ]
        for e in range(many)
    ]
    loads = [
        pltpu.make_async_copy(ref, stage.at[n], stage_sems.at[n])
        for n, ref in enumerate(sums_carried)
    ]
    stores = [
        pltpu.make_async_copy(stage.at[n], ref, stage_sems.at[n]) for n, ref in enumerate(results)
    ]

    @pl.when((expert == 0) & (group == 0))
    def _():
        for k in range(max(groups, many)):
            for copy in (copies[k] if k < groups else []) + (fetches[k] if k < many else []):
                copy.start()
        for load in loads:
            load.start()
        dwr_ref[...] = dw_carried[1][...] if plan["dw"] else jnp.zeros_like(dwr_ref)

    for k, some in enumerate(copies):

        @pl.when((expert == 0) & (group == k))
        def _(some=some):
            for copy in some:
                copy.wait()

    for e, some in enumerate(fetches):

        @pl.when((expert == e) & (group == 0))
        def _(e=e, some=some):
            for copy in some:
                copy.wait()
            if plan["dw"]:
                pltpu.make_async_copy(dw_carried[0].at[first + e], dw_buf, dw_sem).start()

    @pl.when(expert == 0)
    def _():
        if plan["resume"]:
            gate_at(group)[...] = state_in[2, group]
        else:
            chosen = (
                lax.broadcasted_iota(jnp.int32, (MASK_ROWS, LANES), 0)
                == lax.broadcasted_iota(jnp.int32, (MASK_ROWS, LANES), 1)
            ).astype(bf16)
            logits = mm(two_buf[group].reshape(rows, width), wr_ref[...])
            logits = jnp.where(lane < experts, logits, neg_fill)
            shifted = jnp.exp(logits - jnp.max(logits, -1, keepdims=True))
            fixed[0, group] = shifted / jnp.sum(shifted, -1, keepdims=True)
            fixed[1, group] = jnp.concatenate(
                [
                    mm(cot_buf[group, b, span : span + MASK_ROWS, :span], chosen, 0, 0)
                    for b in range(blocks)
                ],
                0,
            )
            gate_at(group)[...] = jnp.zeros((rows, LANES), f32)
        if many > 1:
            out_acc[group] = jnp.zeros((rows, width), f32)
            gin_acc[group] = jnp.zeros((rows, width), f32)

    @pl.when(group == 0)
    def _():
        acc_in[...] = jnp.zeros_like(acc_in)
        acc_dn[...] = jnp.zeros_like(acc_dn)

    two = two_buf[group].reshape(rows, width)
    cot = cot_buf[group, :, :span, :].reshape(rows, width)
    win, wdn = win_buf.at[expert], wdn_buf.at[expert]
    here = lane == expert + first
    gate = jnp.sum(jnp.where(here, fixed[0, group] * fixed[1, group], 0.0), -1, keepdims=True)
    chunk = math.gcd(hidden_rows, 256)
    spots = [slice(c, c + chunk) for c in range(0, hidden_rows, chunk)]
    product = jnp.zeros((rows, 1), f32)
    gated, grad_pre, ready = [], [], []

    def products(at):
        return mm(two, win[at], 1, 1), mm(cot, wdn[at], 1, 1)

    def weight_grads(n):
        acc_in[spots[n]] += mm(grad_pre[n], two, 0, 0)
        acc_dn[spots[n]] += mm(gated[n], cot, 0, 0)

    ready.append(products(spots[0]))
    for n in range(len(spots)):
        if n + 1 < len(spots):
            ready.append(products(spots[n + 1]))
        pre, back_rows = ready[n]
        hidden, slope = gelu_parts(pre)
        product = product + jnp.sum(hidden * back_rows, -1, keepdims=True)
        gated.append((hidden * gate).astype(bf16))
        grad_pre.append((slope * back_rows * gate).astype(bf16))
        if n > 0:
            weight_grads(n - 1)
    out_rows = mm(jnp.concatenate(gated, 1), wdn[...])
    gin_rows = mm(jnp.concatenate(grad_pre, 1), win[...])
    weight_grads(len(spots) - 1)
    gate_at(group)[...] += jnp.where(here, product, 0.0)
    if many > 1:
        out_acc[group] += out_rows
        gin_acc[group] += gin_rows

    @pl.when(group == groups - 1)
    def _():
        size = hidden_rows // plan["halves"]
        if plan["dw"]:
            pltpu.make_async_copy(dw_carried[0].at[first + expert], dw_buf, dw_sem).wait()
        for n in range(plan["halves"]):
            at = slice(n * size, (n + 1) * size)
            for m, acc in enumerate((acc_in, acc_dn)):
                total = acc[at]
                if plan["dw"]:
                    total = total + dw_buf[m, at].astype(f32)
                dw_refs[n][0, m] = total.astype(bf16)

    for k in range(groups):

        @pl.when((expert == many - 1) & (group == k))
        def _(k=k):
            both = [out_acc[k], gin_acc[k]] if many > 1 else [out_rows, gin_rows]
            if plan["final"]:
                probs = fixed[0, k]
                grad_gate = gate_at(k)[...] * fixed[1, k]
                grad_logits = probs * (grad_gate - jnp.sum(probs * grad_gate, -1, keepdims=True))
                grad_logits = grad_logits.astype(bf16)
                dwr_ref[...] += mm(grad_logits, two, 0, 0)[:SMALL]
                both[1] = both[1] + mm(grad_logits, wr_ref[...], 1, 1)
            for n, value in zip((k, groups + k), both):
                if plan["resume"]:
                    loads[n].wait()
                    value = value + stage[n].reshape(rows, width).astype(f32)
                stage[n] = value.astype(bf16).reshape(blocks, span, width)
                stores[n].start()
            if k == groups - 1:
                for store in stores:
                    store.wait()


def experts_call(two, cot, weights, wr, span_of, dw, sums, state, final, name, cost):
    groups = len(two)
    experts, shard, width = weights[0].shape
    hidden = 2 * shard
    first, many = span_of
    blocks = sum(a.shape[0] for a in two[0])
    span = two[0][0].shape[1]
    rows = blocks * span
    resume = sums is not None
    plan = dict(
        groups=groups,
        many=many,
        first=first,
        experts=experts,
        two=[len(parts) for parts in two],
        cot=[len(parts) for parts in cot],
        dw=dw is not None,
        resume=resume,
        final=final,
        halves=1 if dw is None else 2,
    )
    halves = plan["halves"]
    anywhere = pl.BlockSpec(memory_space=pl.ANY)
    once = lambda a: pl.BlockSpec(
        a.shape, lambda e, g: (0,) * len(a.shape), pipeline_mode=pl.Buffered(1)
    )
    result = jax.ShapeDtypeStruct((blocks, span, width), bf16)
    little = jax.ShapeDtypeStruct((SMALL, width), f32)
    kept_state = jax.ShapeDtypeStruct((3, groups, rows, LANES), f32)
    part = jax.ShapeDtypeStruct((many, 2, hidden // halves, width), bf16)
    part_spec = pl.BlockSpec((1, 2, hidden // halves, width), lambda e, g: (e, 0, 0, 0))
    pieces = [a for parts in two for a in parts] + [a for parts in cot for a in parts]
    scratch = [
        pltpu.VMEM((groups, blocks, span, width), bf16),
        pltpu.VMEM((groups, blocks, span + MASK_ROWS, width), bf16),
        pltpu.SemaphoreType.DMA((groups, 4)),
        pltpu.VMEM((many, hidden, width), bf16),
        pltpu.VMEM((many, hidden, width), bf16),
        pltpu.SemaphoreType.DMA((many, 4)),
        pltpu.VMEM((hidden, width), f32),
        pltpu.VMEM((hidden, width), f32),
        pltpu.VMEM((2 * groups, blocks, span, width), bf16),
        pltpu.SemaphoreType.DMA((2 * groups,)),
    ]
    if many > 1:
        scratch += [pltpu.VMEM((groups, rows, width), f32)] * 2
    if dw is not None:
        scratch += [pltpu.VMEM((2, hidden, width), bf16), pltpu.SemaphoreType.DMA(())]
    if final:
        scratch += [pltpu.VMEM((groups, rows, LANES), f32)]
        if not resume:
            scratch += [pltpu.VMEM((2, groups, rows, LANES), f32)]
    outs = pl.pallas_call(
        functools.partial(expert_kernel, plan),
        grid=(many, groups),
        in_specs=[anywhere] * (len(pieces) + 4)
        + [once(wr)]
        + ([anywhere, once(little)] if dw is not None else [])
        + ([anywhere] * (2 * groups) + [once(kept_state)] if resume else []),
        out_specs=[part_spec] * halves
        + [once(little)]
        + [anywhere] * (2 * groups)
        + ([] if final else [once(kept_state)]),
        out_shape=[part] * halves
        + [little]
        + [result] * (2 * groups)
        + ([] if final else [kept_state]),
        scratch_shapes=scratch,
        compiler_params=pltpu.CompilerParams(vmem_limit_bytes=VMEM_BYTES),
        cost_estimate=cost(12 * groups * rows * width * hidden * many),
        name=name,
    )(*pieces, *weights, wr, *(dw or []), *([*sums, state] if resume else []))
    parts, (dwr, *outs) = list(outs[:halves]), outs[halves:]
    state = None if final else outs.pop()
    return parts, dwr, outs[:groups], outs[groups:], state


def flip(array, fsdp, bits):
    return lax.ppermute(array, "fsdp", [(n, n ^ bits) for n in range(fsdp)])


def tie(value, *others):
    return lax.optimization_barrier((value, others))[0]


def plus(*arrays):
    return sum(a.astype(f32) for a in arrays).astype(bf16)


class LineSum:
    def __init__(self, seq):
        self.seq = seq
        self.index = lax.axis_index("seq")
        self.outer = (self.index == 0) | (self.index == seq - 1)
        self.inward = self.exchanged = self.total = None
        self.raw = self.pair = None
        self.ready = []
        self.done = []

    def arrive(self):
        if self.seq != 4:
            return
        total = None if self.pair is None else plus(self.pair, self.exchanged)
        pair = None if self.raw is None else plus(self.raw, self.inward)
        if self.total is not None:
            self.done.append(jnp.where(self.outer, self.inward, self.total))
        ready = [a for a in (pair, total) if a is not None]
        if ready:
            ready, self.index = lax.optimization_barrier((ready, self.index))
            self.outer = (self.index == 0) | (self.index == self.seq - 1)
            pair = ready.pop(0) if pair is not None else None
            total = ready.pop(0) if total is not None else None
        self.raw, self.pair, self.total = None, pair, total
        self.ready = [a for a in (pair, total) if a is not None]

    def send(self, raw=None):
        if self.seq != 4:
            self.done += [] if raw is None else [lax.psum(raw, "seq")]
            return
        self.raw = raw
        if raw is not None:
            self.ready.append(raw)
        if raw is not None or self.total is not None:
            if self.total is None:
                both = raw
            elif raw is None:
                both = self.total
            else:
                both = jnp.where(self.outer, raw, self.total)
            self.inward = lax.ppermute(both, "seq", [(0, 1), (1, 0), (2, 3), (3, 2)])
        if self.pair is not None:
            self.exchanged = lax.ppermute(self.pair, "seq", [(1, 2), (2, 1)])

    def step(self, raw=None):
        self.arrive()
        self.send(raw)

    def finish(self, count):
        while len(self.done) < count:
            self.step()
        return self.done


def back_kernel(
    gin_0, gin_2, gin_4, gin_6, mid_ref, cot_ref, tok_ref, att_ref, proj_ref, prob_ref, wall_ref,
    small_ref, dwr_ref, place_ref, gtok_ref, even_ref, odd_ref, acc, acc_small, gatt, gproj,
):
    blocks, _, span, width = tok_ref.shape
    length = blocks * span
    step = pl.program_id(0)

    @pl.when(step == 0)
    def _():
        acc[...] = jnp.zeros_like(acc)
        acc_small[...] = jnp.zeros_like(acc_small)
        acc_small[:SMALL] = dwr_ref[...]

    gin = sum(ref[...].reshape(length, width).astype(f32) for ref in (gin_0, gin_2, gin_4, gin_6))
    unit_two, inverse_two = unit_norm(mid_ref[...].reshape(length, width))
    acc_small[6:7] += jnp.sum(gin * unit_two, 0, keepdims=True)
    acc_small[7:8] += jnp.sum(gin, 0, keepdims=True)
    grad_middle = cot_ref[...].reshape(length, width).astype(f32) + norm_back(
        gin * small_ref[6:7], unit_two, inverse_two
    )
    branch = grad_middle.astype(bf16)
    acc[:, 3 * width : 4 * width] += mm(att_ref[0], branch, 0, 0)
    gatt[...] = mm(branch, wall_ref[:, 3 * width : 4 * width], 1, 1).astype(bf16)
    lower = lax.broadcasted_iota(jnp.int32, (length, LANES), 1) < HEAD_DIM
    zero = jnp.zeros((length, LANES), bf16)
    scale = HEAD_DIM**-0.5

    def score_grad(weights, grad_weights):
        weights = weights.astype(f32)
        product = weights * grad_weights
        return (product - weights * jnp.sum(product, -1, keepdims=True)).astype(bf16)

    for pair in range(width // LANES):
        places = [slice((3 * pair + n) * LANES, (3 * pair + n + 1) * LANES) for n in range(3)]
        first, second, third = (proj_ref[0, :, place] for place in places)
        first_r, second_r, third_r = half_turn(first), half_turn(second), half_turn(third)
        grad = gatt[:, pair * LANES : (pair + 1) * LANES]
        weights_a, weights_b = prob_ref[0, 2 * pair], prob_ref[0, 2 * pair + 1]
        ds_a = score_grad(weights_a, mm(jnp.where(lower, grad, zero), second, 1, 1))
        ds_b = score_grad(weights_b, mm(jnp.where(lower, zero, grad), third, 1, 1))
        gproj[:, places[0]] = (
            jnp.where(lower, mm(ds_a, first_r), mm(ds_a, first_r, 0, 0)) * scale
        ).astype(bf16)
        gproj[:, places[1]] = jnp.where(
            lower, mm(weights_a, grad, 0, 0), mm(ds_b, third_r) * scale
        ).astype(bf16)
        gproj[:, places[2]] = jnp.where(
            lower, mm(ds_b, second_r, 0, 0) * scale, mm(weights_b, grad, 0, 0)
        ).astype(bf16)
    unit_one, inverse_one = unit_norm(tok_ref[...].reshape(length, width).astype(f32))
    one = (unit_one * small_ref[4:5] + small_ref[5:6]).astype(bf16)
    grad_one = mm(gproj[...], wall_ref[:, : 3 * width], 1, 1)
    acc_small[4:5] += jnp.sum(grad_one * unit_one, 0, keepdims=True)
    acc_small[5:6] += jnp.sum(grad_one, 0, keepdims=True)
    grad_tok = grad_middle + norm_back(grad_one * small_ref[4:5], unit_one, inverse_one)
    gtok_ref[...] = grad_tok.astype(bf16).reshape(gtok_ref.shape)
    acc[:, : 3 * width] += mm(one, gproj[...], 0, 0)

    @pl.when(step == pl.num_programs(0) - 1)
    def _():
        acc[:, 4 * width :] = acc_small[...].T
        shard = width // 8
        for r in range(8):
            start = pl.multiple_of((place_ref[0] ^ r) * shard, 8)
            target = odd_ref if r % 2 else even_ref
            target[r // 2] = acc[pl.ds(start, shard)].astype(bf16)


def back(gins, middle, cot, tok, att, proj, prob, wall, small, dwr, place):
    blocks, images, span, width = tok.shape
    length = blocks * span
    heads = width // HEAD_DIM
    split = pl.BlockSpec((blocks, 1, span, width), lambda i: (0, i, 0, 0))
    whole = lambda a: pl.BlockSpec(a.shape, lambda i: (0,) * len(a.shape))
    parts = jax.ShapeDtypeStruct((4, width // 8, wall.shape[1]), bf16)
    return pl.pallas_call(
        back_kernel,
        grid=(images,),
        in_specs=[split] * 7
        + [
            pl.BlockSpec((1, length, width), lambda i: (i, 0, 0)),
            pl.BlockSpec((1, length, 3 * width), lambda i: (i, 0, 0)),
            pl.BlockSpec((1, heads, length, length), lambda i: (i, 0, 0, 0)),
            whole(wall),
            whole(small),
            whole(dwr),
            pl.BlockSpec(memory_space=pltpu.SMEM),
        ],
        out_specs=[split, whole(parts), whole(parts)],
        out_shape=[jax.ShapeDtypeStruct(tok.shape, bf16), parts, parts],
        scratch_shapes=[
            pltpu.VMEM(wall.shape, f32),
            pltpu.VMEM((LANES, width), f32),
            pltpu.VMEM((length, width), bf16),
            pltpu.VMEM((length, 3 * width), bf16),
        ],
        compiler_params=pltpu.CompilerParams(vmem_limit_bytes=VMEM_BYTES),
        cost_estimate=true_cost(10 * images * length * width * (4 * width + 3 * length)),
        name="back",
    )(*gins, middle, cot, tok, att, proj, prob, wall, small, dwr, place)


def kept_pairs(route_rows, token_live, order_rows, expert_count, capacity):
    labels = jnp.arange(expert_count, dtype=jnp.int32)
    alive = token_live > 0
    first_hot = ((route_rows[:, 0:1] == labels) & alive[:, None]).astype(bf16)
    second_hot = ((route_rows[:, 1:2] == labels) & alive[:, None]).astype(bf16)
    earlier = (order_rows[None, :] < order_rows[:, None]).astype(bf16)
    ahead = mm(earlier, jnp.concatenate([first_hot, second_hot], 1))
    ahead_first = ahead[:, :expert_count]
    ahead_second = ahead[:, expert_count:] + jnp.sum(first_hot.astype(f32), 0)
    return jnp.where(ahead_first < capacity, first_hot, 0) + jnp.where(
        ahead_second < capacity, second_hot, 0
    )


def local(
    fsdp,
    seq,
    tokens,
    ln1_gain,
    ln1_bias,
    w_qkv,
    w_out,
    ln2_gain,
    ln2_bias,
    w_router,
    w_in,
    w_down,
    padding,
    routes,
    priority,
    cotangent,
):
    images, span, width = tokens.shape
    expert_count, shard_rows = w_in.shape[0], w_in.shape[1]
    rows = images * span
    own = images // seq
    length = seq * span
    capacity = (2 * rows + expert_count - 1) // expert_count
    outer = fsdp // 8
    if outer > 1:
        outer_groups = [[o * 8 + n for o in range(outer)] for n in range(8)]
    spread = functools.partial(flip, fsdp=fsdp)
    seq_index = lax.axis_index("seq")
    place = lax.axis_index("fsdp") if outer == 1 else jnp.int32(0)
    place = place.astype(jnp.int32).reshape(1)

    columns = jnp.concatenate(
        [w_router] + [v[:, None] for v in (ln1_gain, ln1_bias, ln2_gain, ln2_bias)], 1
    )
    columns = jnp.pad(columns, ((0, 0), (0, LANES - columns.shape[1])))
    shard = jnp.concatenate([w_qkv, w_out, columns], 1)
    if outer == 1:
        cut = width // 16
        from_x, from_y = spread(shard, bits=2), spread(shard, bits=4)
        even = [
            (0, 0, shard),
            (2, 0, from_x),
            (4, 0, from_y),
            (6, 0, spread(from_x[:cut], bits=4)),
            (6, cut, spread(from_y[cut:], bits=2)),
        ]
        pieces = even + [(r + 1, skip, spread(a, bits=1)) for r, skip, a in even]
        offsets = [(r, skip) for r, skip, _ in pieces]
        pieces = [a for _, _, a in pieces]
    else:
        full = lax.all_gather(shard, "fsdp", axis=0, tiled=True)
        offsets = [(n, 0) for n in range(8)]
        pieces = list(full.reshape(8, width // 8, -1))

    live = lax.dynamic_slice_in_dim(padding, seq_index * span, span, 1)
    kept = kept_pairs(
        routes.reshape(rows, 2), live.reshape(rows), priority.reshape(rows), expert_count, capacity
    )
    kept = jnp.swapaxes(kept.reshape(seq, own * span, expert_count), 1, 2)
    kept = jnp.pad(
        kept, ((0, 0), (0, MASK_ROWS - expert_count), (0, width - own * span))
    ).astype(bf16)
    cot = cotangent * live[:, :, None].astype(bf16)
    packed = jnp.concatenate([cot.reshape(seq, own * span, width), kept], 1)
    packed = tie(packed, pieces if outer > 1 else (from_x, from_y))
    tokens = tie(tokens, packed)
    packed = lax.all_to_all(packed, "seq", split_axis=0, concat_axis=0, tiled=True)
    tok = lax.all_to_all(
        tokens.reshape(seq, own * span, width), "seq", split_axis=0, concat_axis=0, tiled=True
    ).reshape(seq, own, span, width)
    cot_x, cot_y = spread(packed, bits=2), spread(packed, bits=4)
    half = seq // 2
    cot_far = [spread(cot_x[:half], bits=4), spread(cot_y[half:], bits=2)]

    win, wdn = w_in, w_down
    if outer > 1:
        win = lax.all_gather(win, "fsdp", axis=1, tiled=True, axis_index_groups=outer_groups)
        wdn = lax.all_gather(wdn, "fsdp", axis=1, tiled=True, axis_index_groups=outer_groups)
    weights = [win, spread(win, bits=1), wdn, spread(wdn, bits=1)]

    mine = lax.dynamic_slice_in_dim(padding, seq_index * own, own, 0)
    vis = jnp.where(mine > 0, 0.0, neg_fill).astype(f32).reshape(own, 1, length)
    middle, two, proj, att, prob, wall, wr, small = front(tok, pieces, offsets, vis, place)
    two = two.reshape(seq, own * span, width)
    two_far = [[spread(two, bits=bits)] for bits in (2, 4, 6)]

    (dw,), dwr, out_0, gin_0, _ = experts_call(
        [[two]],
        [[packed]],
        weights,
        wr,
        (0, expert_count),
        None,
        None,
        None,
        True,
        "experts_own",
        lambda flops: SHORT,
    )

    def finished(dw_kept, dw_sent):
        raw = plus(dw_kept, spread(dw_sent, bits=1))
        if outer > 1:
            raw = lax.psum_scatter(
                raw, "fsdp", scatter_dimension=2, tiled=True, axis_index_groups=outer_groups
            )
        return lax.optimization_barrier([raw[n : n + 1] for n in range(raw.shape[0])])

    cots = [[cot_x], [cot_y], cot_far]
    line = LineSum(seq)
    parts, dwr, outs, gins, state = experts_call(
        two_far,
        cots,
        weights,
        wr,
        (0, 1),
        [dw, dwr],
        None,
        None,
        False,
        "experts_far_one",
        true_cost,
    )
    line.step(finished(*parts)[0])
    parts, dwr, outs, gins, _ = experts_call(
        two_far,
        cots,
        weights,
        wr,
        (1, expert_count - 1),
        [dw, dwr],
        tie(outs + gins, line.ready),
        state,
        True,
        "experts_far_rest",
        true_cost,
    )
    line.arrive()
    gins, parts = tie((gins, parts), line.ready)
    arrived = [spread(a, bits=bits) for a, bits in zip(gins, (2, 4, 6))]
    raws = finished(*parts)
    line.send(raws.pop(0))
    line.step(raws.pop(0))
    gins = gin_0 + tie(arrived, line.ready)
    outs = [spread(a, bits=bits) for a, bits in zip(tie(outs, arrived), (2, 4, 6))]

    shape4 = (seq, own, span, width)
    grad_tok, dense_even, dense_odd = back(
        [a.reshape(shape4) for a in gins],
        middle,
        packed[:, : own * span].reshape(shape4),
        tok,
        att,
        proj,
        prob,
        wall,
        small,
        dwr,
        place,
    )
    line.step(raws.pop(0))
    grad_tok, dense_even, dense_odd = tie((grad_tok, dense_even, dense_odd), line.ready)
    grad_tokens = lax.all_to_all(
        grad_tok.reshape(seq, own * span, width), "seq", split_axis=0, concat_axis=0, tiled=True
    ).reshape(images, span, width)
    if outer == 1:
        received = spread(dense_odd, bits=1)
        merged = [plus(dense_even[n], received[n]) for n in range(4)]
        dense = plus(merged[0], *[spread(merged[n], bits=2 * n) for n in (1, 2, 3)])
    else:
        dense = jnp.stack([dense_even, dense_odd], 1).reshape(width, -1)
        dense = lax.psum_scatter(dense, "fsdp", scatter_dimension=0, tiled=True)
    alive = jnp.swapaxes(mine.reshape(own, seq, span), 0, 1)[:, :, :, None].astype(f32)
    outs = out_0 + tie(outs, grad_tok)
    combined = sum(a.reshape(shape4).astype(f32) for a in outs)
    outputs = (alive * (middle + combined)).astype(bf16)
    outputs = lax.all_to_all(
        outputs.reshape(seq, own * span, width), "seq", split_axis=0, concat_axis=0, tiled=True
    ).reshape(images, span, width)
    dense_line = LineSum(seq)
    dense_line.step(dense)
    (dense,) = dense_line.finish(1)
    dense = dense.astype(f32)
    grads = line.finish(expert_count)
    expert_grads = [jnp.concatenate([g[:, n] for g in grads], 0).astype(f32) for n in range(2)]
    tail = dense[:, 4 * width :]
    return (
        outputs,
        grad_tokens,
        tail[:, 4],
        tail[:, 5],
        dense[:, : 3 * width],
        dense[:, 3 * width : 4 * width],
        tail[:, 6],
        tail[:, 7],
        tail[:, :expert_count],
        expert_grads[0],
        expert_grads[1],
    )


def solution(mesh):
    rows = P("fsdp", "seq", None)
    in_specs = (
        rows,
        P("fsdp"),
        P("fsdp"),
        P("fsdp", None),
        P("fsdp", None),
        P("fsdp"),
        P("fsdp"),
        P("fsdp", None),
        P(None, "fsdp", None),
        P(None, "fsdp", None),
        P("fsdp", None),
        rows,
        P("fsdp", "seq"),
        rows,
    )
    out_specs = (
        rows,
        rows,
        P("fsdp"),
        P("fsdp"),
        P("fsdp", None),
        P("fsdp", None),
        P("fsdp"),
        P("fsdp"),
        P("fsdp", None),
        P(None, "fsdp", None),
        P(None, "fsdp", None),
    )
    return jax.shard_map(
        functools.partial(local, mesh.shape["fsdp"], mesh.shape["seq"]),
        mesh=mesh,
        in_specs=in_specs,
        out_specs=out_specs,
        check_vma=False,
    )
```

```python
import functools
import math

import jax
import jax.numpy as jnp
from jax import lax
from jax.experimental import pallas as pl
from jax.experimental.pallas import tpu as pltpu
from jax.sharding import PartitionSpec as P

HEAD_DIM = 64
LANES = 128
MASK_ROWS = 16
SMALL = 8
norm_eps = 1e-06
neg_fill = -1e30
f32 = jnp.float32
bf16 = jnp.bfloat16
VMEM_BYTES = 60 * 1024 * 1024
SHORT = pl.CostEstimate(flops=1000, bytes_accessed=1000, transcendentals=0)


def true_cost(flops):
    return pl.CostEstimate(flops=2 * flops, bytes_accessed=16 * 1024 * 1024, transcendentals=0)


def mm(left, right, left_dim=1, right_dim=0):
    return lax.dot_general(
        left, right, (((left_dim,), (right_dim,)), ((), ())), preferred_element_type=f32
    )


def unit_norm(rows):
    centred = rows - jnp.mean(rows, -1, keepdims=True)
    inverse = lax.rsqrt(jnp.mean(centred * centred, -1, keepdims=True) + norm_eps)
    return centred * inverse, inverse


def norm_back(scaled, unit, inverse):
    return inverse * (
        scaled
        - jnp.mean(scaled, -1, keepdims=True)
        - unit * jnp.mean(scaled * unit, -1, keepdims=True)
    )


def half_turn(tile):
    return pltpu.roll(tile.astype(f32), HEAD_DIM, axis=1).astype(bf16)


def wall_copies(pieces, offsets, place_ref, wall_ref, sems):
    copies = []
    for n, (piece, (r, skip)) in enumerate(zip(pieces, offsets)):
        rows = piece.shape[0]
        shard = wall_ref.shape[0] // 8
        start = pl.multiple_of((place_ref[0] ^ r) * shard + skip, 16)
        copies.append(pltpu.make_async_copy(piece, wall_ref.at[pl.ds(start, rows)], sems.at[n]))
    return copies


def front_kernel(offsets, *refs):
    pieces = refs[: len(offsets)]
    tok_ref, vis_ref, place_ref = refs[len(offsets) : len(offsets) + 3]
    mid_ref, two_ref, proj_ref, att_ref, prob_ref, full_ref, wr_ref, small_ref = refs[
        len(offsets) + 3 : len(offsets) + 11
    ]
    wall_ref, sems, full_sem = refs[len(offsets) + 11 :]
    blocks, _, span, width = tok_ref.shape
    length = blocks * span
    save = pltpu.make_async_copy(wall_ref, full_ref, full_sem)

    @pl.when(pl.program_id(0) == 0)
    def _():
        copies = wall_copies(pieces, offsets, place_ref, wall_ref, sems)
        for copy in copies:
            copy.start()
        for copy in copies:
            copy.wait()
        save.start()
        columns = wall_ref[:, 4 * width :]
        wr_ref[...] = columns
        small_ref[...] = columns.astype(f32).T[:SMALL]

    rows = tok_ref[...].reshape(length, width).astype(f32)
    unit, _ = unit_norm(rows)
    one = (unit * small_ref[4:5] + small_ref[5:6]).astype(bf16)
    proj_ref[0] = mm(one, wall_ref[:, : 3 * width]).astype(bf16)
    lower = lax.broadcasted_iota(jnp.int32, (length, LANES), 1) < HEAD_DIM
    zero = jnp.zeros((length, LANES), bf16)
    bias = vis_ref[0]

    def soften(index, queries, keys):
        scores = mm(queries, keys, 1, 1) * (HEAD_DIM**-0.5) + bias
        shifted = jnp.exp(scores - jnp.max(scores, -1, keepdims=True))
        weights = (shifted / jnp.sum(shifted, -1, keepdims=True)).astype(bf16)
        prob_ref[0, index] = weights
        return weights

    for pair in range(width // LANES):
        first, second, third = (
            proj_ref[0, :, (3 * pair + n) * LANES : (3 * pair + n + 1) * LANES] for n in range(3)
        )
        weights_a = soften(2 * pair, jnp.where(lower, first, zero), half_turn(first))
        weights_b = soften(2 * pair + 1, jnp.where(lower, zero, second), half_turn(third))
        both = jnp.where(lower, mm(weights_a, second), mm(weights_b, third))
        att_ref[0, :, pair * LANES : (pair + 1) * LANES] = both.astype(bf16)
    middle = rows + mm(att_ref[0], wall_ref[:, 3 * width : 4 * width])
    mid_ref[...] = middle.reshape(mid_ref.shape)
    unit, _ = unit_norm(middle)
    two_ref[...] = (unit * small_ref[6:7] + small_ref[7:8]).astype(bf16).reshape(two_ref.shape)

    @pl.when(pl.program_id(0) == pl.num_programs(0) - 1)
    def _():
        save.wait()


def front(tok, pieces, offsets, vis, place):
    blocks, images, span, width = tok.shape
    length = blocks * span
    heads = width // HEAD_DIM
    split = pl.BlockSpec((blocks, 1, span, width), lambda i: (0, i, 0, 0))
    anywhere = pl.BlockSpec(memory_space=pl.ANY)
    columns = pieces[0].shape[1]
    return pl.pallas_call(
        functools.partial(front_kernel, offsets),
        grid=(images,),
        in_specs=[anywhere] * len(pieces)
        + [
            split,
            pl.BlockSpec((1, 1, length), lambda i: (i, 0, 0)),
            pl.BlockSpec(memory_space=pltpu.SMEM),
        ],
        out_specs=[
            split,
            split,
            pl.BlockSpec((1, length, 3 * width), lambda i: (i, 0, 0)),
            pl.BlockSpec((1, length, width), lambda i: (i, 0, 0)),
            pl.BlockSpec((1, heads, length, length), lambda i: (i, 0, 0, 0)),
            anywhere,
            pl.BlockSpec((width, LANES), lambda i: (0, 0)),
            pl.BlockSpec((SMALL, width), lambda i: (0, 0)),
        ],
        out_shape=[
            jax.ShapeDtypeStruct(tok.shape, f32),
            jax.ShapeDtypeStruct(tok.shape, bf16),
            jax.ShapeDtypeStruct((images, length, 3 * width), bf16),
            jax.ShapeDtypeStruct((images, length, width), bf16),
            jax.ShapeDtypeStruct((images, heads, length, length), bf16),
            jax.ShapeDtypeStruct((width, columns), bf16),
            jax.ShapeDtypeStruct((width, LANES), bf16),
            jax.ShapeDtypeStruct((SMALL, width), f32),
        ],
        scratch_shapes=[
            pltpu.VMEM((width, columns), bf16),
            pltpu.SemaphoreType.DMA((len(pieces),)),
            pltpu.SemaphoreType.DMA(()),
        ],
        compiler_params=pltpu.CompilerParams(vmem_limit_bytes=VMEM_BYTES),
        cost_estimate=SHORT,
        name="front",
    )(*pieces, tok, vis, place)


def gelu_parts(pre):
    bell = jnp.exp2(pre * pre * (-0.5 * math.log2(math.e)))
    frac = 1.0 / (1.0 + (0.3275911 * math.sqrt(0.5)) * jnp.abs(pre))
    a5, a4, a3, a2, a1 = (
        0.5 * c for c in (1.061405429, -1.453152027, 1.421413741, -0.284496736, 0.254829592)
    )
    tail = frac * (a1 + frac * (a2 + frac * (a3 + frac * (a4 + frac * a5)))) * bell
    cumulative = jnp.where(pre >= 0, 1.0 - tail, tail)
    return pre * cumulative, cumulative + (pre * 0.3989422804014327) * bell


def expert_kernel(plan, *refs):
    refs = list(refs)

    def take(number):
        taken, refs[:] = refs[:number], refs[number:]
        return taken

    groups, many, first, experts = plan["groups"], plan["many"], plan["first"], plan["experts"]
    two_parts = [take(n) for n in plan["two"]]
    cot_parts = [take(n) for n in plan["cot"]]
    weights = take(4)
    (wr_ref,) = take(1)
    dw_carried = take(2) if plan["dw"] else None
    sums_carried = take(2 * groups) if plan["resume"] else []
    (state_in,) = take(1) if plan["resume"] else (None,)
    dw_refs = take(plan["halves"])
    (dwr_ref,) = take(1)
    results = take(2 * groups)
    (state_out,) = take(1) if not plan["final"] else (None,)
    two_buf, cot_buf, sems, win_buf, wdn_buf, weight_sems, acc_in, acc_dn = take(8)
    gated_buf, grad_buf, stage, load_sems, store_sems, dw_sems = take(6)
    dw_buf, dw_load_sems = take(2) if plan["dw"] else (None, None)
    _, blocks, span, width = two_buf.shape
    rows = blocks * span
    hidden = win_buf.shape[0] // many
    shard = hidden // 2
    group = pl.program_id(0)
    lane = lax.broadcasted_iota(jnp.int32, (rows, LANES), 1)

    copies = []
    for k in range(groups):
        some = []
        for parts, buffer in ((two_parts[k], two_buf), (cot_parts[k], cot_buf)):
            at = 0
            for part in parts:
                size = part.shape[0]
                some.append((part, buffer.at[k, pl.ds(at, size)]))
                at += size
        copies.append(
            [pltpu.make_async_copy(s, t, sems.at[k, n]) for n, (s, t) in enumerate(some)]
        )
    fetches = [
        pltpu.make_async_copy(
            ref.at[first + e],
            (win_buf, wdn_buf)[n // 2].at[pl.ds(e * hidden + (n % 2) * shard, shard)],
            weight_sems.at[e, n],
        )
        for e in range(many)
        for n, ref in enumerate(weights)
    ]
    loads = [
        pltpu.make_async_copy(ref, stage.at[n // groups], load_sems.at[n // groups])
        for n, ref in enumerate(sums_carried)
    ]
    stores = [
        pltpu.make_async_copy(stage.at[n // groups], ref, store_sems.at[n // groups])
        for n, ref in enumerate(results)
    ]

    @pl.when(group == 0)
    def _():
        for copy in copies[0] + fetches:
            copy.start()
        for some in copies[1:]:
            for copy in some:
                copy.start()
        dwr_ref[...] = dw_carried[1][...] if plan["dw"] else jnp.zeros_like(dwr_ref)
        for copy in fetches:
            copy.wait()

    for k, some in enumerate(copies):

        @pl.when(group == k)
        def _(k=k, some=some):
            for copy in some:
                copy.wait()
            if k > 0:
                stores[k - 1].wait()
                stores[groups + k - 1].wait()
            if plan["resume"]:
                loads[k].start()
                loads[groups + k].start()

    two = two_buf[group].reshape(rows, width)
    cot = cot_buf[group, :, :span, :].reshape(rows, width)
    if plan["resume"]:
        probs, kept, grad_gate = (state_in[n, group] for n in range(3))
    else:
        chosen = (
            lax.broadcasted_iota(jnp.int32, (MASK_ROWS, LANES), 0)
            == lax.broadcasted_iota(jnp.int32, (MASK_ROWS, LANES), 1)
        ).astype(bf16)
        logits = jnp.where(lane < experts, mm(two, wr_ref[...]), neg_fill)
        shifted = jnp.exp(logits - jnp.max(logits, -1, keepdims=True))
        probs = shifted / jnp.sum(shifted, -1, keepdims=True)
        kept = jnp.concatenate(
            [
                mm(cot_buf[group, b, span : span + MASK_ROWS, :span], chosen, 0, 0)
                for b in range(blocks)
            ],
            0,
        )
        grad_gate = jnp.zeros((rows, LANES), f32)
    gates = probs * kept

    def products(e):
        at = slice(e * hidden, (e + 1) * hidden)
        return mm(two, win_buf[at], 1, 1), mm(cot, wdn_buf[at], 1, 1)

    def weight_grads(e):
        at = slice(e * hidden, (e + 1) * hidden)
        for acc, grads, rows_in in ((acc_in, grad_buf, two), (acc_dn, gated_buf, cot)):
            fresh = mm(grads[:, at], rows_in, 0, 0)
            acc[at] = fresh if groups == 1 else jnp.where(group == 0, 0.0, acc[at]) + fresh

    ready = products(0)
    for e in range(many):
        at = slice(e * hidden, (e + 1) * hidden)
        pre, back_rows = ready
        if e + 1 < many:
            ready = products(e + 1)
        gate = gates[:, first + e : first + e + 1]
        hidden_rows, slope = gelu_parts(pre)
        product = jnp.sum(hidden_rows * back_rows, -1, keepdims=True)
        grad_gate = jnp.where(lane == first + e, product, grad_gate)
        gated_buf[:, at] = (hidden_rows * gate).astype(bf16)
        grad_buf[:, at] = (slope * back_rows * gate).astype(bf16)
        if e > 0:
            weight_grads(e - 1)
    out_rows = mm(gated_buf[...], wdn_buf[...])
    gin_rows = mm(grad_buf[...], win_buf[...])
    weight_grads(many - 1)
    if plan["final"]:
        grad_gate = grad_gate * kept
        grad_logits = probs * (grad_gate - jnp.sum(probs * grad_gate, -1, keepdims=True))
        grad_logits = grad_logits.astype(bf16)
        dwr_ref[...] += mm(grad_logits, two, 0, 0)[:SMALL]
        gin_rows = gin_rows + mm(grad_logits, wr_ref[...], 1, 1)
    else:
        for n, value in enumerate((probs, kept, grad_gate)):
            state_out[n, group] = value
    if plan["resume"]:
        for k in range(groups):

            @pl.when(group == k)
            def _(k=k):
                loads[k].wait()
                loads[groups + k].wait()

        out_rows = out_rows + stage[0].reshape(rows, width).astype(f32)
        gin_rows = gin_rows + stage[1].reshape(rows, width).astype(f32)
    stage[0] = out_rows.astype(bf16).reshape(blocks, span, width)
    stage[1] = gin_rows.astype(bf16).reshape(blocks, span, width)
    for k in range(groups):

        @pl.when(group == k)
        def _(k=k):
            stores[k].start()
            stores[groups + k].start()

    @pl.when(group == groups - 1)
    def _():
        size = hidden // plan["halves"]
        previous = [
            pltpu.make_async_copy(
                dw_carried[0].at[first + e], dw_buf.at[e % 2], dw_load_sems.at[e % 2]
            )
            for e in range(many if plan["dw"] else 0)
        ]
        for copy in previous[:2]:
            copy.start()
        leaving = []
        for e in range(many):
            if plan["dw"]:
                previous[e].wait()
            for m, (acc, buffer) in enumerate(((acc_in, win_buf), (acc_dn, wdn_buf))):
                at = slice(e * hidden, (e + 1) * hidden)
                total = acc[at]
                if plan["dw"]:
                    total = total + dw_buf[e % 2, m].astype(f32)
                buffer[at] = total.astype(bf16)
                for n in range(plan["halves"]):
                    copy = pltpu.make_async_copy(
                        buffer.at[pl.ds(e * hidden + n * size, size)],
                        dw_refs[n].at[e, m],
                        dw_sems.at[e, m, n],
                    )
                    copy.start()
                    leaving.append(copy)
            if e + 2 < len(previous):
                previous[e + 2].start()
        for copy in leaving:
            copy.wait()
        stores[groups - 1].wait()
        stores[2 * groups - 1].wait()


def experts_call(two, cot, weights, wr, span_of, dw, sums, state, final, name, cost):
    groups = len(two)
    experts, shard, width = weights[0].shape
    hidden = 2 * shard
    first, many = span_of
    blocks = sum(a.shape[0] for a in two[0])
    span = two[0][0].shape[1]
    rows = blocks * span
    resume = sums is not None
    plan = dict(
        groups=groups,
        many=many,
        first=first,
        experts=experts,
        two=[len(parts) for parts in two],
        cot=[len(parts) for parts in cot],
        dw=dw is not None,
        resume=resume,
        final=final,
        halves=1 if dw is None else 2,
    )
    halves = plan["halves"]
    anywhere = pl.BlockSpec(memory_space=pl.ANY)
    once = lambda a: pl.BlockSpec(
        a.shape, lambda g: (0,) * len(a.shape), pipeline_mode=pl.Buffered(1)
    )
    result = jax.ShapeDtypeStruct((blocks, span, width), bf16)
    little = jax.ShapeDtypeStruct((SMALL, width), f32)
    kept_state = jax.ShapeDtypeStruct((3, groups, rows, LANES), f32)
    part = jax.ShapeDtypeStruct((many, 2, hidden // halves, width), bf16)
    pieces = [a for parts in two for a in parts] + [a for parts in cot for a in parts]
    scratch = [
        pltpu.VMEM((groups, blocks, span, width), bf16),
        pltpu.VMEM((groups, blocks, span + MASK_ROWS, width), bf16),
        pltpu.SemaphoreType.DMA((groups, 4)),
        pltpu.VMEM((many * hidden, width), bf16),
        pltpu.VMEM((many * hidden, width), bf16),
        pltpu.SemaphoreType.DMA((many, 4)),
        pltpu.VMEM((many * hidden, width), f32),
        pltpu.VMEM((many * hidden, width), f32),
        pltpu.VMEM((rows, many * hidden), bf16),
        pltpu.VMEM((rows, many * hidden), bf16),
        pltpu.VMEM((2, blocks, span, width), bf16),
        pltpu.SemaphoreType.DMA((2,)),
        pltpu.SemaphoreType.DMA((2,)),
        pltpu.SemaphoreType.DMA((many, 2, halves)),
    ]
    if dw is not None:
        scratch += [pltpu.VMEM((2, 2, hidden, width), bf16), pltpu.SemaphoreType.DMA((2,))]
    outs = pl.pallas_call(
        functools.partial(expert_kernel, plan),
        grid=(groups,),
        in_specs=[anywhere] * (len(pieces) + 4)
        + [once(wr)]
        + ([anywhere, once(little)] if dw is not None else [])
        + ([anywhere] * (2 * groups) + [once(kept_state)] if resume else []),
        out_specs=[anywhere] * halves
        + [once(little)]
        + [anywhere] * (2 * groups)
        + ([] if final else [once(kept_state)]),
        out_shape=[part] * halves
        + [little]
        + [result] * (2 * groups)
        + ([] if final else [kept_state]),
        scratch_shapes=scratch,
        compiler_params=pltpu.CompilerParams(vmem_limit_bytes=VMEM_BYTES),
        cost_estimate=cost(12 * groups * rows * width * hidden * many),
        name=name,
    )(*pieces, *weights, wr, *(dw or []), *([*sums, state] if resume else []))
    parts, (dwr, *outs) = list(outs[:halves]), outs[halves:]
    state = None if final else outs.pop()
    return parts, dwr, outs[:groups], outs[groups:], state


def flip(array, fsdp, bits):
    return lax.ppermute(array, "fsdp", [(n, n ^ bits) for n in range(fsdp)])


def tie(value, *others):
    return lax.optimization_barrier((value, others))[0]


def exchange(pieces):
    count = len(pieces)
    return [pieces[0]] + [
        lax.ppermute(pieces[k], "seq", [(n, n ^ k) for n in range(count)]) for k in range(1, count)
    ]


def relative(parts, index):
    count, bit = len(parts), 1
    while bit < count:
        swap = (index & bit) > 0
        parts = [jnp.where(swap, parts[k ^ bit], parts[k]) for k in range(count)]
        bit *= 2
    return parts


def plus(*arrays):
    return sum(a.astype(f32) for a in arrays).astype(bf16)


class LineSum:
    def __init__(self, seq):
        self.seq = seq
        self.index = lax.axis_index("seq")
        self.outer = (self.index == 0) | (self.index == seq - 1)
        self.inward = self.exchanged = self.total = None
        self.raw = self.pair = None
        self.ready = []
        self.done = []

    def hold(self, others):
        if self.seq == 4:
            self.inward, self.exchanged = tie((self.inward, self.exchanged), others)

    def arrive(self):
        if self.seq != 4:
            return
        total = None if self.pair is None else plus(self.pair, self.exchanged)
        pair = None if self.raw is None else plus(self.raw, self.inward)
        if self.total is not None:
            self.done.append(jnp.where(self.outer, self.inward, self.total))
        ready = [a for a in (pair, total) if a is not None]
        if ready:
            ready, self.index = lax.optimization_barrier((ready, self.index))
            self.outer = (self.index == 0) | (self.index == self.seq - 1)
            pair = ready.pop(0) if pair is not None else None
            total = ready.pop(0) if total is not None else None
        self.raw, self.pair, self.total = None, pair, total
        self.ready = [a for a in (pair, total) if a is not None]

    def send(self, raw=None):
        if self.seq != 4:
            self.done += [] if raw is None else [lax.psum(raw, "seq")]
            return
        self.raw = raw
        if raw is not None:
            self.ready.append(raw)
        if raw is not None or self.total is not None:
            if self.total is None:
                both = raw
            elif raw is None:
                both = self.total
            else:
                both = jnp.where(self.outer, raw, self.total)
            self.inward = lax.ppermute(both, "seq", [(0, 1), (1, 0), (2, 3), (3, 2)])
        if self.pair is not None:
            self.exchanged = lax.ppermute(self.pair, "seq", [(1, 2), (2, 1)])

    def step(self, raw=None):
        self.arrive()
        self.send(raw)

    def finish(self, count):
        while len(self.done) < count:
            self.step()
        return self.done


def back_kernel(
    gin_0, gin_2, gin_4, gin_6, mid_ref, cot_ref, tok_ref, att_ref, proj_ref, prob_ref, wall_ref,
    small_ref, dwr_ref, *rest,
):
    blocks, _, span, width = tok_ref.shape
    length = blocks * span
    gtok_refs, (dwall_ref, acc, acc_small, gatt, gproj) = rest[:blocks], rest[blocks:]
    step = pl.program_id(0)

    @pl.when(step == 0)
    def _():
        acc[...] = jnp.zeros_like(acc)
        acc_small[...] = jnp.zeros_like(acc_small)
        acc_small[:SMALL] = dwr_ref[...]

    gin = sum(ref[...].reshape(length, width).astype(f32) for ref in (gin_0, gin_2, gin_4, gin_6))
    unit_two, inverse_two = unit_norm(mid_ref[...].reshape(length, width))
    acc_small[6:7] += jnp.sum(gin * unit_two, 0, keepdims=True)
    acc_small[7:8] += jnp.sum(gin, 0, keepdims=True)
    grad_middle = cot_ref[...].reshape(length, width).astype(f32) + norm_back(
        gin * small_ref[6:7], unit_two, inverse_two
    )
    branch = grad_middle.astype(bf16)
    acc[:, 3 * width : 4 * width] += mm(att_ref[0], branch, 0, 0)
    gatt[...] = mm(branch, wall_ref[:, 3 * width : 4 * width], 1, 1).astype(bf16)
    lower = lax.broadcasted_iota(jnp.int32, (length, LANES), 1) < HEAD_DIM
    zero = jnp.zeros((length, LANES), bf16)
    scale = HEAD_DIM**-0.5

    def score_grad(weights, grad_weights):
        weights = weights.astype(f32)
        product = weights * grad_weights
        return (product - weights * jnp.sum(product, -1, keepdims=True)).astype(bf16)

    for pair in range(width // LANES):
        places = [slice((3 * pair + n) * LANES, (3 * pair + n + 1) * LANES) for n in range(3)]
        first, second, third = (proj_ref[0, :, place] for place in places)
        first_r, second_r, third_r = half_turn(first), half_turn(second), half_turn(third)
        grad = gatt[:, pair * LANES : (pair + 1) * LANES]
        weights_a, weights_b = prob_ref[0, 2 * pair], prob_ref[0, 2 * pair + 1]
        ds_a = score_grad(weights_a, mm(jnp.where(lower, grad, zero), second, 1, 1))
        ds_b = score_grad(weights_b, mm(jnp.where(lower, zero, grad), third, 1, 1))
        gproj[:, places[0]] = (
            jnp.where(lower, mm(ds_a, first_r), mm(ds_a, first_r, 0, 0)) * scale
        ).astype(bf16)
        gproj[:, places[1]] = jnp.where(
            lower, mm(weights_a, grad, 0, 0), mm(ds_b, third_r) * scale
        ).astype(bf16)
        gproj[:, places[2]] = jnp.where(
            lower, mm(ds_b, second_r, 0, 0) * scale, mm(weights_b, grad, 0, 0)
        ).astype(bf16)
    unit_one, inverse_one = unit_norm(tok_ref[...].reshape(length, width).astype(f32))
    one = (unit_one * small_ref[4:5] + small_ref[5:6]).astype(bf16)
    grad_one = mm(gproj[...], wall_ref[:, : 3 * width], 1, 1)
    acc_small[4:5] += jnp.sum(grad_one * unit_one, 0, keepdims=True)
    acc_small[5:6] += jnp.sum(grad_one, 0, keepdims=True)
    grad_tok = grad_middle + norm_back(grad_one * small_ref[4:5], unit_one, inverse_one)
    for k, ref in enumerate(gtok_refs):
        ref[0] = grad_tok[k * span : (k + 1) * span].astype(bf16)
    acc[:, : 3 * width] += mm(one, gproj[...], 0, 0)

    @pl.when(step == pl.num_programs(0) - 1)
    def _():
        dwall_ref[:, : 4 * width] = acc[...].astype(bf16)
        dwall_ref[:, 4 * width :] = acc_small[...].T.astype(bf16)


def back(gins, middle, cot, tok, att, proj, prob, wall, small, dwr):
    blocks, images, span, width = tok.shape
    length = blocks * span
    heads = width // HEAD_DIM
    split = pl.BlockSpec((blocks, 1, span, width), lambda i: (0, i, 0, 0))
    whole = lambda a: pl.BlockSpec(a.shape, lambda i: (0,) * len(a.shape))
    return pl.pallas_call(
        back_kernel,
        grid=(images,),
        in_specs=[split] * 7
        + [
            pl.BlockSpec((1, length, width), lambda i: (i, 0, 0)),
            pl.BlockSpec((1, length, 3 * width), lambda i: (i, 0, 0)),
            pl.BlockSpec((1, heads, length, length), lambda i: (i, 0, 0, 0)),
            whole(wall),
            whole(small),
            whole(dwr),
        ],
        out_specs=[pl.BlockSpec((1, span, width), lambda i: (i, 0, 0))] * blocks + [whole(wall)],
        out_shape=[jax.ShapeDtypeStruct((images, span, width), bf16)] * blocks
        + [jax.ShapeDtypeStruct(wall.shape, bf16)],
        scratch_shapes=[
            pltpu.VMEM((width, 4 * width), f32),
            pltpu.VMEM((LANES, width), f32),
            pltpu.VMEM((length, width), bf16),
            pltpu.VMEM((length, 3 * width), bf16),
        ],
        compiler_params=pltpu.CompilerParams(vmem_limit_bytes=VMEM_BYTES),
        cost_estimate=true_cost(10 * images * length * width * (4 * width + 3 * length)),
        name="back",
    )(*gins, middle, cot, tok, att, proj, prob, wall, small, dwr)


def kept_pairs(route_rows, token_live, order_rows, expert_count, capacity):
    labels = jnp.arange(expert_count, dtype=jnp.int32)
    alive = token_live > 0
    first_hot = ((route_rows[:, 0:1] == labels) & alive[:, None]).astype(bf16)
    second_hot = ((route_rows[:, 1:2] == labels) & alive[:, None]).astype(bf16)
    earlier = (order_rows[None, :] < order_rows[:, None]).astype(bf16)
    ahead = mm(earlier, jnp.concatenate([first_hot, second_hot], 1))
    ahead_first = ahead[:, :expert_count]
    ahead_second = ahead[:, expert_count:] + jnp.sum(first_hot.astype(f32), 0)
    return jnp.where(ahead_first < capacity, first_hot, 0) + jnp.where(
        ahead_second < capacity, second_hot, 0
    )


def local(
    fsdp,
    seq,
    tokens,
    ln1_gain,
    ln1_bias,
    w_qkv,
    w_out,
    ln2_gain,
    ln2_bias,
    w_router,
    w_in,
    w_down,
    padding,
    routes,
    priority,
    cotangent,
):
    images, span, width = tokens.shape
    expert_count, shard_rows = w_in.shape[0], w_in.shape[1]
    rows = images * span
    own = images // seq
    length = seq * span
    capacity = (2 * rows + expert_count - 1) // expert_count
    outer = fsdp // 8
    if outer > 1:
        outer_groups = [[o * 8 + n for o in range(outer)] for n in range(8)]
    spread = functools.partial(flip, fsdp=fsdp)
    seq_index = lax.axis_index("seq")
    place = lax.axis_index("fsdp") if outer == 1 else jnp.int32(0)
    place = place.astype(jnp.int32).reshape(1)

    columns = jnp.concatenate(
        [w_router] + [v[:, None] for v in (ln1_gain, ln1_bias, ln2_gain, ln2_bias)], 1
    )
    columns = jnp.pad(columns, ((0, 0), (0, LANES - columns.shape[1])))
    shard = jnp.concatenate([w_qkv, w_out, columns], 1)
    if outer == 1:
        cut = width // 16
        from_x, from_y = spread(shard, bits=2), spread(shard, bits=4)
        even = [
            (0, 0, shard),
            (2, 0, from_x),
            (4, 0, from_y),
            (6, 0, spread(from_x[:cut], bits=4)),
            (6, cut, spread(from_y[cut:], bits=2)),
        ]
        pieces = even + [(r + 1, skip, spread(a, bits=1)) for r, skip, a in even]
        offsets = [(r, skip) for r, skip, _ in pieces]
        pieces = [a for _, _, a in pieces]
    else:
        full = lax.all_gather(shard, "fsdp", axis=0, tiled=True)
        offsets = [(n, 0) for n in range(8)]
        pieces = list(full.reshape(8, width // 8, -1))

    def picked(array, k):
        return lax.dynamic_index_in_dim(array, seq_index ^ k, 0, keepdims=False)

    tokens = tokens.reshape(seq, own * span, width)
    tok = jnp.stack(exchange([picked(tokens, k) for k in range(seq)]))
    tok = tok.reshape(seq, own, span, width)

    live = lax.dynamic_slice_in_dim(padding, seq_index * span, span, 1)
    kept = kept_pairs(
        routes.reshape(rows, 2), live.reshape(rows), priority.reshape(rows), expert_count, capacity
    )
    kept = jnp.swapaxes(kept.reshape(seq, own * span, expert_count), 1, 2)
    kept = jnp.pad(
        kept, ((0, 0), (0, MASK_ROWS - expert_count), (0, width - own * span))
    ).astype(bf16)
    cot = cotangent * live[:, :, None].astype(bf16)
    packed = jnp.concatenate([cot.reshape(seq, own * span, width), kept], 1)
    packed = tie(packed, pieces if outer > 1 else (from_x, from_y))
    packed = jnp.stack(exchange([picked(packed, k) for k in range(seq)]))
    cot_x, cot_y = spread(packed, bits=2), spread(packed, bits=4)
    half = seq // 2
    cot_far = [spread(cot_x[:half], bits=4), spread(cot_y[half:], bits=2)]

    win, wdn = w_in, w_down
    if outer > 1:
        win = lax.all_gather(win, "fsdp", axis=1, tiled=True, axis_index_groups=outer_groups)
        wdn = lax.all_gather(wdn, "fsdp", axis=1, tiled=True, axis_index_groups=outer_groups)
    win, wdn = tie((win, wdn), tok)
    weights = [win, spread(win, bits=1), wdn, spread(wdn, bits=1)]

    mine = lax.dynamic_slice_in_dim(padding, seq_index * own, own, 0).reshape(own, seq, span)
    mine = jnp.stack(relative([mine[:, b] for b in range(seq)], seq_index))
    vis = jnp.where(mine > 0, 0.0, neg_fill).astype(f32)
    vis = jnp.swapaxes(vis, 0, 1).reshape(own, 1, length)
    middle, two, proj, att, prob, wall, wr, small = front(tok, pieces, offsets, vis, place)
    two = two.reshape(seq, own * span, width)
    two_far = [[spread(two, bits=bits)] for bits in (2, 4, 6)]

    (dw,), dwr, out_0, gin_0, _ = experts_call(
        [[two]],
        [[packed]],
        weights,
        wr,
        (0, expert_count),
        None,
        None,
        None,
        True,
        "experts_own",
        lambda flops: SHORT,
    )

    def finished(dw_kept, dw_sent):
        raw = plus(dw_kept, spread(dw_sent, bits=1))
        if outer > 1:
            raw = lax.psum_scatter(
                raw, "fsdp", scatter_dimension=2, tiled=True, axis_index_groups=outer_groups
            )
        return lax.optimization_barrier([raw[n : n + 1] for n in range(raw.shape[0])])

    cots = [[cot_x], [cot_y], cot_far]
    line = LineSum(seq)
    parts, dwr, outs, gins, state = experts_call(
        two_far,
        cots,
        weights,
        wr,
        (0, 1),
        [dw, dwr],
        None,
        None,
        False,
        "experts_far_one",
        true_cost,
    )
    line.step(finished(*parts)[0])
    parts, dwr, outs, gins, _ = experts_call(
        two_far,
        cots,
        weights,
        wr,
        (1, expert_count - 1),
        [dw, dwr],
        tie(outs + gins, line.ready),
        state,
        True,
        "experts_far_rest",
        true_cost,
    )
    line.arrive()
    gins, parts = tie((gins, parts), line.ready)
    arrived = [spread(a, bits=bits) for a, bits in zip(gins, (2, 4, 6))]
    raws = finished(*parts)
    line.send(raws.pop(0))
    line.hold(arrived)
    line.step(raws.pop(0))
    gins = gin_0 + tie(arrived, line.ready)
    shape4 = (seq, own, span, width)
    outs = [spread(a, bits=bits) for a, bits in zip(tie(outs, arrived), (2, 4, 6))]
    *grad_tok, dense = back(
        [a.reshape(shape4) for a in gins],
        middle,
        packed[:, : own * span].reshape(shape4),
        tok,
        att,
        proj,
        prob,
        wall,
        small,
        dwr,
    )
    dense = lax.psum_scatter(dense, "fsdp", scatter_dimension=0, tiled=True)
    dense = lax.psum(dense, "seq").astype(f32)
    line.hold((grad_tok, outs))
    line.step(raws.pop(0))
    line.step()

    outs, grad_tok = tie((outs, grad_tok), line.ready)
    outs = [a.reshape(shape4) for a in out_0 + outs]
    home = []
    for k in range(seq):
        alive = mine[k][:, :, None].astype(f32)
        combined = sum(a[k].astype(f32) for a in outs)
        home.append(jnp.stack([(alive * (middle[k] + combined)).astype(bf16), grad_tok[k]]))
    home = exchange(home)
    line.step()
    home = relative(tie(home, line.ready), seq_index)
    outputs, grad_tokens = (
        jnp.concatenate([a[n] for a in home], 0).reshape(images, span, width) for n in range(2)
    )
    grads = line.finish(expert_count)
    expert_grads = [jnp.concatenate([g[:, n] for g in grads], 0).astype(f32) for n in range(2)]
    tail = dense[:, 4 * width :]
    return (
        outputs,
        grad_tokens,
        tail[:, 4],
        tail[:, 5],
        dense[:, : 3 * width],
        dense[:, 3 * width : 4 * width],
        tail[:, 6],
        tail[:, 7],
        tail[:, :expert_count],
        expert_grads[0],
        expert_grads[1],
    )


def solution(mesh):
    rows = P("fsdp", "seq", None)
    in_specs = (
        rows,
        P("fsdp"),
        P("fsdp"),
        P("fsdp", None),
        P("fsdp", None),
        P("fsdp"),
        P("fsdp"),
        P("fsdp", None),
        P(None, "fsdp", None),
        P(None, "fsdp", None),
        P("fsdp", None),
        rows,
        P("fsdp", "seq"),
        rows,
    )
    out_specs = (
        rows,
        rows,
        P("fsdp"),
        P("fsdp"),
        P("fsdp", None),
        P("fsdp", None),
        P("fsdp"),
        P("fsdp"),
        P("fsdp", None),
        P(None, "fsdp", None),
        P(None, "fsdp", None),
    )
    return jax.shard_map(
        functools.partial(local, mesh.shape["fsdp"], mesh.shape["seq"]),
        mesh=mesh,
        in_specs=in_specs,
        out_specs=out_specs,
        check_vma=False,
    )
```

```python
import functools
import math

import jax
import jax.numpy as jnp
from jax import lax
from jax.experimental import pallas as pl
from jax.experimental.pallas import tpu as pltpu
from jax.sharding import PartitionSpec as P

HEAD_DIM = 64
LANES = 128
MASK_ROWS = 16
SMALL = 8
norm_eps = 1e-06
neg_fill = -1e30
f32 = jnp.float32
bf16 = jnp.bfloat16
VMEM_BYTES = 60 * 1024 * 1024
SHORT = pl.CostEstimate(flops=1000, bytes_accessed=1000, transcendentals=0)


def true_cost(flops):
    return pl.CostEstimate(flops=2 * flops, bytes_accessed=16 * 1024 * 1024, transcendentals=0)


def mm(left, right, left_dim=1, right_dim=0):
    return lax.dot_general(
        left, right, (((left_dim,), (right_dim,)), ((), ())), preferred_element_type=f32
    )


def unit_norm(rows):
    centred = rows - jnp.mean(rows, -1, keepdims=True)
    inverse = lax.rsqrt(jnp.mean(centred * centred, -1, keepdims=True) + norm_eps)
    return centred * inverse, inverse


def norm_back(scaled, unit, inverse):
    return inverse * (
        scaled
        - jnp.mean(scaled, -1, keepdims=True)
        - unit * jnp.mean(scaled * unit, -1, keepdims=True)
    )


def half_turn(tile):
    return pltpu.roll(tile.astype(f32), HEAD_DIM, axis=1).astype(bf16)


def wall_copies(pieces, offsets, place_ref, wall_ref, sems):
    copies = []
    for n, (piece, (r, skip)) in enumerate(zip(pieces, offsets)):
        rows = piece.shape[0]
        shard = wall_ref.shape[0] // 8
        start = pl.multiple_of((place_ref[0] ^ r) * shard + skip, 16)
        copies.append(pltpu.make_async_copy(piece, wall_ref.at[pl.ds(start, rows)], sems.at[n]))
    return copies


def front_kernel(offsets, *refs):
    pieces = refs[: len(offsets)]
    tok_ref, vis_ref, place_ref = refs[len(offsets) : len(offsets) + 3]
    mid_ref, two_ref, proj_ref, att_ref, prob_ref, full_ref, wr_ref, small_ref = refs[
        len(offsets) + 3 : len(offsets) + 11
    ]
    wall_ref, sems, full_sem = refs[len(offsets) + 11 :]
    blocks, _, span, width = tok_ref.shape
    length = blocks * span
    save = pltpu.make_async_copy(wall_ref, full_ref, full_sem)

    @pl.when(pl.program_id(0) == 0)
    def _():
        copies = wall_copies(pieces, offsets, place_ref, wall_ref, sems)
        for copy in copies:
            copy.start()
        for copy in copies:
            copy.wait()
        save.start()
        columns = wall_ref[:, 4 * width :]
        wr_ref[...] = columns
        small_ref[...] = columns.astype(f32).T[:SMALL]

    rows = tok_ref[...].reshape(length, width).astype(f32)
    unit, _ = unit_norm(rows)
    one = (unit * small_ref[4:5] + small_ref[5:6]).astype(bf16)
    proj_ref[0] = mm(one, wall_ref[:, : 3 * width]).astype(bf16)
    lower = lax.broadcasted_iota(jnp.int32, (length, LANES), 1) < HEAD_DIM
    zero = jnp.zeros((length, LANES), bf16)
    bias = vis_ref[0]

    def soften(index, queries, keys):
        scores = mm(queries, keys, 1, 1) * (HEAD_DIM**-0.5) + bias
        shifted = jnp.exp(scores - jnp.max(scores, -1, keepdims=True))
        weights = (shifted / jnp.sum(shifted, -1, keepdims=True)).astype(bf16)
        prob_ref[0, index] = weights
        return weights

    for pair in range(width // LANES):
        first, second, third = (
            proj_ref[0, :, (3 * pair + n) * LANES : (3 * pair + n + 1) * LANES] for n in range(3)
        )
        weights_a = soften(2 * pair, jnp.where(lower, first, zero), half_turn(first))
        weights_b = soften(2 * pair + 1, jnp.where(lower, zero, second), half_turn(third))
        both = jnp.where(lower, mm(weights_a, second), mm(weights_b, third))
        att_ref[0, :, pair * LANES : (pair + 1) * LANES] = both.astype(bf16)
    middle = rows + mm(att_ref[0], wall_ref[:, 3 * width : 4 * width])
    mid_ref[...] = middle.reshape(mid_ref.shape)
    unit, _ = unit_norm(middle)
    two_ref[...] = (unit * small_ref[6:7] + small_ref[7:8]).astype(bf16).reshape(two_ref.shape)

    @pl.when(pl.program_id(0) == pl.num_programs(0) - 1)
    def _():
        save.wait()


def front(tok, pieces, offsets, vis, place):
    blocks, images, span, width = tok.shape
    length = blocks * span
    heads = width // HEAD_DIM
    split = pl.BlockSpec((blocks, 1, span, width), lambda i: (0, i, 0, 0))
    anywhere = pl.BlockSpec(memory_space=pl.ANY)
    columns = pieces[0].shape[1]
    return pl.pallas_call(
        functools.partial(front_kernel, offsets),
        grid=(images,),
        in_specs=[anywhere] * len(pieces)
        + [
            split,
            pl.BlockSpec((1, 1, length), lambda i: (i, 0, 0)),
            pl.BlockSpec(memory_space=pltpu.SMEM),
        ],
        out_specs=[
            split,
            split,
            pl.BlockSpec((1, length, 3 * width), lambda i: (i, 0, 0)),
            pl.BlockSpec((1, length, width), lambda i: (i, 0, 0)),
            pl.BlockSpec((1, heads, length, length), lambda i: (i, 0, 0, 0)),
            anywhere,
            pl.BlockSpec((width, LANES), lambda i: (0, 0)),
            pl.BlockSpec((SMALL, width), lambda i: (0, 0)),
        ],
        out_shape=[
            jax.ShapeDtypeStruct(tok.shape, f32),
            jax.ShapeDtypeStruct(tok.shape, bf16),
            jax.ShapeDtypeStruct((images, length, 3 * width), bf16),
            jax.ShapeDtypeStruct((images, length, width), bf16),
            jax.ShapeDtypeStruct((images, heads, length, length), bf16),
            jax.ShapeDtypeStruct((width, columns), bf16),
            jax.ShapeDtypeStruct((width, LANES), bf16),
            jax.ShapeDtypeStruct((SMALL, width), f32),
        ],
        scratch_shapes=[
            pltpu.VMEM((width, columns), bf16),
            pltpu.SemaphoreType.DMA((len(pieces),)),
            pltpu.SemaphoreType.DMA(()),
        ],
        compiler_params=pltpu.CompilerParams(vmem_limit_bytes=VMEM_BYTES),
        cost_estimate=SHORT,
        name="front",
    )(*pieces, tok, vis, place)


def gelu_parts(pre):
    bell = jnp.exp2(pre * pre * (-0.5 * math.log2(math.e)))
    frac = 1.0 / (1.0 + (0.3275911 * math.sqrt(0.5)) * jnp.abs(pre))
    a5, a4, a3, a2, a1 = (
        0.5 * c for c in (1.061405429, -1.453152027, 1.421413741, -0.284496736, 0.254829592)
    )
    tail = frac * (a1 + frac * (a2 + frac * (a3 + frac * (a4 + frac * a5)))) * bell
    cumulative = jnp.where(pre >= 0, 1.0 - tail, tail)
    return pre * cumulative, cumulative + (pre * 0.3989422804014327) * bell


def expert_kernel(plan, *refs):
    refs = list(refs)

    def take(number):
        taken, refs[:] = refs[:number], refs[number:]
        return taken

    groups, experts, opening = plan["groups"], plan["experts"], plan["opening"]
    two_parts = [take(n) for n in plan["two"]]
    cot_parts = [take(n) for n in plan["cot"]]
    weights = take(4)
    (wr_ref,) = take(1)
    dwr_carried = None if opening else take(1)[0]
    left = take(1 if opening else 2)
    (dwr_ref,) = take(1)
    results = take(2 * groups)
    two_buf, cot_buf, sems, win_buf, wdn_buf, weight_sems, gated_buf, grad_buf = take(8)
    stage, store_sems, left_sems = take(3)
    _, blocks, span, width = two_buf.shape
    rows = blocks * span
    hidden = win_buf.shape[0] // experts
    shard = hidden // 2
    group = pl.program_id(0)
    slot = group % gated_buf.shape[0]
    lane = lax.broadcasted_iota(jnp.int32, (rows, LANES), 1)

    copies = []
    for k in range(groups):
        some = []
        for parts, buffer in ((two_parts[k], two_buf), (cot_parts[k], cot_buf)):
            at = 0
            for part in parts:
                size = part.shape[0]
                some.append((part, buffer.at[k, pl.ds(at, size)]))
                at += size
        copies.append(
            [pltpu.make_async_copy(s, t, sems.at[k, n]) for n, (s, t) in enumerate(some)]
        )
    fetches = [
        pltpu.make_async_copy(
            ref.at[e],
            (win_buf, wdn_buf)[n // 2].at[pl.ds(e * hidden + (n % 2) * shard, shard)],
            weight_sems.at[e, n],
        )
        for e in range(experts)
        for n, ref in enumerate(weights)
    ]
    stores = [
        [
            pltpu.make_async_copy(stage.at[n], results[n * groups + k], store_sems.at[n])
            for n in range(2)
        ]
        for k in range(groups)
    ]
    if not opening:
        for k in range(groups):
            for n, buffer in enumerate((gated_buf, grad_buf)):
                place = k % buffer.shape[0]
                stores[k].append(
                    pltpu.make_async_copy(
                        buffer.at[place],
                        left[n].at[pl.ds(k * rows, rows)],
                        left_sems.at[place, n],
                    )
                )

    @pl.when(group == 0)
    def _():
        for copy in copies[0] + fetches:
            copy.start()
        for some in copies[1:]:
            for copy in some:
                copy.start()
        dwr_ref[...] = jnp.zeros_like(dwr_ref) if opening else dwr_carried[...]
        for copy in fetches:
            copy.wait()

    for k, some in enumerate(copies):

        @pl.when(group == k)
        def _(k=k, some=some):
            for copy in some:
                copy.wait()
            if k > 0:
                for store in stores[k - 1][:2]:
                    store.wait()
            if k > 1:
                for store in stores[k - 2][2:]:
                    store.wait()

    two = two_buf[group].reshape(rows, width)
    cot = cot_buf[group, :, :span, :].reshape(rows, width)
    chosen = (
        lax.broadcasted_iota(jnp.int32, (MASK_ROWS, LANES), 0)
        == lax.broadcasted_iota(jnp.int32, (MASK_ROWS, LANES), 1)
    ).astype(bf16)
    logits = jnp.where(lane < experts, mm(two, wr_ref[...]), neg_fill)
    shifted = jnp.exp(logits - jnp.max(logits, -1, keepdims=True))
    probs = shifted / jnp.sum(shifted, -1, keepdims=True)
    kept = jnp.concatenate(
        [
            mm(cot_buf[group, b, span : span + MASK_ROWS, :span], chosen, 0, 0)
            for b in range(blocks)
        ],
        0,
    )
    grad_gate = jnp.zeros((rows, LANES), f32)
    gates = probs * kept
    out_rows = gin_rows = None
    for e in range(experts):
        at = slice(e * hidden, (e + 1) * hidden)
        win, wdn = win_buf[at], wdn_buf[at]
        pre = mm(two, win, 1, 1)
        back_rows = mm(cot, wdn, 1, 1)
        gate = gates[:, e : e + 1]
        hidden_rows, slope = gelu_parts(pre)
        product = jnp.sum(hidden_rows * back_rows, -1, keepdims=True)
        grad_gate = jnp.where(lane == e, product, grad_gate)
        gated = (hidden_rows * gate).astype(bf16)
        grad_pre = (slope * back_rows * gate).astype(bf16)
        if opening:
            gated_buf[e, 1] = mm(gated, cot, 0, 0).astype(bf16)
            gated_buf[e, 0] = mm(grad_pre, two, 0, 0).astype(bf16)
        else:
            gated_buf[slot, :, at] = gated
            grad_buf[slot, :, at] = grad_pre
        out_part, gin_part = mm(gated, wdn), mm(grad_pre, win)
        out_rows = out_part if e == 0 else out_rows + out_part
        gin_rows = gin_part if e == 0 else gin_rows + gin_part
    grad_gate = grad_gate * kept
    grad_logits = probs * (grad_gate - jnp.sum(probs * grad_gate, -1, keepdims=True))
    grad_logits = grad_logits.astype(bf16)
    dwr_ref[...] += mm(grad_logits, two, 0, 0)[:SMALL]
    gin_rows = gin_rows + mm(grad_logits, wr_ref[...], 1, 1)
    stage[0] = out_rows.astype(bf16).reshape(blocks, span, width)
    stage[1] = gin_rows.astype(bf16).reshape(blocks, span, width)
    for k in range(groups):

        @pl.when(group == k)
        def _(k=k):
            for store in stores[k]:
                store.start()

    @pl.when(group == groups - 1)
    def _():
        if opening:
            copy = pltpu.make_async_copy(gated_buf, left[0], left_sems.at[0, 0])
            copy.start()
            copy.wait()
        for k in (groups - 1,) if groups == 1 else (groups - 2, groups - 1):
            for store in stores[k][0 if k == groups - 1 else 2 :]:
                store.wait()


def experts_call(two, cot, weights, wr, dwr, name, cost):
    groups = len(two)
    opening = groups == 1
    experts, shard, width = weights[0].shape
    hidden = 2 * shard
    blocks = sum(a.shape[0] for a in two[0])
    span = two[0][0].shape[1]
    rows = blocks * span
    plan = dict(
        groups=groups,
        experts=experts,
        opening=opening,
        two=[len(parts) for parts in two],
        cot=[len(parts) for parts in cot],
    )
    anywhere = pl.BlockSpec(memory_space=pl.ANY)
    once = lambda a: pl.BlockSpec(
        a.shape, lambda g: (0,) * len(a.shape), pipeline_mode=pl.Buffered(1)
    )
    result = jax.ShapeDtypeStruct((blocks, span, width), bf16)
    little = jax.ShapeDtypeStruct((SMALL, width), f32)
    if opening:
        left = [jax.ShapeDtypeStruct((experts, 2, hidden, width), bf16)]
        buffers = [pltpu.VMEM(left[0].shape, bf16), pltpu.VMEM((16, LANES), bf16)]
    else:
        left = [jax.ShapeDtypeStruct((groups * rows, experts * hidden), bf16)] * 2
        buffers = [pltpu.VMEM((2, rows, experts * hidden), bf16)] * 2
    pieces = [a for parts in two for a in parts] + [a for parts in cot for a in parts]
    outs = pl.pallas_call(
        functools.partial(expert_kernel, plan),
        grid=(groups,),
        in_specs=[anywhere] * (len(pieces) + 4)
        + [once(wr)]
        + ([] if opening else [once(little)]),
        out_specs=[anywhere] * len(left) + [once(little)] + [anywhere] * (2 * groups),
        out_shape=left + [little] + [result] * (2 * groups),
        scratch_shapes=[
            pltpu.VMEM((groups, blocks, span, width), bf16),
            pltpu.VMEM((groups, blocks, span + MASK_ROWS, width), bf16),
            pltpu.SemaphoreType.DMA((groups, 4)),
            pltpu.VMEM((experts * hidden, width), bf16),
            pltpu.VMEM((experts * hidden, width), bf16),
            pltpu.SemaphoreType.DMA((experts, 4)),
            *buffers,
            pltpu.VMEM((2, blocks, span, width), bf16),
            pltpu.SemaphoreType.DMA((2,)),
            pltpu.SemaphoreType.DMA((2, 2)),
        ],
        compiler_params=pltpu.CompilerParams(vmem_limit_bytes=VMEM_BYTES),
        cost_estimate=cost(10 * groups * rows * width * hidden * experts),
        name=name,
    )(*pieces, *weights, wr, *([] if opening else [dwr]))
    left, (dwr, *outs) = list(outs[: len(left)]), outs[len(left) :]
    return left, dwr, outs[:groups], outs[groups:]


def grads_kernel(plan, *refs):
    refs = list(refs)

    def take(number):
        taken, refs[:] = refs[:number], refs[number:]
        return taken

    groups = len(plan["two"])
    two_parts = [take(n) for n in plan["two"]]
    cot_parts = [take(n) for n in plan["cot"]]
    gated_ref, grad_ref, own_ref, kept_ref, sent_ref = take(5)
    two_buf, cot_buf, cot_rows, sems = refs
    _, blocks, span, width = two_buf.shape
    rows = blocks * span
    copies = []
    for k in range(groups):
        at = 0
        for n, part in enumerate(two_parts[k]):
            size = part.shape[0]
            copies.append(
                pltpu.make_async_copy(part, two_buf.at[k, pl.ds(at, size)], sems.at[k, n])
            )
            at += size
        at = 0
        for n, part in enumerate(cot_parts[k]):
            size = part.shape[0]
            copies.append(
                pltpu.make_async_copy(
                    part, cot_buf.at[k, pl.ds(at, size)], sems.at[k, 2 + n]
                )
            )
            at += size

    @pl.when(pl.program_id(0) == 0)
    def _():
        for copy in copies:
            copy.start()
        for copy in copies:
            copy.wait()
        for k in range(groups):
            cot_rows[k * rows : (k + 1) * rows] = cot_buf[k, :, :span, :].reshape(rows, width)

    half = own_ref.shape[2] // 2
    two = two_buf[...].reshape(groups * rows, width)
    for n, (left_ref, right) in enumerate(((grad_ref, two), (gated_ref, cot_rows[...]))):
        total = (own_ref[0, n].astype(f32) + mm(left_ref[...], right, 0, 0)).astype(bf16)
        kept_ref[0, n] = total[:half]
        sent_ref[0, n] = total[half:]


def grads_call(two, cot, left, own, first, many):
    groups = len(two)
    blocks = sum(a.shape[0] for a in two[0])
    _, span, width = two[0][0].shape
    rows = blocks * span
    hidden = own.shape[2]
    anywhere = pl.BlockSpec(memory_space=pl.ANY)
    pieces = [a for parts in two for a in parts] + [a for parts in cot for a in parts]
    columns = pl.BlockSpec((groups * rows, hidden), lambda e: (0, e + first))
    part = jax.ShapeDtypeStruct((many, 2, hidden // 2, width), bf16)
    part_spec = pl.BlockSpec((1, 2, hidden // 2, width), lambda e: (e, 0, 0, 0))
    plan = dict(two=[len(parts) for parts in two], cot=[len(parts) for parts in cot])
    return pl.pallas_call(
        functools.partial(grads_kernel, plan),
        grid=(many,),
        in_specs=[anywhere] * len(pieces)
        + [columns, columns, pl.BlockSpec((1, 2, hidden, width), lambda e: (e + first, 0, 0, 0))],
        out_specs=[part_spec, part_spec],
        out_shape=[part, part],
        scratch_shapes=[
            pltpu.VMEM((groups, blocks, span, width), bf16),
            pltpu.VMEM((groups, blocks, span + MASK_ROWS, width), bf16),
            pltpu.VMEM((groups * rows, width), bf16),
            pltpu.SemaphoreType.DMA((groups, 4)),
        ],
        compiler_params=pltpu.CompilerParams(vmem_limit_bytes=VMEM_BYTES),
        cost_estimate=true_cost(8 * groups * rows * width * hidden * many),
        name="expert_grads",
    )(*pieces, *left, own)


def flip(array, fsdp, bits):
    return lax.ppermute(array, "fsdp", [(n, n ^ bits) for n in range(fsdp)])


def tie(value, *others):
    return lax.optimization_barrier((value, others))[0]


def exchange(pieces):
    count = len(pieces)
    return [pieces[0]] + [
        lax.ppermute(pieces[k], "seq", [(n, n ^ k) for n in range(count)]) for k in range(1, count)
    ]


def relative(parts, index):
    count, bit = len(parts), 1
    while bit < count:
        swap = (index & bit) > 0
        parts = [jnp.where(swap, parts[k ^ bit], parts[k]) for k in range(count)]
        bit *= 2
    return parts


def plus(*arrays):
    return sum(a.astype(f32) for a in arrays).astype(bf16)


class LineSum:
    def __init__(self, seq):
        self.seq = seq
        self.index = lax.axis_index("seq")
        self.outer = (self.index == 0) | (self.index == seq - 1)
        self.inward = self.exchanged = self.total = None
        self.raw = self.pair = None
        self.ready = []
        self.done = []

    def hold(self, others):
        if self.seq == 4:
            self.inward, self.exchanged = tie((self.inward, self.exchanged), others)

    def arrive(self):
        if self.seq != 4:
            return
        total = None if self.pair is None else plus(self.pair, self.exchanged)
        pair = None if self.raw is None else plus(self.raw, self.inward)
        if self.total is not None:
            self.done.append(jnp.where(self.outer, self.inward, self.total))
        ready = [a for a in (pair, total) if a is not None]
        if ready:
            ready, self.index = lax.optimization_barrier((ready, self.index))
            self.outer = (self.index == 0) | (self.index == self.seq - 1)
            pair = ready.pop(0) if pair is not None else None
            total = ready.pop(0) if total is not None else None
        self.raw, self.pair, self.total = None, pair, total
        self.ready = [a for a in (pair, total) if a is not None]

    def send(self, raw=None):
        if self.seq != 4:
            self.done += [] if raw is None else [lax.psum(raw, "seq")]
            return
        self.raw = raw
        if raw is not None:
            self.ready.append(raw)
        if raw is not None or self.total is not None:
            if self.total is None:
                both = raw
            elif raw is None:
                both = self.total
            else:
                both = jnp.where(self.outer, raw, self.total)
            self.inward = lax.ppermute(both, "seq", [(0, 1), (1, 0), (2, 3), (3, 2)])
        if self.pair is not None:
            self.exchanged = lax.ppermute(self.pair, "seq", [(1, 2), (2, 1)])

    def step(self, raw=None):
        self.arrive()
        self.send(raw)

    def finish(self, count):
        while len(self.done) < count:
            self.step()
        return self.done


def back_kernel(
    gin_0, gin_2, gin_4, gin_6, mid_ref, cot_ref, tok_ref, att_ref, proj_ref, prob_ref, wall_ref,
    small_ref, dwr_ref, *rest,
):
    blocks, _, span, width = tok_ref.shape
    length = blocks * span
    gtok_refs, (dwall_ref, acc, acc_small, gatt, gproj) = rest[:blocks], rest[blocks:]
    step = pl.program_id(0)

    @pl.when(step == 0)
    def _():
        acc[...] = jnp.zeros_like(acc)
        acc_small[...] = jnp.zeros_like(acc_small)
        acc_small[:SMALL] = dwr_ref[...]

    gin = sum(ref[...].reshape(length, width).astype(f32) for ref in (gin_0, gin_2, gin_4, gin_6))
    unit_two, inverse_two = unit_norm(mid_ref[...].reshape(length, width))
    acc_small[6:7] += jnp.sum(gin * unit_two, 0, keepdims=True)
    acc_small[7:8] += jnp.sum(gin, 0, keepdims=True)
    grad_middle = cot_ref[...].reshape(length, width).astype(f32) + norm_back(
        gin * small_ref[6:7], unit_two, inverse_two
    )
    branch = grad_middle.astype(bf16)
    acc[:, 3 * width : 4 * width] += mm(att_ref[0], branch, 0, 0)
    gatt[...] = mm(branch, wall_ref[:, 3 * width : 4 * width], 1, 1).astype(bf16)
    lower = lax.broadcasted_iota(jnp.int32, (length, LANES), 1) < HEAD_DIM
    zero = jnp.zeros((length, LANES), bf16)
    scale = HEAD_DIM**-0.5

    def score_grad(weights, grad_weights):
        weights = weights.astype(f32)
        product = weights * grad_weights
        return (product - weights * jnp.sum(product, -1, keepdims=True)).astype(bf16)

    for pair in range(width // LANES):
        places = [slice((3 * pair + n) * LANES, (3 * pair + n + 1) * LANES) for n in range(3)]
        first, second, third = (proj_ref[0, :, place] for place in places)
        first_r, second_r, third_r = half_turn(first), half_turn(second), half_turn(third)
        grad = gatt[:, pair * LANES : (pair + 1) * LANES]
        weights_a, weights_b = prob_ref[0, 2 * pair], prob_ref[0, 2 * pair + 1]
        ds_a = score_grad(weights_a, mm(jnp.where(lower, grad, zero), second, 1, 1))
        ds_b = score_grad(weights_b, mm(jnp.where(lower, zero, grad), third, 1, 1))
        gproj[:, places[0]] = (
            jnp.where(lower, mm(ds_a, first_r), mm(ds_a, first_r, 0, 0)) * scale
        ).astype(bf16)
        gproj[:, places[1]] = jnp.where(
            lower, mm(weights_a, grad, 0, 0), mm(ds_b, third_r) * scale
        ).astype(bf16)
        gproj[:, places[2]] = jnp.where(
            lower, mm(ds_b, second_r, 0, 0) * scale, mm(weights_b, grad, 0, 0)
        ).astype(bf16)
    unit_one, inverse_one = unit_norm(tok_ref[...].reshape(length, width).astype(f32))
    one = (unit_one * small_ref[4:5] + small_ref[5:6]).astype(bf16)
    grad_one = mm(gproj[...], wall_ref[:, : 3 * width], 1, 1)
    acc_small[4:5] += jnp.sum(grad_one * unit_one, 0, keepdims=True)
    acc_small[5:6] += jnp.sum(grad_one, 0, keepdims=True)
    grad_tok = grad_middle + norm_back(grad_one * small_ref[4:5], unit_one, inverse_one)
    for k, ref in enumerate(gtok_refs):
        ref[0] = grad_tok[k * span : (k + 1) * span].astype(bf16)
    acc[:, : 3 * width] += mm(one, gproj[...], 0, 0)

    @pl.when(step == pl.num_programs(0) - 1)
    def _():
        dwall_ref[:, : 4 * width] = acc[...].astype(bf16)
        dwall_ref[:, 4 * width :] = acc_small[...].T.astype(bf16)


def back(gins, middle, cot, tok, att, proj, prob, wall, small, dwr):
    blocks, images, span, width = tok.shape
    length = blocks * span
    heads = width // HEAD_DIM
    split = pl.BlockSpec((blocks, 1, span, width), lambda i: (0, i, 0, 0))
    whole = lambda a: pl.BlockSpec(a.shape, lambda i: (0,) * len(a.shape))
    return pl.pallas_call(
        back_kernel,
        grid=(images,),
        in_specs=[split] * 7
        + [
            pl.BlockSpec((1, length, width), lambda i: (i, 0, 0)),
            pl.BlockSpec((1, length, 3 * width), lambda i: (i, 0, 0)),
            pl.BlockSpec((1, heads, length, length), lambda i: (i, 0, 0, 0)),
            whole(wall),
            whole(small),
            whole(dwr),
        ],
        out_specs=[pl.BlockSpec((1, span, width), lambda i: (i, 0, 0))] * blocks + [whole(wall)],
        out_shape=[jax.ShapeDtypeStruct((images, span, width), bf16)] * blocks
        + [jax.ShapeDtypeStruct(wall.shape, bf16)],
        scratch_shapes=[
            pltpu.VMEM((width, 4 * width), f32),
            pltpu.VMEM((LANES, width), f32),
            pltpu.VMEM((length, width), bf16),
            pltpu.VMEM((length, 3 * width), bf16),
        ],
        compiler_params=pltpu.CompilerParams(vmem_limit_bytes=VMEM_BYTES),
        cost_estimate=true_cost(10 * images * length * width * (4 * width + 3 * length)),
        name="back",
    )(*gins, middle, cot, tok, att, proj, prob, wall, small, dwr)


def kept_pairs(route_rows, token_live, order_rows, expert_count, capacity):
    labels = jnp.arange(expert_count, dtype=jnp.int32)
    alive = token_live > 0
    first_hot = ((route_rows[:, 0:1] == labels) & alive[:, None]).astype(bf16)
    second_hot = ((route_rows[:, 1:2] == labels) & alive[:, None]).astype(bf16)
    earlier = (order_rows[None, :] < order_rows[:, None]).astype(bf16)
    ahead = mm(earlier, jnp.concatenate([first_hot, second_hot], 1))
    ahead_first = ahead[:, :expert_count]
    ahead_second = ahead[:, expert_count:] + jnp.sum(first_hot.astype(f32), 0)
    return jnp.where(ahead_first < capacity, first_hot, 0) + jnp.where(
        ahead_second < capacity, second_hot, 0
    )


def local(
    fsdp,
    seq,
    tokens,
    ln1_gain,
    ln1_bias,
    w_qkv,
    w_out,
    ln2_gain,
    ln2_bias,
    w_router,
    w_in,
    w_down,
    padding,
    routes,
    priority,
    cotangent,
):
    images, span, width = tokens.shape
    expert_count, shard_rows = w_in.shape[0], w_in.shape[1]
    rows = images * span
    own = images // seq
    length = seq * span
    capacity = (2 * rows + expert_count - 1) // expert_count
    outer = fsdp // 8
    if outer > 1:
        outer_groups = [[o * 8 + n for o in range(outer)] for n in range(8)]
    spread = functools.partial(flip, fsdp=fsdp)
    seq_index = lax.axis_index("seq")
    place = lax.axis_index("fsdp") if outer == 1 else jnp.int32(0)
    place = place.astype(jnp.int32).reshape(1)

    def picked(array, k):
        return lax.dynamic_index_in_dim(array, seq_index ^ k, 0, keepdims=False)

    tokens = tokens.reshape(seq, own * span, width)
    tok = jnp.stack(exchange([picked(tokens, k) for k in range(seq)]))
    tok = tok.reshape(seq, own, span, width)

    columns = jnp.concatenate(
        [w_router] + [v[:, None] for v in (ln1_gain, ln1_bias, ln2_gain, ln2_bias)], 1
    )
    columns = jnp.pad(columns, ((0, 0), (0, LANES - columns.shape[1])))
    shard = jnp.concatenate([w_qkv, w_out, columns], 1)
    if outer == 1:
        cut = width // 16
        from_x, from_y = spread(shard, bits=2), spread(shard, bits=4)
        from_x, from_y = tie((from_x, from_y), tok)
        near = [(0, 0, shard), (2, 0, from_x), (4, 0, from_y)]
        far = [
            (6, 0, spread(from_x[:cut], bits=4)),
            (6, cut, spread(from_y[cut:], bits=2)),
        ]
        near += [(r + 1, skip, spread(a, bits=1)) for r, skip, a in near]
    else:
        full = lax.all_gather(shard, "fsdp", axis=0, tiled=True)
        from_x = from_y = full
        near, far = [(n, 0, full[n * (width // 8) : (n + 1) * (width // 8)]) for n in range(8)], []

    live = lax.dynamic_slice_in_dim(padding, seq_index * span, span, 1)
    kept = kept_pairs(
        routes.reshape(rows, 2), live.reshape(rows), priority.reshape(rows), expert_count, capacity
    )
    kept = jnp.swapaxes(kept.reshape(seq, own * span, expert_count), 1, 2)
    kept = jnp.pad(
        kept, ((0, 0), (0, MASK_ROWS - expert_count), (0, width - own * span))
    ).astype(bf16)
    cot = cotangent * live[:, :, None].astype(bf16)
    packed = jnp.concatenate([cot.reshape(seq, own * span, width), kept], 1)
    packed = tie(packed, tok, from_x, from_y)
    packed = jnp.stack(exchange([picked(packed, k) for k in range(seq)]))
    late = tie([a for _, _, a in far], packed)
    far += [(r + 1, skip, spread(a, bits=1)) for (r, skip, _), a in zip(far, late)]
    offsets = [(r, skip) for r, skip, _ in near + far]
    pieces = [a for _, _, a in near + far]
    cot_x, cot_y = spread(packed, bits=2), spread(packed, bits=4)
    half = seq // 2
    cot_far = [spread(cot_x[:half], bits=4), spread(cot_y[half:], bits=2)]

    win, wdn = w_in, w_down
    if outer > 1:
        win = lax.all_gather(win, "fsdp", axis=1, tiled=True, axis_index_groups=outer_groups)
        wdn = lax.all_gather(wdn, "fsdp", axis=1, tiled=True, axis_index_groups=outer_groups)
    win, wdn = tie((win, wdn), pieces)
    weights = [win, spread(win, bits=1), wdn, spread(wdn, bits=1)]

    mine = lax.dynamic_slice_in_dim(padding, seq_index * own, own, 0).reshape(own, seq, span)
    mine = jnp.stack(relative([mine[:, b] for b in range(seq)], seq_index))
    vis = jnp.where(mine > 0, 0.0, neg_fill).astype(f32)
    vis = jnp.swapaxes(vis, 0, 1).reshape(own, 1, length)
    middle, two, proj, att, prob, wall, wr, small = front(tok, pieces, offsets, vis, place)
    two = two.reshape(seq, own * span, width)
    two_far = [[spread(two, bits=bits)] for bits in (2, 4, 6)]

    (dw,), dwr, out_0, gin_0 = experts_call(
        [[two]], [[packed]], weights, wr, None, "experts_own", lambda flops: SHORT
    )
    cots = [[cot_x], [cot_y], cot_far]
    left, dwr, outs, gins = experts_call(
        two_far, cots, weights, wr, dwr, "experts_far", true_cost
    )
    arrived = [spread(a, bits=bits) for a, bits in zip(gins, (2, 4, 6))]

    def finished(dw_kept, dw_sent):
        raw = plus(dw_kept, spread(dw_sent, bits=1))
        if outer > 1:
            raw = lax.psum_scatter(
                raw, "fsdp", scatter_dimension=2, tiled=True, axis_index_groups=outer_groups
            )
        return lax.optimization_barrier([raw[n : n + 1] for n in range(raw.shape[0])])

    line = LineSum(seq)
    line.step(finished(*grads_call(two_far, cots, left, dw, 0, 1))[0])
    left, dw = tie((left, dw), line.ready)
    parts = grads_call(two_far, cots, left, dw, 1, expert_count - 1)
    line.hold(arrived)
    line.arrive()
    raws = finished(*tie(parts, line.ready, arrived))
    line.send(raws.pop(0))
    gins = gin_0 + tie(arrived, line.ready)

    shape4 = (seq, own, span, width)
    outs = [spread(a, bits=bits) for a, bits in zip(tie(outs, arrived), (2, 4, 6))]
    *grad_tok, dense = back(
        [a.reshape(shape4) for a in gins],
        middle,
        packed[:, : own * span].reshape(shape4),
        tok,
        att,
        proj,
        prob,
        wall,
        small,
        dwr,
    )
    dense = lax.psum_scatter(dense, "fsdp", scatter_dimension=0, tiled=True)
    line.hold((grad_tok, outs))
    line.step(raws.pop(0))
    line.step(raws.pop(0))
    line.hold(dense)
    line.step()

    outs, grad_tok = tie((outs, grad_tok), line.ready)
    outs = [a.reshape(shape4) for a in out_0 + outs]
    home = []
    for k in range(seq):
        alive = mine[k][:, :, None].astype(f32)
        combined = sum(a[k].astype(f32) for a in outs)
        home.append(jnp.stack([(alive * (middle[k] + combined)).astype(bf16), grad_tok[k]]))
    home = exchange(home)
    line.step()
    home = relative(tie(home, line.ready), seq_index)
    outputs, grad_tokens = (
        jnp.concatenate([a[n] for a in home], 0).reshape(images, span, width) for n in range(2)
    )
    grads = line.finish(expert_count)
    expert_grads = [jnp.concatenate([g[:, n] for g in grads], 0).astype(f32) for n in range(2)]
    dense = lax.psum(dense, "seq").astype(f32)
    tail = dense[:, 4 * width :]
    return (
        outputs,
        grad_tokens,
        tail[:, 4],
        tail[:, 5],
        dense[:, : 3 * width],
        dense[:, 3 * width : 4 * width],
        tail[:, 6],
        tail[:, 7],
        tail[:, :expert_count],
        expert_grads[0],
        expert_grads[1],
    )


def solution(mesh):
    rows = P("fsdp", "seq", None)
    in_specs = (
        rows,
        P("fsdp"),
        P("fsdp"),
        P("fsdp", None),
        P("fsdp", None),
        P("fsdp"),
        P("fsdp"),
        P("fsdp", None),
        P(None, "fsdp", None),
        P(None, "fsdp", None),
        P("fsdp", None),
        rows,
        P("fsdp", "seq"),
        rows,
    )
    out_specs = (
        rows,
        rows,
        P("fsdp"),
        P("fsdp"),
        P("fsdp", None),
        P("fsdp", None),
        P("fsdp"),
        P("fsdp"),
        P("fsdp", None),
        P(None, "fsdp", None),
        P(None, "fsdp", None),
    )
    return jax.shard_map(
        functools.partial(local, mesh.shape["fsdp"], mesh.shape["seq"]),
        mesh=mesh,
        in_specs=in_specs,
        out_specs=out_specs,
        check_vma=False,
    )
```

```python
import functools
import math

import jax
import jax.numpy as jnp
from jax import lax
from jax.experimental import pallas as pl
from jax.experimental.pallas import tpu as pltpu
from jax.sharding import PartitionSpec as P

HEAD_DIM = 64
LANES = 128
MASK_ROWS = 16
SMALL = 8
norm_eps = 1e-06
neg_fill = -1e30
f32 = jnp.float32
bf16 = jnp.bfloat16
VMEM_BYTES = 60 * 1024 * 1024
SHORT = pl.CostEstimate(flops=1000, bytes_accessed=1000, transcendentals=0)


def true_cost(flops):
    return pl.CostEstimate(flops=2 * flops, bytes_accessed=16 * 1024 * 1024, transcendentals=0)


def mm(left, right, left_dim=1, right_dim=0):
    return lax.dot_general(
        left, right, (((left_dim,), (right_dim,)), ((), ())), preferred_element_type=f32
    )


def unit_norm(rows):
    centred = rows - jnp.mean(rows, -1, keepdims=True)
    inverse = lax.rsqrt(jnp.mean(centred * centred, -1, keepdims=True) + norm_eps)
    return centred * inverse, inverse


def norm_back(scaled, unit, inverse):
    return inverse * (
        scaled
        - jnp.mean(scaled, -1, keepdims=True)
        - unit * jnp.mean(scaled * unit, -1, keepdims=True)
    )


def half_turn(tile):
    return pltpu.roll(tile.astype(f32), HEAD_DIM, axis=1).astype(bf16)


def wall_copies(pieces, offsets, place_ref, wall_ref, sems):
    copies = []
    for n, (piece, (r, skip)) in enumerate(zip(pieces, offsets)):
        rows = piece.shape[0]
        shard = wall_ref.shape[0] // 8
        start = pl.multiple_of((place_ref[0] ^ r) * shard + skip, 16)
        copies.append(pltpu.make_async_copy(piece, wall_ref.at[pl.ds(start, rows)], sems.at[n]))
    return copies


def front_kernel(offsets, *refs):
    pieces = refs[: len(offsets)]
    tok_ref, vis_ref, place_ref = refs[len(offsets) : len(offsets) + 3]
    mid_ref, two_ref, proj_ref, att_ref, prob_ref, full_ref, wr_ref, small_ref = refs[
        len(offsets) + 3 : len(offsets) + 11
    ]
    wall_ref, sems, full_sem = refs[len(offsets) + 11 :]
    blocks, _, span, width = tok_ref.shape
    length = blocks * span
    save = pltpu.make_async_copy(wall_ref, full_ref, full_sem)

    @pl.when(pl.program_id(0) == 0)
    def _():
        copies = wall_copies(pieces, offsets, place_ref, wall_ref, sems)
        for copy in copies:
            copy.start()
        for copy in copies:
            copy.wait()
        save.start()
        columns = wall_ref[:, 4 * width :]
        wr_ref[...] = columns
        small_ref[...] = columns.astype(f32).T[:SMALL]

    rows = tok_ref[...].reshape(length, width).astype(f32)
    unit, _ = unit_norm(rows)
    one = (unit * small_ref[4:5] + small_ref[5:6]).astype(bf16)
    proj_ref[0] = mm(one, wall_ref[:, : 3 * width]).astype(bf16)
    lower = lax.broadcasted_iota(jnp.int32, (length, LANES), 1) < HEAD_DIM
    zero = jnp.zeros((length, LANES), bf16)
    bias = vis_ref[0]

    def soften(index, queries, keys):
        scores = mm(queries, keys, 1, 1) * (HEAD_DIM**-0.5) + bias
        shifted = jnp.exp(scores - jnp.max(scores, -1, keepdims=True))
        weights = (shifted / jnp.sum(shifted, -1, keepdims=True)).astype(bf16)
        prob_ref[0, index] = weights
        return weights

    for pair in range(width // LANES):
        first, second, third = (
            proj_ref[0, :, (3 * pair + n) * LANES : (3 * pair + n + 1) * LANES] for n in range(3)
        )
        weights_a = soften(2 * pair, jnp.where(lower, first, zero), half_turn(first))
        weights_b = soften(2 * pair + 1, jnp.where(lower, zero, second), half_turn(third))
        both = jnp.where(lower, mm(weights_a, second), mm(weights_b, third))
        att_ref[0, :, pair * LANES : (pair + 1) * LANES] = both.astype(bf16)
    middle = rows + mm(att_ref[0], wall_ref[:, 3 * width : 4 * width])
    mid_ref[...] = middle.reshape(mid_ref.shape)
    unit, _ = unit_norm(middle)
    two_ref[...] = (unit * small_ref[6:7] + small_ref[7:8]).astype(bf16).reshape(two_ref.shape)

    @pl.when(pl.program_id(0) == pl.num_programs(0) - 1)
    def _():
        save.wait()


def front(tok, pieces, offsets, vis, place):
    blocks, images, span, width = tok.shape
    length = blocks * span
    heads = width // HEAD_DIM
    split = pl.BlockSpec((blocks, 1, span, width), lambda i: (0, i, 0, 0))
    anywhere = pl.BlockSpec(memory_space=pl.ANY)
    columns = pieces[0].shape[1]
    return pl.pallas_call(
        functools.partial(front_kernel, offsets),
        grid=(images,),
        in_specs=[anywhere] * len(pieces)
        + [
            split,
            pl.BlockSpec((1, 1, length), lambda i: (i, 0, 0)),
            pl.BlockSpec(memory_space=pltpu.SMEM),
        ],
        out_specs=[
            split,
            split,
            pl.BlockSpec((1, length, 3 * width), lambda i: (i, 0, 0)),
            pl.BlockSpec((1, length, width), lambda i: (i, 0, 0)),
            pl.BlockSpec((1, heads, length, length), lambda i: (i, 0, 0, 0)),
            anywhere,
            pl.BlockSpec((width, LANES), lambda i: (0, 0)),
            pl.BlockSpec((SMALL, width), lambda i: (0, 0)),
        ],
        out_shape=[
            jax.ShapeDtypeStruct(tok.shape, f32),
            jax.ShapeDtypeStruct(tok.shape, bf16),
            jax.ShapeDtypeStruct((images, length, 3 * width), bf16),
            jax.ShapeDtypeStruct((images, length, width), bf16),
            jax.ShapeDtypeStruct((images, heads, length, length), bf16),
            jax.ShapeDtypeStruct((width, columns), bf16),
            jax.ShapeDtypeStruct((width, LANES), bf16),
            jax.ShapeDtypeStruct((SMALL, width), f32),
        ],
        scratch_shapes=[
            pltpu.VMEM((width, columns), bf16),
            pltpu.SemaphoreType.DMA((len(pieces),)),
            pltpu.SemaphoreType.DMA(()),
        ],
        compiler_params=pltpu.CompilerParams(vmem_limit_bytes=VMEM_BYTES),
        cost_estimate=SHORT,
        name="front",
    )(*pieces, tok, vis, place)


def gelu_parts(pre):
    bell = jnp.exp2(pre * pre * (-0.5 * math.log2(math.e)))
    frac = 1.0 / (1.0 + (0.3275911 * math.sqrt(0.5)) * jnp.abs(pre))
    a5, a4, a3, a2, a1 = (
        0.5 * c for c in (1.061405429, -1.453152027, 1.421413741, -0.284496736, 0.254829592)
    )
    tail = frac * (a1 + frac * (a2 + frac * (a3 + frac * (a4 + frac * a5)))) * bell
    cumulative = jnp.where(pre >= 0, 1.0 - tail, tail)
    return pre * cumulative, cumulative + (pre * 0.3989422804014327) * bell


def expert_kernel(plan, *refs):
    refs = list(refs)

    def take(number):
        taken, refs[:] = refs[:number], refs[number:]
        return taken

    groups, experts, opening = plan["groups"], plan["experts"], plan["opening"]
    two_parts = [take(n) for n in plan["two"]]
    cot_parts = [take(n) for n in plan["cot"]]
    weights = take(4)
    (wr_ref,) = take(1)
    dwr_carried = None if opening else take(1)[0]
    left = take(1 if opening else 2)
    (dwr_ref,) = take(1)
    results = take(2 * groups)
    two_buf, cot_buf, sems, win_buf, wdn_buf, weight_sems, gated_buf, grad_buf = take(8)
    stage, store_sems, left_sems = take(3)
    _, blocks, span, width = two_buf.shape
    rows = blocks * span
    hidden = win_buf.shape[0] // experts
    shard = hidden // 2
    group = pl.program_id(0)
    slot = group % gated_buf.shape[0]
    lane = lax.broadcasted_iota(jnp.int32, (rows, LANES), 1)

    copies = []
    for k in range(groups):
        some = []
        for parts, buffer in ((two_parts[k], two_buf), (cot_parts[k], cot_buf)):
            at = 0
            for part in parts:
                size = part.shape[0]
                some.append((part, buffer.at[k, pl.ds(at, size)]))
                at += size
        copies.append(
            [pltpu.make_async_copy(s, t, sems.at[k, n]) for n, (s, t) in enumerate(some)]
        )
    fetches = [
        pltpu.make_async_copy(
            ref.at[e],
            (win_buf, wdn_buf)[n // 2].at[pl.ds(e * hidden + (n % 2) * shard, shard)],
            weight_sems.at[e, n],
        )
        for e in range(experts)
        for n, ref in enumerate(weights)
    ]
    stores = [
        [
            pltpu.make_async_copy(stage.at[n], results[n * groups + k], store_sems.at[n])
            for n in range(2)
        ]
        for k in range(groups)
    ]
    if not opening:
        for k in range(groups):
            for n, buffer in enumerate((gated_buf, grad_buf)):
                place = k % buffer.shape[0]
                stores[k].append(
                    pltpu.make_async_copy(
                        buffer.at[place],
                        left[n].at[pl.ds(k * rows, rows)],
                        left_sems.at[place, n],
                    )
                )

    @pl.when(group == 0)
    def _():
        for copy in copies[0] + fetches:
            copy.start()
        for some in copies[1:]:
            for copy in some:
                copy.start()
        dwr_ref[...] = jnp.zeros_like(dwr_ref) if opening else dwr_carried[...]
        for copy in fetches:
            copy.wait()

    for k, some in enumerate(copies):

        @pl.when(group == k)
        def _(k=k, some=some):
            for copy in some:
                copy.wait()
            if k > 0:
                for store in stores[k - 1][:2]:
                    store.wait()
            if k > 1:
                for store in stores[k - 2][2:]:
                    store.wait()

    two = two_buf[group].reshape(rows, width)
    cot = cot_buf[group, :, :span, :].reshape(rows, width)
    chosen = (
        lax.broadcasted_iota(jnp.int32, (MASK_ROWS, LANES), 0)
        == lax.broadcasted_iota(jnp.int32, (MASK_ROWS, LANES), 1)
    ).astype(bf16)
    logits = jnp.where(lane < experts, mm(two, wr_ref[...]), neg_fill)
    shifted = jnp.exp(logits - jnp.max(logits, -1, keepdims=True))
    probs = shifted / jnp.sum(shifted, -1, keepdims=True)
    kept = jnp.concatenate(
        [
            mm(cot_buf[group, b, span : span + MASK_ROWS, :span], chosen, 0, 0)
            for b in range(blocks)
        ],
        0,
    )
    grad_gate = jnp.zeros((rows, LANES), f32)
    gates = probs * kept
    out_rows = gin_rows = None
    for e in range(experts):
        at = slice(e * hidden, (e + 1) * hidden)
        win, wdn = win_buf[at], wdn_buf[at]
        pre = mm(two, win, 1, 1)
        back_rows = mm(cot, wdn, 1, 1)
        gate = gates[:, e : e + 1]
        hidden_rows, slope = gelu_parts(pre)
        product = jnp.sum(hidden_rows * back_rows, -1, keepdims=True)
        grad_gate = jnp.where(lane == e, product, grad_gate)
        gated = (hidden_rows * gate).astype(bf16)
        grad_pre = (slope * back_rows * gate).astype(bf16)
        if opening:
            gated_buf[e, 1] = mm(gated, cot, 0, 0).astype(bf16)
            gated_buf[e, 0] = mm(grad_pre, two, 0, 0).astype(bf16)
        else:
            gated_buf[slot, :, at] = gated
            grad_buf[slot, :, at] = grad_pre
        out_part, gin_part = mm(gated, wdn), mm(grad_pre, win)
        out_rows = out_part if e == 0 else out_rows + out_part
        gin_rows = gin_part if e == 0 else gin_rows + gin_part
    grad_gate = grad_gate * kept
    grad_logits = probs * (grad_gate - jnp.sum(probs * grad_gate, -1, keepdims=True))
    grad_logits = grad_logits.astype(bf16)
    dwr_ref[...] += mm(grad_logits, two, 0, 0)[:SMALL]
    gin_rows = gin_rows + mm(grad_logits, wr_ref[...], 1, 1)
    stage[0] = out_rows.astype(bf16).reshape(blocks, span, width)
    stage[1] = gin_rows.astype(bf16).reshape(blocks, span, width)
    for k in range(groups):

        @pl.when(group == k)
        def _(k=k):
            for store in stores[k]:
                store.start()

    @pl.when(group == groups - 1)
    def _():
        if opening:
            copy = pltpu.make_async_copy(gated_buf, left[0], left_sems.at[0, 0])
            copy.start()
            copy.wait()
        for k in (groups - 1,) if groups == 1 else (groups - 2, groups - 1):
            for store in stores[k][0 if k == groups - 1 else 2 :]:
                store.wait()


def experts_call(two, cot, weights, wr, dwr, name, cost):
    groups = len(two)
    opening = groups == 1
    experts, shard, width = weights[0].shape
    hidden = 2 * shard
    blocks = sum(a.shape[0] for a in two[0])
    span = two[0][0].shape[1]
    rows = blocks * span
    plan = dict(
        groups=groups,
        experts=experts,
        opening=opening,
        two=[len(parts) for parts in two],
        cot=[len(parts) for parts in cot],
    )
    anywhere = pl.BlockSpec(memory_space=pl.ANY)
    once = lambda a: pl.BlockSpec(
        a.shape, lambda g: (0,) * len(a.shape), pipeline_mode=pl.Buffered(1)
    )
    result = jax.ShapeDtypeStruct((blocks, span, width), bf16)
    little = jax.ShapeDtypeStruct((SMALL, width), f32)
    if opening:
        left = [jax.ShapeDtypeStruct((experts, 2, hidden, width), bf16)]
        buffers = [pltpu.VMEM(left[0].shape, bf16), pltpu.VMEM((16, LANES), bf16)]
    else:
        left = [jax.ShapeDtypeStruct((groups * rows, experts * hidden), bf16)] * 2
        buffers = [pltpu.VMEM((2, rows, experts * hidden), bf16)] * 2
    pieces = [a for parts in two for a in parts] + [a for parts in cot for a in parts]
    outs = pl.pallas_call(
        functools.partial(expert_kernel, plan),
        grid=(groups,),
        in_specs=[anywhere] * (len(pieces) + 4)
        + [once(wr)]
        + ([] if opening else [once(little)]),
        out_specs=[anywhere] * len(left) + [once(little)] + [anywhere] * (2 * groups),
        out_shape=left + [little] + [result] * (2 * groups),
        scratch_shapes=[
            pltpu.VMEM((groups, blocks, span, width), bf16),
            pltpu.VMEM((groups, blocks, span + MASK_ROWS, width), bf16),
            pltpu.SemaphoreType.DMA((groups, 4)),
            pltpu.VMEM((experts * hidden, width), bf16),
            pltpu.VMEM((experts * hidden, width), bf16),
            pltpu.SemaphoreType.DMA((experts, 4)),
            *buffers,
            pltpu.VMEM((2, blocks, span, width), bf16),
            pltpu.SemaphoreType.DMA((2,)),
            pltpu.SemaphoreType.DMA((2, 2)),
        ],
        compiler_params=pltpu.CompilerParams(vmem_limit_bytes=VMEM_BYTES),
        cost_estimate=cost(10 * groups * rows * width * hidden * experts),
        name=name,
    )(*pieces, *weights, wr, *([] if opening else [dwr]))
    left, (dwr, *outs) = list(outs[: len(left)]), outs[len(left) :]
    return left, dwr, outs[:groups], outs[groups:]


def grads_kernel(plan, *refs):
    refs = list(refs)

    def take(number):
        taken, refs[:] = refs[:number], refs[number:]
        return taken

    groups = len(plan["two"])
    two_parts = [take(n) for n in plan["two"]]
    cot_parts = [take(n) for n in plan["cot"]]
    gated_ref, grad_ref, own_ref, kept_ref, sent_ref = take(5)
    two_buf, cot_buf, cot_rows, sems = refs
    _, blocks, span, width = two_buf.shape
    rows = blocks * span
    copies = []
    for k in range(groups):
        at = 0
        for n, part in enumerate(two_parts[k]):
            size = part.shape[0]
            copies.append(
                pltpu.make_async_copy(part, two_buf.at[k, pl.ds(at, size)], sems.at[k, n])
            )
            at += size
        at = 0
        for n, part in enumerate(cot_parts[k]):
            size = part.shape[0]
            copies.append(
                pltpu.make_async_copy(
                    part, cot_buf.at[k, pl.ds(at, size)], sems.at[k, 2 + n]
                )
            )
            at += size

    @pl.when(pl.program_id(0) == 0)
    def _():
        for copy in copies:
            copy.start()
        for copy in copies:
            copy.wait()
        for k in range(groups):
            cot_rows[k * rows : (k + 1) * rows] = cot_buf[k, :, :span, :].reshape(rows, width)

    half = own_ref.shape[2] // 2
    two = two_buf[...].reshape(groups * rows, width)
    for n, (left_ref, right) in enumerate(((grad_ref, two), (gated_ref, cot_rows[...]))):
        total = (own_ref[0, n].astype(f32) + mm(left_ref[...], right, 0, 0)).astype(bf16)
        kept_ref[0, n] = total[:half]
        sent_ref[0, n] = total[half:]


def grads_call(two, cot, left, own, first, many):
    groups = len(two)
    blocks = sum(a.shape[0] for a in two[0])
    _, span, width = two[0][0].shape
    rows = blocks * span
    hidden = own.shape[2]
    anywhere = pl.BlockSpec(memory_space=pl.ANY)
    pieces = [a for parts in two for a in parts] + [a for parts in cot for a in parts]
    columns = pl.BlockSpec((groups * rows, hidden), lambda e: (0, e + first))
    part = jax.ShapeDtypeStruct((many, 2, hidden // 2, width), bf16)
    part_spec = pl.BlockSpec((1, 2, hidden // 2, width), lambda e: (e, 0, 0, 0))
    plan = dict(two=[len(parts) for parts in two], cot=[len(parts) for parts in cot])
    return pl.pallas_call(
        functools.partial(grads_kernel, plan),
        grid=(many,),
        in_specs=[anywhere] * len(pieces)
        + [columns, columns, pl.BlockSpec((1, 2, hidden, width), lambda e: (e + first, 0, 0, 0))],
        out_specs=[part_spec, part_spec],
        out_shape=[part, part],
        scratch_shapes=[
            pltpu.VMEM((groups, blocks, span, width), bf16),
            pltpu.VMEM((groups, blocks, span + MASK_ROWS, width), bf16),
            pltpu.VMEM((groups * rows, width), bf16),
            pltpu.SemaphoreType.DMA((groups, 4)),
        ],
        compiler_params=pltpu.CompilerParams(vmem_limit_bytes=VMEM_BYTES),
        cost_estimate=true_cost(8 * groups * rows * width * hidden * many),
        name="expert_grads",
    )(*pieces, *left, own)


def flip(array, fsdp, bits):
    return lax.ppermute(array, "fsdp", [(n, n ^ bits) for n in range(fsdp)])


def tie(value, *others):
    return lax.optimization_barrier((value, others))[0]


def exchange(pieces):
    count = len(pieces)
    return [pieces[0]] + [
        lax.ppermute(pieces[k], "seq", [(n, n ^ k) for n in range(count)]) for k in range(1, count)
    ]


def relative(parts, index):
    count, bit = len(parts), 1
    while bit < count:
        swap = (index & bit) > 0
        parts = [jnp.where(swap, parts[k ^ bit], parts[k]) for k in range(count)]
        bit *= 2
    return parts


def plus(*arrays):
    return sum(a.astype(f32) for a in arrays).astype(bf16)


class LineSum:
    def __init__(self, seq):
        self.seq = seq
        self.index = lax.axis_index("seq")
        self.outer = (self.index == 0) | (self.index == seq - 1)
        self.inward = self.exchanged = self.total = None
        self.raw = self.pair = None
        self.ready = []
        self.done = []

    def hold(self, others):
        if self.seq == 4:
            self.inward, self.exchanged = tie((self.inward, self.exchanged), others)

    def waiting(self):
        return [a for a in (self.inward, self.exchanged) if a is not None]

    def arrive(self):
        if self.seq != 4:
            return
        total = None if self.pair is None else plus(self.pair, self.exchanged)
        pair = None if self.raw is None else plus(self.raw, self.inward)
        if self.total is not None:
            self.done.append(jnp.where(self.outer, self.inward, self.total))
        ready = [a for a in (pair, total) if a is not None]
        if ready:
            ready, self.index = lax.optimization_barrier((ready, self.index))
            self.outer = (self.index == 0) | (self.index == self.seq - 1)
            pair = ready.pop(0) if pair is not None else None
            total = ready.pop(0) if total is not None else None
        self.raw, self.pair, self.total = None, pair, total
        self.ready = [a for a in (pair, total) if a is not None]

    def send(self, raw=None):
        if self.seq != 4:
            self.done += [] if raw is None else [lax.psum(raw, "seq")]
            return
        self.raw = raw
        if raw is not None:
            self.ready.append(raw)
        if raw is not None or self.total is not None:
            if self.total is None:
                both = raw
            elif raw is None:
                both = self.total
            else:
                both = jnp.where(self.outer, raw, self.total)
            self.inward = lax.ppermute(both, "seq", [(0, 1), (1, 0), (2, 3), (3, 2)])
        if self.pair is not None:
            self.exchanged = lax.ppermute(self.pair, "seq", [(1, 2), (2, 1)])

    def step(self, raw=None):
        self.arrive()
        self.send(raw)

    def finish(self, count):
        while len(self.done) < count:
            self.step()
        return self.done


def back_kernel(
    gin_0, gin_2, gin_4, gin_6, mid_ref, cot_ref, tok_ref, att_ref, proj_ref, prob_ref, wall_ref,
    small_ref, dwr_ref, *rest,
):
    blocks, _, span, width = tok_ref.shape
    length = blocks * span
    gtok_refs, (dwall_ref, acc, acc_small, gatt, gproj) = rest[:blocks], rest[blocks:]
    step = pl.program_id(0)

    @pl.when(step == 0)
    def _():
        acc[...] = jnp.zeros_like(acc)
        acc_small[...] = jnp.zeros_like(acc_small)
        acc_small[:SMALL] = dwr_ref[...]

    gin = sum(ref[...].reshape(length, width).astype(f32) for ref in (gin_0, gin_2, gin_4, gin_6))
    unit_two, inverse_two = unit_norm(mid_ref[...].reshape(length, width))
    acc_small[6:7] += jnp.sum(gin * unit_two, 0, keepdims=True)
    acc_small[7:8] += jnp.sum(gin, 0, keepdims=True)
    grad_middle = cot_ref[...].reshape(length, width).astype(f32) + norm_back(
        gin * small_ref[6:7], unit_two, inverse_two
    )
    branch = grad_middle.astype(bf16)
    acc[:, 3 * width : 4 * width] += mm(att_ref[0], branch, 0, 0)
    gatt[...] = mm(branch, wall_ref[:, 3 * width : 4 * width], 1, 1).astype(bf16)
    lower = lax.broadcasted_iota(jnp.int32, (length, LANES), 1) < HEAD_DIM
    zero = jnp.zeros((length, LANES), bf16)
    scale = HEAD_DIM**-0.5

    def score_grad(weights, grad_weights):
        weights = weights.astype(f32)
        product = weights * grad_weights
        return (product - weights * jnp.sum(product, -1, keepdims=True)).astype(bf16)

    for pair in range(width // LANES):
        places = [slice((3 * pair + n) * LANES, (3 * pair + n + 1) * LANES) for n in range(3)]
        first, second, third = (proj_ref[0, :, place] for place in places)
        first_r, second_r, third_r = half_turn(first), half_turn(second), half_turn(third)
        grad = gatt[:, pair * LANES : (pair + 1) * LANES]
        weights_a, weights_b = prob_ref[0, 2 * pair], prob_ref[0, 2 * pair + 1]
        ds_a = score_grad(weights_a, mm(jnp.where(lower, grad, zero), second, 1, 1))
        ds_b = score_grad(weights_b, mm(jnp.where(lower, zero, grad), third, 1, 1))
        gproj[:, places[0]] = (
            jnp.where(lower, mm(ds_a, first_r), mm(ds_a, first_r, 0, 0)) * scale
        ).astype(bf16)
        gproj[:, places[1]] = jnp.where(
            lower, mm(weights_a, grad, 0, 0), mm(ds_b, third_r) * scale
        ).astype(bf16)
        gproj[:, places[2]] = jnp.where(
            lower, mm(ds_b, second_r, 0, 0) * scale, mm(weights_b, grad, 0, 0)
        ).astype(bf16)
    unit_one, inverse_one = unit_norm(tok_ref[...].reshape(length, width).astype(f32))
    one = (unit_one * small_ref[4:5] + small_ref[5:6]).astype(bf16)
    grad_one = mm(gproj[...], wall_ref[:, : 3 * width], 1, 1)
    acc_small[4:5] += jnp.sum(grad_one * unit_one, 0, keepdims=True)
    acc_small[5:6] += jnp.sum(grad_one, 0, keepdims=True)
    grad_tok = grad_middle + norm_back(grad_one * small_ref[4:5], unit_one, inverse_one)
    for k, ref in enumerate(gtok_refs):
        ref[0] = grad_tok[k * span : (k + 1) * span].astype(bf16)
    acc[:, : 3 * width] += mm(one, gproj[...], 0, 0)

    @pl.when(step == pl.num_programs(0) - 1)
    def _():
        dwall_ref[:, : 4 * width] = acc[...].astype(bf16)
        dwall_ref[:, 4 * width :] = acc_small[...].T.astype(bf16)


def back(gins, middle, cot, tok, att, proj, prob, wall, small, dwr):
    blocks, images, span, width = tok.shape
    length = blocks * span
    heads = width // HEAD_DIM
    split = pl.BlockSpec((blocks, 1, span, width), lambda i: (0, i, 0, 0))
    whole = lambda a: pl.BlockSpec(a.shape, lambda i: (0,) * len(a.shape))
    return pl.pallas_call(
        back_kernel,
        grid=(images,),
        in_specs=[split] * 7
        + [
            pl.BlockSpec((1, length, width), lambda i: (i, 0, 0)),
            pl.BlockSpec((1, length, 3 * width), lambda i: (i, 0, 0)),
            pl.BlockSpec((1, heads, length, length), lambda i: (i, 0, 0, 0)),
            whole(wall),
            whole(small),
            whole(dwr),
        ],
        out_specs=[pl.BlockSpec((1, span, width), lambda i: (i, 0, 0))] * blocks + [whole(wall)],
        out_shape=[jax.ShapeDtypeStruct((images, span, width), bf16)] * blocks
        + [jax.ShapeDtypeStruct(wall.shape, bf16)],
        scratch_shapes=[
            pltpu.VMEM((width, 4 * width), f32),
            pltpu.VMEM((LANES, width), f32),
            pltpu.VMEM((length, width), bf16),
            pltpu.VMEM((length, 3 * width), bf16),
        ],
        compiler_params=pltpu.CompilerParams(vmem_limit_bytes=VMEM_BYTES),
        cost_estimate=true_cost(10 * images * length * width * (4 * width + 3 * length)),
        name="back",
    )(*gins, middle, cot, tok, att, proj, prob, wall, small, dwr)


def kept_pairs(route_rows, token_live, order_rows, expert_count, capacity):
    labels = jnp.arange(expert_count, dtype=jnp.int32)
    alive = token_live > 0
    first_hot = ((route_rows[:, 0:1] == labels) & alive[:, None]).astype(bf16)
    second_hot = ((route_rows[:, 1:2] == labels) & alive[:, None]).astype(bf16)
    earlier = (order_rows[None, :] < order_rows[:, None]).astype(bf16)
    ahead = mm(earlier, jnp.concatenate([first_hot, second_hot], 1))
    ahead_first = ahead[:, :expert_count]
    ahead_second = ahead[:, expert_count:] + jnp.sum(first_hot.astype(f32), 0)
    return jnp.where(ahead_first < capacity, first_hot, 0) + jnp.where(
        ahead_second < capacity, second_hot, 0
    )


def local(
    fsdp,
    seq,
    tokens,
    ln1_gain,
    ln1_bias,
    w_qkv,
    w_out,
    ln2_gain,
    ln2_bias,
    w_router,
    w_in,
    w_down,
    padding,
    routes,
    priority,
    cotangent,
):
    images, span, width = tokens.shape
    expert_count, shard_rows = w_in.shape[0], w_in.shape[1]
    rows = images * span
    own = images // seq
    length = seq * span
    capacity = (2 * rows + expert_count - 1) // expert_count
    outer = fsdp // 8
    if outer > 1:
        outer_groups = [[o * 8 + n for o in range(outer)] for n in range(8)]
    spread = functools.partial(flip, fsdp=fsdp)
    seq_index = lax.axis_index("seq")
    place = lax.axis_index("fsdp") if outer == 1 else jnp.int32(0)
    place = place.astype(jnp.int32).reshape(1)

    def picked(array, k):
        return lax.dynamic_index_in_dim(array, seq_index ^ k, 0, keepdims=False)

    tokens = tokens.reshape(seq, own * span, width)
    tok = jnp.stack(exchange([picked(tokens, k) for k in range(seq)]))
    tok = tok.reshape(seq, own, span, width)

    columns = jnp.concatenate(
        [w_router] + [v[:, None] for v in (ln1_gain, ln1_bias, ln2_gain, ln2_bias)], 1
    )
    columns = jnp.pad(columns, ((0, 0), (0, LANES - columns.shape[1])))
    shard = jnp.concatenate([w_qkv, w_out, columns], 1)
    if outer == 1:
        cut = width // 16
        from_x, from_y = spread(shard, bits=2), spread(shard, bits=4)
        from_x, from_y = tie((from_x, from_y), tok)
        near = [(0, 0, shard), (2, 0, from_x), (4, 0, from_y)]
        far = [
            (6, 0, spread(from_x[:cut], bits=4)),
            (6, cut, spread(from_y[cut:], bits=2)),
        ]
        near += [(r + 1, skip, spread(a, bits=1)) for r, skip, a in near]
    else:
        full = lax.all_gather(shard, "fsdp", axis=0, tiled=True)
        from_x = from_y = full
        near, far = [(n, 0, full[n * (width // 8) : (n + 1) * (width // 8)]) for n in range(8)], []

    live = lax.dynamic_slice_in_dim(padding, seq_index * span, span, 1)
    kept = kept_pairs(
        routes.reshape(rows, 2), live.reshape(rows), priority.reshape(rows), expert_count, capacity
    )
    kept = jnp.swapaxes(kept.reshape(seq, own * span, expert_count), 1, 2)
    kept = jnp.pad(
        kept, ((0, 0), (0, MASK_ROWS - expert_count), (0, width - own * span))
    ).astype(bf16)
    cot = cotangent * live[:, :, None].astype(bf16)
    packed = jnp.concatenate([cot.reshape(seq, own * span, width), kept], 1)
    packed = tie(packed, tok, from_x, from_y)
    packed = jnp.stack(exchange([picked(packed, k) for k in range(seq)]))
    late = tie([a for _, _, a in far], packed)
    far += [(r + 1, skip, spread(a, bits=1)) for (r, skip, _), a in zip(far, late)]
    offsets = [(r, skip) for r, skip, _ in near + far]
    pieces = [a for _, _, a in near + far]
    cot_x, cot_y = spread(packed, bits=2), spread(packed, bits=4)
    half = seq // 2
    cot_far = [spread(cot_x[:half], bits=4), spread(cot_y[half:], bits=2)]

    win, wdn = w_in, w_down
    if outer > 1:
        win = lax.all_gather(win, "fsdp", axis=1, tiled=True, axis_index_groups=outer_groups)
        wdn = lax.all_gather(wdn, "fsdp", axis=1, tiled=True, axis_index_groups=outer_groups)
    win, wdn = tie((win, wdn), pieces)
    weights = [win, spread(win, bits=1), wdn, spread(wdn, bits=1)]

    mine = lax.dynamic_slice_in_dim(padding, seq_index * own, own, 0).reshape(own, seq, span)
    mine = jnp.stack(relative([mine[:, b] for b in range(seq)], seq_index))
    vis = jnp.where(mine > 0, 0.0, neg_fill).astype(f32)
    vis = jnp.swapaxes(vis, 0, 1).reshape(own, 1, length)
    middle, two, proj, att, prob, wall, wr, small = front(tok, pieces, offsets, vis, place)
    two = two.reshape(seq, own * span, width)
    two_far = [[spread(two, bits=bits)] for bits in (2, 4, 6)]

    (dw,), dwr, out_0, gin_0 = experts_call(
        [[two]], [[packed]], weights, wr, None, "experts_own", lambda flops: SHORT
    )
    cots = [[cot_x], [cot_y], cot_far]
    left, dwr, outs, gins = experts_call(
        two_far, cots, weights, wr, dwr, "experts_far", true_cost
    )
    arrived = [spread(a, bits=bits) for a, bits in zip(gins, (2, 4, 6))]

    def finished(dw_kept, dw_sent):
        raw = plus(dw_kept, spread(dw_sent, bits=1))
        if outer > 1:
            raw = lax.psum_scatter(
                raw, "fsdp", scatter_dimension=2, tiled=True, axis_index_groups=outer_groups
            )
        return lax.optimization_barrier([raw[n : n + 1] for n in range(raw.shape[0])])

    line = LineSum(seq)
    line.step(finished(*grads_call(two_far, cots, left, dw, 0, 1))[0])
    left, dw = tie((left, dw), line.ready)
    parts = grads_call(two_far, cots, left, dw, 1, expert_count - 1)
    line.hold(arrived)
    line.arrive()
    raws = finished(*tie(parts, line.ready, arrived))
    line.send(raws.pop(0))
    gins = gin_0 + tie(arrived, line.ready)

    shape4 = (seq, own, span, width)
    outs = [spread(a, bits=bits) for a, bits in zip(tie(outs, arrived), (2, 4, 6))]
    *grad_tok, dense = back(
        [a.reshape(shape4) for a in gins],
        middle,
        packed[:, : own * span].reshape(shape4),
        tok,
        att,
        proj,
        prob,
        wall,
        small,
        dwr,
    )
    line.hold((grad_tok, outs))
    dense = tie(dense, outs, line.waiting())
    dense = lax.psum_scatter(dense, "fsdp", scatter_dimension=0, tiled=True)
    line.step(raws.pop(0))
    line.step(raws.pop(0))
    line.hold(dense)
    line.step()

    outs, grad_tok = tie((outs, grad_tok), line.ready)
    outs = [a.reshape(shape4) for a in out_0 + outs]
    home = []
    for k in range(seq):
        alive = mine[k][:, :, None].astype(f32)
        combined = sum(a[k].astype(f32) for a in outs)
        home.append(jnp.stack([(alive * (middle[k] + combined)).astype(bf16), grad_tok[k]]))
    home = exchange(home)
    dense = lax.psum(dense, "seq")
    line.step()
    home = relative(tie(home, line.ready), seq_index)
    outputs, grad_tokens = (
        jnp.concatenate([a[n] for a in home], 0).reshape(images, span, width) for n in range(2)
    )
    grads = line.finish(expert_count)
    dense = tie(dense, grads, home).astype(f32)
    expert_grads = [jnp.concatenate([g[:, n] for g in grads], 0).astype(f32) for n in range(2)]
    tail = dense[:, 4 * width :]
    return (
        outputs,
        grad_tokens,
        tail[:, 4],
        tail[:, 5],
        dense[:, : 3 * width],
        dense[:, 3 * width : 4 * width],
        tail[:, 6],
        tail[:, 7],
        tail[:, :expert_count],
        expert_grads[0],
        expert_grads[1],
    )


def solution(mesh):
    rows = P("fsdp", "seq", None)
    in_specs = (
        rows,
        P("fsdp"),
        P("fsdp"),
        P("fsdp", None),
        P("fsdp", None),
        P("fsdp"),
        P("fsdp"),
        P("fsdp", None),
        P(None, "fsdp", None),
        P(None, "fsdp", None),
        P("fsdp", None),
        rows,
        P("fsdp", "seq"),
        rows,
    )
    out_specs = (
        rows,
        rows,
        P("fsdp"),
        P("fsdp"),
        P("fsdp", None),
        P("fsdp", None),
        P("fsdp"),
        P("fsdp"),
        P("fsdp", None),
        P(None, "fsdp", None),
        P(None, "fsdp", None),
    )
    return jax.shard_map(
        functools.partial(local, mesh.shape["fsdp"], mesh.shape["seq"]),
        mesh=mesh,
        in_specs=in_specs,
        out_specs=out_specs,
        check_vma=False,
    )
```

```python
import functools
import math

import jax
import jax.numpy as jnp
from jax import lax
from jax.experimental import pallas as pl
from jax.experimental.pallas import tpu as pltpu
from jax.sharding import PartitionSpec as P

HEAD_DIM = 64
LANES = 128
MASK_ROWS = 16
SMALL = 8
norm_eps = 1e-06
neg_fill = -1e30
f32 = jnp.float32
bf16 = jnp.bfloat16
VMEM_BYTES = 60 * 1024 * 1024
SHORT = pl.CostEstimate(flops=1000, bytes_accessed=1000, transcendentals=0)


def true_cost(flops):
    return pl.CostEstimate(flops=2 * flops, bytes_accessed=16 * 1024 * 1024, transcendentals=0)


def mm(left, right, left_dim=1, right_dim=0):
    return lax.dot_general(
        left, right, (((left_dim,), (right_dim,)), ((), ())), preferred_element_type=f32
    )


def unit_norm(rows):
    centred = rows - jnp.mean(rows, -1, keepdims=True)
    inverse = lax.rsqrt(jnp.mean(centred * centred, -1, keepdims=True) + norm_eps)
    return centred * inverse, inverse


def norm_back(scaled, unit, inverse):
    return inverse * (
        scaled
        - jnp.mean(scaled, -1, keepdims=True)
        - unit * jnp.mean(scaled * unit, -1, keepdims=True)
    )


def half_turn(tile):
    return pltpu.roll(tile.astype(f32), HEAD_DIM, axis=1).astype(bf16)


def wall_copies(pieces, offsets, place_ref, wall_ref, sems):
    copies = []
    for n, (piece, (r, skip)) in enumerate(zip(pieces, offsets)):
        rows = piece.shape[0]
        shard = wall_ref.shape[0] // 8
        start = pl.multiple_of((place_ref[0] ^ r) * shard + skip, 16)
        copies.append(pltpu.make_async_copy(piece, wall_ref.at[pl.ds(start, rows)], sems.at[n]))
    return copies


def front_kernel(offsets, *refs):
    pieces = refs[: len(offsets)]
    tok_ref, vis_ref, place_ref = refs[len(offsets) : len(offsets) + 3]
    mid_ref, two_ref, proj_ref, att_ref, prob_ref, full_ref, wr_ref, small_ref = refs[
        len(offsets) + 3 : len(offsets) + 11
    ]
    wall_ref, sems, full_sem = refs[len(offsets) + 11 :]
    blocks, _, span, width = tok_ref.shape
    length = blocks * span
    save = pltpu.make_async_copy(wall_ref, full_ref, full_sem)

    @pl.when(pl.program_id(0) == 0)
    def _():
        copies = wall_copies(pieces, offsets, place_ref, wall_ref, sems)
        for copy in copies:
            copy.start()
        for copy in copies:
            copy.wait()
        save.start()
        columns = wall_ref[:, 4 * width :]
        wr_ref[...] = columns
        small_ref[...] = columns.astype(f32).T[:SMALL]

    rows = tok_ref[...].reshape(length, width).astype(f32)
    unit, _ = unit_norm(rows)
    one = (unit * small_ref[4:5] + small_ref[5:6]).astype(bf16)
    proj_ref[0] = mm(one, wall_ref[:, : 3 * width]).astype(bf16)
    lower = lax.broadcasted_iota(jnp.int32, (length, LANES), 1) < HEAD_DIM
    zero = jnp.zeros((length, LANES), bf16)
    bias = vis_ref[0]

    def soften(index, queries, keys):
        scores = mm(queries, keys, 1, 1) * (HEAD_DIM**-0.5) + bias
        shifted = jnp.exp(scores - jnp.max(scores, -1, keepdims=True))
        weights = (shifted / jnp.sum(shifted, -1, keepdims=True)).astype(bf16)
        prob_ref[0, index] = weights
        return weights

    for pair in range(width // LANES):
        first, second, third = (
            proj_ref[0, :, (3 * pair + n) * LANES : (3 * pair + n + 1) * LANES] for n in range(3)
        )
        weights_a = soften(2 * pair, jnp.where(lower, first, zero), half_turn(first))
        weights_b = soften(2 * pair + 1, jnp.where(lower, zero, second), half_turn(third))
        both = jnp.where(lower, mm(weights_a, second), mm(weights_b, third))
        att_ref[0, :, pair * LANES : (pair + 1) * LANES] = both.astype(bf16)
    middle = rows + mm(att_ref[0], wall_ref[:, 3 * width : 4 * width])
    mid_ref[...] = middle.reshape(mid_ref.shape)
    unit, _ = unit_norm(middle)
    two_ref[...] = (unit * small_ref[6:7] + small_ref[7:8]).astype(bf16).reshape(two_ref.shape)

    @pl.when(pl.program_id(0) == pl.num_programs(0) - 1)
    def _():
        save.wait()


def front(tok, pieces, offsets, vis, place):
    blocks, images, span, width = tok.shape
    length = blocks * span
    heads = width // HEAD_DIM
    split = pl.BlockSpec((blocks, 1, span, width), lambda i: (0, i, 0, 0))
    anywhere = pl.BlockSpec(memory_space=pl.ANY)
    columns = pieces[0].shape[1]
    return pl.pallas_call(
        functools.partial(front_kernel, offsets),
        grid=(images,),
        in_specs=[anywhere] * len(pieces)
        + [
            split,
            pl.BlockSpec((1, 1, length), lambda i: (i, 0, 0)),
            pl.BlockSpec(memory_space=pltpu.SMEM),
        ],
        out_specs=[
            split,
            split,
            pl.BlockSpec((1, length, 3 * width), lambda i: (i, 0, 0)),
            pl.BlockSpec((1, length, width), lambda i: (i, 0, 0)),
            pl.BlockSpec((1, heads, length, length), lambda i: (i, 0, 0, 0)),
            anywhere,
            pl.BlockSpec((width, LANES), lambda i: (0, 0)),
            pl.BlockSpec((SMALL, width), lambda i: (0, 0)),
        ],
        out_shape=[
            jax.ShapeDtypeStruct(tok.shape, f32),
            jax.ShapeDtypeStruct(tok.shape, bf16),
            jax.ShapeDtypeStruct((images, length, 3 * width), bf16),
            jax.ShapeDtypeStruct((images, length, width), bf16),
            jax.ShapeDtypeStruct((images, heads, length, length), bf16),
            jax.ShapeDtypeStruct((width, columns), bf16),
            jax.ShapeDtypeStruct((width, LANES), bf16),
            jax.ShapeDtypeStruct((SMALL, width), f32),
        ],
        scratch_shapes=[
            pltpu.VMEM((width, columns), bf16),
            pltpu.SemaphoreType.DMA((len(pieces),)),
            pltpu.SemaphoreType.DMA(()),
        ],
        compiler_params=pltpu.CompilerParams(vmem_limit_bytes=VMEM_BYTES),
        cost_estimate=SHORT,
        name="front",
    )(*pieces, tok, vis, place)


def gelu_parts(pre):
    bell = jnp.exp2(pre * pre * (-0.5 * math.log2(math.e)))
    frac = 1.0 / (1.0 + (0.3275911 * math.sqrt(0.5)) * jnp.abs(pre))
    a5, a4, a3, a2, a1 = (
        0.5 * c for c in (1.061405429, -1.453152027, 1.421413741, -0.284496736, 0.254829592)
    )
    tail = frac * (a1 + frac * (a2 + frac * (a3 + frac * (a4 + frac * a5)))) * bell
    cumulative = jnp.where(pre >= 0, 1.0 - tail, tail)
    return pre * cumulative, cumulative + (pre * 0.3989422804014327) * bell


def expert_kernel(plan, *refs):
    refs = list(refs)

    def take(number):
        taken, refs[:] = refs[:number], refs[number:]
        return taken

    groups, experts, opening = plan["groups"], plan["experts"], plan["opening"]
    first, many, resume = plan["first"], plan["many"], plan["resume"]
    two_parts = [take(n) for n in plan["two"]]
    cot_parts = [take(n) for n in plan["cot"]]
    weights = take(4)
    (wr_ref,) = take(1)
    dwr_carried = None if opening else take(1)[0]
    sums_carried = take(2 * groups) if resume else []
    left = take(1 if opening else 2)
    (dwr_ref,) = take(1)
    results = take(2 * groups)
    two_buf, cot_buf, sems, win_buf, wdn_buf, weight_sems, gated_buf, grad_buf = take(8)
    stage, load_sems, store_sems, left_sems = take(4)
    _, blocks, span, width = two_buf.shape
    rows = blocks * span
    hidden = win_buf.shape[0] // many
    shard = hidden // 2
    group = pl.program_id(0)
    slot = group % gated_buf.shape[0]
    lane = lax.broadcasted_iota(jnp.int32, (rows, LANES), 1)

    copies = []
    for k in range(groups):
        some = []
        for parts, buffer in ((two_parts[k], two_buf), (cot_parts[k], cot_buf)):
            at = 0
            for part in parts:
                size = part.shape[0]
                some.append((part, buffer.at[k, pl.ds(at, size)]))
                at += size
        copies.append(
            [pltpu.make_async_copy(s, t, sems.at[k, n]) for n, (s, t) in enumerate(some)]
        )
    fetches = [
        pltpu.make_async_copy(
            ref.at[first + e],
            (win_buf, wdn_buf)[n // 2].at[pl.ds(e * hidden + (n % 2) * shard, shard)],
            weight_sems.at[e, n],
        )
        for e in range(many)
        for n, ref in enumerate(weights)
    ]
    loads = [
        pltpu.make_async_copy(ref, stage.at[n // groups], load_sems.at[n // groups])
        for n, ref in enumerate(sums_carried)
    ]
    stores = [
        [
            pltpu.make_async_copy(stage.at[n], results[n * groups + k], store_sems.at[n])
            for n in range(2)
        ]
        for k in range(groups)
    ]
    if not opening:
        for k in range(groups):
            for n, buffer in enumerate((gated_buf, grad_buf)):
                place = k % buffer.shape[0]
                stores[k].append(
                    pltpu.make_async_copy(
                        buffer.at[place],
                        left[n].at[pl.ds(k * rows, rows)],
                        left_sems.at[place, n],
                    )
                )

    @pl.when(group == 0)
    def _():
        for copy in copies[0] + fetches:
            copy.start()
        for some in copies[1:]:
            for copy in some:
                copy.start()
        dwr_ref[...] = jnp.zeros_like(dwr_ref) if opening else dwr_carried[...]
        for copy in fetches:
            copy.wait()

    for k, some in enumerate(copies):

        @pl.when(group == k)
        def _(k=k, some=some):
            for copy in some:
                copy.wait()
            if k > 0:
                for store in stores[k - 1][:2]:
                    store.wait()
            if k > 1:
                for store in stores[k - 2][2:]:
                    store.wait()
            if resume:
                loads[k].start()
                loads[groups + k].start()

    two = two_buf[group].reshape(rows, width)
    cot = cot_buf[group, :, :span, :].reshape(rows, width)
    chosen = (
        lax.broadcasted_iota(jnp.int32, (MASK_ROWS, LANES), 0)
        == lax.broadcasted_iota(jnp.int32, (MASK_ROWS, LANES), 1)
    ).astype(bf16)
    logits = jnp.where(lane < experts, mm(two, wr_ref[...]), neg_fill)
    shifted = jnp.exp(logits - jnp.max(logits, -1, keepdims=True))
    probs = shifted / jnp.sum(shifted, -1, keepdims=True)
    kept = jnp.concatenate(
        [
            mm(cot_buf[group, b, span : span + MASK_ROWS, :span], chosen, 0, 0)
            for b in range(blocks)
        ],
        0,
    )
    grad_gate = jnp.zeros((rows, LANES), f32)
    gates = probs * kept
    out_rows = gin_rows = None
    for e in range(many):
        at = slice(e * hidden, (e + 1) * hidden)
        win, wdn = win_buf[at], wdn_buf[at]
        pre = mm(two, win, 1, 1)
        back_rows = mm(cot, wdn, 1, 1)
        gate = gates[:, first + e : first + e + 1]
        hidden_rows, slope = gelu_parts(pre)
        product = jnp.sum(hidden_rows * back_rows, -1, keepdims=True)
        grad_gate = jnp.where(lane == first + e, product, grad_gate)
        gated = (hidden_rows * gate).astype(bf16)
        grad_pre = (slope * back_rows * gate).astype(bf16)
        if opening:
            gated_buf[e, 1] = mm(gated, cot, 0, 0).astype(bf16)
            gated_buf[e, 0] = mm(grad_pre, two, 0, 0).astype(bf16)
        else:
            gated_buf[slot, :, at] = gated
            grad_buf[slot, :, at] = grad_pre
        out_part, gin_part = mm(gated, wdn), mm(grad_pre, win)
        out_rows = out_part if e == 0 else out_rows + out_part
        gin_rows = gin_part if e == 0 else gin_rows + gin_part
    grad_gate = grad_gate * kept
    grad_logits = probs * (grad_gate - jnp.sum(probs * grad_gate, -1, keepdims=True))
    grad_logits = grad_logits.astype(bf16)
    dwr_ref[...] += mm(grad_logits, two, 0, 0)[:SMALL]
    gin_rows = gin_rows + mm(grad_logits, wr_ref[...], 1, 1)
    if resume:
        for k in range(groups):

            @pl.when(group == k)
            def _(k=k):
                loads[k].wait()
                loads[groups + k].wait()

        out_rows = out_rows + stage[0].reshape(rows, width).astype(f32)
        gin_rows = gin_rows + stage[1].reshape(rows, width).astype(f32)
    stage[0] = out_rows.astype(bf16).reshape(blocks, span, width)
    stage[1] = gin_rows.astype(bf16).reshape(blocks, span, width)
    for k in range(groups):

        @pl.when(group == k)
        def _(k=k):
            for store in stores[k]:
                store.start()

    @pl.when(group == groups - 1)
    def _():
        if opening:
            copy = pltpu.make_async_copy(gated_buf, left[0], left_sems.at[0, 0])
            copy.start()
            copy.wait()
        for k in (groups - 1,) if groups == 1 else (groups - 2, groups - 1):
            for store in stores[k][0 if k == groups - 1 else 2 :]:
                store.wait()


def experts_call(two, cot, weights, wr, span_of, dwr, sums, name, cost):
    groups = len(two)
    opening = groups == 1
    experts, shard, width = weights[0].shape
    hidden = 2 * shard
    first, many = span_of
    blocks = sum(a.shape[0] for a in two[0])
    span = two[0][0].shape[1]
    rows = blocks * span
    plan = dict(
        first=first,
        many=many,
        resume=sums is not None,
        groups=groups,
        experts=experts,
        opening=opening,
        two=[len(parts) for parts in two],
        cot=[len(parts) for parts in cot],
    )
    anywhere = pl.BlockSpec(memory_space=pl.ANY)
    once = lambda a: pl.BlockSpec(
        a.shape, lambda g: (0,) * len(a.shape), pipeline_mode=pl.Buffered(1)
    )
    result = jax.ShapeDtypeStruct((blocks, span, width), bf16)
    little = jax.ShapeDtypeStruct((SMALL, width), f32)
    if opening:
        left = [jax.ShapeDtypeStruct((experts, 2, hidden, width), bf16)]
        buffers = [pltpu.VMEM(left[0].shape, bf16), pltpu.VMEM((16, LANES), bf16)]
    else:
        left = [jax.ShapeDtypeStruct((groups * rows, many * hidden), bf16)] * 2
        buffers = [pltpu.VMEM((2, rows, many * hidden), bf16)] * 2
    pieces = [a for parts in two for a in parts] + [a for parts in cot for a in parts]
    outs = pl.pallas_call(
        functools.partial(expert_kernel, plan),
        grid=(groups,),
        in_specs=[anywhere] * (len(pieces) + 4)
        + [once(wr)]
        + ([] if opening else [once(little)])
        + [anywhere] * len(sums or []),
        out_specs=[anywhere] * len(left) + [once(little)] + [anywhere] * (2 * groups),
        out_shape=left + [little] + [result] * (2 * groups),
        scratch_shapes=[
            pltpu.VMEM((groups, blocks, span, width), bf16),
            pltpu.VMEM((groups, blocks, span + MASK_ROWS, width), bf16),
            pltpu.SemaphoreType.DMA((groups, 4)),
            pltpu.VMEM((many * hidden, width), bf16),
            pltpu.VMEM((many * hidden, width), bf16),
            pltpu.SemaphoreType.DMA((many, 4)),
            *buffers,
            pltpu.VMEM((2, blocks, span, width), bf16),
            pltpu.SemaphoreType.DMA((2,)),
            pltpu.SemaphoreType.DMA((2,)),
            pltpu.SemaphoreType.DMA((2, 2)),
        ],
        compiler_params=pltpu.CompilerParams(vmem_limit_bytes=VMEM_BYTES),
        cost_estimate=cost(10 * groups * rows * width * hidden * many),
        name=name,
    )(*pieces, *weights, wr, *([] if opening else [dwr]), *(sums or []))
    left, (dwr, *outs) = list(outs[: len(left)]), outs[len(left) :]
    return left, dwr, outs[:groups], outs[groups:]


def grads_kernel(plan, *refs):
    refs = list(refs)

    def take(number):
        taken, refs[:] = refs[:number], refs[number:]
        return taken

    groups = len(plan["two"])
    two_parts = [take(n) for n in plan["two"]]
    cot_parts = [take(n) for n in plan["cot"]]
    gated_ref, grad_ref, own_ref, kept_ref, sent_ref = take(5)
    two_buf, cot_buf, cot_rows, sems = refs
    _, blocks, span, width = two_buf.shape
    rows = blocks * span
    copies = []
    for k in range(groups):
        at = 0
        for n, part in enumerate(two_parts[k]):
            size = part.shape[0]
            copies.append(
                pltpu.make_async_copy(part, two_buf.at[k, pl.ds(at, size)], sems.at[k, n])
            )
            at += size
        at = 0
        for n, part in enumerate(cot_parts[k]):
            size = part.shape[0]
            copies.append(
                pltpu.make_async_copy(
                    part, cot_buf.at[k, pl.ds(at, size)], sems.at[k, 2 + n]
                )
            )
            at += size

    @pl.when(pl.program_id(0) == 0)
    def _():
        for copy in copies:
            copy.start()
        for copy in copies:
            copy.wait()
        for k in range(groups):
            cot_rows[k * rows : (k + 1) * rows] = cot_buf[k, :, :span, :].reshape(rows, width)

    half = own_ref.shape[2] // 2
    two = two_buf[...].reshape(groups * rows, width)
    for n, (left_ref, right) in enumerate(((grad_ref, two), (gated_ref, cot_rows[...]))):
        total = (own_ref[0, n].astype(f32) + mm(left_ref[...], right, 0, 0)).astype(bf16)
        kept_ref[0, n] = total[:half]
        sent_ref[0, n] = total[half:]


def grads_call(two, cot, left, own, first, many):
    groups = len(two)
    blocks = sum(a.shape[0] for a in two[0])
    _, span, width = two[0][0].shape
    rows = blocks * span
    hidden = own.shape[2]
    anywhere = pl.BlockSpec(memory_space=pl.ANY)
    pieces = [a for parts in two for a in parts] + [a for parts in cot for a in parts]
    columns = pl.BlockSpec((groups * rows, hidden), lambda e: (0, e))
    part = jax.ShapeDtypeStruct((many, 2, hidden // 2, width), bf16)
    part_spec = pl.BlockSpec((1, 2, hidden // 2, width), lambda e: (e, 0, 0, 0))
    plan = dict(two=[len(parts) for parts in two], cot=[len(parts) for parts in cot])
    return pl.pallas_call(
        functools.partial(grads_kernel, plan),
        grid=(many,),
        in_specs=[anywhere] * len(pieces)
        + [columns, columns, pl.BlockSpec((1, 2, hidden, width), lambda e: (e + first, 0, 0, 0))],
        out_specs=[part_spec, part_spec],
        out_shape=[part, part],
        scratch_shapes=[
            pltpu.VMEM((groups, blocks, span, width), bf16),
            pltpu.VMEM((groups, blocks, span + MASK_ROWS, width), bf16),
            pltpu.VMEM((groups * rows, width), bf16),
            pltpu.SemaphoreType.DMA((groups, 4)),
        ],
        compiler_params=pltpu.CompilerParams(vmem_limit_bytes=VMEM_BYTES),
        cost_estimate=true_cost(8 * groups * rows * width * hidden * many),
        name="expert_grads",
    )(*pieces, *left, own)


def flip(array, fsdp, bits):
    return lax.ppermute(array, "fsdp", [(n, n ^ bits) for n in range(fsdp)])


def tie(value, *others):
    return lax.optimization_barrier((value, others))[0]


def exchange(pieces):
    count = len(pieces)
    return [pieces[0]] + [
        lax.ppermute(pieces[k], "seq", [(n, n ^ k) for n in range(count)]) for k in range(1, count)
    ]


def relative(parts, index):
    count, bit = len(parts), 1
    while bit < count:
        swap = (index & bit) > 0
        parts = [jnp.where(swap, parts[k ^ bit], parts[k]) for k in range(count)]
        bit *= 2
    return parts


def plus(*arrays):
    return sum(a.astype(f32) for a in arrays).astype(bf16)


class LineSum:
    def __init__(self, seq):
        self.seq = seq
        self.index = lax.axis_index("seq")
        self.outer = (self.index == 0) | (self.index == seq - 1)
        self.inward = self.exchanged = self.total = None
        self.raw = self.pair = None
        self.ready = []
        self.done = []

    def hold(self, others):
        if self.seq == 4:
            self.inward, self.exchanged = tie((self.inward, self.exchanged), others)

    def waiting(self):
        return [a for a in (self.inward, self.exchanged) if a is not None]

    def arrive(self):
        if self.seq != 4:
            return
        total = None if self.pair is None else plus(self.pair, self.exchanged)
        pair = None if self.raw is None else plus(self.raw, self.inward)
        if self.total is not None:
            self.done.append(jnp.where(self.outer, self.inward, self.total))
        ready = [a for a in (pair, total) if a is not None]
        if ready:
            ready, self.index = lax.optimization_barrier((ready, self.index))
            self.outer = (self.index == 0) | (self.index == self.seq - 1)
            pair = ready.pop(0) if pair is not None else None
            total = ready.pop(0) if total is not None else None
        self.raw, self.pair, self.total = None, pair, total
        self.ready = [a for a in (pair, total) if a is not None]

    def send(self, raw=None):
        if self.seq != 4:
            self.done += [] if raw is None else [lax.psum(raw, "seq")]
            return
        self.raw = raw
        if raw is not None:
            self.ready.append(raw)
        if raw is not None or self.total is not None:
            if self.total is None:
                both = raw
            elif raw is None:
                both = self.total
            else:
                both = jnp.where(self.outer, raw, self.total)
            self.inward = lax.ppermute(both, "seq", [(0, 1), (1, 0), (2, 3), (3, 2)])
        if self.pair is not None:
            self.exchanged = lax.ppermute(self.pair, "seq", [(1, 2), (2, 1)])

    def step(self, raw=None):
        self.arrive()
        self.send(raw)

    def finish(self, count):
        while len(self.done) < count:
            self.step()
        return self.done


def back_kernel(
    gin_0, gin_2, gin_4, gin_6, mid_ref, cot_ref, tok_ref, att_ref, proj_ref, prob_ref, wall_ref,
    small_ref, dwr_ref, *rest,
):
    blocks, _, span, width = tok_ref.shape
    length = blocks * span
    gtok_refs, (dwall_ref, acc, acc_small, gatt, gproj) = rest[:blocks], rest[blocks:]
    step = pl.program_id(0)

    @pl.when(step == 0)
    def _():
        acc[...] = jnp.zeros_like(acc)
        acc_small[...] = jnp.zeros_like(acc_small)
        acc_small[:SMALL] = dwr_ref[...]

    gin = sum(ref[...].reshape(length, width).astype(f32) for ref in (gin_0, gin_2, gin_4, gin_6))
    unit_two, inverse_two = unit_norm(mid_ref[...].reshape(length, width))
    acc_small[6:7] += jnp.sum(gin * unit_two, 0, keepdims=True)
    acc_small[7:8] += jnp.sum(gin, 0, keepdims=True)
    grad_middle = cot_ref[...].reshape(length, width).astype(f32) + norm_back(
        gin * small_ref[6:7], unit_two, inverse_two
    )
    branch = grad_middle.astype(bf16)
    acc[:, 3 * width : 4 * width] += mm(att_ref[0], branch, 0, 0)
    gatt[...] = mm(branch, wall_ref[:, 3 * width : 4 * width], 1, 1).astype(bf16)
    lower = lax.broadcasted_iota(jnp.int32, (length, LANES), 1) < HEAD_DIM
    zero = jnp.zeros((length, LANES), bf16)
    scale = HEAD_DIM**-0.5

    def score_grad(weights, grad_weights):
        weights = weights.astype(f32)
        product = weights * grad_weights
        return (product - weights * jnp.sum(product, -1, keepdims=True)).astype(bf16)

    for pair in range(width // LANES):
        places = [slice((3 * pair + n) * LANES, (3 * pair + n + 1) * LANES) for n in range(3)]
        first, second, third = (proj_ref[0, :, place] for place in places)
        first_r, second_r, third_r = half_turn(first), half_turn(second), half_turn(third)
        grad = gatt[:, pair * LANES : (pair + 1) * LANES]
        weights_a, weights_b = prob_ref[0, 2 * pair], prob_ref[0, 2 * pair + 1]
        ds_a = score_grad(weights_a, mm(jnp.where(lower, grad, zero), second, 1, 1))
        ds_b = score_grad(weights_b, mm(jnp.where(lower, zero, grad), third, 1, 1))
        gproj[:, places[0]] = (
            jnp.where(lower, mm(ds_a, first_r), mm(ds_a, first_r, 0, 0)) * scale
        ).astype(bf16)
        gproj[:, places[1]] = jnp.where(
            lower, mm(weights_a, grad, 0, 0), mm(ds_b, third_r) * scale
        ).astype(bf16)
        gproj[:, places[2]] = jnp.where(
            lower, mm(ds_b, second_r, 0, 0) * scale, mm(weights_b, grad, 0, 0)
        ).astype(bf16)
    unit_one, inverse_one = unit_norm(tok_ref[...].reshape(length, width).astype(f32))
    one = (unit_one * small_ref[4:5] + small_ref[5:6]).astype(bf16)
    grad_one = mm(gproj[...], wall_ref[:, : 3 * width], 1, 1)
    acc_small[4:5] += jnp.sum(grad_one * unit_one, 0, keepdims=True)
    acc_small[5:6] += jnp.sum(grad_one, 0, keepdims=True)
    grad_tok = grad_middle + norm_back(grad_one * small_ref[4:5], unit_one, inverse_one)
    for k, ref in enumerate(gtok_refs):
        ref[0] = grad_tok[k * span : (k + 1) * span].astype(bf16)
    acc[:, : 3 * width] += mm(one, gproj[...], 0, 0)

    @pl.when(step == pl.num_programs(0) - 1)
    def _():
        dwall_ref[:, : 4 * width] = acc[...].astype(bf16)
        dwall_ref[:, 4 * width :] = acc_small[...].T.astype(bf16)


def back(gins, middle, cot, tok, att, proj, prob, wall, small, dwr):
    blocks, images, span, width = tok.shape
    length = blocks * span
    heads = width // HEAD_DIM
    split = pl.BlockSpec((blocks, 1, span, width), lambda i: (0, i, 0, 0))
    whole = lambda a: pl.BlockSpec(a.shape, lambda i: (0,) * len(a.shape))
    return pl.pallas_call(
        back_kernel,
        grid=(images,),
        in_specs=[split] * 7
        + [
            pl.BlockSpec((1, length, width), lambda i: (i, 0, 0)),
            pl.BlockSpec((1, length, 3 * width), lambda i: (i, 0, 0)),
            pl.BlockSpec((1, heads, length, length), lambda i: (i, 0, 0, 0)),
            whole(wall),
            whole(small),
            whole(dwr),
        ],
        out_specs=[pl.BlockSpec((1, span, width), lambda i: (i, 0, 0))] * blocks + [whole(wall)],
        out_shape=[jax.ShapeDtypeStruct((images, span, width), bf16)] * blocks
        + [jax.ShapeDtypeStruct(wall.shape, bf16)],
        scratch_shapes=[
            pltpu.VMEM((width, 4 * width), f32),
            pltpu.VMEM((LANES, width), f32),
            pltpu.VMEM((length, width), bf16),
            pltpu.VMEM((length, 3 * width), bf16),
        ],
        compiler_params=pltpu.CompilerParams(vmem_limit_bytes=VMEM_BYTES),
        cost_estimate=true_cost(10 * images * length * width * (4 * width + 3 * length)),
        name="back",
    )(*gins, middle, cot, tok, att, proj, prob, wall, small, dwr)


def kept_pairs(route_rows, token_live, order_rows, expert_count, capacity):
    labels = jnp.arange(expert_count, dtype=jnp.int32)
    alive = token_live > 0
    first_hot = ((route_rows[:, 0:1] == labels) & alive[:, None]).astype(bf16)
    second_hot = ((route_rows[:, 1:2] == labels) & alive[:, None]).astype(bf16)
    earlier = (order_rows[None, :] < order_rows[:, None]).astype(bf16)
    ahead = mm(earlier, jnp.concatenate([first_hot, second_hot], 1))
    ahead_first = ahead[:, :expert_count]
    ahead_second = ahead[:, expert_count:] + jnp.sum(first_hot.astype(f32), 0)
    return jnp.where(ahead_first < capacity, first_hot, 0) + jnp.where(
        ahead_second < capacity, second_hot, 0
    )


def local(
    fsdp,
    seq,
    tokens,
    ln1_gain,
    ln1_bias,
    w_qkv,
    w_out,
    ln2_gain,
    ln2_bias,
    w_router,
    w_in,
    w_down,
    padding,
    routes,
    priority,
    cotangent,
):
    images, span, width = tokens.shape
    expert_count, shard_rows = w_in.shape[0], w_in.shape[1]
    rows = images * span
    own = images // seq
    length = seq * span
    capacity = (2 * rows + expert_count - 1) // expert_count
    outer = fsdp // 8
    if outer > 1:
        outer_groups = [[o * 8 + n for o in range(outer)] for n in range(8)]
    spread = functools.partial(flip, fsdp=fsdp)
    seq_index = lax.axis_index("seq")
    place = lax.axis_index("fsdp") if outer == 1 else jnp.int32(0)
    place = place.astype(jnp.int32).reshape(1)

    def picked(array, k):
        return lax.dynamic_index_in_dim(array, seq_index ^ k, 0, keepdims=False)

    tokens = tokens.reshape(seq, own * span, width)
    tok = jnp.stack(exchange([picked(tokens, k) for k in range(seq)]))
    tok = tok.reshape(seq, own, span, width)

    columns = jnp.concatenate(
        [w_router] + [v[:, None] for v in (ln1_gain, ln1_bias, ln2_gain, ln2_bias)], 1
    )
    columns = jnp.pad(columns, ((0, 0), (0, LANES - columns.shape[1])))
    shard = jnp.concatenate([w_qkv, w_out, columns], 1)
    if outer == 1:
        cut = width // 16
        from_x, from_y = spread(shard, bits=2), spread(shard, bits=4)
        from_x, from_y = tie((from_x, from_y), tok)
        near = [(0, 0, shard), (2, 0, from_x), (4, 0, from_y)]
        far = [
            (6, 0, spread(from_x[:cut], bits=4)),
            (6, cut, spread(from_y[cut:], bits=2)),
        ]
        near += [(r + 1, skip, spread(a, bits=1)) for r, skip, a in near]
    else:
        full = lax.all_gather(shard, "fsdp", axis=0, tiled=True)
        from_x = from_y = full
        near, far = [(n, 0, full[n * (width // 8) : (n + 1) * (width // 8)]) for n in range(8)], []

    live = lax.dynamic_slice_in_dim(padding, seq_index * span, span, 1)
    kept = kept_pairs(
        routes.reshape(rows, 2), live.reshape(rows), priority.reshape(rows), expert_count, capacity
    )
    kept = jnp.swapaxes(kept.reshape(seq, own * span, expert_count), 1, 2)
    kept = jnp.pad(
        kept, ((0, 0), (0, MASK_ROWS - expert_count), (0, width - own * span))
    ).astype(bf16)
    cot = cotangent * live[:, :, None].astype(bf16)
    packed = jnp.concatenate([cot.reshape(seq, own * span, width), kept], 1)
    packed = tie(packed, tok, from_x, from_y)
    packed = jnp.stack(exchange([picked(packed, k) for k in range(seq)]))
    late = tie([a for _, _, a in far], packed)
    far += [(r + 1, skip, spread(a, bits=1)) for (r, skip, _), a in zip(far, late)]
    offsets = [(r, skip) for r, skip, _ in near + far]
    pieces = [a for _, _, a in near + far]
    cot_x, cot_y = spread(packed, bits=2), spread(packed, bits=4)
    half = seq // 2
    cot_far = [spread(cot_x[:half], bits=4), spread(cot_y[half:], bits=2)]

    win, wdn = w_in, w_down
    if outer > 1:
        win = lax.all_gather(win, "fsdp", axis=1, tiled=True, axis_index_groups=outer_groups)
        wdn = lax.all_gather(wdn, "fsdp", axis=1, tiled=True, axis_index_groups=outer_groups)
    win, wdn = tie((win, wdn), pieces)
    weights = [win, spread(win, bits=1), wdn, spread(wdn, bits=1)]

    mine = lax.dynamic_slice_in_dim(padding, seq_index * own, own, 0).reshape(own, seq, span)
    mine = jnp.stack(relative([mine[:, b] for b in range(seq)], seq_index))
    vis = jnp.where(mine > 0, 0.0, neg_fill).astype(f32)
    vis = jnp.swapaxes(vis, 0, 1).reshape(own, 1, length)
    middle, two, proj, att, prob, wall, wr, small = front(tok, pieces, offsets, vis, place)
    two = two.reshape(seq, own * span, width)
    two_far = [[spread(two, bits=bits)] for bits in (2, 4, 6)]

    (dw,), dwr, out_0, gin_0 = experts_call(
        [[two]],
        [[packed]],
        weights,
        wr,
        (0, expert_count),
        None,
        None,
        "experts_own",
        lambda flops: SHORT,
    )

    def finished(dw_kept, dw_sent):
        raw = plus(dw_kept, spread(dw_sent, bits=1))
        if outer > 1:
            raw = lax.psum_scatter(
                raw, "fsdp", scatter_dimension=2, tiled=True, axis_index_groups=outer_groups
            )
        return lax.optimization_barrier([raw[n : n + 1] for n in range(raw.shape[0])])

    cots = [[cot_x], [cot_y], cot_far]
    half = expert_count // 2
    line = LineSum(seq)
    left, dwr, outs, gins = experts_call(
        two_far, cots, weights, wr, (0, half), dwr, None, "experts_far", true_cost
    )
    raws = finished(*grads_call(two_far, cots, left, dw, 0, half))
    line.send(raws.pop(0))
    left, dwr, outs, gins = experts_call(
        two_far,
        cots,
        weights,
        wr,
        (half, expert_count - half),
        dwr,
        tie(outs + gins, line.ready, raws),
        "experts_far_rest",
        true_cost,
    )
    line.arrive()
    gins, left = tie((gins, left), line.ready)
    arrived = [spread(gins[n], bits=2 * n + 2) for n in (2, 1, 0)]
    line.send(raws.pop(0))
    parts = grads_call(two_far, cots, left, dw, half, expert_count - half)
    raws += finished(*tie(parts, arrived, line.waiting()))
    line.hold(raws)
    line.step(raws.pop(0))
    gins = gin_0 + tie(arrived, line.ready)

    shape4 = (seq, own, span, width)
    outs = [spread(a, bits=bits) for a, bits in zip(tie(outs, arrived), (2, 4, 6))]
    *grad_tok, dense = back(
        [a.reshape(shape4) for a in gins],
        middle,
        packed[:, : own * span].reshape(shape4),
        tok,
        att,
        proj,
        prob,
        wall,
        small,
        dwr,
    )
    line.hold((grad_tok, outs))
    dense = tie(dense, outs, line.waiting())
    dense = lax.psum_scatter(dense, "fsdp", scatter_dimension=0, tiled=True)
    line.step(raws.pop(0))
    line.step()
    line.hold(dense)
    dense_line = LineSum(seq)
    line.step()
    dense_line.send(dense)

    outs, grad_tok = tie((outs, grad_tok), line.ready)
    outs = [a.reshape(shape4) for a in out_0 + outs]
    home = []
    for k in range(seq):
        alive = mine[k][:, :, None].astype(f32)
        combined = sum(a[k].astype(f32) for a in outs)
        home.append(jnp.stack([(alive * (middle[k] + combined)).astype(bf16), grad_tok[k]]))
    home = exchange(home)
    line.step()
    home = relative(tie(home, line.ready), seq_index)
    outputs, grad_tokens = (
        jnp.concatenate([a[n] for a in home], 0).reshape(images, span, width) for n in range(2)
    )
    grads = line.finish(expert_count)
    (dense,) = dense_line.finish(1)
    dense = dense.astype(f32)
    expert_grads = [jnp.concatenate([g[:, n] for g in grads], 0).astype(f32) for n in range(2)]
    tail = dense[:, 4 * width :]
    return (
        outputs,
        grad_tokens,
        tail[:, 4],
        tail[:, 5],
        dense[:, : 3 * width],
        dense[:, 3 * width : 4 * width],
        tail[:, 6],
        tail[:, 7],
        tail[:, :expert_count],
        expert_grads[0],
        expert_grads[1],
    )


def solution(mesh):
    rows = P("fsdp", "seq", None)
    in_specs = (
        rows,
        P("fsdp"),
        P("fsdp"),
        P("fsdp", None),
        P("fsdp", None),
        P("fsdp"),
        P("fsdp"),
        P("fsdp", None),
        P(None, "fsdp", None),
        P(None, "fsdp", None),
        P("fsdp", None),
        rows,
        P("fsdp", "seq"),
        rows,
    )
    out_specs = (
        rows,
        rows,
        P("fsdp"),
        P("fsdp"),
        P("fsdp", None),
        P("fsdp", None),
        P("fsdp"),
        P("fsdp"),
        P("fsdp", None),
        P(None, "fsdp", None),
        P(None, "fsdp", None),
    )
    return jax.shard_map(
        functools.partial(local, mesh.shape["fsdp"], mesh.shape["seq"]),
        mesh=mesh,
        in_specs=in_specs,
        out_specs=out_specs,
        check_vma=False,
    )
```

```python
import functools
import math

import jax
import jax.numpy as jnp
from jax import lax
from jax.experimental import pallas as pl
from jax.experimental.pallas import tpu as pltpu
from jax.sharding import PartitionSpec as P

HEAD_DIM = 64
LANES = 128
MASK_ROWS = 16
SMALL = 8
norm_eps = 1e-06
neg_fill = -1e30
f32 = jnp.float32
bf16 = jnp.bfloat16
VMEM_BYTES = 60 * 1024 * 1024
SHORT = pl.CostEstimate(flops=1000, bytes_accessed=1000, transcendentals=0)


def true_cost(flops):
    return pl.CostEstimate(flops=2 * flops, bytes_accessed=16 * 1024 * 1024, transcendentals=0)


def mm(left, right, left_dim=1, right_dim=0):
    return lax.dot_general(
        left, right, (((left_dim,), (right_dim,)), ((), ())), preferred_element_type=f32
    )


def unit_norm(rows):
    centred = rows - jnp.mean(rows, -1, keepdims=True)
    inverse = lax.rsqrt(jnp.mean(centred * centred, -1, keepdims=True) + norm_eps)
    return centred * inverse, inverse


def norm_back(scaled, unit, inverse):
    return inverse * (
        scaled
        - jnp.mean(scaled, -1, keepdims=True)
        - unit * jnp.mean(scaled * unit, -1, keepdims=True)
    )


def half_turn(tile):
    return pltpu.roll(tile.astype(f32), HEAD_DIM, axis=1).astype(bf16)


def wall_copies(pieces, offsets, place_ref, wall_ref, sems):
    copies = []
    for n, (piece, (r, skip)) in enumerate(zip(pieces, offsets)):
        rows = piece.shape[0]
        shard = wall_ref.shape[0] // 8
        start = pl.multiple_of((place_ref[0] ^ r) * shard + skip, 16)
        copies.append(pltpu.make_async_copy(piece, wall_ref.at[pl.ds(start, rows)], sems.at[n]))
    return copies


def front_kernel(offsets, *refs):
    pieces = refs[: len(offsets)]
    tok_ref, vis_ref, place_ref = refs[len(offsets) : len(offsets) + 3]
    mid_ref, two_ref, proj_ref, att_ref, prob_ref, full_ref, wr_ref, small_ref = refs[
        len(offsets) + 3 : len(offsets) + 11
    ]
    wall_ref, sems, full_sem = refs[len(offsets) + 11 :]
    blocks, _, span, width = tok_ref.shape
    length = blocks * span
    save = pltpu.make_async_copy(wall_ref, full_ref, full_sem)

    @pl.when(pl.program_id(0) == 0)
    def _():
        copies = wall_copies(pieces, offsets, place_ref, wall_ref, sems)
        for copy in copies:
            copy.start()
        for copy in copies:
            copy.wait()
        save.start()
        columns = wall_ref[:, 4 * width :]
        wr_ref[...] = columns
        small_ref[...] = columns.astype(f32).T[:SMALL]

    rows = tok_ref[...].reshape(length, width).astype(f32)
    unit, _ = unit_norm(rows)
    one = (unit * small_ref[4:5] + small_ref[5:6]).astype(bf16)
    proj_ref[0] = mm(one, wall_ref[:, : 3 * width]).astype(bf16)
    lower = lax.broadcasted_iota(jnp.int32, (length, LANES), 1) < HEAD_DIM
    zero = jnp.zeros((length, LANES), bf16)
    bias = vis_ref[0]

    def soften(index, queries, keys):
        scores = mm(queries, keys, 1, 1) * (HEAD_DIM**-0.5) + bias
        shifted = jnp.exp(scores - jnp.max(scores, -1, keepdims=True))
        weights = (shifted / jnp.sum(shifted, -1, keepdims=True)).astype(bf16)
        prob_ref[0, index] = weights
        return weights

    for pair in range(width // LANES):
        first, second, third = (
            proj_ref[0, :, (3 * pair + n) * LANES : (3 * pair + n + 1) * LANES] for n in range(3)
        )
        weights_a = soften(2 * pair, jnp.where(lower, first, zero), half_turn(first))
        weights_b = soften(2 * pair + 1, jnp.where(lower, zero, second), half_turn(third))
        both = jnp.where(lower, mm(weights_a, second), mm(weights_b, third))
        att_ref[0, :, pair * LANES : (pair + 1) * LANES] = both.astype(bf16)
    middle = rows + mm(att_ref[0], wall_ref[:, 3 * width : 4 * width])
    mid_ref[...] = middle.reshape(mid_ref.shape)
    unit, _ = unit_norm(middle)
    two_ref[...] = (unit * small_ref[6:7] + small_ref[7:8]).astype(bf16).reshape(two_ref.shape)

    @pl.when(pl.program_id(0) == pl.num_programs(0) - 1)
    def _():
        save.wait()


def front(tok, pieces, offsets, vis, place):
    blocks, images, span, width = tok.shape
    length = blocks * span
    heads = width // HEAD_DIM
    split = pl.BlockSpec((blocks, 1, span, width), lambda i: (0, i, 0, 0))
    anywhere = pl.BlockSpec(memory_space=pl.ANY)
    columns = pieces[0].shape[1]
    return pl.pallas_call(
        functools.partial(front_kernel, offsets),
        grid=(images,),
        in_specs=[anywhere] * len(pieces)
        + [
            split,
            pl.BlockSpec((1, 1, length), lambda i: (i, 0, 0)),
            pl.BlockSpec(memory_space=pltpu.SMEM),
        ],
        out_specs=[
            split,
            split,
            pl.BlockSpec((1, length, 3 * width), lambda i: (i, 0, 0)),
            pl.BlockSpec((1, length, width), lambda i: (i, 0, 0)),
            pl.BlockSpec((1, heads, length, length), lambda i: (i, 0, 0, 0)),
            anywhere,
            pl.BlockSpec((width, LANES), lambda i: (0, 0)),
            pl.BlockSpec((SMALL, width), lambda i: (0, 0)),
        ],
        out_shape=[
            jax.ShapeDtypeStruct(tok.shape, f32),
            jax.ShapeDtypeStruct(tok.shape, bf16),
            jax.ShapeDtypeStruct((images, length, 3 * width), bf16),
            jax.ShapeDtypeStruct((images, length, width), bf16),
            jax.ShapeDtypeStruct((images, heads, length, length), bf16),
            jax.ShapeDtypeStruct((width, columns), bf16),
            jax.ShapeDtypeStruct((width, LANES), bf16),
            jax.ShapeDtypeStruct((SMALL, width), f32),
        ],
        scratch_shapes=[
            pltpu.VMEM((width, columns), bf16),
            pltpu.SemaphoreType.DMA((len(pieces),)),
            pltpu.SemaphoreType.DMA(()),
        ],
        compiler_params=pltpu.CompilerParams(vmem_limit_bytes=VMEM_BYTES),
        cost_estimate=SHORT,
        name="front",
    )(*pieces, tok, vis, place)


def gelu_parts(pre):
    bell = jnp.exp2(pre * pre * (-0.5 * math.log2(math.e)))
    frac = 1.0 / (1.0 + (0.3275911 * math.sqrt(0.5)) * jnp.abs(pre))
    a5, a4, a3, a2, a1 = (
        0.5 * c for c in (1.061405429, -1.453152027, 1.421413741, -0.284496736, 0.254829592)
    )
    tail = frac * (a1 + frac * (a2 + frac * (a3 + frac * (a4 + frac * a5)))) * bell
    cumulative = jnp.where(pre >= 0, 1.0 - tail, tail)
    return pre * cumulative, cumulative + (pre * 0.3989422804014327) * bell


def expert_kernel(plan, *refs):
    refs = list(refs)

    def take(number):
        taken, refs[:] = refs[:number], refs[number:]
        return taken

    groups, experts, opening = plan["groups"], plan["experts"], plan["opening"]
    two_parts = [take(n) for n in plan["two"]]
    cot_parts = [take(n) for n in plan["cot"]]
    weights = take(4)
    (wr_ref,) = take(1)
    dwr_carried = None if opening else take(1)[0]
    left = take(1 if opening else 2)
    (dwr_ref,) = take(1)
    results = take(2 * groups)
    two_buf, cot_buf, sems, win_buf, wdn_buf, weight_sems, gated_buf, grad_buf = take(8)
    stage, store_sems, left_sems = take(3)
    _, blocks, span, width = two_buf.shape
    rows = blocks * span
    hidden = win_buf.shape[0] // experts
    shard = hidden // 2
    group = pl.program_id(0)
    slot = group % gated_buf.shape[0]
    lane = lax.broadcasted_iota(jnp.int32, (rows, LANES), 1)

    copies = []
    for k in range(groups):
        some = []
        for parts, buffer in ((two_parts[k], two_buf), (cot_parts[k], cot_buf)):
            at = 0
            for part in parts:
                size = part.shape[0]
                some.append((part, buffer.at[k, pl.ds(at, size)]))
                at += size
        copies.append(
            [pltpu.make_async_copy(s, t, sems.at[k, n]) for n, (s, t) in enumerate(some)]
        )
    fetches = [
        pltpu.make_async_copy(
            ref.at[e],
            (win_buf, wdn_buf)[n // 2].at[pl.ds(e * hidden + (n % 2) * shard, shard)],
            weight_sems.at[e, n],
        )
        for e in range(experts)
        for n, ref in enumerate(weights)
    ]
    stores = [
        [
            pltpu.make_async_copy(stage.at[n], results[n * groups + k], store_sems.at[n])
            for n in range(2)
        ]
        for k in range(groups)
    ]
    if not opening:
        for k in range(groups):
            for n, buffer in enumerate((gated_buf, grad_buf)):
                place = k % buffer.shape[0]
                stores[k].append(
                    pltpu.make_async_copy(
                        buffer.at[place],
                        left[n].at[pl.ds(k * rows, rows)],
                        left_sems.at[place, n],
                    )
                )

    @pl.when(group == 0)
    def _():
        for copy in copies[0] + fetches:
            copy.start()
        for some in copies[1:]:
            for copy in some:
                copy.start()
        dwr_ref[...] = jnp.zeros_like(dwr_ref) if opening else dwr_carried[...]
        for copy in fetches:
            copy.wait()

    for k, some in enumerate(copies):

        @pl.when(group == k)
        def _(k=k, some=some):
            for copy in some:
                copy.wait()
            if k > 0:
                for store in stores[k - 1][:2]:
                    store.wait()
            if k > 1:
                for store in stores[k - 2][2:]:
                    store.wait()

    two = two_buf[group].reshape(rows, width)
    cot = cot_buf[group, :, :span, :].reshape(rows, width)
    chosen = (
        lax.broadcasted_iota(jnp.int32, (MASK_ROWS, LANES), 0)
        == lax.broadcasted_iota(jnp.int32, (MASK_ROWS, LANES), 1)
    ).astype(bf16)
    logits = jnp.where(lane < experts, mm(two, wr_ref[...]), neg_fill)
    shifted = jnp.exp(logits - jnp.max(logits, -1, keepdims=True))
    probs = shifted / jnp.sum(shifted, -1, keepdims=True)
    kept = jnp.concatenate(
        [
            mm(cot_buf[group, b, span : span + MASK_ROWS, :span], chosen, 0, 0)
            for b in range(blocks)
        ],
        0,
    )
    grad_gate = jnp.zeros((rows, LANES), f32)
    gates = probs * kept
    out_rows = gin_rows = None
    for e in range(experts):
        at = slice(e * hidden, (e + 1) * hidden)
        win, wdn = win_buf[at], wdn_buf[at]
        pre = mm(two, win, 1, 1)
        back_rows = mm(cot, wdn, 1, 1)
        gate = gates[:, e : e + 1]
        hidden_rows, slope = gelu_parts(pre)
        product = jnp.sum(hidden_rows * back_rows, -1, keepdims=True)
        grad_gate = jnp.where(lane == e, product, grad_gate)
        gated = (hidden_rows * gate).astype(bf16)
        grad_pre = (slope * back_rows * gate).astype(bf16)
        if opening:
            gated_buf[e, 1] = mm(gated, cot, 0, 0).astype(bf16)
            gated_buf[e, 0] = mm(grad_pre, two, 0, 0).astype(bf16)
        else:
            gated_buf[slot, :, at] = gated
            grad_buf[slot, :, at] = grad_pre
        out_part, gin_part = mm(gated, wdn), mm(grad_pre, win)
        out_rows = out_part if e == 0 else out_rows + out_part
        gin_rows = gin_part if e == 0 else gin_rows + gin_part
    grad_gate = grad_gate * kept
    grad_logits = probs * (grad_gate - jnp.sum(probs * grad_gate, -1, keepdims=True))
    grad_logits = grad_logits.astype(bf16)
    dwr_ref[...] += mm(grad_logits, two, 0, 0)[:SMALL]
    gin_rows = gin_rows + mm(grad_logits, wr_ref[...], 1, 1)
    stage[0] = out_rows.astype(bf16).reshape(blocks, span, width)
    stage[1] = gin_rows.astype(bf16).reshape(blocks, span, width)
    for k in range(groups):

        @pl.when(group == k)
        def _(k=k):
            for store in stores[k]:
                store.start()

    @pl.when(group == groups - 1)
    def _():
        if opening:
            copy = pltpu.make_async_copy(gated_buf, left[0], left_sems.at[0, 0])
            copy.start()
            copy.wait()
        for k in (groups - 1,) if groups == 1 else (groups - 2, groups - 1):
            for store in stores[k][0 if k == groups - 1 else 2 :]:
                store.wait()


def experts_call(two, cot, weights, wr, dwr, name, cost):
    groups = len(two)
    opening = groups == 1
    experts, shard, width = weights[0].shape
    hidden = 2 * shard
    blocks = sum(a.shape[0] for a in two[0])
    span = two[0][0].shape[1]
    rows = blocks * span
    plan = dict(
        groups=groups,
        experts=experts,
        opening=opening,
        two=[len(parts) for parts in two],
        cot=[len(parts) for parts in cot],
    )
    anywhere = pl.BlockSpec(memory_space=pl.ANY)
    once = lambda a: pl.BlockSpec(
        a.shape, lambda g: (0,) * len(a.shape), pipeline_mode=pl.Buffered(1)
    )
    result = jax.ShapeDtypeStruct((blocks, span, width), bf16)
    little = jax.ShapeDtypeStruct((SMALL, width), f32)
    if opening:
        left = [jax.ShapeDtypeStruct((experts, 2, hidden, width), bf16)]
        buffers = [pltpu.VMEM(left[0].shape, bf16), pltpu.VMEM((16, LANES), bf16)]
    else:
        left = [jax.ShapeDtypeStruct((groups * rows, experts * hidden), bf16)] * 2
        buffers = [pltpu.VMEM((2, rows, experts * hidden), bf16)] * 2
    pieces = [a for parts in two for a in parts] + [a for parts in cot for a in parts]
    outs = pl.pallas_call(
        functools.partial(expert_kernel, plan),
        grid=(groups,),
        in_specs=[anywhere] * (len(pieces) + 4)
        + [once(wr)]
        + ([] if opening else [once(little)]),
        out_specs=[anywhere] * len(left) + [once(little)] + [anywhere] * (2 * groups),
        out_shape=left + [little] + [result] * (2 * groups),
        scratch_shapes=[
            pltpu.VMEM((groups, blocks, span, width), bf16),
            pltpu.VMEM((groups, blocks, span + MASK_ROWS, width), bf16),
            pltpu.SemaphoreType.DMA((groups, 4)),
            pltpu.VMEM((experts * hidden, width), bf16),
            pltpu.VMEM((experts * hidden, width), bf16),
            pltpu.SemaphoreType.DMA((experts, 4)),
            *buffers,
            pltpu.VMEM((2, blocks, span, width), bf16),
            pltpu.SemaphoreType.DMA((2,)),
            pltpu.SemaphoreType.DMA((2, 2)),
        ],
        compiler_params=pltpu.CompilerParams(vmem_limit_bytes=VMEM_BYTES),
        cost_estimate=cost(10 * groups * rows * width * hidden * experts),
        name=name,
    )(*pieces, *weights, wr, *([] if opening else [dwr]))
    left, (dwr, *outs) = list(outs[: len(left)]), outs[len(left) :]
    return left, dwr, outs[:groups], outs[groups:]


def grads_kernel(plan, *refs):
    refs = list(refs)

    def take(number):
        taken, refs[:] = refs[:number], refs[number:]
        return taken

    groups = len(plan["two"])
    two_parts = [take(n) for n in plan["two"]]
    cot_parts = [take(n) for n in plan["cot"]]
    gated_ref, grad_ref, own_ref, kept_ref, sent_ref = take(5)
    two_buf, cot_buf, cot_rows, sems = refs
    _, blocks, span, width = two_buf.shape
    rows = blocks * span
    copies = []
    for k in range(groups):
        at = 0
        for n, part in enumerate(two_parts[k]):
            size = part.shape[0]
            copies.append(
                pltpu.make_async_copy(part, two_buf.at[k, pl.ds(at, size)], sems.at[k, n])
            )
            at += size
        at = 0
        for n, part in enumerate(cot_parts[k]):
            size = part.shape[0]
            copies.append(
                pltpu.make_async_copy(
                    part, cot_buf.at[k, pl.ds(at, size)], sems.at[k, 2 + n]
                )
            )
            at += size

    @pl.when(pl.program_id(0) == 0)
    def _():
        for copy in copies:
            copy.start()
        for copy in copies:
            copy.wait()
        for k in range(groups):
            cot_rows[k * rows : (k + 1) * rows] = cot_buf[k, :, :span, :].reshape(rows, width)

    half = own_ref.shape[2] // 2
    two = two_buf[...].reshape(groups * rows, width)
    for n, (left_ref, right) in enumerate(((grad_ref, two), (gated_ref, cot_rows[...]))):
        total = (own_ref[0, n].astype(f32) + mm(left_ref[...], right, 0, 0)).astype(bf16)
        kept_ref[0, n] = total[:half]
        sent_ref[0, n] = total[half:]


def grads_call(two, cot, left, own, first, many):
    groups = len(two)
    blocks = sum(a.shape[0] for a in two[0])
    _, span, width = two[0][0].shape
    rows = blocks * span
    hidden = own.shape[2]
    anywhere = pl.BlockSpec(memory_space=pl.ANY)
    pieces = [a for parts in two for a in parts] + [a for parts in cot for a in parts]
    columns = pl.BlockSpec((groups * rows, hidden), lambda e: (0, e + first))
    part = jax.ShapeDtypeStruct((many, 2, hidden // 2, width), bf16)
    part_spec = pl.BlockSpec((1, 2, hidden // 2, width), lambda e: (e, 0, 0, 0))
    plan = dict(two=[len(parts) for parts in two], cot=[len(parts) for parts in cot])
    return pl.pallas_call(
        functools.partial(grads_kernel, plan),
        grid=(many,),
        in_specs=[anywhere] * len(pieces)
        + [columns, columns, pl.BlockSpec((1, 2, hidden, width), lambda e: (e + first, 0, 0, 0))],
        out_specs=[part_spec, part_spec],
        out_shape=[part, part],
        scratch_shapes=[
            pltpu.VMEM((groups, blocks, span, width), bf16),
            pltpu.VMEM((groups, blocks, span + MASK_ROWS, width), bf16),
            pltpu.VMEM((groups * rows, width), bf16),
            pltpu.SemaphoreType.DMA((groups, 4)),
        ],
        compiler_params=pltpu.CompilerParams(vmem_limit_bytes=VMEM_BYTES),
        cost_estimate=true_cost(8 * groups * rows * width * hidden * many),
        name="expert_grads",
    )(*pieces, *left, own)


def flip(array, fsdp, bits):
    return lax.ppermute(array, "fsdp", [(n, n ^ bits) for n in range(fsdp)])


def tie(value, *others):
    return lax.optimization_barrier((value, others))[0]


def exchange(pieces):
    count = len(pieces)
    return [pieces[0]] + [
        lax.ppermute(pieces[k], "seq", [(n, n ^ k) for n in range(count)]) for k in range(1, count)
    ]


def relative(parts, index):
    count, bit = len(parts), 1
    while bit < count:
        swap = (index & bit) > 0
        parts = [jnp.where(swap, parts[k ^ bit], parts[k]) for k in range(count)]
        bit *= 2
    return parts


def plus(*arrays):
    return sum(a.astype(f32) for a in arrays).astype(bf16)


class Line:
    def __init__(self, seq, raw):
        self.seq, self.raw = seq, raw
        if seq != 4:
            self.total = lax.psum(raw, "seq")

    def inwards(self):
        if self.seq == 4:
            self.moving = lax.ppermute(self.raw, "seq", [(0, 1), (3, 2)])
        return self

    def across(self, *others):
        if self.seq == 4:
            self.pair = plus(self.raw, tie(self.moving, others))
            self.moving = lax.ppermute(self.pair, "seq", [(1, 2), (2, 1)])
            return self.pair
        return self.raw

    def outwards(self, *others):
        if self.seq == 4:
            self.total = plus(self.pair, tie(self.moving, others))
            self.moving = lax.ppermute(self.total, "seq", [(1, 0), (2, 3)])
        return self.total

    def finish(self):
        if self.seq != 4:
            return self.total
        index = lax.axis_index("seq")
        return jnp.where((index == 0) | (index == 3), self.moving, self.total)

    def waiting(self):
        return [self.moving] if self.seq == 4 else []


def back_kernel(
    gin_0, gin_2, gin_4, gin_6, mid_ref, cot_ref, tok_ref, att_ref, proj_ref, prob_ref, wall_ref,
    small_ref, dwr_ref, *rest,
):
    blocks, _, span, width = tok_ref.shape
    length = blocks * span
    gtok_refs, (dwall_ref, acc, acc_small, gatt, gproj) = rest[:blocks], rest[blocks:]
    step = pl.program_id(0)

    @pl.when(step == 0)
    def _():
        acc[...] = jnp.zeros_like(acc)
        acc_small[...] = jnp.zeros_like(acc_small)
        acc_small[:SMALL] = dwr_ref[...]

    gin = sum(ref[...].reshape(length, width).astype(f32) for ref in (gin_0, gin_2, gin_4, gin_6))
    unit_two, inverse_two = unit_norm(mid_ref[...].reshape(length, width))
    acc_small[6:7] += jnp.sum(gin * unit_two, 0, keepdims=True)
    acc_small[7:8] += jnp.sum(gin, 0, keepdims=True)
    grad_middle = cot_ref[...].reshape(length, width).astype(f32) + norm_back(
        gin * small_ref[6:7], unit_two, inverse_two
    )
    branch = grad_middle.astype(bf16)
    acc[:, 3 * width : 4 * width] += mm(att_ref[0], branch, 0, 0)
    gatt[...] = mm(branch, wall_ref[:, 3 * width : 4 * width], 1, 1).astype(bf16)
    lower = lax.broadcasted_iota(jnp.int32, (length, LANES), 1) < HEAD_DIM
    zero = jnp.zeros((length, LANES), bf16)
    scale = HEAD_DIM**-0.5

    def score_grad(weights, grad_weights):
        weights = weights.astype(f32)
        product = weights * grad_weights
        return (product - weights * jnp.sum(product, -1, keepdims=True)).astype(bf16)

    for pair in range(width // LANES):
        places = [slice((3 * pair + n) * LANES, (3 * pair + n + 1) * LANES) for n in range(3)]
        first, second, third = (proj_ref[0, :, place] for place in places)
        first_r, second_r, third_r = half_turn(first), half_turn(second), half_turn(third)
        grad = gatt[:, pair * LANES : (pair + 1) * LANES]
        weights_a, weights_b = prob_ref[0, 2 * pair], prob_ref[0, 2 * pair + 1]
        ds_a = score_grad(weights_a, mm(jnp.where(lower, grad, zero), second, 1, 1))
        ds_b = score_grad(weights_b, mm(jnp.where(lower, zero, grad), third, 1, 1))
        gproj[:, places[0]] = (
            jnp.where(lower, mm(ds_a, first_r), mm(ds_a, first_r, 0, 0)) * scale
        ).astype(bf16)
        gproj[:, places[1]] = jnp.where(
            lower, mm(weights_a, grad, 0, 0), mm(ds_b, third_r) * scale
        ).astype(bf16)
        gproj[:, places[2]] = jnp.where(
            lower, mm(ds_b, second_r, 0, 0) * scale, mm(weights_b, grad, 0, 0)
        ).astype(bf16)
    unit_one, inverse_one = unit_norm(tok_ref[...].reshape(length, width).astype(f32))
    one = (unit_one * small_ref[4:5] + small_ref[5:6]).astype(bf16)
    grad_one = mm(gproj[...], wall_ref[:, : 3 * width], 1, 1)
    acc_small[4:5] += jnp.sum(grad_one * unit_one, 0, keepdims=True)
    acc_small[5:6] += jnp.sum(grad_one, 0, keepdims=True)
    grad_tok = grad_middle + norm_back(grad_one * small_ref[4:5], unit_one, inverse_one)
    for k, ref in enumerate(gtok_refs):
        ref[0] = grad_tok[k * span : (k + 1) * span].astype(bf16)
    acc[:, : 3 * width] += mm(one, gproj[...], 0, 0)

    @pl.when(step == pl.num_programs(0) - 1)
    def _():
        dwall_ref[:, : 4 * width] = acc[...].astype(bf16)
        dwall_ref[:, 4 * width :] = acc_small[...].T.astype(bf16)


def back(gins, middle, cot, tok, att, proj, prob, wall, small, dwr):
    blocks, images, span, width = tok.shape
    length = blocks * span
    heads = width // HEAD_DIM
    split = pl.BlockSpec((blocks, 1, span, width), lambda i: (0, i, 0, 0))
    whole = lambda a: pl.BlockSpec(a.shape, lambda i: (0,) * len(a.shape))
    return pl.pallas_call(
        back_kernel,
        grid=(images,),
        in_specs=[split] * 7
        + [
            pl.BlockSpec((1, length, width), lambda i: (i, 0, 0)),
            pl.BlockSpec((1, length, 3 * width), lambda i: (i, 0, 0)),
            pl.BlockSpec((1, heads, length, length), lambda i: (i, 0, 0, 0)),
            whole(wall),
            whole(small),
            whole(dwr),
        ],
        out_specs=[pl.BlockSpec((1, span, width), lambda i: (i, 0, 0))] * blocks + [whole(wall)],
        out_shape=[jax.ShapeDtypeStruct((images, span, width), bf16)] * blocks
        + [jax.ShapeDtypeStruct(wall.shape, bf16)],
        scratch_shapes=[
            pltpu.VMEM((width, 4 * width), f32),
            pltpu.VMEM((LANES, width), f32),
            pltpu.VMEM((length, width), bf16),
            pltpu.VMEM((length, 3 * width), bf16),
        ],
        compiler_params=pltpu.CompilerParams(vmem_limit_bytes=VMEM_BYTES),
        cost_estimate=true_cost(10 * images * length * width * (4 * width + 3 * length)),
        name="back",
    )(*gins, middle, cot, tok, att, proj, prob, wall, small, dwr)


def kept_pairs(route_rows, token_live, order_rows, expert_count, capacity):
    labels = jnp.arange(expert_count, dtype=jnp.int32)
    alive = token_live > 0
    first_hot = ((route_rows[:, 0:1] == labels) & alive[:, None]).astype(bf16)
    second_hot = ((route_rows[:, 1:2] == labels) & alive[:, None]).astype(bf16)
    earlier = (order_rows[None, :] < order_rows[:, None]).astype(bf16)
    ahead = mm(earlier, jnp.concatenate([first_hot, second_hot], 1))
    ahead_first = ahead[:, :expert_count]
    ahead_second = ahead[:, expert_count:] + jnp.sum(first_hot.astype(f32), 0)
    return jnp.where(ahead_first < capacity, first_hot, 0) + jnp.where(
        ahead_second < capacity, second_hot, 0
    )


def local(
    fsdp,
    seq,
    tokens,
    ln1_gain,
    ln1_bias,
    w_qkv,
    w_out,
    ln2_gain,
    ln2_bias,
    w_router,
    w_in,
    w_down,
    padding,
    routes,
    priority,
    cotangent,
):
    images, span, width = tokens.shape
    expert_count, shard_rows = w_in.shape[0], w_in.shape[1]
    rows = images * span
    own = images // seq
    length = seq * span
    capacity = (2 * rows + expert_count - 1) // expert_count
    outer = fsdp // 8
    if outer > 1:
        outer_groups = [[o * 8 + n for o in range(outer)] for n in range(8)]
    spread = functools.partial(flip, fsdp=fsdp)
    seq_index = lax.axis_index("seq")
    place = lax.axis_index("fsdp") if outer == 1 else jnp.int32(0)
    place = place.astype(jnp.int32).reshape(1)

    def picked(array, k):
        return lax.dynamic_index_in_dim(array, seq_index ^ k, 0, keepdims=False)

    tokens = tokens.reshape(seq, own * span, width)
    tok = jnp.stack(exchange([picked(tokens, k) for k in range(seq)]))
    tok = tok.reshape(seq, own, span, width)

    columns = jnp.concatenate(
        [w_router] + [v[:, None] for v in (ln1_gain, ln1_bias, ln2_gain, ln2_bias)], 1
    )
    columns = jnp.pad(columns, ((0, 0), (0, LANES - columns.shape[1])))
    shard = jnp.concatenate([w_qkv, w_out, columns], 1)
    if outer == 1:
        cut = width // 16
        from_x, from_y = spread(shard, bits=2), spread(shard, bits=4)
        from_x, from_y = tie((from_x, from_y), tok)
        near = [(0, 0, shard), (2, 0, from_x), (4, 0, from_y)]
        far = [
            (6, 0, spread(from_x[:cut], bits=4)),
            (6, cut, spread(from_y[cut:], bits=2)),
        ]
        near += [(r + 1, skip, spread(a, bits=1)) for r, skip, a in near]
    else:
        full = lax.all_gather(shard, "fsdp", axis=0, tiled=True)
        from_x = from_y = full
        near, far = [(n, 0, full[n * (width // 8) : (n + 1) * (width // 8)]) for n in range(8)], []

    live = lax.dynamic_slice_in_dim(padding, seq_index * span, span, 1)
    kept = kept_pairs(
        routes.reshape(rows, 2), live.reshape(rows), priority.reshape(rows), expert_count, capacity
    )
    kept = jnp.swapaxes(kept.reshape(seq, own * span, expert_count), 1, 2)
    kept = jnp.pad(
        kept, ((0, 0), (0, MASK_ROWS - expert_count), (0, width - own * span))
    ).astype(bf16)
    cot = cotangent * live[:, :, None].astype(bf16)
    packed = jnp.concatenate([cot.reshape(seq, own * span, width), kept], 1)
    packed = tie(packed, tok, from_x, from_y)
    packed = jnp.stack(exchange([picked(packed, k) for k in range(seq)]))
    late = tie([a for _, _, a in far], packed)
    far += [(r + 1, skip, spread(a, bits=1)) for (r, skip, _), a in zip(far, late)]
    offsets = [(r, skip) for r, skip, _ in near + far]
    pieces = [a for _, _, a in near + far]
    cot_x, cot_y = spread(packed, bits=2), spread(packed, bits=4)
    half = seq // 2
    cot_far = [spread(cot_x[:half], bits=4), spread(cot_y[half:], bits=2)]

    win, wdn = w_in, w_down
    if outer > 1:
        win = lax.all_gather(win, "fsdp", axis=1, tiled=True, axis_index_groups=outer_groups)
        wdn = lax.all_gather(wdn, "fsdp", axis=1, tiled=True, axis_index_groups=outer_groups)
    win, wdn = tie((win, wdn), pieces)
    weights = [win, spread(win, bits=1), wdn, spread(wdn, bits=1)]

    mine = lax.dynamic_slice_in_dim(padding, seq_index * own, own, 0).reshape(own, seq, span)
    mine = jnp.stack(relative([mine[:, b] for b in range(seq)], seq_index))
    vis = jnp.where(mine > 0, 0.0, neg_fill).astype(f32)
    vis = jnp.swapaxes(vis, 0, 1).reshape(own, 1, length)
    middle, two, proj, att, prob, wall, wr, small = front(tok, pieces, offsets, vis, place)
    two = two.reshape(seq, own * span, width)
    two_far = [[spread(two, bits=bits)] for bits in (2, 4, 6)]

    (dw,), dwr, out_0, gin_0 = experts_call(
        [[two]], [[packed]], weights, wr, None, "experts_own", lambda flops: SHORT
    )
    cots = [[cot_x], [cot_y], cot_far]
    left, dwr, outs, gins = experts_call(
        two_far, cots, weights, wr, dwr, "experts_far", true_cost
    )
    arrived = [spread(a, bits=bits) for a, bits in zip(gins, (2, 4, 6))]

    def finished(dw_kept, dw_sent):
        raw = plus(dw_kept, spread(dw_sent, bits=1))
        if outer > 1:
            raw = lax.psum_scatter(
                raw, "fsdp", scatter_dimension=2, tiled=True, axis_index_groups=outer_groups
            )
        return lax.optimization_barrier([raw[n : n + 1] for n in range(raw.shape[0])])

    first = Line(seq, finished(*grads_call(two_far, cots, left, dw, 0, 1))[0]).inwards()
    left, dw = tie((left, dw), first.raw)
    parts = grads_call(two_far, cots, left, dw, 1, expert_count - 1)
    ready = first.across(arrived)
    lines = [Line(seq, raw) for raw in finished(*tie(parts, ready, arrived))]
    lines[0].inwards()
    gins = gin_0 + tie(arrived, ready, [line.raw for line in lines])
    lines = [first] + lines

    shape4 = (seq, own, span, width)
    outs = [spread(a, bits=bits) for a, bits in zip(tie(outs, arrived), (2, 4, 6))]
    *grad_tok, dense = back(
        [a.reshape(shape4) for a in gins],
        middle,
        packed[:, : own * span].reshape(shape4),
        tok,
        att,
        proj,
        prob,
        wall,
        small,
        dwr,
    )
    flying = (outs, lines[0].waiting(), lines[1].waiting())
    dense = tie(dense, flying)
    dense = lax.psum_scatter(dense, "fsdp", scatter_dimension=0, tiled=True)
    lines[2].raw, lines[3].raw = tie((lines[2].raw, lines[3].raw), grad_tok)
    lines[2].inwards()
    ready = lines[1].across(grad_tok, flying)
    ready = lines[0].outwards(ready)
    lines[3].inwards()
    ready = lines[2].across(ready)
    ready = lines[1].outwards(ready)
    ready = lines[3].across(ready)
    ready = lines[2].outwards(ready)
    dense_line = Line(seq, tie(dense, ready)).inwards()
    ready = lines[3].outwards(dense_line.raw)

    ready = dense_line.across(ready)
    outs, grad_tok = tie((outs, grad_tok), ready)
    outs = [a.reshape(shape4) for a in out_0 + outs]
    home = []
    for k in range(seq):
        alive = mine[k][:, :, None].astype(f32)
        combined = sum(a[k].astype(f32) for a in outs)
        home.append(jnp.stack([(alive * (middle[k] + combined)).astype(bf16), grad_tok[k]]))
    home = exchange(home)
    ready = dense_line.outwards(ready)
    home = relative(tie(home, ready), seq_index)
    outputs, grad_tokens = (
        jnp.concatenate([a[n] for a in home], 0).reshape(images, span, width) for n in range(2)
    )
    grads = [line.finish() for line in lines]
    dense = dense_line.finish().astype(f32)
    expert_grads = [jnp.concatenate([g[:, n] for g in grads], 0).astype(f32) for n in range(2)]
    tail = dense[:, 4 * width :]
    return (
        outputs,
        grad_tokens,
        tail[:, 4],
        tail[:, 5],
        dense[:, : 3 * width],
        dense[:, 3 * width : 4 * width],
        tail[:, 6],
        tail[:, 7],
        tail[:, :expert_count],
        expert_grads[0],
        expert_grads[1],
    )


def solution(mesh):
    rows = P("fsdp", "seq", None)
    in_specs = (
        rows,
        P("fsdp"),
        P("fsdp"),
        P("fsdp", None),
        P("fsdp", None),
        P("fsdp"),
        P("fsdp"),
        P("fsdp", None),
        P(None, "fsdp", None),
        P(None, "fsdp", None),
        P("fsdp", None),
        rows,
        P("fsdp", "seq"),
        rows,
    )
    out_specs = (
        rows,
        rows,
        P("fsdp"),
        P("fsdp"),
        P("fsdp", None),
        P("fsdp", None),
        P("fsdp"),
        P("fsdp"),
        P("fsdp", None),
        P(None, "fsdp", None),
        P(None, "fsdp", None),
    )
    return jax.shard_map(
        functools.partial(local, mesh.shape["fsdp"], mesh.shape["seq"]),
        mesh=mesh,
        in_specs=in_specs,
        out_specs=out_specs,
        check_vma=False,
    )
```

```python
import functools
import math

import jax
import jax.numpy as jnp
from jax import lax
from jax.experimental import pallas as pl
from jax.experimental.pallas import tpu as pltpu
from jax.sharding import PartitionSpec as P

HEAD_DIM = 64
LANES = 128
MASK_ROWS = 16
SMALL = 8
norm_eps = 1e-06
neg_fill = -1e30
f32 = jnp.float32
bf16 = jnp.bfloat16
VMEM_BYTES = 60 * 1024 * 1024
SHORT = pl.CostEstimate(flops=1000, bytes_accessed=1000, transcendentals=0)


def true_cost(flops):
    return pl.CostEstimate(flops=2 * flops, bytes_accessed=16 * 1024 * 1024, transcendentals=0)


def mm(left, right, left_dim=1, right_dim=0):
    return lax.dot_general(
        left, right, (((left_dim,), (right_dim,)), ((), ())), preferred_element_type=f32
    )


def unit_norm(rows):
    centred = rows - jnp.mean(rows, -1, keepdims=True)
    inverse = lax.rsqrt(jnp.mean(centred * centred, -1, keepdims=True) + norm_eps)
    return centred * inverse, inverse


def norm_back(scaled, unit, inverse):
    return inverse * (
        scaled
        - jnp.mean(scaled, -1, keepdims=True)
        - unit * jnp.mean(scaled * unit, -1, keepdims=True)
    )


def half_turn(tile):
    return pltpu.roll(tile.astype(f32), HEAD_DIM, axis=1).astype(bf16)


def wall_copies(pieces, offsets, place_ref, wall_ref, sems):
    copies = []
    for n, (piece, (r, skip)) in enumerate(zip(pieces, offsets)):
        rows = piece.shape[0]
        shard = wall_ref.shape[0] // 8
        start = pl.multiple_of((place_ref[0] ^ r) * shard + skip, 16)
        copies.append(pltpu.make_async_copy(piece, wall_ref.at[pl.ds(start, rows)], sems.at[n]))
    return copies


def front_kernel(offsets, *refs):
    pieces = refs[: len(offsets)]
    tok_ref, vis_ref, place_ref = refs[len(offsets) : len(offsets) + 3]
    mid_ref, two_ref, proj_ref, att_ref, prob_ref, full_ref, wr_ref, small_ref = refs[
        len(offsets) + 3 : len(offsets) + 11
    ]
    wall_ref, sems, full_sem = refs[len(offsets) + 11 :]
    blocks, _, span, width = tok_ref.shape
    length = blocks * span
    save = pltpu.make_async_copy(wall_ref, full_ref, full_sem)

    @pl.when(pl.program_id(0) == 0)
    def _():
        copies = wall_copies(pieces, offsets, place_ref, wall_ref, sems)
        for copy in copies:
            copy.start()
        for copy in copies:
            copy.wait()
        save.start()
        columns = wall_ref[:, 4 * width :]
        wr_ref[...] = columns
        small_ref[...] = columns.astype(f32).T[:SMALL]

    rows = tok_ref[...].reshape(length, width).astype(f32)
    unit, _ = unit_norm(rows)
    one = (unit * small_ref[4:5] + small_ref[5:6]).astype(bf16)
    proj_ref[0] = mm(one, wall_ref[:, : 3 * width]).astype(bf16)
    lower = lax.broadcasted_iota(jnp.int32, (length, LANES), 1) < HEAD_DIM
    zero = jnp.zeros((length, LANES), bf16)
    bias = vis_ref[0]

    def soften(index, queries, keys):
        scores = mm(queries, keys, 1, 1) * (HEAD_DIM**-0.5) + bias
        shifted = jnp.exp(scores - jnp.max(scores, -1, keepdims=True))
        weights = (shifted / jnp.sum(shifted, -1, keepdims=True)).astype(bf16)
        prob_ref[0, index] = weights
        return weights

    for pair in range(width // LANES):
        first, second, third = (
            proj_ref[0, :, (3 * pair + n) * LANES : (3 * pair + n + 1) * LANES] for n in range(3)
        )
        weights_a = soften(2 * pair, jnp.where(lower, first, zero), half_turn(first))
        weights_b = soften(2 * pair + 1, jnp.where(lower, zero, second), half_turn(third))
        both = jnp.where(lower, mm(weights_a, second), mm(weights_b, third))
        att_ref[0, :, pair * LANES : (pair + 1) * LANES] = both.astype(bf16)
    middle = rows + mm(att_ref[0], wall_ref[:, 3 * width : 4 * width])
    mid_ref[...] = middle.reshape(mid_ref.shape)
    unit, _ = unit_norm(middle)
    two_ref[...] = (unit * small_ref[6:7] + small_ref[7:8]).astype(bf16).reshape(two_ref.shape)

    @pl.when(pl.program_id(0) == pl.num_programs(0) - 1)
    def _():
        save.wait()


def front(tok, pieces, offsets, vis, place):
    blocks, images, span, width = tok.shape
    length = blocks * span
    heads = width // HEAD_DIM
    split = pl.BlockSpec((blocks, 1, span, width), lambda i: (0, i, 0, 0))
    anywhere = pl.BlockSpec(memory_space=pl.ANY)
    columns = pieces[0].shape[1]
    return pl.pallas_call(
        functools.partial(front_kernel, offsets),
        grid=(images,),
        in_specs=[anywhere] * len(pieces)
        + [
            split,
            pl.BlockSpec((1, 1, length), lambda i: (i, 0, 0)),
            pl.BlockSpec(memory_space=pltpu.SMEM),
        ],
        out_specs=[
            split,
            split,
            pl.BlockSpec((1, length, 3 * width), lambda i: (i, 0, 0)),
            pl.BlockSpec((1, length, width), lambda i: (i, 0, 0)),
            pl.BlockSpec((1, heads, length, length), lambda i: (i, 0, 0, 0)),
            anywhere,
            pl.BlockSpec((width, LANES), lambda i: (0, 0)),
            pl.BlockSpec((SMALL, width), lambda i: (0, 0)),
        ],
        out_shape=[
            jax.ShapeDtypeStruct(tok.shape, f32),
            jax.ShapeDtypeStruct(tok.shape, bf16),
            jax.ShapeDtypeStruct((images, length, 3 * width), bf16),
            jax.ShapeDtypeStruct((images, length, width), bf16),
            jax.ShapeDtypeStruct((images, heads, length, length), bf16),
            jax.ShapeDtypeStruct((width, columns), bf16),
            jax.ShapeDtypeStruct((width, LANES), bf16),
            jax.ShapeDtypeStruct((SMALL, width), f32),
        ],
        scratch_shapes=[
            pltpu.VMEM((width, columns), bf16),
            pltpu.SemaphoreType.DMA((len(pieces),)),
            pltpu.SemaphoreType.DMA(()),
        ],
        compiler_params=pltpu.CompilerParams(vmem_limit_bytes=VMEM_BYTES),
        cost_estimate=SHORT,
        name="front",
    )(*pieces, tok, vis, place)


def gelu_parts(pre):
    bell = jnp.exp2(pre * pre * (-0.5 * math.log2(math.e)))
    frac = 1.0 / (1.0 + (0.3275911 * math.sqrt(0.5)) * jnp.abs(pre))
    a5, a4, a3, a2, a1 = (
        0.5 * c for c in (1.061405429, -1.453152027, 1.421413741, -0.284496736, 0.254829592)
    )
    tail = frac * (a1 + frac * (a2 + frac * (a3 + frac * (a4 + frac * a5)))) * bell
    cumulative = jnp.where(pre >= 0, 1.0 - tail, tail)
    return pre * cumulative, cumulative + (pre * 0.3989422804014327) * bell


def expert_kernel(plan, *refs):
    refs = list(refs)

    def take(number):
        taken, refs[:] = refs[:number], refs[number:]
        return taken

    groups, experts, opening = plan["groups"], plan["experts"], plan["opening"]
    two_parts = [take(n) for n in plan["two"]]
    cot_parts = [take(n) for n in plan["cot"]]
    weights = take(4)
    (wr_ref,) = take(1)
    dwr_carried = None if opening else take(1)[0]
    left = take(1 if opening else 2)
    (dwr_ref,) = take(1)
    results = take(2 * groups)
    two_buf, cot_buf, sems, win_buf, wdn_buf, weight_sems, gated_buf, grad_buf = take(8)
    stage, store_sems, left_sems = take(3)
    _, blocks, span, width = two_buf.shape
    rows = blocks * span
    hidden = win_buf.shape[0] // experts
    shard = hidden // 2
    group = pl.program_id(0)
    slot = group % gated_buf.shape[0]
    lane = lax.broadcasted_iota(jnp.int32, (rows, LANES), 1)

    copies = []
    for k in range(groups):
        some = []
        for parts, buffer in ((two_parts[k], two_buf), (cot_parts[k], cot_buf)):
            at = 0
            for part in parts:
                size = part.shape[0]
                some.append((part, buffer.at[k, pl.ds(at, size)]))
                at += size
        copies.append(
            [pltpu.make_async_copy(s, t, sems.at[k, n]) for n, (s, t) in enumerate(some)]
        )
    fetches = [
        pltpu.make_async_copy(
            ref.at[e],
            (win_buf, wdn_buf)[n // 2].at[pl.ds(e * hidden + (n % 2) * shard, shard)],
            weight_sems.at[e, n],
        )
        for e in range(experts)
        for n, ref in enumerate(weights)
    ]
    stores = [
        [
            pltpu.make_async_copy(stage.at[n], results[n * groups + k], store_sems.at[n])
            for n in range(2)
        ]
        for k in range(groups)
    ]
    if not opening:
        for k in range(groups):
            for n, buffer in enumerate((gated_buf, grad_buf)):
                place = k % buffer.shape[0]
                stores[k].append(
                    pltpu.make_async_copy(
                        buffer.at[place],
                        left[n].at[pl.ds(k * rows, rows)],
                        left_sems.at[place, n],
                    )
                )

    @pl.when(group == 0)
    def _():
        for copy in copies[0] + fetches:
            copy.start()
        for some in copies[1:]:
            for copy in some:
                copy.start()
        dwr_ref[...] = jnp.zeros_like(dwr_ref) if opening else dwr_carried[...]
        for copy in fetches:
            copy.wait()

    for k, some in enumerate(copies):

        @pl.when(group == k)
        def _(k=k, some=some):
            for copy in some:
                copy.wait()
            if k > 0:
                for store in stores[k - 1][:2]:
                    store.wait()
            if k > 1:
                for store in stores[k - 2][2:]:
                    store.wait()

    two = two_buf[group].reshape(rows, width)
    cot = cot_buf[group, :, :span, :].reshape(rows, width)
    chosen = (
        lax.broadcasted_iota(jnp.int32, (MASK_ROWS, LANES), 0)
        == lax.broadcasted_iota(jnp.int32, (MASK_ROWS, LANES), 1)
    ).astype(bf16)
    logits = jnp.where(lane < experts, mm(two, wr_ref[...]), neg_fill)
    shifted = jnp.exp(logits - jnp.max(logits, -1, keepdims=True))
    probs = shifted / jnp.sum(shifted, -1, keepdims=True)
    kept = jnp.concatenate(
        [
            mm(cot_buf[group, b, span : span + MASK_ROWS, :span], chosen, 0, 0)
            for b in range(blocks)
        ],
        0,
    )
    grad_gate = jnp.zeros((rows, LANES), f32)
    gates = probs * kept
    out_rows = gin_rows = None
    for e in range(experts):
        at = slice(e * hidden, (e + 1) * hidden)
        win, wdn = win_buf[at], wdn_buf[at]
        pre = mm(two, win, 1, 1)
        back_rows = mm(cot, wdn, 1, 1)
        gate = gates[:, e : e + 1]
        hidden_rows, slope = gelu_parts(pre)
        product = jnp.sum(hidden_rows * back_rows, -1, keepdims=True)
        grad_gate = jnp.where(lane == e, product, grad_gate)
        gated = (hidden_rows * gate).astype(bf16)
        grad_pre = (slope * back_rows * gate).astype(bf16)
        if opening:
            gated_buf[e, 1] = mm(gated, cot, 0, 0).astype(bf16)
            gated_buf[e, 0] = mm(grad_pre, two, 0, 0).astype(bf16)
        else:
            gated_buf[slot, :, at] = gated
            grad_buf[slot, :, at] = grad_pre
        out_part, gin_part = mm(gated, wdn), mm(grad_pre, win)
        out_rows = out_part if e == 0 else out_rows + out_part
        gin_rows = gin_part if e == 0 else gin_rows + gin_part
    grad_gate = grad_gate * kept
    grad_logits = probs * (grad_gate - jnp.sum(probs * grad_gate, -1, keepdims=True))
    grad_logits = grad_logits.astype(bf16)
    dwr_ref[...] += mm(grad_logits, two, 0, 0)[:SMALL]
    gin_rows = gin_rows + mm(grad_logits, wr_ref[...], 1, 1)
    stage[0] = out_rows.astype(bf16).reshape(blocks, span, width)
    stage[1] = gin_rows.astype(bf16).reshape(blocks, span, width)
    for k in range(groups):

        @pl.when(group == k)
        def _(k=k):
            for store in stores[k]:
                store.start()

    @pl.when(group == groups - 1)
    def _():
        if opening:
            copy = pltpu.make_async_copy(gated_buf, left[0], left_sems.at[0, 0])
            copy.start()
            copy.wait()
        for k in (groups - 1,) if groups == 1 else (groups - 2, groups - 1):
            for store in stores[k][0 if k == groups - 1 else 2 :]:
                store.wait()


def experts_call(two, cot, weights, wr, dwr, name, cost):
    groups = len(two)
    opening = groups == 1
    experts, shard, width = weights[0].shape
    hidden = 2 * shard
    blocks = sum(a.shape[0] for a in two[0])
    span = two[0][0].shape[1]
    rows = blocks * span
    plan = dict(
        groups=groups,
        experts=experts,
        opening=opening,
        two=[len(parts) for parts in two],
        cot=[len(parts) for parts in cot],
    )
    anywhere = pl.BlockSpec(memory_space=pl.ANY)
    once = lambda a: pl.BlockSpec(
        a.shape, lambda g: (0,) * len(a.shape), pipeline_mode=pl.Buffered(1)
    )
    result = jax.ShapeDtypeStruct((blocks, span, width), bf16)
    little = jax.ShapeDtypeStruct((SMALL, width), f32)
    if opening:
        left = [jax.ShapeDtypeStruct((experts, 2, hidden, width), bf16)]
        buffers = [pltpu.VMEM(left[0].shape, bf16), pltpu.VMEM((16, LANES), bf16)]
    else:
        left = [jax.ShapeDtypeStruct((groups * rows, experts * hidden), bf16)] * 2
        buffers = [pltpu.VMEM((2, rows, experts * hidden), bf16)] * 2
    pieces = [a for parts in two for a in parts] + [a for parts in cot for a in parts]
    outs = pl.pallas_call(
        functools.partial(expert_kernel, plan),
        grid=(groups,),
        in_specs=[anywhere] * (len(pieces) + 4)
        + [once(wr)]
        + ([] if opening else [once(little)]),
        out_specs=[anywhere] * len(left) + [once(little)] + [anywhere] * (2 * groups),
        out_shape=left + [little] + [result] * (2 * groups),
        scratch_shapes=[
            pltpu.VMEM((groups, blocks, span, width), bf16),
            pltpu.VMEM((groups, blocks, span + MASK_ROWS, width), bf16),
            pltpu.SemaphoreType.DMA((groups, 4)),
            pltpu.VMEM((experts * hidden, width), bf16),
            pltpu.VMEM((experts * hidden, width), bf16),
            pltpu.SemaphoreType.DMA((experts, 4)),
            *buffers,
            pltpu.VMEM((2, blocks, span, width), bf16),
            pltpu.SemaphoreType.DMA((2,)),
            pltpu.SemaphoreType.DMA((2, 2)),
        ],
        compiler_params=pltpu.CompilerParams(vmem_limit_bytes=VMEM_BYTES),
        cost_estimate=cost(10 * groups * rows * width * hidden * experts),
        name=name,
    )(*pieces, *weights, wr, *([] if opening else [dwr]))
    left, (dwr, *outs) = list(outs[: len(left)]), outs[len(left) :]
    return left, dwr, outs[:groups], outs[groups:]


def grads_kernel(plan, *refs):
    refs = list(refs)

    def take(number):
        taken, refs[:] = refs[:number], refs[number:]
        return taken

    groups = len(plan["two"])
    two_parts = [take(n) for n in plan["two"]]
    cot_parts = [take(n) for n in plan["cot"]]
    gated_ref, grad_ref, own_ref, kept_ref, sent_ref = take(5)
    two_buf, cot_buf, cot_rows, sems = refs
    _, blocks, span, width = two_buf.shape
    rows = blocks * span
    copies = []
    for k in range(groups):
        at = 0
        for n, part in enumerate(two_parts[k]):
            size = part.shape[0]
            copies.append(
                pltpu.make_async_copy(part, two_buf.at[k, pl.ds(at, size)], sems.at[k, n])
            )
            at += size
        at = 0
        for n, part in enumerate(cot_parts[k]):
            size = part.shape[0]
            copies.append(
                pltpu.make_async_copy(
                    part, cot_buf.at[k, pl.ds(at, size)], sems.at[k, 2 + n]
                )
            )
            at += size

    @pl.when(pl.program_id(0) == 0)
    def _():
        for copy in copies:
            copy.start()
        for copy in copies:
            copy.wait()
        for k in range(groups):
            cot_rows[k * rows : (k + 1) * rows] = cot_buf[k, :, :span, :].reshape(rows, width)

    half = own_ref.shape[2] // 2
    two = two_buf[...].reshape(groups * rows, width)
    for n, (left_ref, right) in enumerate(((grad_ref, two), (gated_ref, cot_rows[...]))):
        total = (own_ref[0, n].astype(f32) + mm(left_ref[...], right, 0, 0)).astype(bf16)
        kept_ref[0, n] = total[:half]
        sent_ref[0, n] = total[half:]


def grads_call(two, cot, left, own, first, many):
    groups = len(two)
    blocks = sum(a.shape[0] for a in two[0])
    _, span, width = two[0][0].shape
    rows = blocks * span
    hidden = own.shape[2]
    anywhere = pl.BlockSpec(memory_space=pl.ANY)
    pieces = [a for parts in two for a in parts] + [a for parts in cot for a in parts]
    columns = pl.BlockSpec((groups * rows, hidden), lambda e: (0, e + first))
    part = jax.ShapeDtypeStruct((many, 2, hidden // 2, width), bf16)
    part_spec = pl.BlockSpec((1, 2, hidden // 2, width), lambda e: (e, 0, 0, 0))
    plan = dict(two=[len(parts) for parts in two], cot=[len(parts) for parts in cot])
    return pl.pallas_call(
        functools.partial(grads_kernel, plan),
        grid=(many,),
        in_specs=[anywhere] * len(pieces)
        + [columns, columns, pl.BlockSpec((1, 2, hidden, width), lambda e: (e + first, 0, 0, 0))],
        out_specs=[part_spec, part_spec],
        out_shape=[part, part],
        scratch_shapes=[
            pltpu.VMEM((groups, blocks, span, width), bf16),
            pltpu.VMEM((groups, blocks, span + MASK_ROWS, width), bf16),
            pltpu.VMEM((groups * rows, width), bf16),
            pltpu.SemaphoreType.DMA((groups, 4)),
        ],
        compiler_params=pltpu.CompilerParams(vmem_limit_bytes=VMEM_BYTES),
        cost_estimate=true_cost(8 * groups * rows * width * hidden * many),
        name="expert_grads",
    )(*pieces, *left, own)


def flip(array, fsdp, bits):
    return lax.ppermute(array, "fsdp", [(n, n ^ bits) for n in range(fsdp)])


def tie(value, *others):
    return lax.optimization_barrier((value, others))[0]


def exchange(pieces):
    count = len(pieces)
    return [pieces[0]] + [
        lax.ppermute(pieces[k], "seq", [(n, n ^ k) for n in range(count)]) for k in range(1, count)
    ]


def relative(parts, index):
    count, bit = len(parts), 1
    while bit < count:
        swap = (index & bit) > 0
        parts = [jnp.where(swap, parts[k ^ bit], parts[k]) for k in range(count)]
        bit *= 2
    return parts


def plus(*arrays):
    return sum(a.astype(f32) for a in arrays).astype(bf16)


class Line:
    def __init__(self, seq, raw):
        self.seq, self.raw = seq, raw
        if seq != 4:
            self.total = lax.psum(raw, "seq")

    def inwards(self):
        if self.seq == 4:
            self.moving = lax.ppermute(self.raw, "seq", [(0, 1), (3, 2)])
        return self

    def across(self, *others):
        if self.seq == 4:
            self.pair = plus(self.raw, tie(self.moving, others))
            self.moving = lax.ppermute(self.pair, "seq", [(1, 2), (2, 1)])
            return self.pair
        return self.raw

    def outwards(self, *others):
        if self.seq == 4:
            self.total = plus(self.pair, tie(self.moving, others))
            self.moving = lax.ppermute(self.total, "seq", [(1, 0), (2, 3)])
        return self.total

    def finish(self):
        if self.seq != 4:
            return self.total
        index = lax.axis_index("seq")
        return jnp.where((index == 0) | (index == 3), self.moving, self.total)

    def hold(self, others):
        if self.seq == 4:
            self.moving = tie(self.moving, others)

    def waiting(self):
        return [self.moving] if self.seq == 4 else []


def back_kernel(
    gin_0, gin_2, gin_4, gin_6, mid_ref, cot_ref, tok_ref, att_ref, proj_ref, prob_ref, wall_ref,
    small_ref, dwr_ref, *rest,
):
    blocks, _, span, width = tok_ref.shape
    length = blocks * span
    gtok_refs, (dwall_ref, acc, acc_small, gatt, gproj) = rest[:blocks], rest[blocks:]
    step = pl.program_id(0)

    @pl.when(step == 0)
    def _():
        acc[...] = jnp.zeros_like(acc)
        acc_small[...] = jnp.zeros_like(acc_small)
        acc_small[:SMALL] = dwr_ref[...]

    gin = sum(ref[...].reshape(length, width).astype(f32) for ref in (gin_0, gin_2, gin_4, gin_6))
    unit_two, inverse_two = unit_norm(mid_ref[...].reshape(length, width))
    acc_small[6:7] += jnp.sum(gin * unit_two, 0, keepdims=True)
    acc_small[7:8] += jnp.sum(gin, 0, keepdims=True)
    grad_middle = cot_ref[...].reshape(length, width).astype(f32) + norm_back(
        gin * small_ref[6:7], unit_two, inverse_two
    )
    branch = grad_middle.astype(bf16)
    acc[:, 3 * width : 4 * width] += mm(att_ref[0], branch, 0, 0)
    gatt[...] = mm(branch, wall_ref[:, 3 * width : 4 * width], 1, 1).astype(bf16)
    lower = lax.broadcasted_iota(jnp.int32, (length, LANES), 1) < HEAD_DIM
    zero = jnp.zeros((length, LANES), bf16)
    scale = HEAD_DIM**-0.5

    def score_grad(weights, grad_weights):
        weights = weights.astype(f32)
        product = weights * grad_weights
        return (product - weights * jnp.sum(product, -1, keepdims=True)).astype(bf16)

    for pair in range(width // LANES):
        places = [slice((3 * pair + n) * LANES, (3 * pair + n + 1) * LANES) for n in range(3)]
        first, second, third = (proj_ref[0, :, place] for place in places)
        first_r, second_r, third_r = half_turn(first), half_turn(second), half_turn(third)
        grad = gatt[:, pair * LANES : (pair + 1) * LANES]
        weights_a, weights_b = prob_ref[0, 2 * pair], prob_ref[0, 2 * pair + 1]
        ds_a = score_grad(weights_a, mm(jnp.where(lower, grad, zero), second, 1, 1))
        ds_b = score_grad(weights_b, mm(jnp.where(lower, zero, grad), third, 1, 1))
        gproj[:, places[0]] = (
            jnp.where(lower, mm(ds_a, first_r), mm(ds_a, first_r, 0, 0)) * scale
        ).astype(bf16)
        gproj[:, places[1]] = jnp.where(
            lower, mm(weights_a, grad, 0, 0), mm(ds_b, third_r) * scale
        ).astype(bf16)
        gproj[:, places[2]] = jnp.where(
            lower, mm(ds_b, second_r, 0, 0) * scale, mm(weights_b, grad, 0, 0)
        ).astype(bf16)
    unit_one, inverse_one = unit_norm(tok_ref[...].reshape(length, width).astype(f32))
    one = (unit_one * small_ref[4:5] + small_ref[5:6]).astype(bf16)
    grad_one = mm(gproj[...], wall_ref[:, : 3 * width], 1, 1)
    acc_small[4:5] += jnp.sum(grad_one * unit_one, 0, keepdims=True)
    acc_small[5:6] += jnp.sum(grad_one, 0, keepdims=True)
    grad_tok = grad_middle + norm_back(grad_one * small_ref[4:5], unit_one, inverse_one)
    for k, ref in enumerate(gtok_refs):
        ref[0] = grad_tok[k * span : (k + 1) * span].astype(bf16)
    acc[:, : 3 * width] += mm(one, gproj[...], 0, 0)

    @pl.when(step == pl.num_programs(0) - 1)
    def _():
        dwall_ref[:, : 4 * width] = acc[...].astype(bf16)
        dwall_ref[:, 4 * width :] = acc_small[...].T.astype(bf16)


def back(gins, middle, cot, tok, att, proj, prob, wall, small, dwr):
    blocks, images, span, width = tok.shape
    length = blocks * span
    heads = width // HEAD_DIM
    split = pl.BlockSpec((blocks, 1, span, width), lambda i: (0, i, 0, 0))
    whole = lambda a: pl.BlockSpec(a.shape, lambda i: (0,) * len(a.shape))
    return pl.pallas_call(
        back_kernel,
        grid=(images,),
        in_specs=[split] * 7
        + [
            pl.BlockSpec((1, length, width), lambda i: (i, 0, 0)),
            pl.BlockSpec((1, length, 3 * width), lambda i: (i, 0, 0)),
            pl.BlockSpec((1, heads, length, length), lambda i: (i, 0, 0, 0)),
            whole(wall),
            whole(small),
            whole(dwr),
        ],
        out_specs=[pl.BlockSpec((1, span, width), lambda i: (i, 0, 0))] * blocks + [whole(wall)],
        out_shape=[jax.ShapeDtypeStruct((images, span, width), bf16)] * blocks
        + [jax.ShapeDtypeStruct(wall.shape, bf16)],
        scratch_shapes=[
            pltpu.VMEM((width, 4 * width), f32),
            pltpu.VMEM((LANES, width), f32),
            pltpu.VMEM((length, width), bf16),
            pltpu.VMEM((length, 3 * width), bf16),
        ],
        compiler_params=pltpu.CompilerParams(vmem_limit_bytes=VMEM_BYTES),
        cost_estimate=true_cost(10 * images * length * width * (4 * width + 3 * length)),
        name="back",
    )(*gins, middle, cot, tok, att, proj, prob, wall, small, dwr)


def kept_pairs(route_rows, token_live, order_rows, expert_count, capacity):
    labels = jnp.arange(expert_count, dtype=jnp.int32)
    alive = token_live > 0
    first_hot = ((route_rows[:, 0:1] == labels) & alive[:, None]).astype(bf16)
    second_hot = ((route_rows[:, 1:2] == labels) & alive[:, None]).astype(bf16)
    earlier = (order_rows[None, :] < order_rows[:, None]).astype(bf16)
    ahead = mm(earlier, jnp.concatenate([first_hot, second_hot], 1))
    ahead_first = ahead[:, :expert_count]
    ahead_second = ahead[:, expert_count:] + jnp.sum(first_hot.astype(f32), 0)
    return jnp.where(ahead_first < capacity, first_hot, 0) + jnp.where(
        ahead_second < capacity, second_hot, 0
    )


def local(
    fsdp,
    seq,
    tokens,
    ln1_gain,
    ln1_bias,
    w_qkv,
    w_out,
    ln2_gain,
    ln2_bias,
    w_router,
    w_in,
    w_down,
    padding,
    routes,
    priority,
    cotangent,
):
    images, span, width = tokens.shape
    expert_count, shard_rows = w_in.shape[0], w_in.shape[1]
    rows = images * span
    own = images // seq
    length = seq * span
    capacity = (2 * rows + expert_count - 1) // expert_count
    outer = fsdp // 8
    if outer > 1:
        outer_groups = [[o * 8 + n for o in range(outer)] for n in range(8)]
    spread = functools.partial(flip, fsdp=fsdp)
    seq_index = lax.axis_index("seq")
    place = lax.axis_index("fsdp") if outer == 1 else jnp.int32(0)
    place = place.astype(jnp.int32).reshape(1)

    def picked(array, k):
        return lax.dynamic_index_in_dim(array, seq_index ^ k, 0, keepdims=False)

    tokens = tokens.reshape(seq, own * span, width)
    tok = jnp.stack(exchange([picked(tokens, k) for k in range(seq)]))
    tok = tok.reshape(seq, own, span, width)

    columns = jnp.concatenate(
        [w_router] + [v[:, None] for v in (ln1_gain, ln1_bias, ln2_gain, ln2_bias)], 1
    )
    columns = jnp.pad(columns, ((0, 0), (0, LANES - columns.shape[1])))
    shard = jnp.concatenate([w_qkv, w_out, columns], 1)
    if outer == 1:
        cut = width // 16
        from_x, from_y = spread(shard, bits=2), spread(shard, bits=4)
        from_x, from_y = tie((from_x, from_y), tok)
        near = [(0, 0, shard), (2, 0, from_x), (4, 0, from_y)]
        far = [
            (6, 0, spread(from_x[:cut], bits=4)),
            (6, cut, spread(from_y[cut:], bits=2)),
        ]
        near += [(r + 1, skip, spread(a, bits=1)) for r, skip, a in near]
    else:
        full = lax.all_gather(shard, "fsdp", axis=0, tiled=True)
        from_x = from_y = full
        near, far = [(n, 0, full[n * (width // 8) : (n + 1) * (width // 8)]) for n in range(8)], []

    live = lax.dynamic_slice_in_dim(padding, seq_index * span, span, 1)
    kept = kept_pairs(
        routes.reshape(rows, 2), live.reshape(rows), priority.reshape(rows), expert_count, capacity
    )
    kept = jnp.swapaxes(kept.reshape(seq, own * span, expert_count), 1, 2)
    kept = jnp.pad(
        kept, ((0, 0), (0, MASK_ROWS - expert_count), (0, width - own * span))
    ).astype(bf16)
    cot = cotangent * live[:, :, None].astype(bf16)
    packed = jnp.concatenate([cot.reshape(seq, own * span, width), kept], 1)
    packed = tie(packed, tok, from_x, from_y)
    packed = jnp.stack(exchange([picked(packed, k) for k in range(seq)]))
    late = tie([a for _, _, a in far], packed)
    far += [(r + 1, skip, spread(a, bits=1)) for (r, skip, _), a in zip(far, late)]
    offsets = [(r, skip) for r, skip, _ in near + far]
    pieces = [a for _, _, a in near + far]
    cot_x, cot_y = spread(packed, bits=2), spread(packed, bits=4)
    half = seq // 2
    cot_far = [spread(cot_x[:half], bits=4), spread(cot_y[half:], bits=2)]

    win, wdn = w_in, w_down
    if outer > 1:
        win = lax.all_gather(win, "fsdp", axis=1, tiled=True, axis_index_groups=outer_groups)
        wdn = lax.all_gather(wdn, "fsdp", axis=1, tiled=True, axis_index_groups=outer_groups)
    win, wdn = tie((win, wdn), pieces)
    weights = [win, spread(win, bits=1), wdn, spread(wdn, bits=1)]

    mine = lax.dynamic_slice_in_dim(padding, seq_index * own, own, 0).reshape(own, seq, span)
    mine = jnp.stack(relative([mine[:, b] for b in range(seq)], seq_index))
    vis = jnp.where(mine > 0, 0.0, neg_fill).astype(f32)
    vis = jnp.swapaxes(vis, 0, 1).reshape(own, 1, length)
    middle, two, proj, att, prob, wall, wr, small = front(tok, pieces, offsets, vis, place)
    two = two.reshape(seq, own * span, width)
    two_far = [[spread(two, bits=bits)] for bits in (2, 4, 6)]

    (dw,), dwr, out_0, gin_0 = experts_call(
        [[two]], [[packed]], weights, wr, None, "experts_own", lambda flops: SHORT
    )
    cots = [[cot_x], [cot_y], cot_far]
    left, dwr, outs, gins = experts_call(
        two_far, cots, weights, wr, dwr, "experts_far", true_cost
    )
    arrived = [spread(a, bits=bits) for a, bits in zip(gins, (2, 4, 6))]

    def finished(dw_kept, dw_sent):
        raw = plus(dw_kept, spread(dw_sent, bits=1))
        if outer > 1:
            raw = lax.psum_scatter(
                raw, "fsdp", scatter_dimension=2, tiled=True, axis_index_groups=outer_groups
            )
        return lax.optimization_barrier([raw[n : n + 1] for n in range(raw.shape[0])])

    first = Line(seq, finished(*grads_call(two_far, cots, left, dw, 0, 1))[0]).inwards()
    left, dw = tie((left, dw), first.raw)
    parts = grads_call(two_far, cots, left, dw, 1, expert_count - 1)
    ready = first.across()
    lines = [Line(seq, raw) for raw in finished(*tie(parts, ready, arrived[:2]))]
    lines[0].inwards()
    gins = gin_0 + tie(arrived, ready, [line.raw for line in lines])
    lines = [first] + lines

    shape4 = (seq, own, span, width)
    *grad_tok, dense = back(
        [a.reshape(shape4) for a in gins],
        middle,
        packed[:, : own * span].reshape(shape4),
        tok,
        att,
        proj,
        prob,
        wall,
        small,
        dwr,
    )
    flying = (lines[0].waiting(), lines[1].waiting())
    dense, outs = tie((dense, outs), flying, grad_tok)
    outs = [spread(a, bits=bits) for a, bits in zip(outs, (2, 4, 6))]
    dense = lax.psum_scatter(dense, "fsdp", scatter_dimension=0, tiled=True)
    lines[2].raw, lines[3].raw = tie((lines[2].raw, lines[3].raw), grad_tok)
    lines[2].inwards()
    ready = lines[1].across(grad_tok, flying)
    ready = lines[0].outwards(ready)
    lines[3].inwards()
    ready = lines[2].across(ready)
    ready = lines[1].outwards(ready)
    ready = lines[3].across(ready, lines[0].waiting())
    ready = lines[2].outwards(ready)
    dense_line = Line(seq, tie(dense, ready)).inwards()
    ready = lines[3].outwards(dense_line.raw, lines[1].waiting())

    ready = dense_line.across(ready)
    outs, grad_tok = tie((outs, grad_tok), ready)
    outs = [a.reshape(shape4) for a in out_0 + outs]
    home = []
    for k in range(seq):
        alive = mine[k][:, :, None].astype(f32)
        combined = sum(a[k].astype(f32) for a in outs)
        home.append(jnp.stack([(alive * (middle[k] + combined)).astype(bf16), grad_tok[k]]))
    home = exchange(home)
    ready = dense_line.outwards(ready)
    home = relative(tie(home, ready), seq_index)
    outputs, grad_tokens = (
        jnp.concatenate([a[n] for a in home], 0).reshape(images, span, width) for n in range(2)
    )
    lines[3].hold(dense_line.waiting())
    grads = [line.finish() for line in lines]
    dense = dense_line.finish().astype(f32)
    expert_grads = [jnp.concatenate([g[:, n] for g in grads], 0).astype(f32) for n in range(2)]
    tail = dense[:, 4 * width :]
    return (
        outputs,
        grad_tokens,
        tail[:, 4],
        tail[:, 5],
        dense[:, : 3 * width],
        dense[:, 3 * width : 4 * width],
        tail[:, 6],
        tail[:, 7],
        tail[:, :expert_count],
        expert_grads[0],
        expert_grads[1],
    )


def solution(mesh):
    rows = P("fsdp", "seq", None)
    in_specs = (
        rows,
        P("fsdp"),
        P("fsdp"),
        P("fsdp", None),
        P("fsdp", None),
        P("fsdp"),
        P("fsdp"),
        P("fsdp", None),
        P(None, "fsdp", None),
        P(None, "fsdp", None),
        P("fsdp", None),
        rows,
        P("fsdp", "seq"),
        rows,
    )
    out_specs = (
        rows,
        rows,
        P("fsdp"),
        P("fsdp"),
        P("fsdp", None),
        P("fsdp", None),
        P("fsdp"),
        P("fsdp"),
        P("fsdp", None),
        P(None, "fsdp", None),
        P(None, "fsdp", None),
    )
    return jax.shard_map(
        functools.partial(local, mesh.shape["fsdp"], mesh.shape["seq"]),
        mesh=mesh,
        in_specs=in_specs,
        out_specs=out_specs,
        check_vma=False,
    )
```

```python
import functools
import math

import jax
import jax.numpy as jnp
from jax import lax
from jax.experimental import pallas as pl
from jax.experimental.pallas import tpu as pltpu
from jax.sharding import PartitionSpec as P

HEAD_DIM = 64
LANES = 128
MASK_ROWS = 16
SMALL = 8
norm_eps = 1e-06
neg_fill = -1e30
f32 = jnp.float32
bf16 = jnp.bfloat16
VMEM_BYTES = 60 * 1024 * 1024
SHORT = pl.CostEstimate(flops=1000, bytes_accessed=1000, transcendentals=0)


def true_cost(flops):
    return pl.CostEstimate(flops=2 * flops, bytes_accessed=16 * 1024 * 1024, transcendentals=0)


def mm(left, right, left_dim=1, right_dim=0):
    return lax.dot_general(
        left, right, (((left_dim,), (right_dim,)), ((), ())), preferred_element_type=f32
    )


def unit_norm(rows):
    centred = rows - jnp.mean(rows, -1, keepdims=True)
    inverse = lax.rsqrt(jnp.mean(centred * centred, -1, keepdims=True) + norm_eps)
    return centred * inverse, inverse


def norm_back(scaled, unit, inverse):
    return inverse * (
        scaled
        - jnp.mean(scaled, -1, keepdims=True)
        - unit * jnp.mean(scaled * unit, -1, keepdims=True)
    )


def half_turn(tile):
    return pltpu.roll(tile.astype(f32), HEAD_DIM, axis=1).astype(bf16)


def wall_copies(pieces, offsets, place_ref, wall_ref, sems):
    copies = []
    for n, (piece, (r, skip)) in enumerate(zip(pieces, offsets)):
        rows = piece.shape[0]
        shard = wall_ref.shape[0] // 8
        start = pl.multiple_of((place_ref[0] ^ r) * shard + skip, 16)
        copies.append(pltpu.make_async_copy(piece, wall_ref.at[pl.ds(start, rows)], sems.at[n]))
    return copies


def front_kernel(offsets, *refs):
    pieces = refs[: len(offsets)]
    tok_ref, vis_ref, place_ref = refs[len(offsets) : len(offsets) + 3]
    mid_ref, two_ref, proj_ref, att_ref, prob_ref, full_ref, wr_ref, small_ref = refs[
        len(offsets) + 3 : len(offsets) + 11
    ]
    wall_ref, sems, full_sem = refs[len(offsets) + 11 :]
    blocks, _, span, width = tok_ref.shape
    length = blocks * span
    save = pltpu.make_async_copy(wall_ref, full_ref, full_sem)

    @pl.when(pl.program_id(0) == 0)
    def _():
        copies = wall_copies(pieces, offsets, place_ref, wall_ref, sems)
        for copy in copies:
            copy.start()
        for copy in copies:
            copy.wait()
        save.start()
        columns = wall_ref[:, 4 * width :]
        wr_ref[...] = columns
        small_ref[...] = columns.astype(f32).T[:SMALL]

    rows = tok_ref[...].reshape(length, width).astype(f32)
    unit, _ = unit_norm(rows)
    one = (unit * small_ref[4:5] + small_ref[5:6]).astype(bf16)
    proj_ref[0] = mm(one, wall_ref[:, : 3 * width]).astype(bf16)
    lower = lax.broadcasted_iota(jnp.int32, (length, LANES), 1) < HEAD_DIM
    zero = jnp.zeros((length, LANES), bf16)
    bias = vis_ref[0]

    def soften(index, queries, keys):
        scores = mm(queries, keys, 1, 1) * (HEAD_DIM**-0.5) + bias
        shifted = jnp.exp(scores - jnp.max(scores, -1, keepdims=True))
        weights = (shifted / jnp.sum(shifted, -1, keepdims=True)).astype(bf16)
        prob_ref[0, index] = weights
        return weights

    for pair in range(width // LANES):
        first, second, third = (
            proj_ref[0, :, (3 * pair + n) * LANES : (3 * pair + n + 1) * LANES] for n in range(3)
        )
        weights_a = soften(2 * pair, jnp.where(lower, first, zero), half_turn(first))
        weights_b = soften(2 * pair + 1, jnp.where(lower, zero, second), half_turn(third))
        both = jnp.where(lower, mm(weights_a, second), mm(weights_b, third))
        att_ref[0, :, pair * LANES : (pair + 1) * LANES] = both.astype(bf16)
    middle = rows + mm(att_ref[0], wall_ref[:, 3 * width : 4 * width])
    mid_ref[...] = middle.reshape(mid_ref.shape)
    unit, _ = unit_norm(middle)
    two_ref[...] = (unit * small_ref[6:7] + small_ref[7:8]).astype(bf16).reshape(two_ref.shape)

    @pl.when(pl.program_id(0) == pl.num_programs(0) - 1)
    def _():
        save.wait()


def front(tok, pieces, offsets, vis, place):
    blocks, images, span, width = tok.shape
    length = blocks * span
    heads = width // HEAD_DIM
    split = pl.BlockSpec((blocks, 1, span, width), lambda i: (0, i, 0, 0))
    anywhere = pl.BlockSpec(memory_space=pl.ANY)
    columns = pieces[0].shape[1]
    return pl.pallas_call(
        functools.partial(front_kernel, offsets),
        grid=(images,),
        in_specs=[anywhere] * len(pieces)
        + [
            split,
            pl.BlockSpec((1, 1, length), lambda i: (i, 0, 0)),
            pl.BlockSpec(memory_space=pltpu.SMEM),
        ],
        out_specs=[
            split,
            split,
            pl.BlockSpec((1, length, 3 * width), lambda i: (i, 0, 0)),
            pl.BlockSpec((1, length, width), lambda i: (i, 0, 0)),
            pl.BlockSpec((1, heads, length, length), lambda i: (i, 0, 0, 0)),
            anywhere,
            pl.BlockSpec((width, LANES), lambda i: (0, 0)),
            pl.BlockSpec((SMALL, width), lambda i: (0, 0)),
        ],
        out_shape=[
            jax.ShapeDtypeStruct(tok.shape, f32),
            jax.ShapeDtypeStruct(tok.shape, bf16),
            jax.ShapeDtypeStruct((images, length, 3 * width), bf16),
            jax.ShapeDtypeStruct((images, length, width), bf16),
            jax.ShapeDtypeStruct((images, heads, length, length), bf16),
            jax.ShapeDtypeStruct((width, columns), bf16),
            jax.ShapeDtypeStruct((width, LANES), bf16),
            jax.ShapeDtypeStruct((SMALL, width), f32),
        ],
        scratch_shapes=[
            pltpu.VMEM((width, columns), bf16),
            pltpu.SemaphoreType.DMA((len(pieces),)),
            pltpu.SemaphoreType.DMA(()),
        ],
        compiler_params=pltpu.CompilerParams(vmem_limit_bytes=VMEM_BYTES),
        cost_estimate=SHORT,
        name="front",
    )(*pieces, tok, vis, place)


def gelu_parts(pre):
    bell = jnp.exp2(pre * pre * (-0.5 * math.log2(math.e)))
    size = 1.0 + (0.3275911 * math.sqrt(0.5)) * jnp.abs(pre)
    frac = pl.reciprocal(size, approx=True)
    frac = frac * (2.0 - size * frac)
    a5, a4, a3, a2, a1 = (
        0.5 * c for c in (1.061405429, -1.453152027, 1.421413741, -0.284496736, 0.254829592)
    )
    tail = frac * (a1 + frac * (a2 + frac * (a3 + frac * (a4 + frac * a5)))) * bell
    cumulative = jnp.where(pre >= 0, 1.0 - tail, tail)
    return pre * cumulative, cumulative + (pre * 0.3989422804014327) * bell


def expert_kernel(plan, *refs):
    refs = list(refs)

    def take(number):
        taken, refs[:] = refs[:number], refs[number:]
        return taken

    groups, experts, opening = plan["groups"], plan["experts"], plan["opening"]
    two_parts = [take(n) for n in plan["two"]]
    cot_parts = [take(n) for n in plan["cot"]]
    weights = take(4)
    (wr_ref,) = take(1)
    dwr_carried = None if opening else take(1)[0]
    left = take(1 if opening else 2)
    (dwr_ref,) = take(1)
    results = take(2 * groups)
    two_buf, cot_buf, sems, win_buf, wdn_buf, weight_sems, gated_buf, grad_buf = take(8)
    stage, store_sems, left_sems = take(3)
    _, blocks, span, width = two_buf.shape
    rows = blocks * span
    hidden = win_buf.shape[0] // experts
    shard = hidden // 2
    group = pl.program_id(0)
    slot = group % gated_buf.shape[0]
    lane = lax.broadcasted_iota(jnp.int32, (rows, LANES), 1)

    copies = []
    for k in range(groups):
        some = []
        for parts, buffer in ((two_parts[k], two_buf), (cot_parts[k], cot_buf)):
            at = 0
            for part in parts:
                size = part.shape[0]
                some.append((part, buffer.at[k, pl.ds(at, size)]))
                at += size
        copies.append(
            [pltpu.make_async_copy(s, t, sems.at[k, n]) for n, (s, t) in enumerate(some)]
        )
    fetches = [
        pltpu.make_async_copy(
            ref.at[e],
            (win_buf, wdn_buf)[n // 2].at[pl.ds(e * hidden + (n % 2) * shard, shard)],
            weight_sems.at[e, n],
        )
        for e in range(experts)
        for n, ref in enumerate(weights)
    ]
    stores = [
        [
            pltpu.make_async_copy(stage.at[n], results[n * groups + k], store_sems.at[n])
            for n in range(2)
        ]
        for k in range(groups)
    ]
    if not opening:
        for k in range(groups):
            for n, buffer in enumerate((gated_buf, grad_buf)):
                place = k % buffer.shape[0]
                stores[k].append(
                    pltpu.make_async_copy(
                        buffer.at[place],
                        left[n].at[pl.ds(k * rows, rows)],
                        left_sems.at[place, n],
                    )
                )

    @pl.when(group == 0)
    def _():
        for copy in copies[0] + fetches:
            copy.start()
        for some in copies[1:]:
            for copy in some:
                copy.start()
        dwr_ref[...] = jnp.zeros_like(dwr_ref) if opening else dwr_carried[...]
        for copy in fetches:
            copy.wait()

    for k, some in enumerate(copies):

        @pl.when(group == k)
        def _(k=k, some=some):
            for copy in some:
                copy.wait()
            if k > 0:
                for store in stores[k - 1][:2]:
                    store.wait()
            if k > 1:
                for store in stores[k - 2][2:]:
                    store.wait()

    two = two_buf[group].reshape(rows, width)
    cot = cot_buf[group, :, :span, :].reshape(rows, width)
    chosen = (
        lax.broadcasted_iota(jnp.int32, (MASK_ROWS, LANES), 0)
        == lax.broadcasted_iota(jnp.int32, (MASK_ROWS, LANES), 1)
    ).astype(bf16)
    logits = jnp.where(lane < experts, mm(two, wr_ref[...]), neg_fill)
    shifted = jnp.exp(logits - jnp.max(logits, -1, keepdims=True))
    probs = shifted / jnp.sum(shifted, -1, keepdims=True)
    kept = jnp.concatenate(
        [
            mm(cot_buf[group, b, span : span + MASK_ROWS, :span], chosen, 0, 0)
            for b in range(blocks)
        ],
        0,
    )
    grad_gate = jnp.zeros((rows, LANES), f32)
    gates = probs * kept
    out_rows = gin_rows = None
    products = lambda at: (mm(two, win_buf[at], 1, 1), mm(cot, wdn_buf[at], 1, 1))
    spots = [slice(e * hidden, (e + 1) * hidden) for e in range(experts)]
    ready = products(spots[0])
    for e, at in enumerate(spots):
        win, wdn = win_buf[at], wdn_buf[at]
        pre, back_rows = ready
        if e + 1 < experts:
            ready = products(spots[e + 1])
        gate = gates[:, e : e + 1]
        hidden_rows, slope = gelu_parts(pre)
        product = jnp.sum(hidden_rows * back_rows, -1, keepdims=True)
        grad_gate = jnp.where(lane == e, product, grad_gate)
        gated = (hidden_rows * gate).astype(bf16)
        grad_pre = (slope * back_rows * gate).astype(bf16)
        if opening:
            gated_buf[e, 1] = mm(gated, cot, 0, 0).astype(bf16)
            gated_buf[e, 0] = mm(grad_pre, two, 0, 0).astype(bf16)
        else:
            gated_buf[slot, :, at] = gated
            grad_buf[slot, :, at] = grad_pre
        out_part, gin_part = mm(gated, wdn), mm(grad_pre, win)
        out_rows = out_part if e == 0 else out_rows + out_part
        gin_rows = gin_part if e == 0 else gin_rows + gin_part
    grad_gate = grad_gate * kept
    grad_logits = probs * (grad_gate - jnp.sum(probs * grad_gate, -1, keepdims=True))
    grad_logits = grad_logits.astype(bf16)
    dwr_ref[...] += mm(grad_logits, two, 0, 0)[:SMALL]
    gin_rows = gin_rows + mm(grad_logits, wr_ref[...], 1, 1)
    stage[0] = out_rows.astype(bf16).reshape(blocks, span, width)
    stage[1] = gin_rows.astype(bf16).reshape(blocks, span, width)
    for k in range(groups):

        @pl.when(group == k)
        def _(k=k):
            for store in stores[k]:
                store.start()

    @pl.when(group == groups - 1)
    def _():
        if opening:
            copy = pltpu.make_async_copy(gated_buf, left[0], left_sems.at[0, 0])
            copy.start()
            copy.wait()
        for k in (groups - 1,) if groups == 1 else (groups - 2, groups - 1):
            for store in stores[k][0 if k == groups - 1 else 2 :]:
                store.wait()


def experts_call(two, cot, weights, wr, dwr, name, cost):
    groups = len(two)
    opening = groups == 1
    experts, shard, width = weights[0].shape
    hidden = 2 * shard
    blocks = sum(a.shape[0] for a in two[0])
    span = two[0][0].shape[1]
    rows = blocks * span
    plan = dict(
        groups=groups,
        experts=experts,
        opening=opening,
        two=[len(parts) for parts in two],
        cot=[len(parts) for parts in cot],
    )
    anywhere = pl.BlockSpec(memory_space=pl.ANY)
    once = lambda a: pl.BlockSpec(
        a.shape, lambda g: (0,) * len(a.shape), pipeline_mode=pl.Buffered(1)
    )
    result = jax.ShapeDtypeStruct((blocks, span, width), bf16)
    little = jax.ShapeDtypeStruct((SMALL, width), f32)
    if opening:
        left = [jax.ShapeDtypeStruct((experts, 2, hidden, width), bf16)]
        buffers = [pltpu.VMEM(left[0].shape, bf16), pltpu.VMEM((16, LANES), bf16)]
    else:
        left = [jax.ShapeDtypeStruct((groups * rows, experts * hidden), bf16)] * 2
        buffers = [pltpu.VMEM((2, rows, experts * hidden), bf16)] * 2
    pieces = [a for parts in two for a in parts] + [a for parts in cot for a in parts]
    outs = pl.pallas_call(
        functools.partial(expert_kernel, plan),
        grid=(groups,),
        in_specs=[anywhere] * (len(pieces) + 4)
        + [once(wr)]
        + ([] if opening else [once(little)]),
        out_specs=[anywhere] * len(left) + [once(little)] + [anywhere] * (2 * groups),
        out_shape=left + [little] + [result] * (2 * groups),
        scratch_shapes=[
            pltpu.VMEM((groups, blocks, span, width), bf16),
            pltpu.VMEM((groups, blocks, span + MASK_ROWS, width), bf16),
            pltpu.SemaphoreType.DMA((groups, 4)),
            pltpu.VMEM((experts * hidden, width), bf16),
            pltpu.VMEM((experts * hidden, width), bf16),
            pltpu.SemaphoreType.DMA((experts, 4)),
            *buffers,
            pltpu.VMEM((2, blocks, span, width), bf16),
            pltpu.SemaphoreType.DMA((2,)),
            pltpu.SemaphoreType.DMA((2, 2)),
        ],
        compiler_params=pltpu.CompilerParams(vmem_limit_bytes=VMEM_BYTES),
        cost_estimate=cost(10 * groups * rows * width * hidden * experts),
        name=name,
    )(*pieces, *weights, wr, *([] if opening else [dwr]))
    left, (dwr, *outs) = list(outs[: len(left)]), outs[len(left) :]
    return left, dwr, outs[:groups], outs[groups:]


def grads_kernel(plan, *refs):
    refs = list(refs)

    def take(number):
        taken, refs[:] = refs[:number], refs[number:]
        return taken

    groups = len(plan["two"])
    two_parts = [take(n) for n in plan["two"]]
    cot_parts = [take(n) for n in plan["cot"]]
    gated_ref, grad_ref, own_ref, kept_ref, sent_ref = take(5)
    two_buf, cot_buf, cot_rows, sems = refs
    _, blocks, span, width = two_buf.shape
    rows = blocks * span
    copies = []
    for k in range(groups):
        at = 0
        for n, part in enumerate(two_parts[k]):
            size = part.shape[0]
            copies.append(
                pltpu.make_async_copy(part, two_buf.at[k, pl.ds(at, size)], sems.at[k, n])
            )
            at += size
        at = 0
        for n, part in enumerate(cot_parts[k]):
            size = part.shape[0]
            copies.append(
                pltpu.make_async_copy(
                    part, cot_buf.at[k, pl.ds(at, size)], sems.at[k, 2 + n]
                )
            )
            at += size

    @pl.when(pl.program_id(0) == 0)
    def _():
        for copy in copies:
            copy.start()
        for copy in copies:
            copy.wait()
        for k in range(groups):
            cot_rows[k * rows : (k + 1) * rows] = cot_buf[k, :, :span, :].reshape(rows, width)

    half = own_ref.shape[2] // 2
    two = two_buf[...].reshape(groups * rows, width)
    for n, (left_ref, right) in enumerate(((grad_ref, two), (gated_ref, cot_rows[...]))):
        total = (own_ref[0, n].astype(f32) + mm(left_ref[...], right, 0, 0)).astype(bf16)
        kept_ref[0, n] = total[:half]
        sent_ref[0, n] = total[half:]


def grads_call(two, cot, left, own, first, many):
    groups = len(two)
    blocks = sum(a.shape[0] for a in two[0])
    _, span, width = two[0][0].shape
    rows = blocks * span
    hidden = own.shape[2]
    anywhere = pl.BlockSpec(memory_space=pl.ANY)
    pieces = [a for parts in two for a in parts] + [a for parts in cot for a in parts]
    columns = pl.BlockSpec((groups * rows, hidden), lambda e: (0, e + first))
    part = jax.ShapeDtypeStruct((many, 2, hidden // 2, width), bf16)
    part_spec = pl.BlockSpec((1, 2, hidden // 2, width), lambda e: (e, 0, 0, 0))
    plan = dict(two=[len(parts) for parts in two], cot=[len(parts) for parts in cot])
    return pl.pallas_call(
        functools.partial(grads_kernel, plan),
        grid=(many,),
        in_specs=[anywhere] * len(pieces)
        + [columns, columns, pl.BlockSpec((1, 2, hidden, width), lambda e: (e + first, 0, 0, 0))],
        out_specs=[part_spec, part_spec],
        out_shape=[part, part],
        scratch_shapes=[
            pltpu.VMEM((groups, blocks, span, width), bf16),
            pltpu.VMEM((groups, blocks, span + MASK_ROWS, width), bf16),
            pltpu.VMEM((groups * rows, width), bf16),
            pltpu.SemaphoreType.DMA((groups, 4)),
        ],
        compiler_params=pltpu.CompilerParams(vmem_limit_bytes=VMEM_BYTES),
        cost_estimate=true_cost(8 * groups * rows * width * hidden * many),
        name="expert_grads",
    )(*pieces, *left, own)


def flip(array, fsdp, bits):
    return lax.ppermute(array, "fsdp", [(n, n ^ bits) for n in range(fsdp)])


def tie(value, *others):
    return lax.optimization_barrier((value, others))[0]


def exchange(pieces):
    count = len(pieces)
    return [pieces[0]] + [
        lax.ppermute(pieces[k], "seq", [(n, n ^ k) for n in range(count)]) for k in range(1, count)
    ]


def relative(parts, index):
    count, bit = len(parts), 1
    while bit < count:
        swap = (index & bit) > 0
        parts = [jnp.where(swap, parts[k ^ bit], parts[k]) for k in range(count)]
        bit *= 2
    return parts


def plus(*arrays):
    return sum(a.astype(f32) for a in arrays).astype(bf16)


class Line:
    def __init__(self, seq, raw):
        self.seq, self.raw = seq, raw
        if seq != 4:
            self.total = lax.psum(raw, "seq")

    def inwards(self):
        if self.seq == 4:
            self.moving = lax.ppermute(self.raw, "seq", [(0, 1), (3, 2)])
        return self

    def inwards_with(self, other, *others):
        if self.seq != 4:
            return
        other.total = plus(other.pair, tie(other.moving, others))
        index = lax.axis_index("seq")
        both = jnp.where((index == 0) | (index == 3), self.raw, other.total)
        self.moving = lax.ppermute(both, "seq", [(0, 1), (1, 0), (2, 3), (3, 2)])
        other.moving = self.moving

    def hold(self, others):
        if self.seq == 4:
            self.moving = tie(self.moving, others)

    def across(self, *others):
        if self.seq == 4:
            self.pair = plus(self.raw, tie(self.moving, others))
            self.moving = lax.ppermute(self.pair, "seq", [(1, 2), (2, 1)])
            return self.pair
        return self.raw

    def outwards(self, *others):
        if self.seq == 4:
            self.total = plus(self.pair, tie(self.moving, others))
            self.moving = lax.ppermute(self.total, "seq", [(1, 0), (2, 3)])
        return self.total

    def finish(self):
        if self.seq != 4:
            return self.total
        index = lax.axis_index("seq")
        return jnp.where((index == 0) | (index == 3), self.moving, self.total)

    def waiting(self):
        return [self.moving] if self.seq == 4 else []


def back_kernel(
    gin_0, gin_2, gin_4, gin_6, mid_ref, cot_ref, tok_ref, att_ref, proj_ref, prob_ref, wall_ref,
    small_ref, dwr_ref, *rest,
):
    blocks, _, span, width = tok_ref.shape
    length = blocks * span
    gtok_refs, (dwall_ref, acc, acc_small, gatt, gproj) = rest[:blocks], rest[blocks:]
    step = pl.program_id(0)

    @pl.when(step == 0)
    def _():
        acc[...] = jnp.zeros_like(acc)
        acc_small[...] = jnp.zeros_like(acc_small)
        acc_small[:SMALL] = dwr_ref[...]

    gin = sum(ref[...].reshape(length, width).astype(f32) for ref in (gin_0, gin_2, gin_4, gin_6))
    unit_two, inverse_two = unit_norm(mid_ref[...].reshape(length, width))
    acc_small[6:7] += jnp.sum(gin * unit_two, 0, keepdims=True)
    acc_small[7:8] += jnp.sum(gin, 0, keepdims=True)
    grad_middle = cot_ref[...].reshape(length, width).astype(f32) + norm_back(
        gin * small_ref[6:7], unit_two, inverse_two
    )
    branch = grad_middle.astype(bf16)
    acc[:, 3 * width : 4 * width] += mm(att_ref[0], branch, 0, 0)
    gatt[...] = mm(branch, wall_ref[:, 3 * width : 4 * width], 1, 1).astype(bf16)
    lower = lax.broadcasted_iota(jnp.int32, (length, LANES), 1) < HEAD_DIM
    zero = jnp.zeros((length, LANES), bf16)
    scale = HEAD_DIM**-0.5

    def score_grad(weights, grad_weights):
        weights = weights.astype(f32)
        product = weights * grad_weights
        return (product - weights * jnp.sum(product, -1, keepdims=True)).astype(bf16)

    for pair in range(width // LANES):
        places = [slice((3 * pair + n) * LANES, (3 * pair + n + 1) * LANES) for n in range(3)]
        first, second, third = (proj_ref[0, :, place] for place in places)
        first_r, second_r, third_r = half_turn(first), half_turn(second), half_turn(third)
        grad = gatt[:, pair * LANES : (pair + 1) * LANES]
        weights_a, weights_b = prob_ref[0, 2 * pair], prob_ref[0, 2 * pair + 1]
        ds_a = score_grad(weights_a, mm(jnp.where(lower, grad, zero), second, 1, 1))
        ds_b = score_grad(weights_b, mm(jnp.where(lower, zero, grad), third, 1, 1))
        gproj[:, places[0]] = (
            jnp.where(lower, mm(ds_a, first_r), mm(ds_a, first_r, 0, 0)) * scale
        ).astype(bf16)
        gproj[:, places[1]] = jnp.where(
            lower, mm(weights_a, grad, 0, 0), mm(ds_b, third_r) * scale
        ).astype(bf16)
        gproj[:, places[2]] = jnp.where(
            lower, mm(ds_b, second_r, 0, 0) * scale, mm(weights_b, grad, 0, 0)
        ).astype(bf16)
    unit_one, inverse_one = unit_norm(tok_ref[...].reshape(length, width).astype(f32))
    one = (unit_one * small_ref[4:5] + small_ref[5:6]).astype(bf16)
    grad_one = mm(gproj[...], wall_ref[:, : 3 * width], 1, 1)
    acc_small[4:5] += jnp.sum(grad_one * unit_one, 0, keepdims=True)
    acc_small[5:6] += jnp.sum(grad_one, 0, keepdims=True)
    grad_tok = grad_middle + norm_back(grad_one * small_ref[4:5], unit_one, inverse_one)
    for k, ref in enumerate(gtok_refs):
        ref[0] = grad_tok[k * span : (k + 1) * span].astype(bf16)
    acc[:, : 3 * width] += mm(one, gproj[...], 0, 0)

    @pl.when(step == pl.num_programs(0) - 1)
    def _():
        dwall_ref[:, : 4 * width] = acc[...].astype(bf16)
        dwall_ref[:, 4 * width :] = acc_small[...].T.astype(bf16)


def back(gins, middle, cot, tok, att, proj, prob, wall, small, dwr):
    blocks, images, span, width = tok.shape
    length = blocks * span
    heads = width // HEAD_DIM
    split = pl.BlockSpec((blocks, 1, span, width), lambda i: (0, i, 0, 0))
    whole = lambda a: pl.BlockSpec(a.shape, lambda i: (0,) * len(a.shape))
    return pl.pallas_call(
        back_kernel,
        grid=(images,),
        in_specs=[split] * 7
        + [
            pl.BlockSpec((1, length, width), lambda i: (i, 0, 0)),
            pl.BlockSpec((1, length, 3 * width), lambda i: (i, 0, 0)),
            pl.BlockSpec((1, heads, length, length), lambda i: (i, 0, 0, 0)),
            whole(wall),
            whole(small),
            whole(dwr),
        ],
        out_specs=[pl.BlockSpec((1, span, width), lambda i: (i, 0, 0))] * blocks + [whole(wall)],
        out_shape=[jax.ShapeDtypeStruct((images, span, width), bf16)] * blocks
        + [jax.ShapeDtypeStruct(wall.shape, bf16)],
        scratch_shapes=[
            pltpu.VMEM((width, 4 * width), f32),
            pltpu.VMEM((LANES, width), f32),
            pltpu.VMEM((length, width), bf16),
            pltpu.VMEM((length, 3 * width), bf16),
        ],
        compiler_params=pltpu.CompilerParams(vmem_limit_bytes=VMEM_BYTES),
        cost_estimate=true_cost(10 * images * length * width * (4 * width + 3 * length)),
        name="back",
    )(*gins, middle, cot, tok, att, proj, prob, wall, small, dwr)


def kept_pairs(route_rows, token_live, order_rows, expert_count, capacity):
    labels = jnp.arange(expert_count, dtype=jnp.int32)
    alive = token_live > 0
    first_hot = ((route_rows[:, 0:1] == labels) & alive[:, None]).astype(bf16)
    second_hot = ((route_rows[:, 1:2] == labels) & alive[:, None]).astype(bf16)
    earlier = (order_rows[None, :] < order_rows[:, None]).astype(bf16)
    ahead = mm(earlier, jnp.concatenate([first_hot, second_hot], 1))
    ahead_first = ahead[:, :expert_count]
    ahead_second = ahead[:, expert_count:] + jnp.sum(first_hot.astype(f32), 0)
    return jnp.where(ahead_first < capacity, first_hot, 0) + jnp.where(
        ahead_second < capacity, second_hot, 0
    )


def local(
    fsdp,
    seq,
    tokens,
    ln1_gain,
    ln1_bias,
    w_qkv,
    w_out,
    ln2_gain,
    ln2_bias,
    w_router,
    w_in,
    w_down,
    padding,
    routes,
    priority,
    cotangent,
):
    images, span, width = tokens.shape
    expert_count, shard_rows = w_in.shape[0], w_in.shape[1]
    rows = images * span
    own = images // seq
    length = seq * span
    capacity = (2 * rows + expert_count - 1) // expert_count
    outer = fsdp // 8
    if outer > 1:
        outer_groups = [[o * 8 + n for o in range(outer)] for n in range(8)]
    spread = functools.partial(flip, fsdp=fsdp)
    seq_index = lax.axis_index("seq")
    place = lax.axis_index("fsdp") if outer == 1 else jnp.int32(0)
    place = place.astype(jnp.int32).reshape(1)

    def picked(array, k):
        return lax.dynamic_index_in_dim(array, seq_index ^ k, 0, keepdims=False)

    tokens = tokens.reshape(seq, own * span, width)
    tok = jnp.stack(exchange([picked(tokens, k) for k in range(seq)]))
    tok = tok.reshape(seq, own, span, width)

    columns = jnp.concatenate(
        [w_router] + [v[:, None] for v in (ln1_gain, ln1_bias, ln2_gain, ln2_bias)], 1
    )
    columns = jnp.pad(columns, ((0, 0), (0, LANES - columns.shape[1])))
    shard = jnp.concatenate([w_qkv, w_out, columns], 1)
    if outer == 1:
        cut = width // 16
        from_x, from_y = spread(shard, bits=2), spread(shard, bits=4)
        from_x, from_y = tie((from_x, from_y), tok)
        near = [(0, 0, shard), (2, 0, from_x), (4, 0, from_y)]
        far = [
            (6, 0, spread(from_x[:cut], bits=4)),
            (6, cut, spread(from_y[cut:], bits=2)),
        ]
        near += [(r + 1, skip, spread(a, bits=1)) for r, skip, a in near]
    else:
        full = lax.all_gather(shard, "fsdp", axis=0, tiled=True)
        from_x = from_y = full
        near, far = [(n, 0, full[n * (width // 8) : (n + 1) * (width // 8)]) for n in range(8)], []

    live = lax.dynamic_slice_in_dim(padding, seq_index * span, span, 1)
    kept = kept_pairs(
        routes.reshape(rows, 2), live.reshape(rows), priority.reshape(rows), expert_count, capacity
    )
    kept = jnp.swapaxes(kept.reshape(seq, own * span, expert_count), 1, 2)
    kept = jnp.pad(
        kept, ((0, 0), (0, MASK_ROWS - expert_count), (0, width - own * span))
    ).astype(bf16)
    cot = cotangent * live[:, :, None].astype(bf16)
    packed = jnp.concatenate([cot.reshape(seq, own * span, width), kept], 1)
    packed = tie(packed, tok, from_x, from_y)
    packed = jnp.stack(exchange([picked(packed, k) for k in range(seq)]))
    late = tie([a for _, _, a in far], packed)
    far += [(r + 1, skip, spread(a, bits=1)) for (r, skip, _), a in zip(far, late)]
    offsets = [(r, skip) for r, skip, _ in near + far]
    pieces = [a for _, _, a in near + far]
    cot_x, cot_y = spread(packed, bits=2), spread(packed, bits=4)
    half = seq // 2
    cot_far = [spread(cot_x[:half], bits=4), spread(cot_y[half:], bits=2)]

    win, wdn = w_in, w_down
    if outer > 1:
        win = lax.all_gather(win, "fsdp", axis=1, tiled=True, axis_index_groups=outer_groups)
        wdn = lax.all_gather(wdn, "fsdp", axis=1, tiled=True, axis_index_groups=outer_groups)
    win, wdn = tie((win, wdn), pieces)
    weights = [win, spread(win, bits=1), wdn, spread(wdn, bits=1)]

    mine = lax.dynamic_slice_in_dim(padding, seq_index * own, own, 0).reshape(own, seq, span)
    mine = jnp.stack(relative([mine[:, b] for b in range(seq)], seq_index))
    vis = jnp.where(mine > 0, 0.0, neg_fill).astype(f32)
    vis = jnp.swapaxes(vis, 0, 1).reshape(own, 1, length)
    middle, two, proj, att, prob, wall, wr, small = front(tok, pieces, offsets, vis, place)
    two = two.reshape(seq, own * span, width)
    two_far = [[spread(two, bits=bits)] for bits in (2, 4, 6)]

    (dw,), dwr, out_0, gin_0 = experts_call(
        [[two]], [[packed]], weights, wr, None, "experts_own", lambda flops: SHORT
    )
    cots = [[cot_x], [cot_y], cot_far]
    left, dwr, outs, gins = experts_call(
        two_far, cots, weights, wr, dwr, "experts_far", true_cost
    )
    arrived = [spread(a, bits=bits) for a, bits in zip(gins, (2, 4, 6))]

    def finished(dw_kept, dw_sent):
        raw = plus(dw_kept, spread(dw_sent, bits=1))
        if outer > 1:
            raw = lax.psum_scatter(
                raw, "fsdp", scatter_dimension=2, tiled=True, axis_index_groups=outer_groups
            )
        return lax.optimization_barrier([raw[n : n + 1] for n in range(raw.shape[0])])

    first = Line(seq, finished(*grads_call(two_far, cots, left, dw, 0, 1))[0]).inwards()
    left, dw = tie((left, dw), first.raw)
    parts = grads_call(two_far, cots, left, dw, 1, expert_count - 1)
    ready = first.across(arrived)
    lines = [Line(seq, raw) for raw in finished(*tie(parts, ready, arrived))]
    lines[0].inwards()
    gins = gin_0 + tie(arrived, ready, [line.raw for line in lines])
    lines = [first] + lines

    shape4 = (seq, own, span, width)
    outs = [spread(a, bits=bits) for a, bits in zip(tie(outs, arrived), (2, 4, 6))]
    *grad_tok, dense = back(
        [a.reshape(shape4) for a in gins],
        middle,
        packed[:, : own * span].reshape(shape4),
        tok,
        att,
        proj,
        prob,
        wall,
        small,
        dwr,
    )
    flying = (outs, lines[0].waiting(), lines[1].waiting())
    dense = tie(dense, flying)
    dense = lax.psum_scatter(dense, "fsdp", scatter_dimension=0, tiled=True)
    lines[2].raw, lines[3].raw = tie((lines[2].raw, lines[3].raw), grad_tok)
    lines[2].inwards()
    ready = lines[1].across(grad_tok, flying)
    lines[3].inwards_with(lines[0], ready)
    ready = lines[2].across(ready)
    ready = lines[1].outwards(ready)
    ready = lines[3].across(ready)
    ready = lines[2].outwards(ready)
    dense_line = Line(seq, tie(dense, ready)).inwards()
    ready = lines[3].outwards(dense_line.raw)

    ready = dense_line.across(ready)
    outs, grad_tok = tie((outs, grad_tok), ready)
    outs = [a.reshape(shape4) for a in out_0 + outs]
    home = []
    for k in range(seq):
        alive = mine[k][:, :, None].astype(f32)
        combined = sum(a[k].astype(f32) for a in outs)
        home.append(jnp.stack([(alive * (middle[k] + combined)).astype(bf16), grad_tok[k]]))
    home = exchange(home)
    ready = dense_line.outwards(ready)
    home = relative(tie(home, ready), seq_index)
    outputs, grad_tokens = (
        jnp.concatenate([a[n] for a in home], 0).reshape(images, span, width) for n in range(2)
    )
    lines[3].hold(dense_line.waiting())
    grads = [line.finish() for line in lines]
    dense = dense_line.finish().astype(f32)
    expert_grads = [jnp.concatenate([g[:, n] for g in grads], 0).astype(f32) for n in range(2)]
    tail = dense[:, 4 * width :]
    return (
        outputs,
        grad_tokens,
        tail[:, 4],
        tail[:, 5],
        dense[:, : 3 * width],
        dense[:, 3 * width : 4 * width],
        tail[:, 6],
        tail[:, 7],
        tail[:, :expert_count],
        expert_grads[0],
        expert_grads[1],
    )


def solution(mesh):
    rows = P("fsdp", "seq", None)
    in_specs = (
        rows,
        P("fsdp"),
        P("fsdp"),
        P("fsdp", None),
        P("fsdp", None),
        P("fsdp"),
        P("fsdp"),
        P("fsdp", None),
        P(None, "fsdp", None),
        P(None, "fsdp", None),
        P("fsdp", None),
        rows,
        P("fsdp", "seq"),
        rows,
    )
    out_specs = (
        rows,
        rows,
        P("fsdp"),
        P("fsdp"),
        P("fsdp", None),
        P("fsdp", None),
        P("fsdp"),
        P("fsdp"),
        P("fsdp", None),
        P(None, "fsdp", None),
        P(None, "fsdp", None),
    )
    return jax.shard_map(
        functools.partial(local, mesh.shape["fsdp"], mesh.shape["seq"]),
        mesh=mesh,
        in_specs=in_specs,
        out_specs=out_specs,
        check_vma=False,
    )
```

```python
import functools
import math

import jax
import jax.numpy as jnp
from jax import lax
from jax.experimental import pallas as pl
from jax.experimental.pallas import tpu as pltpu
from jax.sharding import PartitionSpec as P

HEAD_DIM = 64
LANES = 128
MASK_ROWS = 16
SMALL = 8
norm_eps = 1e-06
neg_fill = -1e30
f32 = jnp.float32
bf16 = jnp.bfloat16
VMEM_BYTES = 60 * 1024 * 1024
SHORT = pl.CostEstimate(flops=1000, bytes_accessed=1000, transcendentals=0)


def true_cost(flops):
    return pl.CostEstimate(flops=2 * flops, bytes_accessed=16 * 1024 * 1024, transcendentals=0)


def mm(left, right, left_dim=1, right_dim=0):
    return lax.dot_general(
        left, right, (((left_dim,), (right_dim,)), ((), ())), preferred_element_type=f32
    )


def unit_norm(rows):
    centred = rows - jnp.mean(rows, -1, keepdims=True)
    inverse = lax.rsqrt(jnp.mean(centred * centred, -1, keepdims=True) + norm_eps)
    return centred * inverse, inverse


def norm_back(scaled, unit, inverse):
    return inverse * (
        scaled
        - jnp.mean(scaled, -1, keepdims=True)
        - unit * jnp.mean(scaled * unit, -1, keepdims=True)
    )


def half_turn(tile):
    return pltpu.roll(tile.astype(f32), HEAD_DIM, axis=1).astype(bf16)


def wall_copies(pieces, offsets, place_ref, wall_ref, sems):
    copies = []
    for n, (piece, (r, skip)) in enumerate(zip(pieces, offsets)):
        rows = piece.shape[0]
        shard = wall_ref.shape[0] // 8
        start = pl.multiple_of((place_ref[0] ^ r) * shard + skip, 16)
        copies.append(pltpu.make_async_copy(piece, wall_ref.at[pl.ds(start, rows)], sems.at[n]))
    return copies


def front_kernel(offsets, *refs):
    pieces = refs[: len(offsets)]
    tok_ref, vis_ref, place_ref = refs[len(offsets) : len(offsets) + 3]
    mid_ref, two_ref, proj_ref, att_ref, prob_ref, full_ref, wr_ref, small_ref = refs[
        len(offsets) + 3 : len(offsets) + 11
    ]
    wall_ref, sems, full_sem = refs[len(offsets) + 11 :]
    blocks, _, span, width = tok_ref.shape
    length = blocks * span
    save = pltpu.make_async_copy(wall_ref, full_ref, full_sem)

    @pl.when(pl.program_id(0) == 0)
    def _():
        copies = wall_copies(pieces, offsets, place_ref, wall_ref, sems)
        for copy in copies:
            copy.start()
        for copy in copies:
            copy.wait()
        save.start()
        columns = wall_ref[:, 4 * width :]
        wr_ref[...] = columns
        small_ref[...] = columns.astype(f32).T[:SMALL]

    rows = tok_ref[...].reshape(length, width).astype(f32)
    unit, _ = unit_norm(rows)
    one = (unit * small_ref[4:5] + small_ref[5:6]).astype(bf16)
    proj_ref[0] = mm(one, wall_ref[:, : 3 * width]).astype(bf16)
    lower = lax.broadcasted_iota(jnp.int32, (length, LANES), 1) < HEAD_DIM
    zero = jnp.zeros((length, LANES), bf16)
    bias = vis_ref[0]

    def soften(index, queries, keys):
        scores = mm(queries, keys, 1, 1) * (HEAD_DIM**-0.5) + bias
        shifted = jnp.exp(scores - jnp.max(scores, -1, keepdims=True))
        weights = (shifted / jnp.sum(shifted, -1, keepdims=True)).astype(bf16)
        prob_ref[0, index] = weights
        return weights

    for pair in range(width // LANES):
        first, second, third = (
            proj_ref[0, :, (3 * pair + n) * LANES : (3 * pair + n + 1) * LANES] for n in range(3)
        )
        weights_a = soften(2 * pair, jnp.where(lower, first, zero), half_turn(first))
        weights_b = soften(2 * pair + 1, jnp.where(lower, zero, second), half_turn(third))
        both = jnp.where(lower, mm(weights_a, second), mm(weights_b, third))
        att_ref[0, :, pair * LANES : (pair + 1) * LANES] = both.astype(bf16)
    middle = rows + mm(att_ref[0], wall_ref[:, 3 * width : 4 * width])
    mid_ref[...] = middle.reshape(mid_ref.shape)
    unit, _ = unit_norm(middle)
    two_ref[...] = (unit * small_ref[6:7] + small_ref[7:8]).astype(bf16).reshape(two_ref.shape)

    @pl.when(pl.program_id(0) == pl.num_programs(0) - 1)
    def _():
        save.wait()


def front(tok, pieces, offsets, vis, place):
    blocks, images, span, width = tok.shape
    length = blocks * span
    heads = width // HEAD_DIM
    split = pl.BlockSpec((blocks, 1, span, width), lambda i: (0, i, 0, 0))
    anywhere = pl.BlockSpec(memory_space=pl.ANY)
    columns = pieces[0].shape[1]
    return pl.pallas_call(
        functools.partial(front_kernel, offsets),
        grid=(images,),
        in_specs=[anywhere] * len(pieces)
        + [
            split,
            pl.BlockSpec((1, 1, length), lambda i: (i, 0, 0)),
            pl.BlockSpec(memory_space=pltpu.SMEM),
        ],
        out_specs=[
            split,
            split,
            pl.BlockSpec((1, length, 3 * width), lambda i: (i, 0, 0)),
            pl.BlockSpec((1, length, width), lambda i: (i, 0, 0)),
            pl.BlockSpec((1, heads, length, length), lambda i: (i, 0, 0, 0)),
            anywhere,
            pl.BlockSpec((width, LANES), lambda i: (0, 0)),
            pl.BlockSpec((SMALL, width), lambda i: (0, 0)),
        ],
        out_shape=[
            jax.ShapeDtypeStruct(tok.shape, f32),
            jax.ShapeDtypeStruct(tok.shape, bf16),
            jax.ShapeDtypeStruct((images, length, 3 * width), bf16),
            jax.ShapeDtypeStruct((images, length, width), bf16),
            jax.ShapeDtypeStruct((images, heads, length, length), bf16),
            jax.ShapeDtypeStruct((width, columns), bf16),
            jax.ShapeDtypeStruct((width, LANES), bf16),
            jax.ShapeDtypeStruct((SMALL, width), f32),
        ],
        scratch_shapes=[
            pltpu.VMEM((width, columns), bf16),
            pltpu.SemaphoreType.DMA((len(pieces),)),
            pltpu.SemaphoreType.DMA(()),
        ],
        compiler_params=pltpu.CompilerParams(vmem_limit_bytes=VMEM_BYTES),
        cost_estimate=SHORT,
        name="front",
    )(*pieces, tok, vis, place)


def gelu_parts(pre):
    bell = jnp.exp2(pre * pre * (-0.5 * math.log2(math.e)))
    frac = 1.0 / (1.0 + (0.3275911 * math.sqrt(0.5)) * jnp.abs(pre))
    a5, a4, a3, a2, a1 = (
        0.5 * c for c in (1.061405429, -1.453152027, 1.421413741, -0.284496736, 0.254829592)
    )
    tail = frac * (a1 + frac * (a2 + frac * (a3 + frac * (a4 + frac * a5)))) * bell
    cumulative = jnp.where(pre >= 0, 1.0 - tail, tail)
    return pre * cumulative, cumulative + (pre * 0.3989422804014327) * bell


def expert_kernel(plan, *refs):
    refs = list(refs)

    def take(number):
        taken, refs[:] = refs[:number], refs[number:]
        return taken

    groups, experts, opening = plan["groups"], plan["experts"], plan["opening"]
    two_parts = [take(n) for n in plan["two"]]
    cot_parts = [take(n) for n in plan["cot"]]
    weights = take(4)
    (wr_ref,) = take(1)
    dwr_carried, own_ref = (None, None) if opening else take(2)
    left = take(1 if opening else 2)
    early = [] if opening else take(2)
    (dwr_ref,) = take(1)
    results = take(2 * groups)
    two_buf, cot_buf, sems, win_buf, wdn_buf, weight_sems, gated_buf, grad_buf = take(8)
    stage, store_sems, left_sems = take(3)
    acc, own_buf, early_buf, own_sem, early_sems = [None] * 5 if opening else take(5)
    _, blocks, span, width = two_buf.shape
    rows = blocks * span
    hidden = win_buf.shape[0] // experts
    shard = hidden // 2
    group = pl.program_id(0)
    slot = group % gated_buf.shape[0]
    lane = lax.broadcasted_iota(jnp.int32, (rows, LANES), 1)

    copies = []
    for k in range(groups):
        some = []
        for parts, buffer in ((two_parts[k], two_buf), (cot_parts[k], cot_buf)):
            at = 0
            for part in parts:
                size = part.shape[0]
                some.append((part, buffer.at[k, pl.ds(at, size)]))
                at += size
        copies.append(
            [pltpu.make_async_copy(s, t, sems.at[k, n]) for n, (s, t) in enumerate(some)]
        )
    fetches = [
        pltpu.make_async_copy(
            ref.at[e],
            (win_buf, wdn_buf)[n // 2].at[pl.ds(e * hidden + (n % 2) * shard, shard)],
            weight_sems.at[e, n],
        )
        for e in range(experts)
        for n, ref in enumerate(weights)
    ]
    stores = [
        [
            pltpu.make_async_copy(stage.at[n], results[n * groups + k], store_sems.at[n])
            for n in range(2)
        ]
        for k in range(groups)
    ]
    if not opening:
        for k in range(groups):
            for n, buffer in enumerate((gated_buf, grad_buf)):
                place = k % buffer.shape[0]
                stores[k].append(
                    pltpu.make_async_copy(
                        buffer.at[place, :, pl.ds(hidden, (experts - 1) * hidden)],
                        left[n].at[pl.ds(k * rows, rows)],
                        left_sems.at[place, n],
                    )
                )

    @pl.when(group == 0)
    def _():
        for copy in copies[0] + fetches:
            copy.start()
        for some in copies[1:]:
            for copy in some:
                copy.start()
        if not opening:
            pltpu.make_async_copy(own_ref.at[0], own_buf, own_sem).start()
        dwr_ref[...] = jnp.zeros_like(dwr_ref) if opening else dwr_carried[...]
        for copy in fetches:
            copy.wait()

    for k, some in enumerate(copies):

        @pl.when(group == k)
        def _(k=k, some=some):
            for copy in some:
                copy.wait()
            if k > 0:
                for store in stores[k - 1][:2]:
                    store.wait()
            if k > 1:
                for store in stores[k - 2][2:]:
                    store.wait()

    two = two_buf[group].reshape(rows, width)
    cot = cot_buf[group, :, :span, :].reshape(rows, width)
    chosen = (
        lax.broadcasted_iota(jnp.int32, (MASK_ROWS, LANES), 0)
        == lax.broadcasted_iota(jnp.int32, (MASK_ROWS, LANES), 1)
    ).astype(bf16)
    logits = jnp.where(lane < experts, mm(two, wr_ref[...]), neg_fill)
    shifted = jnp.exp(logits - jnp.max(logits, -1, keepdims=True))
    probs = shifted / jnp.sum(shifted, -1, keepdims=True)
    kept = jnp.concatenate(
        [
            mm(cot_buf[group, b, span : span + MASK_ROWS, :span], chosen, 0, 0)
            for b in range(blocks)
        ],
        0,
    )
    grad_gate = jnp.zeros((rows, LANES), f32)
    gates = probs * kept
    out_rows = gin_rows = None
    for e in range(experts):
        at = slice(e * hidden, (e + 1) * hidden)
        win, wdn = win_buf[at], wdn_buf[at]
        pre = mm(two, win, 1, 1)
        back_rows = mm(cot, wdn, 1, 1)
        gate = gates[:, e : e + 1]
        hidden_rows, slope = gelu_parts(pre)
        product = jnp.sum(hidden_rows * back_rows, -1, keepdims=True)
        grad_gate = jnp.where(lane == e, product, grad_gate)
        gated = (hidden_rows * gate).astype(bf16)
        grad_pre = (slope * back_rows * gate).astype(bf16)
        if opening:
            gated_buf[e, 1] = mm(gated, cot, 0, 0).astype(bf16)
            gated_buf[e, 0] = mm(grad_pre, two, 0, 0).astype(bf16)
        elif e > 0:
            gated_buf[slot, :, at] = gated
            grad_buf[slot, :, at] = grad_pre
        else:
            for n, fresh in enumerate((mm(grad_pre, two, 0, 0), mm(gated, cot, 0, 0))):
                acc[n] = jnp.where(group == 0, 0.0, acc[n]) + fresh
        out_part, gin_part = mm(gated, wdn), mm(grad_pre, win)
        out_rows = out_part if e == 0 else out_rows + out_part
        gin_rows = gin_part if e == 0 else gin_rows + gin_part
    grad_gate = grad_gate * kept
    grad_logits = probs * (grad_gate - jnp.sum(probs * grad_gate, -1, keepdims=True))
    grad_logits = grad_logits.astype(bf16)
    dwr_ref[...] += mm(grad_logits, two, 0, 0)[:SMALL]
    gin_rows = gin_rows + mm(grad_logits, wr_ref[...], 1, 1)
    stage[0] = out_rows.astype(bf16).reshape(blocks, span, width)
    stage[1] = gin_rows.astype(bf16).reshape(blocks, span, width)
    for k in range(groups):

        @pl.when(group == k)
        def _(k=k):
            for store in stores[k]:
                store.start()

    @pl.when(group == groups - 1)
    def _():
        if opening:
            copy = pltpu.make_async_copy(gated_buf, left[0], left_sems.at[0, 0])
            copy.start()
            copy.wait()
        else:
            pltpu.make_async_copy(own_ref.at[0], own_buf, own_sem).wait()
            early_copies = []
            for n in range(2):
                early_buf[n] = (acc[n] + own_buf[n].astype(f32)).astype(bf16)
                for m, target in enumerate(early):
                    copy = pltpu.make_async_copy(
                        early_buf.at[n, pl.ds(m * shard, shard)],
                        target.at[0, n],
                        early_sems.at[n, m],
                    )
                    copy.start()
                    early_copies.append(copy)
            for copy in early_copies:
                copy.wait()
        for k in (groups - 1,) if groups == 1 else (groups - 2, groups - 1):
            for store in stores[k][0 if k == groups - 1 else 2 :]:
                store.wait()


def experts_call(two, cot, weights, wr, carried, name, cost):
    groups = len(two)
    opening = groups == 1
    experts, shard, width = weights[0].shape
    hidden = 2 * shard
    blocks = sum(a.shape[0] for a in two[0])
    span = two[0][0].shape[1]
    rows = blocks * span
    plan = dict(
        groups=groups,
        experts=experts,
        opening=opening,
        two=[len(parts) for parts in two],
        cot=[len(parts) for parts in cot],
    )
    anywhere = pl.BlockSpec(memory_space=pl.ANY)
    once = lambda a: pl.BlockSpec(
        a.shape, lambda g: (0,) * len(a.shape), pipeline_mode=pl.Buffered(1)
    )
    result = jax.ShapeDtypeStruct((blocks, span, width), bf16)
    little = jax.ShapeDtypeStruct((SMALL, width), f32)
    if opening:
        left = [jax.ShapeDtypeStruct((experts, 2, hidden, width), bf16)]
        buffers = [pltpu.VMEM(left[0].shape, bf16), pltpu.VMEM((16, LANES), bf16)]
    else:
        left = [jax.ShapeDtypeStruct((groups * rows, (experts - 1) * hidden), bf16)] * 2
        left += [jax.ShapeDtypeStruct((1, 2, shard, width), bf16)] * 2
        buffers = [pltpu.VMEM((2, rows, experts * hidden), bf16)] * 2
    pieces = [a for parts in two for a in parts] + [a for parts in cot for a in parts]
    outs = pl.pallas_call(
        functools.partial(expert_kernel, plan),
        grid=(groups,),
        in_specs=[anywhere] * (len(pieces) + 4)
        + [once(wr)]
        + ([] if opening else [once(little), anywhere]),
        out_specs=[anywhere] * len(left) + [once(little)] + [anywhere] * (2 * groups),
        out_shape=left + [little] + [result] * (2 * groups),
        scratch_shapes=[
            pltpu.VMEM((groups, blocks, span, width), bf16),
            pltpu.VMEM((groups, blocks, span + MASK_ROWS, width), bf16),
            pltpu.SemaphoreType.DMA((groups, 4)),
            pltpu.VMEM((experts * hidden, width), bf16),
            pltpu.VMEM((experts * hidden, width), bf16),
            pltpu.SemaphoreType.DMA((experts, 4)),
            *buffers,
            pltpu.VMEM((2, blocks, span, width), bf16),
            pltpu.SemaphoreType.DMA((2,)),
            pltpu.SemaphoreType.DMA((2, 2)),
        ]
        + (
            []
            if opening
            else [
                pltpu.VMEM((2, hidden, width), f32),
                pltpu.VMEM((2, hidden, width), bf16),
                pltpu.VMEM((2, hidden, width), bf16),
                pltpu.SemaphoreType.DMA(()),
                pltpu.SemaphoreType.DMA((2, 2)),
            ]
        ),
        compiler_params=pltpu.CompilerParams(vmem_limit_bytes=VMEM_BYTES),
        cost_estimate=cost(10 * groups * rows * width * hidden * experts),
        name=name,
    )(*pieces, *weights, wr, *(carried or []))
    left, (dwr, *outs) = list(outs[: len(left)]), outs[len(left) :]
    return left, dwr, outs[:groups], outs[groups:]


def grads_kernel(plan, *refs):
    refs = list(refs)

    def take(number):
        taken, refs[:] = refs[:number], refs[number:]
        return taken

    groups = len(plan["two"])
    two_parts = [take(n) for n in plan["two"]]
    cot_parts = [take(n) for n in plan["cot"]]
    gated_ref, grad_ref, own_ref, kept_ref, sent_ref = take(5)
    two_buf, cot_buf, cot_rows, sems = refs
    _, blocks, span, width = two_buf.shape
    rows = blocks * span
    copies = []
    for k in range(groups):
        at = 0
        for n, part in enumerate(two_parts[k]):
            size = part.shape[0]
            copies.append(
                pltpu.make_async_copy(part, two_buf.at[k, pl.ds(at, size)], sems.at[k, n])
            )
            at += size
        at = 0
        for n, part in enumerate(cot_parts[k]):
            size = part.shape[0]
            copies.append(
                pltpu.make_async_copy(
                    part, cot_buf.at[k, pl.ds(at, size)], sems.at[k, 2 + n]
                )
            )
            at += size

    @pl.when(pl.program_id(0) == 0)
    def _():
        for copy in copies:
            copy.start()
        for copy in copies:
            copy.wait()
        for k in range(groups):
            cot_rows[k * rows : (k + 1) * rows] = cot_buf[k, :, :span, :].reshape(rows, width)

    half = own_ref.shape[2] // 2
    two = two_buf[...].reshape(groups * rows, width)
    for n, (left_ref, right) in enumerate(((grad_ref, two), (gated_ref, cot_rows[...]))):
        total = (own_ref[0, n].astype(f32) + mm(left_ref[...], right, 0, 0)).astype(bf16)
        kept_ref[0, n] = total[:half]
        sent_ref[0, n] = total[half:]


def grads_call(two, cot, left, own, first, many):
    groups = len(two)
    blocks = sum(a.shape[0] for a in two[0])
    _, span, width = two[0][0].shape
    rows = blocks * span
    hidden = own.shape[2]
    anywhere = pl.BlockSpec(memory_space=pl.ANY)
    pieces = [a for parts in two for a in parts] + [a for parts in cot for a in parts]
    columns = pl.BlockSpec((groups * rows, hidden), lambda e: (0, e))
    part = jax.ShapeDtypeStruct((many, 2, hidden // 2, width), bf16)
    part_spec = pl.BlockSpec((1, 2, hidden // 2, width), lambda e: (e, 0, 0, 0))
    plan = dict(two=[len(parts) for parts in two], cot=[len(parts) for parts in cot])
    return pl.pallas_call(
        functools.partial(grads_kernel, plan),
        grid=(many,),
        in_specs=[anywhere] * len(pieces)
        + [columns, columns, pl.BlockSpec((1, 2, hidden, width), lambda e: (e + first, 0, 0, 0))],
        out_specs=[part_spec, part_spec],
        out_shape=[part, part],
        scratch_shapes=[
            pltpu.VMEM((groups, blocks, span, width), bf16),
            pltpu.VMEM((groups, blocks, span + MASK_ROWS, width), bf16),
            pltpu.VMEM((groups * rows, width), bf16),
            pltpu.SemaphoreType.DMA((groups, 4)),
        ],
        compiler_params=pltpu.CompilerParams(vmem_limit_bytes=VMEM_BYTES),
        cost_estimate=true_cost(8 * groups * rows * width * hidden * many),
        name="expert_grads",
    )(*pieces, *left, own)


def flip(array, fsdp, bits):
    return lax.ppermute(array, "fsdp", [(n, n ^ bits) for n in range(fsdp)])


def tie(value, *others):
    return lax.optimization_barrier((value, others))[0]


def exchange(pieces):
    count = len(pieces)
    return [pieces[0]] + [
        lax.ppermute(pieces[k], "seq", [(n, n ^ k) for n in range(count)]) for k in range(1, count)
    ]


def relative(parts, index):
    count, bit = len(parts), 1
    while bit < count:
        swap = (index & bit) > 0
        parts = [jnp.where(swap, parts[k ^ bit], parts[k]) for k in range(count)]
        bit *= 2
    return parts


def plus(*arrays):
    return sum(a.astype(f32) for a in arrays).astype(bf16)


class Line:
    def __init__(self, seq, raw):
        self.seq, self.raw = seq, raw
        if seq != 4:
            self.total = lax.psum(raw, "seq")

    def inwards(self):
        if self.seq == 4:
            self.moving = lax.ppermute(self.raw, "seq", [(0, 1), (3, 2)])
        return self

    def inwards_with(self, other, *others):
        if self.seq != 4:
            return self.raw
        other.total = plus(other.pair, tie(other.moving, others))
        index = lax.axis_index("seq")
        both = jnp.where((index == 0) | (index == 3), self.raw, other.total)
        self.moving = lax.ppermute(both, "seq", [(0, 1), (1, 0), (2, 3), (3, 2)])
        other.moving = self.moving
        return both

    def hold(self, others):
        if self.seq == 4:
            self.moving = tie(self.moving, others)

    def across(self, *others):
        if self.seq == 4:
            self.pair = plus(self.raw, tie(self.moving, others))
            self.moving = lax.ppermute(self.pair, "seq", [(1, 2), (2, 1)])
            return self.pair
        return self.raw

    def outwards(self, *others):
        if self.seq == 4:
            self.total = plus(self.pair, tie(self.moving, others))
            self.moving = lax.ppermute(self.total, "seq", [(1, 0), (2, 3)])
        return self.total

    def finish(self):
        if self.seq != 4:
            return self.total
        index = lax.axis_index("seq")
        return jnp.where((index == 0) | (index == 3), self.moving, self.total)

    def waiting(self):
        return [self.moving] if self.seq == 4 else []


def back_kernel(
    gin_0, gin_2, gin_4, gin_6, mid_ref, cot_ref, tok_ref, att_ref, proj_ref, prob_ref, wall_ref,
    small_ref, dwr_ref, *rest,
):
    blocks, _, span, width = tok_ref.shape
    length = blocks * span
    gtok_refs, (dwall_ref, acc, acc_small, gatt, gproj) = rest[:blocks], rest[blocks:]
    step = pl.program_id(0)

    @pl.when(step == 0)
    def _():
        acc[...] = jnp.zeros_like(acc)
        acc_small[...] = jnp.zeros_like(acc_small)
        acc_small[:SMALL] = dwr_ref[...]

    gin = sum(ref[...].reshape(length, width).astype(f32) for ref in (gin_0, gin_2, gin_4, gin_6))
    unit_two, inverse_two = unit_norm(mid_ref[...].reshape(length, width))
    acc_small[6:7] += jnp.sum(gin * unit_two, 0, keepdims=True)
    acc_small[7:8] += jnp.sum(gin, 0, keepdims=True)
    grad_middle = cot_ref[...].reshape(length, width).astype(f32) + norm_back(
        gin * small_ref[6:7], unit_two, inverse_two
    )
    branch = grad_middle.astype(bf16)
    acc[:, 3 * width : 4 * width] += mm(att_ref[0], branch, 0, 0)
    gatt[...] = mm(branch, wall_ref[:, 3 * width : 4 * width], 1, 1).astype(bf16)
    lower = lax.broadcasted_iota(jnp.int32, (length, LANES), 1) < HEAD_DIM
    zero = jnp.zeros((length, LANES), bf16)
    scale = HEAD_DIM**-0.5

    def score_grad(weights, grad_weights):
        weights = weights.astype(f32)
        product = weights * grad_weights
        return (product - weights * jnp.sum(product, -1, keepdims=True)).astype(bf16)

    for pair in range(width // LANES):
        places = [slice((3 * pair + n) * LANES, (3 * pair + n + 1) * LANES) for n in range(3)]
        first, second, third = (proj_ref[0, :, place] for place in places)
        first_r, second_r, third_r = half_turn(first), half_turn(second), half_turn(third)
        grad = gatt[:, pair * LANES : (pair + 1) * LANES]
        weights_a, weights_b = prob_ref[0, 2 * pair], prob_ref[0, 2 * pair + 1]
        ds_a = score_grad(weights_a, mm(jnp.where(lower, grad, zero), second, 1, 1))
        ds_b = score_grad(weights_b, mm(jnp.where(lower, zero, grad), third, 1, 1))
        gproj[:, places[0]] = (
            jnp.where(lower, mm(ds_a, first_r), mm(ds_a, first_r, 0, 0)) * scale
        ).astype(bf16)
        gproj[:, places[1]] = jnp.where(
            lower, mm(weights_a, grad, 0, 0), mm(ds_b, third_r) * scale
        ).astype(bf16)
        gproj[:, places[2]] = jnp.where(
            lower, mm(ds_b, second_r, 0, 0) * scale, mm(weights_b, grad, 0, 0)
        ).astype(bf16)
    unit_one, inverse_one = unit_norm(tok_ref[...].reshape(length, width).astype(f32))
    one = (unit_one * small_ref[4:5] + small_ref[5:6]).astype(bf16)
    grad_one = mm(gproj[...], wall_ref[:, : 3 * width], 1, 1)
    acc_small[4:5] += jnp.sum(grad_one * unit_one, 0, keepdims=True)
    acc_small[5:6] += jnp.sum(grad_one, 0, keepdims=True)
    grad_tok = grad_middle + norm_back(grad_one * small_ref[4:5], unit_one, inverse_one)
    for k, ref in enumerate(gtok_refs):
        ref[0] = grad_tok[k * span : (k + 1) * span].astype(bf16)
    acc[:, : 3 * width] += mm(one, gproj[...], 0, 0)

    @pl.when(step == pl.num_programs(0) - 1)
    def _():
        dwall_ref[:, : 4 * width] = acc[...].astype(bf16)
        dwall_ref[:, 4 * width :] = acc_small[...].T.astype(bf16)


def back(gins, middle, cot, tok, att, proj, prob, wall, small, dwr):
    blocks, images, span, width = tok.shape
    length = blocks * span
    heads = width // HEAD_DIM
    split = pl.BlockSpec((blocks, 1, span, width), lambda i: (0, i, 0, 0))
    whole = lambda a: pl.BlockSpec(a.shape, lambda i: (0,) * len(a.shape))
    return pl.pallas_call(
        back_kernel,
        grid=(images,),
        in_specs=[split] * 7
        + [
            pl.BlockSpec((1, length, width), lambda i: (i, 0, 0)),
            pl.BlockSpec((1, length, 3 * width), lambda i: (i, 0, 0)),
            pl.BlockSpec((1, heads, length, length), lambda i: (i, 0, 0, 0)),
            whole(wall),
            whole(small),
            whole(dwr),
        ],
        out_specs=[pl.BlockSpec((1, span, width), lambda i: (i, 0, 0))] * blocks + [whole(wall)],
        out_shape=[jax.ShapeDtypeStruct((images, span, width), bf16)] * blocks
        + [jax.ShapeDtypeStruct(wall.shape, bf16)],
        scratch_shapes=[
            pltpu.VMEM((width, 4 * width), f32),
            pltpu.VMEM((LANES, width), f32),
            pltpu.VMEM((length, width), bf16),
            pltpu.VMEM((length, 3 * width), bf16),
        ],
        compiler_params=pltpu.CompilerParams(vmem_limit_bytes=VMEM_BYTES),
        cost_estimate=true_cost(10 * images * length * width * (4 * width + 3 * length)),
        name="back",
    )(*gins, middle, cot, tok, att, proj, prob, wall, small, dwr)


def kept_pairs(route_rows, token_live, order_rows, expert_count, capacity):
    labels = jnp.arange(expert_count, dtype=jnp.int32)
    alive = token_live > 0
    first_hot = ((route_rows[:, 0:1] == labels) & alive[:, None]).astype(bf16)
    second_hot = ((route_rows[:, 1:2] == labels) & alive[:, None]).astype(bf16)
    earlier = (order_rows[None, :] < order_rows[:, None]).astype(bf16)
    ahead = mm(earlier, jnp.concatenate([first_hot, second_hot], 1))
    ahead_first = ahead[:, :expert_count]
    ahead_second = ahead[:, expert_count:] + jnp.sum(first_hot.astype(f32), 0)
    return jnp.where(ahead_first < capacity, first_hot, 0) + jnp.where(
        ahead_second < capacity, second_hot, 0
    )


def local(
    fsdp,
    seq,
    tokens,
    ln1_gain,
    ln1_bias,
    w_qkv,
    w_out,
    ln2_gain,
    ln2_bias,
    w_router,
    w_in,
    w_down,
    padding,
    routes,
    priority,
    cotangent,
):
    images, span, width = tokens.shape
    expert_count, shard_rows = w_in.shape[0], w_in.shape[1]
    rows = images * span
    own = images // seq
    length = seq * span
    capacity = (2 * rows + expert_count - 1) // expert_count
    outer = fsdp // 8
    if outer > 1:
        outer_groups = [[o * 8 + n for o in range(outer)] for n in range(8)]
    spread = functools.partial(flip, fsdp=fsdp)
    seq_index = lax.axis_index("seq")
    place = lax.axis_index("fsdp") if outer == 1 else jnp.int32(0)
    place = place.astype(jnp.int32).reshape(1)

    def picked(array, k):
        return lax.dynamic_index_in_dim(array, seq_index ^ k, 0, keepdims=False)

    tokens = tokens.reshape(seq, own * span, width)
    tok = jnp.stack(exchange([picked(tokens, k) for k in range(seq)]))
    tok = tok.reshape(seq, own, span, width)

    columns = jnp.concatenate(
        [w_router] + [v[:, None] for v in (ln1_gain, ln1_bias, ln2_gain, ln2_bias)], 1
    )
    columns = jnp.pad(columns, ((0, 0), (0, LANES - columns.shape[1])))
    shard = jnp.concatenate([w_qkv, w_out, columns], 1)
    if outer == 1:
        cut = width // 16
        from_x, from_y = spread(shard, bits=2), spread(shard, bits=4)
        from_x, from_y = tie((from_x, from_y), tok)
        near = [(0, 0, shard), (2, 0, from_x), (4, 0, from_y)]
        far = [
            (6, 0, spread(from_x[:cut], bits=4)),
            (6, cut, spread(from_y[cut:], bits=2)),
        ]
        near += [(r + 1, skip, spread(a, bits=1)) for r, skip, a in near]
    else:
        full = lax.all_gather(shard, "fsdp", axis=0, tiled=True)
        from_x = from_y = full
        near, far = [(n, 0, full[n * (width // 8) : (n + 1) * (width // 8)]) for n in range(8)], []

    live = lax.dynamic_slice_in_dim(padding, seq_index * span, span, 1)
    kept = kept_pairs(
        routes.reshape(rows, 2), live.reshape(rows), priority.reshape(rows), expert_count, capacity
    )
    kept = jnp.swapaxes(kept.reshape(seq, own * span, expert_count), 1, 2)
    kept = jnp.pad(
        kept, ((0, 0), (0, MASK_ROWS - expert_count), (0, width - own * span))
    ).astype(bf16)
    cot = cotangent * live[:, :, None].astype(bf16)
    packed = jnp.concatenate([cot.reshape(seq, own * span, width), kept], 1)
    packed = tie(packed, tok, from_x, from_y)
    packed = jnp.stack(exchange([picked(packed, k) for k in range(seq)]))
    late = tie([a for _, _, a in far], packed)
    far += [(r + 1, skip, spread(a, bits=1)) for (r, skip, _), a in zip(far, late)]
    offsets = [(r, skip) for r, skip, _ in near + far]
    pieces = [a for _, _, a in near + far]
    cot_x, cot_y = spread(packed, bits=2), spread(packed, bits=4)
    half = seq // 2
    cot_far = [spread(cot_x[:half], bits=4), spread(cot_y[half:], bits=2)]

    win, wdn = w_in, w_down
    if outer > 1:
        win = lax.all_gather(win, "fsdp", axis=1, tiled=True, axis_index_groups=outer_groups)
        wdn = lax.all_gather(wdn, "fsdp", axis=1, tiled=True, axis_index_groups=outer_groups)
    win, wdn = tie((win, wdn), pieces)
    weights = [win, spread(win, bits=1), wdn, spread(wdn, bits=1)]

    mine = lax.dynamic_slice_in_dim(padding, seq_index * own, own, 0).reshape(own, seq, span)
    mine = jnp.stack(relative([mine[:, b] for b in range(seq)], seq_index))
    vis = jnp.where(mine > 0, 0.0, neg_fill).astype(f32)
    vis = jnp.swapaxes(vis, 0, 1).reshape(own, 1, length)
    middle, two, proj, att, prob, wall, wr, small = front(tok, pieces, offsets, vis, place)
    two = two.reshape(seq, own * span, width)
    two_far = [[spread(two, bits=bits)] for bits in (2, 4, 6)]

    (dw,), dwr, out_0, gin_0 = experts_call(
        [[two]], [[packed]], weights, wr, None, "experts_own", lambda flops: SHORT
    )
    cots = [[cot_x], [cot_y], cot_far]
    (*left, dw_kept, dw_sent), dwr, outs, gins = experts_call(
        two_far, cots, weights, wr, [dwr, dw], "experts_far", true_cost
    )
    arrived = [spread(a, bits=bits) for a, bits in zip(gins, (2, 4, 6))]

    def finished(dw_kept, dw_sent):
        raw = plus(dw_kept, spread(dw_sent, bits=1))
        if outer > 1:
            raw = lax.psum_scatter(
                raw, "fsdp", scatter_dimension=2, tiled=True, axis_index_groups=outer_groups
            )
        return lax.optimization_barrier([raw[n : n + 1] for n in range(raw.shape[0])])

    first = Line(seq, finished(dw_kept, dw_sent)[0]).inwards()
    left, dw = tie((left, dw), first.raw)
    parts = grads_call(two_far, cots, left, dw, 1, expert_count - 1)
    ready = first.across(arrived)
    lines = [Line(seq, raw) for raw in finished(*tie(parts, ready, arrived))]
    lines[0].inwards()
    gins = gin_0 + tie(arrived, ready, [line.raw for line in lines])
    lines = [first] + lines

    shape4 = (seq, own, span, width)
    outs = [spread(a, bits=bits) for a, bits in zip(tie(outs, arrived), (2, 4, 6))]
    *grad_tok, dense = back(
        [a.reshape(shape4) for a in gins],
        middle,
        packed[:, : own * span].reshape(shape4),
        tok,
        att,
        proj,
        prob,
        wall,
        small,
        dwr,
    )
    flying = (outs, lines[0].waiting(), lines[1].waiting())
    dense = tie(dense, flying)
    dense = lax.psum_scatter(dense, "fsdp", scatter_dimension=0, tiled=True)
    lines[2].raw, lines[3].raw = tie((lines[2].raw, lines[3].raw), grad_tok)
    lines[2].inwards()
    ready = lines[1].across(grad_tok, flying)
    ready = lines[3].inwards_with(lines[0], ready)
    ready = lines[2].across(ready)
    ready = lines[1].outwards(ready)
    ready = lines[3].across(ready)
    ready = lines[2].outwards(ready, lines[1].waiting())
    dense_line = Line(seq, tie(dense, ready)).inwards()
    ready = lines[3].outwards(dense_line.raw)

    ready = dense_line.across(ready)
    outs, grad_tok = tie((outs, grad_tok), ready)
    outs = [a.reshape(shape4) for a in out_0 + outs]
    home = []
    for k in range(seq):
        alive = mine[k][:, :, None].astype(f32)
        combined = sum(a[k].astype(f32) for a in outs)
        home.append(jnp.stack([(alive * (middle[k] + combined)).astype(bf16), grad_tok[k]]))
    home = exchange(home)
    ready = dense_line.outwards(ready)
    home = relative(tie(home, ready), seq_index)
    outputs, grad_tokens = (
        jnp.concatenate([a[n] for a in home], 0).reshape(images, span, width) for n in range(2)
    )
    lines[3].hold(dense_line.waiting())
    grads = [line.finish() for line in lines]
    dense = dense_line.finish().astype(f32)
    expert_grads = [jnp.concatenate([g[:, n] for g in grads], 0).astype(f32) for n in range(2)]
    tail = dense[:, 4 * width :]
    return (
        outputs,
        grad_tokens,
        tail[:, 4],
        tail[:, 5],
        dense[:, : 3 * width],
        dense[:, 3 * width : 4 * width],
        tail[:, 6],
        tail[:, 7],
        tail[:, :expert_count],
        expert_grads[0],
        expert_grads[1],
    )


def solution(mesh):
    rows = P("fsdp", "seq", None)
    in_specs = (
        rows,
        P("fsdp"),
        P("fsdp"),
        P("fsdp", None),
        P("fsdp", None),
        P("fsdp"),
        P("fsdp"),
        P("fsdp", None),
        P(None, "fsdp", None),
        P(None, "fsdp", None),
        P("fsdp", None),
        rows,
        P("fsdp", "seq"),
        rows,
    )
    out_specs = (
        rows,
        rows,
        P("fsdp"),
        P("fsdp"),
        P("fsdp", None),
        P("fsdp", None),
        P("fsdp"),
        P("fsdp"),
        P("fsdp", None),
        P(None, "fsdp", None),
        P(None, "fsdp", None),
    )
    return jax.shard_map(
        functools.partial(local, mesh.shape["fsdp"], mesh.shape["seq"]),
        mesh=mesh,
        in_specs=in_specs,
        out_specs=out_specs,
        check_vma=False,
    )
```

```python
import functools
import math

import jax
import jax.numpy as jnp
from jax import lax
from jax.experimental import pallas as pl
from jax.experimental.pallas import tpu as pltpu
from jax.sharding import PartitionSpec as P

HEAD_DIM = 64
LANES = 128
MASK_ROWS = 16
SMALL = 8
norm_eps = 1e-06
neg_fill = -1e30
f32 = jnp.float32
bf16 = jnp.bfloat16
VMEM_BYTES = 60 * 1024 * 1024
SHORT = pl.CostEstimate(flops=1000, bytes_accessed=1000, transcendentals=0)


def true_cost(flops):
    return pl.CostEstimate(flops=2 * flops, bytes_accessed=16 * 1024 * 1024, transcendentals=0)


def mm(left, right, left_dim=1, right_dim=0):
    return lax.dot_general(
        left, right, (((left_dim,), (right_dim,)), ((), ())), preferred_element_type=f32
    )


def unit_norm(rows):
    centred = rows - jnp.mean(rows, -1, keepdims=True)
    inverse = lax.rsqrt(jnp.mean(centred * centred, -1, keepdims=True) + norm_eps)
    return centred * inverse, inverse


def norm_back(scaled, unit, inverse):
    return inverse * (
        scaled
        - jnp.mean(scaled, -1, keepdims=True)
        - unit * jnp.mean(scaled * unit, -1, keepdims=True)
    )


def half_turn(tile):
    return pltpu.roll(tile.astype(f32), HEAD_DIM, axis=1).astype(bf16)


def wall_copies(pieces, offsets, place_ref, wall_ref, sems):
    copies = []
    for n, (piece, (r, skip)) in enumerate(zip(pieces, offsets)):
        rows = piece.shape[0]
        shard = wall_ref.shape[0] // 8
        start = pl.multiple_of((place_ref[0] ^ r) * shard + skip, 16)
        copies.append(pltpu.make_async_copy(piece, wall_ref.at[pl.ds(start, rows)], sems.at[n]))
    return copies


def front_kernel(offsets, *refs):
    pieces = refs[: len(offsets)]
    tok_ref, vis_ref, place_ref = refs[len(offsets) : len(offsets) + 3]
    mid_ref, two_ref, proj_ref, att_ref, prob_ref, full_ref, wr_ref, small_ref = refs[
        len(offsets) + 3 : len(offsets) + 11
    ]
    wall_ref, sems, full_sem = refs[len(offsets) + 11 :]
    blocks, _, span, width = tok_ref.shape
    length = blocks * span
    save = pltpu.make_async_copy(wall_ref, full_ref, full_sem)

    @pl.when(pl.program_id(0) == 0)
    def _():
        copies = wall_copies(pieces, offsets, place_ref, wall_ref, sems)
        for copy in copies:
            copy.start()
        for copy in copies:
            copy.wait()
        save.start()
        columns = wall_ref[:, 4 * width :]
        wr_ref[...] = columns
        small_ref[...] = columns.astype(f32).T[:SMALL]

    rows = tok_ref[...].reshape(length, width).astype(f32)
    unit, _ = unit_norm(rows)
    one = (unit * small_ref[4:5] + small_ref[5:6]).astype(bf16)
    proj_ref[0] = mm(one, wall_ref[:, : 3 * width]).astype(bf16)
    lower = lax.broadcasted_iota(jnp.int32, (length, LANES), 1) < HEAD_DIM
    zero = jnp.zeros((length, LANES), bf16)
    bias = vis_ref[0]

    def soften(index, queries, keys):
        scores = mm(queries, keys, 1, 1) * (HEAD_DIM**-0.5) + bias
        shifted = jnp.exp(scores - jnp.max(scores, -1, keepdims=True))
        weights = (shifted / jnp.sum(shifted, -1, keepdims=True)).astype(bf16)
        prob_ref[0, index] = weights
        return weights

    for pair in range(width // LANES):
        first, second, third = (
            proj_ref[0, :, (3 * pair + n) * LANES : (3 * pair + n + 1) * LANES] for n in range(3)
        )
        weights_a = soften(2 * pair, jnp.where(lower, first, zero), half_turn(first))
        weights_b = soften(2 * pair + 1, jnp.where(lower, zero, second), half_turn(third))
        both = jnp.where(lower, mm(weights_a, second), mm(weights_b, third))
        att_ref[0, :, pair * LANES : (pair + 1) * LANES] = both.astype(bf16)
    middle = rows + mm(att_ref[0], wall_ref[:, 3 * width : 4 * width])
    mid_ref[...] = middle.reshape(mid_ref.shape)
    unit, _ = unit_norm(middle)
    two_ref[...] = (unit * small_ref[6:7] + small_ref[7:8]).astype(bf16).reshape(two_ref.shape)

    @pl.when(pl.program_id(0) == pl.num_programs(0) - 1)
    def _():
        save.wait()


def front(tok, pieces, offsets, vis, place):
    blocks, images, span, width = tok.shape
    length = blocks * span
    heads = width // HEAD_DIM
    split = pl.BlockSpec((blocks, 1, span, width), lambda i: (0, i, 0, 0))
    anywhere = pl.BlockSpec(memory_space=pl.ANY)
    columns = pieces[0].shape[1]
    return pl.pallas_call(
        functools.partial(front_kernel, offsets),
        grid=(images,),
        in_specs=[anywhere] * len(pieces)
        + [
            split,
            pl.BlockSpec((1, 1, length), lambda i: (i, 0, 0)),
            pl.BlockSpec(memory_space=pltpu.SMEM),
        ],
        out_specs=[
            split,
            split,
            pl.BlockSpec((1, length, 3 * width), lambda i: (i, 0, 0)),
            pl.BlockSpec((1, length, width), lambda i: (i, 0, 0)),
            pl.BlockSpec((1, heads, length, length), lambda i: (i, 0, 0, 0)),
            anywhere,
            pl.BlockSpec((width, LANES), lambda i: (0, 0)),
            pl.BlockSpec((SMALL, width), lambda i: (0, 0)),
        ],
        out_shape=[
            jax.ShapeDtypeStruct(tok.shape, f32),
            jax.ShapeDtypeStruct(tok.shape, bf16),
            jax.ShapeDtypeStruct((images, length, 3 * width), bf16),
            jax.ShapeDtypeStruct((images, length, width), bf16),
            jax.ShapeDtypeStruct((images, heads, length, length), bf16),
            jax.ShapeDtypeStruct((width, columns), bf16),
            jax.ShapeDtypeStruct((width, LANES), bf16),
            jax.ShapeDtypeStruct((SMALL, width), f32),
        ],
        scratch_shapes=[
            pltpu.VMEM((width, columns), bf16),
            pltpu.SemaphoreType.DMA((len(pieces),)),
            pltpu.SemaphoreType.DMA(()),
        ],
        compiler_params=pltpu.CompilerParams(vmem_limit_bytes=VMEM_BYTES),
        cost_estimate=SHORT,
        name="front",
    )(*pieces, tok, vis, place)


def gelu_parts(pre):
    bell = jnp.exp2(pre * pre * (-0.5 * math.log2(math.e)))
    frac = 1.0 / (1.0 + (0.3275911 * math.sqrt(0.5)) * jnp.abs(pre))
    a5, a4, a3, a2, a1 = (
        0.5 * c for c in (1.061405429, -1.453152027, 1.421413741, -0.284496736, 0.254829592)
    )
    tail = frac * (a1 + frac * (a2 + frac * (a3 + frac * (a4 + frac * a5)))) * bell
    cumulative = jnp.where(pre >= 0, 1.0 - tail, tail)
    return pre * cumulative, cumulative + (pre * 0.3989422804014327) * bell


def expert_kernel(plan, *refs):
    refs = list(refs)

    def take(number):
        taken, refs[:] = refs[:number], refs[number:]
        return taken

    groups, experts, opening = plan["groups"], plan["experts"], plan["opening"]
    two_parts = [take(n) for n in plan["two"]]
    cot_parts = [take(n) for n in plan["cot"]]
    weights = take(4)
    (wr_ref,) = take(1)
    dwr_carried, own_ref = (None, None) if opening else take(2)
    left = take(1 if opening else 2)
    early = [] if opening else take(2)
    (dwr_ref,) = take(1)
    results = take(2 * groups)
    two_buf, cot_buf, sems, win_buf, wdn_buf, weight_sems, gated_buf, grad_buf = take(8)
    stage, store_sems, left_sems = take(3)
    acc, own_buf, early_buf, own_sem, early_sems = [None] * 5 if opening else take(5)
    _, blocks, span, width = two_buf.shape
    rows = blocks * span
    hidden = win_buf.shape[0] // experts
    shard = hidden // 2
    group = pl.program_id(0)
    slot = group % gated_buf.shape[0]
    lane = lax.broadcasted_iota(jnp.int32, (rows, LANES), 1)

    copies = []
    for k in range(groups):
        some = []
        for parts, buffer in ((two_parts[k], two_buf), (cot_parts[k], cot_buf)):
            at = 0
            for part in parts:
                size = part.shape[0]
                some.append((part, buffer.at[k, pl.ds(at, size)]))
                at += size
        copies.append(
            [pltpu.make_async_copy(s, t, sems.at[k, n]) for n, (s, t) in enumerate(some)]
        )
    fetches = [
        pltpu.make_async_copy(
            ref.at[e],
            (win_buf, wdn_buf)[n // 2].at[pl.ds(e * hidden + (n % 2) * shard, shard)],
            weight_sems.at[e, n],
        )
        for e in range(experts)
        for n, ref in enumerate(weights)
    ]
    stores = [
        [
            pltpu.make_async_copy(stage.at[n], results[n * groups + k], store_sems.at[n])
            for n in range(2)
        ]
        for k in range(groups)
    ]
    if not opening:
        for k in range(groups):
            for n, buffer in enumerate((gated_buf, grad_buf)):
                place = k % buffer.shape[0]
                stores[k].append(
                    pltpu.make_async_copy(
                        buffer.at[place, :, pl.ds(hidden, (experts - 1) * hidden)],
                        left[n].at[pl.ds(k * rows, rows)],
                        left_sems.at[place, n],
                    )
                )

    @pl.when(group == 0)
    def _():
        for copy in copies[0] + fetches:
            copy.start()
        for some in copies[1:]:
            for copy in some:
                copy.start()
        if not opening:
            pltpu.make_async_copy(own_ref.at[0], own_buf, own_sem).start()
        dwr_ref[...] = jnp.zeros_like(dwr_ref) if opening else dwr_carried[...]
        for copy in fetches:
            copy.wait()

    for k, some in enumerate(copies):

        @pl.when(group == k)
        def _(k=k, some=some):
            for copy in some:
                copy.wait()
            if k > 0:
                for store in stores[k - 1][:2]:
                    store.wait()
            if k > 1:
                for store in stores[k - 2][2:]:
                    store.wait()

    two = two_buf[group].reshape(rows, width)
    cot = cot_buf[group, :, :span, :].reshape(rows, width)
    chosen = (
        lax.broadcasted_iota(jnp.int32, (MASK_ROWS, LANES), 0)
        == lax.broadcasted_iota(jnp.int32, (MASK_ROWS, LANES), 1)
    ).astype(bf16)
    logits = jnp.where(lane < experts, mm(two, wr_ref[...]), neg_fill)
    shifted = jnp.exp(logits - jnp.max(logits, -1, keepdims=True))
    probs = shifted / jnp.sum(shifted, -1, keepdims=True)
    kept = jnp.concatenate(
        [
            mm(cot_buf[group, b, span : span + MASK_ROWS, :span], chosen, 0, 0)
            for b in range(blocks)
        ],
        0,
    )
    grad_gate = jnp.zeros((rows, LANES), f32)
    gates = probs * kept
    out_rows = gin_rows = None
    for e in range(experts):
        at = slice(e * hidden, (e + 1) * hidden)
        win, wdn = win_buf[at], wdn_buf[at]
        pre = mm(two, win, 1, 1)
        back_rows = mm(cot, wdn, 1, 1)
        gate = gates[:, e : e + 1]
        hidden_rows, slope = gelu_parts(pre)
        product = jnp.sum(hidden_rows * back_rows, -1, keepdims=True)
        grad_gate = jnp.where(lane == e, product, grad_gate)
        gated = (hidden_rows * gate).astype(bf16)
        grad_pre = (slope * back_rows * gate).astype(bf16)
        if opening:
            gated_buf[e, 1] = mm(gated, cot, 0, 0).astype(bf16)
            gated_buf[e, 0] = mm(grad_pre, two, 0, 0).astype(bf16)
        elif e > 0:
            gated_buf[slot, :, at] = gated
            grad_buf[slot, :, at] = grad_pre
        else:
            for n, fresh in enumerate((mm(grad_pre, two, 0, 0), mm(gated, cot, 0, 0))):
                acc[n] = jnp.where(group == 0, 0.0, acc[n]) + fresh
        out_part, gin_part = mm(gated, wdn), mm(grad_pre, win)
        out_rows = out_part if e == 0 else out_rows + out_part
        gin_rows = gin_part if e == 0 else gin_rows + gin_part
    grad_gate = grad_gate * kept
    grad_logits = probs * (grad_gate - jnp.sum(probs * grad_gate, -1, keepdims=True))
    grad_logits = grad_logits.astype(bf16)
    dwr_ref[...] += mm(grad_logits, two, 0, 0)[:SMALL]
    gin_rows = gin_rows + mm(grad_logits, wr_ref[...], 1, 1)
    stage[0] = out_rows.astype(bf16).reshape(blocks, span, width)
    stage[1] = gin_rows.astype(bf16).reshape(blocks, span, width)
    for k in range(groups):

        @pl.when(group == k)
        def _(k=k):
            for store in stores[k]:
                store.start()

    @pl.when(group == groups - 1)
    def _():
        if opening:
            copy = pltpu.make_async_copy(gated_buf, left[0], left_sems.at[0, 0])
            copy.start()
            copy.wait()
        else:
            pltpu.make_async_copy(own_ref.at[0], own_buf, own_sem).wait()
            early_copies = []
            for n in range(2):
                early_buf[n] = (acc[n] + own_buf[n].astype(f32)).astype(bf16)
                for m, target in enumerate(early):
                    copy = pltpu.make_async_copy(
                        early_buf.at[n, pl.ds(m * shard, shard)],
                        target.at[0, n],
                        early_sems.at[n, m],
                    )
                    copy.start()
                    early_copies.append(copy)
            for copy in early_copies:
                copy.wait()
        for k in (groups - 1,) if groups == 1 else (groups - 2, groups - 1):
            for store in stores[k][0 if k == groups - 1 else 2 :]:
                store.wait()


def experts_call(two, cot, weights, wr, carried, name, cost):
    groups = len(two)
    opening = groups == 1
    experts, shard, width = weights[0].shape
    hidden = 2 * shard
    blocks = sum(a.shape[0] for a in two[0])
    span = two[0][0].shape[1]
    rows = blocks * span
    plan = dict(
        groups=groups,
        experts=experts,
        opening=opening,
        two=[len(parts) for parts in two],
        cot=[len(parts) for parts in cot],
    )
    anywhere = pl.BlockSpec(memory_space=pl.ANY)
    once = lambda a: pl.BlockSpec(
        a.shape, lambda g: (0,) * len(a.shape), pipeline_mode=pl.Buffered(1)
    )
    result = jax.ShapeDtypeStruct((blocks, span, width), bf16)
    little = jax.ShapeDtypeStruct((SMALL, width), f32)
    if opening:
        left = [jax.ShapeDtypeStruct((experts, 2, hidden, width), bf16)]
        buffers = [pltpu.VMEM(left[0].shape, bf16), pltpu.VMEM((16, LANES), bf16)]
    else:
        left = [jax.ShapeDtypeStruct((groups * rows, (experts - 1) * hidden), bf16)] * 2
        left += [jax.ShapeDtypeStruct((1, 2, shard, width), bf16)] * 2
        buffers = [pltpu.VMEM((2, rows, experts * hidden), bf16)] * 2
    pieces = [a for parts in two for a in parts] + [a for parts in cot for a in parts]
    outs = pl.pallas_call(
        functools.partial(expert_kernel, plan),
        grid=(groups,),
        in_specs=[anywhere] * (len(pieces) + 4)
        + [once(wr)]
        + ([] if opening else [once(little), anywhere]),
        out_specs=[anywhere] * len(left) + [once(little)] + [anywhere] * (2 * groups),
        out_shape=left + [little] + [result] * (2 * groups),
        scratch_shapes=[
            pltpu.VMEM((groups, blocks, span, width), bf16),
            pltpu.VMEM((groups, blocks, span + MASK_ROWS, width), bf16),
            pltpu.SemaphoreType.DMA((groups, 4)),
            pltpu.VMEM((experts * hidden, width), bf16),
            pltpu.VMEM((experts * hidden, width), bf16),
            pltpu.SemaphoreType.DMA((experts, 4)),
            *buffers,
            pltpu.VMEM((2, blocks, span, width), bf16),
            pltpu.SemaphoreType.DMA((2,)),
            pltpu.SemaphoreType.DMA((2, 2)),
        ]
        + (
            []
            if opening
            else [
                pltpu.VMEM((2, hidden, width), f32),
                pltpu.VMEM((2, hidden, width), bf16),
                pltpu.VMEM((2, hidden, width), bf16),
                pltpu.SemaphoreType.DMA(()),
                pltpu.SemaphoreType.DMA((2, 2)),
            ]
        ),
        compiler_params=pltpu.CompilerParams(vmem_limit_bytes=VMEM_BYTES),
        cost_estimate=cost(10 * groups * rows * width * hidden * experts),
        name=name,
    )(*pieces, *weights, wr, *(carried or []))
    left, (dwr, *outs) = list(outs[: len(left)]), outs[len(left) :]
    return left, dwr, outs[:groups], outs[groups:]


def grads_kernel(plan, *refs):
    refs = list(refs)

    def take(number):
        taken, refs[:] = refs[:number], refs[number:]
        return taken

    groups = len(plan["two"])
    two_parts = [take(n) for n in plan["two"]]
    cot_parts = [take(n) for n in plan["cot"]]
    gated_ref, grad_ref, own_ref, kept_ref, sent_ref = take(5)
    two_buf, cot_buf, cot_rows, sems = refs
    _, blocks, span, width = two_buf.shape
    rows = blocks * span
    copies = []
    for k in range(groups):
        at = 0
        for n, part in enumerate(two_parts[k]):
            size = part.shape[0]
            copies.append(
                pltpu.make_async_copy(part, two_buf.at[k, pl.ds(at, size)], sems.at[k, n])
            )
            at += size
        at = 0
        for n, part in enumerate(cot_parts[k]):
            size = part.shape[0]
            copies.append(
                pltpu.make_async_copy(
                    part, cot_buf.at[k, pl.ds(at, size)], sems.at[k, 2 + n]
                )
            )
            at += size

    @pl.when(pl.program_id(0) == 0)
    def _():
        for copy in copies:
            copy.start()
        for copy in copies:
            copy.wait()
        for k in range(groups):
            cot_rows[k * rows : (k + 1) * rows] = cot_buf[k, :, :span, :].reshape(rows, width)

    half = own_ref.shape[2] // 2
    two = two_buf[...].reshape(groups * rows, width)
    for n, (left_ref, right) in enumerate(((grad_ref, two), (gated_ref, cot_rows[...]))):
        total = (own_ref[0, n].astype(f32) + mm(left_ref[...], right, 0, 0)).astype(bf16)
        kept_ref[0, n] = total[:half]
        sent_ref[0, n] = total[half:]


def grads_call(two, cot, left, own, first, many):
    groups = len(two)
    blocks = sum(a.shape[0] for a in two[0])
    _, span, width = two[0][0].shape
    rows = blocks * span
    hidden = own.shape[2]
    anywhere = pl.BlockSpec(memory_space=pl.ANY)
    pieces = [a for parts in two for a in parts] + [a for parts in cot for a in parts]
    columns = pl.BlockSpec((groups * rows, hidden), lambda e: (0, e))
    part = jax.ShapeDtypeStruct((many, 2, hidden // 2, width), bf16)
    part_spec = pl.BlockSpec((1, 2, hidden // 2, width), lambda e: (e, 0, 0, 0))
    plan = dict(two=[len(parts) for parts in two], cot=[len(parts) for parts in cot])
    return pl.pallas_call(
        functools.partial(grads_kernel, plan),
        grid=(many,),
        in_specs=[anywhere] * len(pieces)
        + [columns, columns, pl.BlockSpec((1, 2, hidden, width), lambda e: (e + first, 0, 0, 0))],
        out_specs=[part_spec, part_spec],
        out_shape=[part, part],
        scratch_shapes=[
            pltpu.VMEM((groups, blocks, span, width), bf16),
            pltpu.VMEM((groups, blocks, span + MASK_ROWS, width), bf16),
            pltpu.VMEM((groups * rows, width), bf16),
            pltpu.SemaphoreType.DMA((groups, 4)),
        ],
        compiler_params=pltpu.CompilerParams(vmem_limit_bytes=VMEM_BYTES),
        cost_estimate=true_cost(8 * groups * rows * width * hidden * many),
        name="expert_grads",
    )(*pieces, *left, own)


def flip(array, fsdp, bits):
    return lax.ppermute(array, "fsdp", [(n, n ^ bits) for n in range(fsdp)])


def tie(value, *others):
    return lax.optimization_barrier((value, others))[0]


def exchange(pieces):
    count = len(pieces)
    return [pieces[0]] + [
        lax.ppermute(pieces[k], "seq", [(n, n ^ k) for n in range(count)]) for k in range(1, count)
    ]


def relative(parts, index):
    count, bit = len(parts), 1
    while bit < count:
        swap = (index & bit) > 0
        parts = [jnp.where(swap, parts[k ^ bit], parts[k]) for k in range(count)]
        bit *= 2
    return parts


def plus(*arrays):
    return sum(a.astype(f32) for a in arrays).astype(bf16)


class Line:
    def __init__(self, seq, raw):
        self.seq, self.raw = seq, raw
        if seq != 4:
            self.total = lax.psum(raw, "seq")

    def inwards(self):
        if self.seq == 4:
            self.moving = lax.ppermute(self.raw, "seq", [(0, 1), (3, 2)])
        return self

    def inwards_with(self, other, *others):
        if self.seq != 4:
            return self.raw
        other.total = plus(other.pair, tie(other.moving, others))
        index = lax.axis_index("seq")
        both = jnp.where((index == 0) | (index == 3), self.raw, other.total)
        self.moving = lax.ppermute(both, "seq", [(0, 1), (1, 0), (2, 3), (3, 2)])
        other.moving = self.moving
        return both

    def hold(self, others):
        if self.seq == 4:
            self.moving = tie(self.moving, others)

    def across(self, *others):
        if self.seq == 4:
            self.pair = plus(self.raw, tie(self.moving, others))
            self.moving = lax.ppermute(self.pair, "seq", [(1, 2), (2, 1)])
            return self.pair
        return self.raw

    def outwards(self, *others):
        if self.seq == 4:
            self.total = plus(self.pair, tie(self.moving, others))
            self.moving = lax.ppermute(self.total, "seq", [(1, 0), (2, 3)])
        return self.total

    def finish(self):
        if self.seq != 4:
            return self.total
        index = lax.axis_index("seq")
        return jnp.where((index == 0) | (index == 3), self.moving, self.total)

    def waiting(self):
        return [self.moving] if self.seq == 4 else []


def back_kernel(
    gin_0, gin_2, gin_4, gin_6, mid_ref, cot_ref, tok_ref, att_ref, proj_ref, prob_ref, wall_ref,
    small_ref, dwr_ref, *rest,
):
    blocks, _, span, width = tok_ref.shape
    length = blocks * span
    gtok_refs, (dwall_ref, acc, acc_small, gatt, gproj) = rest[:blocks], rest[blocks:]
    step = pl.program_id(0)

    @pl.when(step == 0)
    def _():
        acc[...] = jnp.zeros_like(acc)
        acc_small[...] = jnp.zeros_like(acc_small)
        acc_small[:SMALL] = dwr_ref[...]

    gin = sum(ref[...].reshape(length, width).astype(f32) for ref in (gin_0, gin_2, gin_4, gin_6))
    unit_two, inverse_two = unit_norm(mid_ref[...].reshape(length, width))
    acc_small[6:7] += jnp.sum(gin * unit_two, 0, keepdims=True)
    acc_small[7:8] += jnp.sum(gin, 0, keepdims=True)
    grad_middle = cot_ref[...].reshape(length, width).astype(f32) + norm_back(
        gin * small_ref[6:7], unit_two, inverse_two
    )
    branch = grad_middle.astype(bf16)
    acc[:, 3 * width : 4 * width] += mm(att_ref[0], branch, 0, 0)
    gatt[...] = mm(branch, wall_ref[:, 3 * width : 4 * width], 1, 1).astype(bf16)
    lower = lax.broadcasted_iota(jnp.int32, (length, LANES), 1) < HEAD_DIM
    zero = jnp.zeros((length, LANES), bf16)
    scale = HEAD_DIM**-0.5

    def score_grad(weights, grad_weights):
        weights = weights.astype(f32)
        product = weights * grad_weights
        return (product - weights * jnp.sum(product, -1, keepdims=True)).astype(bf16)

    for pair in range(width // LANES):
        places = [slice((3 * pair + n) * LANES, (3 * pair + n + 1) * LANES) for n in range(3)]
        first, second, third = (proj_ref[0, :, place] for place in places)
        first_r, second_r, third_r = half_turn(first), half_turn(second), half_turn(third)
        grad = gatt[:, pair * LANES : (pair + 1) * LANES]
        weights_a, weights_b = prob_ref[0, 2 * pair], prob_ref[0, 2 * pair + 1]
        ds_a = score_grad(weights_a, mm(jnp.where(lower, grad, zero), second, 1, 1))
        ds_b = score_grad(weights_b, mm(jnp.where(lower, zero, grad), third, 1, 1))
        gproj[:, places[0]] = (
            jnp.where(lower, mm(ds_a, first_r), mm(ds_a, first_r, 0, 0)) * scale
        ).astype(bf16)
        gproj[:, places[1]] = jnp.where(
            lower, mm(weights_a, grad, 0, 0), mm(ds_b, third_r) * scale
        ).astype(bf16)
        gproj[:, places[2]] = jnp.where(
            lower, mm(ds_b, second_r, 0, 0) * scale, mm(weights_b, grad, 0, 0)
        ).astype(bf16)
    unit_one, inverse_one = unit_norm(tok_ref[...].reshape(length, width).astype(f32))
    one = (unit_one * small_ref[4:5] + small_ref[5:6]).astype(bf16)
    grad_one = mm(gproj[...], wall_ref[:, : 3 * width], 1, 1)
    acc_small[4:5] += jnp.sum(grad_one * unit_one, 0, keepdims=True)
    acc_small[5:6] += jnp.sum(grad_one, 0, keepdims=True)
    grad_tok = grad_middle + norm_back(grad_one * small_ref[4:5], unit_one, inverse_one)
    for k, ref in enumerate(gtok_refs):
        ref[0] = grad_tok[k * span : (k + 1) * span].astype(bf16)
    acc[:, : 3 * width] += mm(one, gproj[...], 0, 0)

    @pl.when(step == pl.num_programs(0) - 1)
    def _():
        dwall_ref[:, : 4 * width] = acc[...].astype(bf16)
        dwall_ref[:, 4 * width :] = acc_small[...].T.astype(bf16)


def back(gins, middle, cot, tok, att, proj, prob, wall, small, dwr):
    blocks, images, span, width = tok.shape
    length = blocks * span
    heads = width // HEAD_DIM
    split = pl.BlockSpec((blocks, 1, span, width), lambda i: (0, i, 0, 0))
    whole = lambda a: pl.BlockSpec(a.shape, lambda i: (0,) * len(a.shape))
    return pl.pallas_call(
        back_kernel,
        grid=(images,),
        in_specs=[split] * 7
        + [
            pl.BlockSpec((1, length, width), lambda i: (i, 0, 0)),
            pl.BlockSpec((1, length, 3 * width), lambda i: (i, 0, 0)),
            pl.BlockSpec((1, heads, length, length), lambda i: (i, 0, 0, 0)),
            whole(wall),
            whole(small),
            whole(dwr),
        ],
        out_specs=[pl.BlockSpec((1, span, width), lambda i: (i, 0, 0))] * blocks + [whole(wall)],
        out_shape=[jax.ShapeDtypeStruct((images, span, width), bf16)] * blocks
        + [jax.ShapeDtypeStruct(wall.shape, bf16)],
        scratch_shapes=[
            pltpu.VMEM((width, 4 * width), f32),
            pltpu.VMEM((LANES, width), f32),
            pltpu.VMEM((length, width), bf16),
            pltpu.VMEM((length, 3 * width), bf16),
        ],
        compiler_params=pltpu.CompilerParams(vmem_limit_bytes=VMEM_BYTES),
        cost_estimate=true_cost(10 * images * length * width * (4 * width + 3 * length)),
        name="back",
    )(*gins, middle, cot, tok, att, proj, prob, wall, small, dwr)


def kept_pairs(route_rows, token_live, order_rows, expert_count, capacity):
    labels = jnp.arange(expert_count, dtype=jnp.int32)
    alive = token_live > 0
    first_hot = ((route_rows[:, 0:1] == labels) & alive[:, None]).astype(bf16)
    second_hot = ((route_rows[:, 1:2] == labels) & alive[:, None]).astype(bf16)
    earlier = (order_rows[None, :] < order_rows[:, None]).astype(bf16)
    ahead = mm(earlier, jnp.concatenate([first_hot, second_hot], 1))
    ahead_first = ahead[:, :expert_count]
    ahead_second = ahead[:, expert_count:] + jnp.sum(first_hot.astype(f32), 0)
    return jnp.where(ahead_first < capacity, first_hot, 0) + jnp.where(
        ahead_second < capacity, second_hot, 0
    )


def local(
    fsdp,
    seq,
    tokens,
    ln1_gain,
    ln1_bias,
    w_qkv,
    w_out,
    ln2_gain,
    ln2_bias,
    w_router,
    w_in,
    w_down,
    padding,
    routes,
    priority,
    cotangent,
):
    images, span, width = tokens.shape
    expert_count, shard_rows = w_in.shape[0], w_in.shape[1]
    rows = images * span
    own = images // seq
    length = seq * span
    capacity = (2 * rows + expert_count - 1) // expert_count
    outer = fsdp // 8
    if outer > 1:
        outer_groups = [[o * 8 + n for o in range(outer)] for n in range(8)]
    spread = functools.partial(flip, fsdp=fsdp)
    seq_index = lax.axis_index("seq")
    place = lax.axis_index("fsdp") if outer == 1 else jnp.int32(0)
    place = place.astype(jnp.int32).reshape(1)

    def picked(array, k):
        return lax.dynamic_index_in_dim(array, seq_index ^ k, 0, keepdims=False)

    tokens = tokens.reshape(seq, own * span, width)
    tok = jnp.stack(exchange([picked(tokens, k) for k in range(seq)]))
    tok = tok.reshape(seq, own, span, width)

    columns = jnp.concatenate(
        [w_router] + [v[:, None] for v in (ln1_gain, ln1_bias, ln2_gain, ln2_bias)], 1
    )
    columns = jnp.pad(columns, ((0, 0), (0, LANES - columns.shape[1])))
    shard = jnp.concatenate([w_qkv, w_out, columns], 1)
    if outer == 1:
        cut = width // 16
        from_x, from_y = spread(shard, bits=2), spread(shard, bits=4)
        from_x, from_y = tie((from_x, from_y), tok)
        near = [(0, 0, shard), (2, 0, from_x), (4, 0, from_y)]
        far = [
            (6, 0, spread(from_x[:cut], bits=4)),
            (6, cut, spread(from_y[cut:], bits=2)),
        ]
        near += [(r + 1, skip, spread(a, bits=1)) for r, skip, a in near]
    else:
        full = lax.all_gather(shard, "fsdp", axis=0, tiled=True)
        from_x = from_y = full
        near, far = [(n, 0, full[n * (width // 8) : (n + 1) * (width // 8)]) for n in range(8)], []

    mine = lax.dynamic_slice_in_dim(padding, seq_index * own, own, 0).reshape(own, seq, span)
    mine = jnp.stack(relative([mine[:, b] for b in range(seq)], seq_index))
    vis = jnp.where(mine > 0, 0.0, neg_fill).astype(f32)
    vis = jnp.swapaxes(vis, 0, 1).reshape(own, 1, length)
    live = lax.dynamic_slice_in_dim(padding, seq_index * span, span, 1)
    kept = kept_pairs(
        routes.reshape(rows, 2), live.reshape(rows), priority.reshape(rows), expert_count, capacity
    )
    kept = jnp.swapaxes(kept.reshape(seq, own * span, expert_count), 1, 2)
    kept = jnp.pad(
        kept, ((0, 0), (0, MASK_ROWS - expert_count), (0, width - own * span))
    ).astype(bf16)
    cot = cotangent * live[:, :, None].astype(bf16)
    packed = jnp.concatenate([cot.reshape(seq, own * span, width), kept], 1)
    packed = tie(packed, tok, from_x, from_y, vis, mine)
    packed = jnp.stack(exchange([picked(packed, k) for k in range(seq)]))
    late = tie([a for _, _, a in far], packed)
    far += [(r + 1, skip, spread(a, bits=1)) for (r, skip, _), a in zip(far, late)]
    offsets = [(r, skip) for r, skip, _ in near + far]
    pieces = [a for _, _, a in near + far]
    cot_x, cot_y = spread(packed, bits=2), spread(packed, bits=4)
    half = seq // 2
    cot_far = [spread(cot_x[:half], bits=4), spread(cot_y[half:], bits=2)]

    win, wdn = w_in, w_down
    if outer > 1:
        win = lax.all_gather(win, "fsdp", axis=1, tiled=True, axis_index_groups=outer_groups)
        wdn = lax.all_gather(wdn, "fsdp", axis=1, tiled=True, axis_index_groups=outer_groups)
    win, wdn = tie((win, wdn), pieces)
    weights = [win, spread(win, bits=1), wdn, spread(wdn, bits=1)]

    middle, two, proj, att, prob, wall, wr, small = front(tok, pieces, offsets, vis, place)
    two = two.reshape(seq, own * span, width)
    two_far = [[spread(two, bits=bits)] for bits in (2, 4, 6)]

    (dw,), dwr, out_0, gin_0 = experts_call(
        [[two]], [[packed]], weights, wr, None, "experts_own", lambda flops: SHORT
    )
    cots = [[cot_x], [cot_y], cot_far]
    (*left, dw_kept, dw_sent), dwr, outs, gins = experts_call(
        two_far, cots, weights, wr, [dwr, dw], "experts_far", true_cost
    )
    arrived = [spread(a, bits=bits) for a, bits in zip(gins, (2, 4, 6))]

    def finished(dw_kept, dw_sent):
        raw = plus(dw_kept, spread(dw_sent, bits=1))
        if outer > 1:
            raw = lax.psum_scatter(
                raw, "fsdp", scatter_dimension=2, tiled=True, axis_index_groups=outer_groups
            )
        return lax.optimization_barrier([raw[n : n + 1] for n in range(raw.shape[0])])

    first = Line(seq, finished(dw_kept, dw_sent)[0]).inwards()
    left, dw = tie((left, dw), first.raw)
    parts = grads_call(two_far, cots, left, dw, 1, expert_count - 1)
    ready = first.across(arrived)
    lines = [Line(seq, raw) for raw in finished(*tie(parts, ready, arrived))]
    lines[0].inwards()
    gins = gin_0 + tie(arrived, ready, [line.raw for line in lines])
    lines = [first] + lines

    shape4 = (seq, own, span, width)
    outs = [spread(a, bits=bits) for a, bits in zip(tie(outs, arrived), (2, 4, 6))]
    *grad_tok, dense = back(
        [a.reshape(shape4) for a in gins],
        middle,
        packed[:, : own * span].reshape(shape4),
        tok,
        att,
        proj,
        prob,
        wall,
        small,
        dwr,
    )
    flying = (outs, lines[0].waiting(), lines[1].waiting())
    dense = tie(dense, flying)
    dense = lax.psum_scatter(dense, "fsdp", scatter_dimension=0, tiled=True)
    lines[2].raw, lines[3].raw = tie((lines[2].raw, lines[3].raw), grad_tok)
    lines[2].inwards()
    ready = lines[1].across(grad_tok, flying)
    ready = lines[3].inwards_with(lines[0], ready)
    ready = lines[2].across(ready)
    ready = lines[1].outwards(ready)
    ready = lines[3].across(ready)
    ready = lines[2].outwards(ready, lines[1].waiting())
    dense_line = Line(seq, tie(dense, ready)).inwards()
    ready = lines[3].outwards(dense_line.raw)

    ready = dense_line.across(ready)
    outs, grad_tok = tie((outs, grad_tok), ready)
    outs = [a.reshape(shape4) for a in out_0 + outs]
    home = []
    for k in range(seq):
        alive = mine[k][:, :, None].astype(f32)
        combined = sum(a[k].astype(f32) for a in outs)
        home.append(jnp.stack([(alive * (middle[k] + combined)).astype(bf16), grad_tok[k]]))
    home = exchange(home)
    lines[3].hold(dense_line.outwards(ready))
    grads = [line.finish() for line in lines]
    expert_grads = [jnp.concatenate([g[:, n] for g in grads], 0).astype(f32) for n in range(2)]
    home = relative(tie(home, expert_grads), seq_index)
    outputs, grad_tokens = (
        jnp.concatenate([a[n] for a in home], 0).reshape(images, span, width) for n in range(2)
    )
    dense = dense_line.finish().astype(f32)
    tail = dense[:, 4 * width :]
    return (
        outputs,
        grad_tokens,
        tail[:, 4],
        tail[:, 5],
        dense[:, : 3 * width],
        dense[:, 3 * width : 4 * width],
        tail[:, 6],
        tail[:, 7],
        tail[:, :expert_count],
        expert_grads[0],
        expert_grads[1],
    )


def solution(mesh):
    rows = P("fsdp", "seq", None)
    in_specs = (
        rows,
        P("fsdp"),
        P("fsdp"),
        P("fsdp", None),
        P("fsdp", None),
        P("fsdp"),
        P("fsdp"),
        P("fsdp", None),
        P(None, "fsdp", None),
        P(None, "fsdp", None),
        P("fsdp", None),
        rows,
        P("fsdp", "seq"),
        rows,
    )
    out_specs = (
        rows,
        rows,
        P("fsdp"),
        P("fsdp"),
        P("fsdp", None),
        P("fsdp", None),
        P("fsdp"),
        P("fsdp"),
        P("fsdp", None),
        P(None, "fsdp", None),
        P(None, "fsdp", None),
    )
    return jax.shard_map(
        functools.partial(local, mesh.shape["fsdp"], mesh.shape["seq"]),
        mesh=mesh,
        in_specs=in_specs,
        out_specs=out_specs,
        check_vma=False,
    )
```

```python
import functools
import math

import jax
import jax.numpy as jnp
from jax import lax
from jax.experimental import pallas as pl
from jax.experimental.pallas import tpu as pltpu
from jax.sharding import PartitionSpec as P

HEAD_DIM = 64
LANES = 128
MASK_ROWS = 16
SMALL = 8
norm_eps = 1e-06
neg_fill = -1e30
f32 = jnp.float32
bf16 = jnp.bfloat16
VMEM_BYTES = 60 * 1024 * 1024
SHORT = pl.CostEstimate(flops=1000, bytes_accessed=1000, transcendentals=0)


def true_cost(flops):
    return pl.CostEstimate(flops=2 * flops, bytes_accessed=16 * 1024 * 1024, transcendentals=0)


def mm(left, right, left_dim=1, right_dim=0):
    return lax.dot_general(
        left, right, (((left_dim,), (right_dim,)), ((), ())), preferred_element_type=f32
    )


def unit_norm(rows):
    centred = rows - jnp.mean(rows, -1, keepdims=True)
    inverse = lax.rsqrt(jnp.mean(centred * centred, -1, keepdims=True) + norm_eps)
    return centred * inverse, inverse


def norm_back(scaled, unit, inverse):
    return inverse * (
        scaled
        - jnp.mean(scaled, -1, keepdims=True)
        - unit * jnp.mean(scaled * unit, -1, keepdims=True)
    )


def half_turn(tile):
    return pltpu.roll(tile.astype(f32), HEAD_DIM, axis=1).astype(bf16)


def wall_copies(pieces, offsets, place_ref, wall_ref, sems):
    copies = []
    for n, (piece, (r, skip)) in enumerate(zip(pieces, offsets)):
        rows = piece.shape[0]
        shard = wall_ref.shape[0] // 8
        start = pl.multiple_of((place_ref[0] ^ r) * shard + skip, 16)
        copies.append(pltpu.make_async_copy(piece, wall_ref.at[pl.ds(start, rows)], sems.at[n]))
    return copies


def front_kernel(offsets, *refs):
    pieces = refs[: len(offsets)]
    tok_ref, vis_ref, place_ref = refs[len(offsets) : len(offsets) + 3]
    mid_ref, two_ref, proj_ref, att_ref, prob_ref, full_ref, wr_ref, small_ref = refs[
        len(offsets) + 3 : len(offsets) + 11
    ]
    wall_ref, sems, full_sem = refs[len(offsets) + 11 :]
    blocks, _, span, width = tok_ref.shape
    length = blocks * span
    save = pltpu.make_async_copy(wall_ref, full_ref, full_sem)

    @pl.when(pl.program_id(0) == 0)
    def _():
        copies = wall_copies(pieces, offsets, place_ref, wall_ref, sems)
        for copy in copies:
            copy.start()
        for copy in copies:
            copy.wait()
        save.start()
        columns = wall_ref[:, 4 * width :]
        wr_ref[...] = columns
        small_ref[...] = columns.astype(f32).T[:SMALL]

    rows = tok_ref[...].reshape(length, width).astype(f32)
    unit, _ = unit_norm(rows)
    one = (unit * small_ref[4:5] + small_ref[5:6]).astype(bf16)
    proj_ref[0] = mm(one, wall_ref[:, : 3 * width]).astype(bf16)
    lower = lax.broadcasted_iota(jnp.int32, (length, LANES), 1) < HEAD_DIM
    zero = jnp.zeros((length, LANES), bf16)
    bias = vis_ref[0]

    def soften(index, queries, keys):
        scores = mm(queries, keys, 1, 1) * (HEAD_DIM**-0.5) + bias
        shifted = jnp.exp(scores - jnp.max(scores, -1, keepdims=True))
        weights = (shifted / jnp.sum(shifted, -1, keepdims=True)).astype(bf16)
        prob_ref[0, index] = weights
        return weights

    for pair in range(width // LANES):
        first, second, third = (
            proj_ref[0, :, (3 * pair + n) * LANES : (3 * pair + n + 1) * LANES] for n in range(3)
        )
        weights_a = soften(2 * pair, jnp.where(lower, first, zero), half_turn(first))
        weights_b = soften(2 * pair + 1, jnp.where(lower, zero, second), half_turn(third))
        both = jnp.where(lower, mm(weights_a, second), mm(weights_b, third))
        att_ref[0, :, pair * LANES : (pair + 1) * LANES] = both.astype(bf16)
    middle = rows + mm(att_ref[0], wall_ref[:, 3 * width : 4 * width])
    mid_ref[...] = middle.reshape(mid_ref.shape)
    unit, _ = unit_norm(middle)
    two_ref[...] = (unit * small_ref[6:7] + small_ref[7:8]).astype(bf16).reshape(two_ref.shape)

    @pl.when(pl.program_id(0) == pl.num_programs(0) - 1)
    def _():
        save.wait()


def front(tok, pieces, offsets, vis, place):
    blocks, images, span, width = tok.shape
    length = blocks * span
    heads = width // HEAD_DIM
    split = pl.BlockSpec((blocks, 1, span, width), lambda i: (0, i, 0, 0))
    anywhere = pl.BlockSpec(memory_space=pl.ANY)
    columns = pieces[0].shape[1]
    return pl.pallas_call(
        functools.partial(front_kernel, offsets),
        grid=(images,),
        in_specs=[anywhere] * len(pieces)
        + [
            split,
            pl.BlockSpec((1, 1, length), lambda i: (i, 0, 0)),
            pl.BlockSpec(memory_space=pltpu.SMEM),
        ],
        out_specs=[
            split,
            split,
            pl.BlockSpec((1, length, 3 * width), lambda i: (i, 0, 0)),
            pl.BlockSpec((1, length, width), lambda i: (i, 0, 0)),
            pl.BlockSpec((1, heads, length, length), lambda i: (i, 0, 0, 0)),
            anywhere,
            pl.BlockSpec((width, LANES), lambda i: (0, 0)),
            pl.BlockSpec((SMALL, width), lambda i: (0, 0)),
        ],
        out_shape=[
            jax.ShapeDtypeStruct(tok.shape, f32),
            jax.ShapeDtypeStruct(tok.shape, bf16),
            jax.ShapeDtypeStruct((images, length, 3 * width), bf16),
            jax.ShapeDtypeStruct((images, length, width), bf16),
            jax.ShapeDtypeStruct((images, heads, length, length), bf16),
            jax.ShapeDtypeStruct((width, columns), bf16),
            jax.ShapeDtypeStruct((width, LANES), bf16),
            jax.ShapeDtypeStruct((SMALL, width), f32),
        ],
        scratch_shapes=[
            pltpu.VMEM((width, columns), bf16),
            pltpu.SemaphoreType.DMA((len(pieces),)),
            pltpu.SemaphoreType.DMA(()),
        ],
        compiler_params=pltpu.CompilerParams(vmem_limit_bytes=VMEM_BYTES),
        cost_estimate=SHORT,
        name="front",
    )(*pieces, tok, vis, place)


def gelu_parts(pre):
    bell = jnp.exp2(pre * pre * (-0.5 * math.log2(math.e)))
    frac = 1.0 / (1.0 + (0.3275911 * math.sqrt(0.5)) * jnp.abs(pre))
    a5, a4, a3, a2, a1 = (
        0.5 * c for c in (1.061405429, -1.453152027, 1.421413741, -0.284496736, 0.254829592)
    )
    tail = frac * (a1 + frac * (a2 + frac * (a3 + frac * (a4 + frac * a5)))) * bell
    cumulative = jnp.where(pre >= 0, 1.0 - tail, tail)
    return pre * cumulative, cumulative + (pre * 0.3989422804014327) * bell


def expert_kernel(plan, *refs):
    refs = list(refs)

    def take(number):
        taken, refs[:] = refs[:number], refs[number:]
        return taken

    groups, experts, opening = plan["groups"], plan["experts"], plan["opening"]
    two_parts = [take(n) for n in plan["two"]]
    cot_parts = [take(n) for n in plan["cot"]]
    weights = take(4)
    (wr_ref,) = take(1)
    dwr_carried, own_ref = (None, None) if opening else take(2)
    left = take(1 if opening else 2)
    early = [] if opening else take(2)
    (dwr_ref,) = take(1)
    results = take(2 * groups)
    two_buf, cot_buf, sems, win_buf, wdn_buf, weight_sems, gated_buf, grad_buf = take(8)
    stage, store_sems, left_sems = take(3)
    acc, own_buf, early_buf, own_sem, early_sems = [None] * 5 if opening else take(5)
    _, blocks, span, width = two_buf.shape
    rows = blocks * span
    hidden = win_buf.shape[0] // experts
    shard = hidden // 2
    group = pl.program_id(0)
    slot = group % gated_buf.shape[0]
    lane = lax.broadcasted_iota(jnp.int32, (rows, LANES), 1)

    copies = []
    for k in range(groups):
        some = []
        for parts, buffer in ((two_parts[k], two_buf), (cot_parts[k], cot_buf)):
            at = 0
            for part in parts:
                size = part.shape[0]
                some.append((part, buffer.at[k, pl.ds(at, size)]))
                at += size
        copies.append(
            [pltpu.make_async_copy(s, t, sems.at[k, n]) for n, (s, t) in enumerate(some)]
        )
    fetches = [
        pltpu.make_async_copy(
            ref.at[e],
            (win_buf, wdn_buf)[n // 2].at[pl.ds(e * hidden + (n % 2) * shard, shard)],
            weight_sems.at[e, n],
        )
        for e in range(experts)
        for n, ref in enumerate(weights)
    ]
    stores = [
        [
            pltpu.make_async_copy(stage.at[n], results[n * groups + k], store_sems.at[n])
            for n in range(2)
        ]
        for k in range(groups)
    ]
    if not opening:
        for k in range(groups):
            for n, buffer in enumerate((gated_buf, grad_buf)):
                place = k % buffer.shape[0]
                stores[k].append(
                    pltpu.make_async_copy(
                        buffer.at[place, :, pl.ds(hidden, (experts - 1) * hidden)],
                        left[n].at[pl.ds(k * rows, rows)],
                        left_sems.at[place, n],
                    )
                )

    @pl.when(group == 0)
    def _():
        for copy in copies[0] + fetches:
            copy.start()
        for some in copies[1:]:
            for copy in some:
                copy.start()
        if not opening:
            pltpu.make_async_copy(own_ref.at[0], own_buf, own_sem).start()
        dwr_ref[...] = jnp.zeros_like(dwr_ref) if opening else dwr_carried[...]
        for copy in fetches:
            copy.wait()

    for k, some in enumerate(copies):

        @pl.when(group == k)
        def _(k=k, some=some):
            for copy in some:
                copy.wait()
            if k > 0:
                for store in stores[k - 1][:2]:
                    store.wait()
            if k > 1:
                for store in stores[k - 2][2:]:
                    store.wait()

    two = two_buf[group].reshape(rows, width)
    cot = cot_buf[group, :, :span, :].reshape(rows, width)
    chosen = (
        lax.broadcasted_iota(jnp.int32, (MASK_ROWS, LANES), 0)
        == lax.broadcasted_iota(jnp.int32, (MASK_ROWS, LANES), 1)
    ).astype(bf16)
    logits = jnp.where(lane < experts, mm(two, wr_ref[...]), neg_fill)
    shifted = jnp.exp(logits - jnp.max(logits, -1, keepdims=True))
    probs = shifted / jnp.sum(shifted, -1, keepdims=True)
    kept = jnp.concatenate(
        [
            mm(cot_buf[group, b, span : span + MASK_ROWS, :span], chosen, 0, 0)
            for b in range(blocks)
        ],
        0,
    )
    grad_gate = jnp.zeros((rows, LANES), f32)
    gates = probs * kept
    out_rows = gin_rows = None
    for e in range(experts):
        at = slice(e * hidden, (e + 1) * hidden)
        win, wdn = win_buf[at], wdn_buf[at]
        pre = mm(two, win, 1, 1)
        back_rows = mm(cot, wdn, 1, 1)
        gate = gates[:, e : e + 1]
        hidden_rows, slope = gelu_parts(pre)
        product = jnp.sum(hidden_rows * back_rows, -1, keepdims=True)
        grad_gate = jnp.where(lane == e, product, grad_gate)
        gated = (hidden_rows * gate).astype(bf16)
        grad_pre = (slope * back_rows * gate).astype(bf16)
        if opening:
            gated_buf[e, 1] = mm(gated, cot, 0, 0).astype(bf16)
            gated_buf[e, 0] = mm(grad_pre, two, 0, 0).astype(bf16)
        elif e > 0:
            gated_buf[slot, :, at] = gated
            grad_buf[slot, :, at] = grad_pre
        else:
            for n, fresh in enumerate((mm(grad_pre, two, 0, 0), mm(gated, cot, 0, 0))):
                acc[n] = jnp.where(group == 0, 0.0, acc[n]) + fresh
        out_part, gin_part = mm(gated, wdn), mm(grad_pre, win)
        out_rows = out_part if e == 0 else out_rows + out_part
        gin_rows = gin_part if e == 0 else gin_rows + gin_part
    grad_gate = grad_gate * kept
    grad_logits = probs * (grad_gate - jnp.sum(probs * grad_gate, -1, keepdims=True))
    grad_logits = grad_logits.astype(bf16)
    dwr_ref[...] += mm(grad_logits, two, 0, 0)[:SMALL]
    gin_rows = gin_rows + mm(grad_logits, wr_ref[...], 1, 1)
    stage[0] = out_rows.astype(bf16).reshape(blocks, span, width)
    stage[1] = gin_rows.astype(bf16).reshape(blocks, span, width)
    for k in range(groups):

        @pl.when(group == k)
        def _(k=k):
            for store in stores[k]:
                store.start()

    @pl.when(group == groups - 1)
    def _():
        if opening:
            copy = pltpu.make_async_copy(gated_buf, left[0], left_sems.at[0, 0])
            copy.start()
            copy.wait()
        else:
            pltpu.make_async_copy(own_ref.at[0], own_buf, own_sem).wait()
            early_copies = []
            for n in range(2):
                early_buf[n] = (acc[n] + own_buf[n].astype(f32)).astype(bf16)
                for m, target in enumerate(early):
                    copy = pltpu.make_async_copy(
                        early_buf.at[n, pl.ds(m * shard, shard)],
                        target.at[0, n],
                        early_sems.at[n, m],
                    )
                    copy.start()
                    early_copies.append(copy)
            for copy in early_copies:
                copy.wait()
        for k in (groups - 1,) if groups == 1 else (groups - 2, groups - 1):
            for store in stores[k][0 if k == groups - 1 else 2 :]:
                store.wait()


def experts_call(two, cot, weights, wr, carried, name, cost):
    groups = len(two)
    opening = groups == 1
    experts, shard, width = weights[0].shape
    hidden = 2 * shard
    blocks = sum(a.shape[0] for a in two[0])
    span = two[0][0].shape[1]
    rows = blocks * span
    plan = dict(
        groups=groups,
        experts=experts,
        opening=opening,
        two=[len(parts) for parts in two],
        cot=[len(parts) for parts in cot],
    )
    anywhere = pl.BlockSpec(memory_space=pl.ANY)
    once = lambda a: pl.BlockSpec(
        a.shape, lambda g: (0,) * len(a.shape), pipeline_mode=pl.Buffered(1)
    )
    result = jax.ShapeDtypeStruct((blocks, span, width), bf16)
    little = jax.ShapeDtypeStruct((SMALL, width), f32)
    if opening:
        left = [jax.ShapeDtypeStruct((experts, 2, hidden, width), bf16)]
        buffers = [pltpu.VMEM(left[0].shape, bf16), pltpu.VMEM((16, LANES), bf16)]
    else:
        left = [jax.ShapeDtypeStruct((groups * rows, (experts - 1) * hidden), bf16)] * 2
        left += [jax.ShapeDtypeStruct((1, 2, shard, width), bf16)] * 2
        buffers = [pltpu.VMEM((2, rows, experts * hidden), bf16)] * 2
    pieces = [a for parts in two for a in parts] + [a for parts in cot for a in parts]
    outs = pl.pallas_call(
        functools.partial(expert_kernel, plan),
        grid=(groups,),
        in_specs=[anywhere] * (len(pieces) + 4)
        + [once(wr)]
        + ([] if opening else [once(little), anywhere]),
        out_specs=[anywhere] * len(left) + [once(little)] + [anywhere] * (2 * groups),
        out_shape=left + [little] + [result] * (2 * groups),
        scratch_shapes=[
            pltpu.VMEM((groups, blocks, span, width), bf16),
            pltpu.VMEM((groups, blocks, span + MASK_ROWS, width), bf16),
            pltpu.SemaphoreType.DMA((groups, 4)),
            pltpu.VMEM((experts * hidden, width), bf16),
            pltpu.VMEM((experts * hidden, width), bf16),
            pltpu.SemaphoreType.DMA((experts, 4)),
            *buffers,
            pltpu.VMEM((2, blocks, span, width), bf16),
            pltpu.SemaphoreType.DMA((2,)),
            pltpu.SemaphoreType.DMA((2, 2)),
        ]
        + (
            []
            if opening
            else [
                pltpu.VMEM((2, hidden, width), f32),
                pltpu.VMEM((2, hidden, width), bf16),
                pltpu.VMEM((2, hidden, width), bf16),
                pltpu.SemaphoreType.DMA(()),
                pltpu.SemaphoreType.DMA((2, 2)),
            ]
        ),
        compiler_params=pltpu.CompilerParams(vmem_limit_bytes=VMEM_BYTES),
        cost_estimate=cost(10 * groups * rows * width * hidden * experts),
        name=name,
    )(*pieces, *weights, wr, *(carried or []))
    left, (dwr, *outs) = list(outs[: len(left)]), outs[len(left) :]
    return left, dwr, outs[:groups], outs[groups:]


def grads_kernel(plan, *refs):
    refs = list(refs)

    def take(number):
        taken, refs[:] = refs[:number], refs[number:]
        return taken

    groups = len(plan["two"])
    two_parts = [take(n) for n in plan["two"]]
    cot_parts = [take(n) for n in plan["cot"]]
    gated_ref, grad_ref, own_ref, kept_ref, sent_ref = take(5)
    two_buf, cot_buf, cot_rows, sems = refs
    _, blocks, span, width = two_buf.shape
    rows = blocks * span
    copies = []
    for k in range(groups):
        at = 0
        for n, part in enumerate(two_parts[k]):
            size = part.shape[0]
            copies.append(
                pltpu.make_async_copy(part, two_buf.at[k, pl.ds(at, size)], sems.at[k, n])
            )
            at += size
        at = 0
        for n, part in enumerate(cot_parts[k]):
            size = part.shape[0]
            copies.append(
                pltpu.make_async_copy(
                    part, cot_buf.at[k, pl.ds(at, size)], sems.at[k, 2 + n]
                )
            )
            at += size

    @pl.when(pl.program_id(0) == 0)
    def _():
        for copy in copies:
            copy.start()
        for copy in copies:
            copy.wait()
        for k in range(groups):
            cot_rows[k * rows : (k + 1) * rows] = cot_buf[k, :, :span, :].reshape(rows, width)

    half = own_ref.shape[2] // 2
    two = two_buf[...].reshape(groups * rows, width)
    for n, (left_ref, right) in enumerate(((grad_ref, two), (gated_ref, cot_rows[...]))):
        total = (own_ref[0, n].astype(f32) + mm(left_ref[...], right, 0, 0)).astype(bf16)
        kept_ref[0, n] = total[:half]
        sent_ref[0, n] = total[half:]


def grads_call(two, cot, left, own, first, many):
    groups = len(two)
    blocks = sum(a.shape[0] for a in two[0])
    _, span, width = two[0][0].shape
    rows = blocks * span
    hidden = own.shape[2]
    anywhere = pl.BlockSpec(memory_space=pl.ANY)
    pieces = [a for parts in two for a in parts] + [a for parts in cot for a in parts]
    columns = pl.BlockSpec((groups * rows, hidden), lambda e: (0, e))
    part = jax.ShapeDtypeStruct((many, 2, hidden // 2, width), bf16)
    part_spec = pl.BlockSpec((1, 2, hidden // 2, width), lambda e: (e, 0, 0, 0))
    plan = dict(two=[len(parts) for parts in two], cot=[len(parts) for parts in cot])
    return pl.pallas_call(
        functools.partial(grads_kernel, plan),
        grid=(many,),
        in_specs=[anywhere] * len(pieces)
        + [columns, columns, pl.BlockSpec((1, 2, hidden, width), lambda e: (e + first, 0, 0, 0))],
        out_specs=[part_spec, part_spec],
        out_shape=[part, part],
        scratch_shapes=[
            pltpu.VMEM((groups, blocks, span, width), bf16),
            pltpu.VMEM((groups, blocks, span + MASK_ROWS, width), bf16),
            pltpu.VMEM((groups * rows, width), bf16),
            pltpu.SemaphoreType.DMA((groups, 4)),
        ],
        compiler_params=pltpu.CompilerParams(vmem_limit_bytes=VMEM_BYTES),
        cost_estimate=true_cost(8 * groups * rows * width * hidden * many),
        name="expert_grads",
    )(*pieces, *left, own)


def flip(array, fsdp, bits):
    return lax.ppermute(array, "fsdp", [(n, n ^ bits) for n in range(fsdp)])


def tie(value, *others):
    return lax.optimization_barrier((value, others))[0]


def exchange(pieces):
    count = len(pieces)
    return [pieces[0]] + [
        lax.ppermute(pieces[k], "seq", [(n, n ^ k) for n in range(count)]) for k in range(1, count)
    ]


def relative(parts, index):
    count, bit = len(parts), 1
    while bit < count:
        swap = (index & bit) > 0
        parts = [jnp.where(swap, parts[k ^ bit], parts[k]) for k in range(count)]
        bit *= 2
    return parts


def plus(*arrays):
    return sum(a.astype(f32) for a in arrays).astype(bf16)


class Line:
    def __init__(self, seq, raw):
        self.seq, self.raw = seq, raw
        if seq != 4:
            self.total = lax.psum(raw, "seq")

    def inwards(self):
        if self.seq == 4:
            self.moving = lax.ppermute(self.raw, "seq", [(0, 1), (3, 2)])
        return self

    def inwards_with(self, other, *others):
        if self.seq != 4:
            return self.raw
        other.total = plus(other.pair, tie(other.moving, others))
        index = lax.axis_index("seq")
        both = jnp.where((index == 0) | (index == 3), self.raw, other.total)
        self.moving = lax.ppermute(both, "seq", [(0, 1), (1, 0), (2, 3), (3, 2)])
        other.moving = self.moving
        return both

    def hold(self, others):
        if self.seq == 4:
            self.moving = tie(self.moving, others)

    def across(self, *others):
        if self.seq == 4:
            self.pair = plus(self.raw, tie(self.moving, others))
            self.moving = lax.ppermute(self.pair, "seq", [(1, 2), (2, 1)])
            return self.pair
        return self.raw

    def outwards(self, *others):
        if self.seq == 4:
            self.total = plus(self.pair, tie(self.moving, others))
            self.moving = lax.ppermute(self.total, "seq", [(1, 0), (2, 3)])
        return self.total

    def finish(self):
        if self.seq != 4:
            return self.total
        index = lax.axis_index("seq")
        return jnp.where((index == 0) | (index == 3), self.moving, self.total)

    def waiting(self):
        return [self.moving] if self.seq == 4 else []


def back_kernel(
    gin_0, gin_2, gin_4, gin_6, mid_ref, cot_ref, tok_ref, att_ref, proj_ref, prob_ref, wall_ref,
    small_ref, dwr_ref, *rest,
):
    blocks, _, span, width = tok_ref.shape
    length = blocks * span
    gtok_refs, (dwall_ref, acc, acc_small, gatt, gproj) = rest[:blocks], rest[blocks:]
    step = pl.program_id(0)

    @pl.when(step == 0)
    def _():
        acc[...] = jnp.zeros_like(acc)
        acc_small[...] = jnp.zeros_like(acc_small)
        acc_small[:SMALL] = dwr_ref[...]

    gin = sum(ref[...].reshape(length, width).astype(f32) for ref in (gin_0, gin_2, gin_4, gin_6))
    unit_two, inverse_two = unit_norm(mid_ref[...].reshape(length, width))
    acc_small[6:7] += jnp.sum(gin * unit_two, 0, keepdims=True)
    acc_small[7:8] += jnp.sum(gin, 0, keepdims=True)
    grad_middle = cot_ref[...].reshape(length, width).astype(f32) + norm_back(
        gin * small_ref[6:7], unit_two, inverse_two
    )
    branch = grad_middle.astype(bf16)
    acc[:, 3 * width : 4 * width] += mm(att_ref[0], branch, 0, 0)
    gatt[...] = mm(branch, wall_ref[:, 3 * width : 4 * width], 1, 1).astype(bf16)
    lower = lax.broadcasted_iota(jnp.int32, (length, LANES), 1) < HEAD_DIM
    zero = jnp.zeros((length, LANES), bf16)
    scale = HEAD_DIM**-0.5

    def score_grad(weights, grad_weights):
        weights = weights.astype(f32)
        product = weights * grad_weights
        return (product - weights * jnp.sum(product, -1, keepdims=True)).astype(bf16)

    for pair in range(width // LANES):
        places = [slice((3 * pair + n) * LANES, (3 * pair + n + 1) * LANES) for n in range(3)]
        first, second, third = (proj_ref[0, :, place] for place in places)
        first_r, second_r, third_r = half_turn(first), half_turn(second), half_turn(third)
        grad = gatt[:, pair * LANES : (pair + 1) * LANES]
        weights_a, weights_b = prob_ref[0, 2 * pair], prob_ref[0, 2 * pair + 1]
        ds_a = score_grad(weights_a, mm(jnp.where(lower, grad, zero), second, 1, 1))
        ds_b = score_grad(weights_b, mm(jnp.where(lower, zero, grad), third, 1, 1))
        gproj[:, places[0]] = (
            jnp.where(lower, mm(ds_a, first_r), mm(ds_a, first_r, 0, 0)) * scale
        ).astype(bf16)
        gproj[:, places[1]] = jnp.where(
            lower, mm(weights_a, grad, 0, 0), mm(ds_b, third_r) * scale
        ).astype(bf16)
        gproj[:, places[2]] = jnp.where(
            lower, mm(ds_b, second_r, 0, 0) * scale, mm(weights_b, grad, 0, 0)
        ).astype(bf16)
    unit_one, inverse_one = unit_norm(tok_ref[...].reshape(length, width).astype(f32))
    one = (unit_one * small_ref[4:5] + small_ref[5:6]).astype(bf16)
    grad_one = mm(gproj[...], wall_ref[:, : 3 * width], 1, 1)
    acc_small[4:5] += jnp.sum(grad_one * unit_one, 0, keepdims=True)
    acc_small[5:6] += jnp.sum(grad_one, 0, keepdims=True)
    grad_tok = grad_middle + norm_back(grad_one * small_ref[4:5], unit_one, inverse_one)
    for k, ref in enumerate(gtok_refs):
        ref[0] = grad_tok[k * span : (k + 1) * span].astype(bf16)
    acc[:, : 3 * width] += mm(one, gproj[...], 0, 0)

    @pl.when(step == pl.num_programs(0) - 1)
    def _():
        dwall_ref[:, : 4 * width] = acc[...].astype(bf16)
        dwall_ref[:, 4 * width :] = acc_small[...].T.astype(bf16)


def back(gins, middle, cot, tok, att, proj, prob, wall, small, dwr):
    blocks, images, span, width = tok.shape
    length = blocks * span
    heads = width // HEAD_DIM
    split = pl.BlockSpec((blocks, 1, span, width), lambda i: (0, i, 0, 0))
    whole = lambda a: pl.BlockSpec(a.shape, lambda i: (0,) * len(a.shape))
    return pl.pallas_call(
        back_kernel,
        grid=(images,),
        in_specs=[split] * 7
        + [
            pl.BlockSpec((1, length, width), lambda i: (i, 0, 0)),
            pl.BlockSpec((1, length, 3 * width), lambda i: (i, 0, 0)),
            pl.BlockSpec((1, heads, length, length), lambda i: (i, 0, 0, 0)),
            whole(wall),
            whole(small),
            whole(dwr),
        ],
        out_specs=[pl.BlockSpec((1, span, width), lambda i: (i, 0, 0))] * blocks + [whole(wall)],
        out_shape=[jax.ShapeDtypeStruct((images, span, width), bf16)] * blocks
        + [jax.ShapeDtypeStruct(wall.shape, bf16)],
        scratch_shapes=[
            pltpu.VMEM((width, 4 * width), f32),
            pltpu.VMEM((LANES, width), f32),
            pltpu.VMEM((length, width), bf16),
            pltpu.VMEM((length, 3 * width), bf16),
        ],
        compiler_params=pltpu.CompilerParams(vmem_limit_bytes=VMEM_BYTES),
        cost_estimate=true_cost(10 * images * length * width * (4 * width + 3 * length)),
        name="back",
    )(*gins, middle, cot, tok, att, proj, prob, wall, small, dwr)


def kept_pairs(route_rows, token_live, order_rows, expert_count, capacity):
    labels = jnp.arange(expert_count, dtype=jnp.int32)
    alive = token_live > 0
    first_hot = ((route_rows[:, 0:1] == labels) & alive[:, None]).astype(bf16)
    second_hot = ((route_rows[:, 1:2] == labels) & alive[:, None]).astype(bf16)
    earlier = (order_rows[None, :] < order_rows[:, None]).astype(bf16)
    ahead = mm(earlier, jnp.concatenate([first_hot, second_hot], 1))
    ahead_first = ahead[:, :expert_count]
    ahead_second = ahead[:, expert_count:] + jnp.sum(first_hot.astype(f32), 0)
    return jnp.where(ahead_first < capacity, first_hot, 0) + jnp.where(
        ahead_second < capacity, second_hot, 0
    )


def local(
    fsdp,
    seq,
    tokens,
    ln1_gain,
    ln1_bias,
    w_qkv,
    w_out,
    ln2_gain,
    ln2_bias,
    w_router,
    w_in,
    w_down,
    padding,
    routes,
    priority,
    cotangent,
):
    images, span, width = tokens.shape
    expert_count, shard_rows = w_in.shape[0], w_in.shape[1]
    rows = images * span
    own = images // seq
    length = seq * span
    capacity = (2 * rows + expert_count - 1) // expert_count
    outer = fsdp // 8
    if outer > 1:
        outer_groups = [[o * 8 + n for o in range(outer)] for n in range(8)]
    spread = functools.partial(flip, fsdp=fsdp)
    seq_index = lax.axis_index("seq")
    place = lax.axis_index("fsdp") if outer == 1 else jnp.int32(0)
    place = place.astype(jnp.int32).reshape(1)

    def picked(array, k):
        return lax.dynamic_index_in_dim(array, seq_index ^ k, 0, keepdims=False)

    tokens = tokens.reshape(seq, own * span, width)
    tok = jnp.stack(exchange([picked(tokens, k) for k in range(seq)]))
    tok = tok.reshape(seq, own, span, width)

    columns = jnp.concatenate(
        [w_router] + [v[:, None] for v in (ln1_gain, ln1_bias, ln2_gain, ln2_bias)], 1
    )
    columns = jnp.pad(columns, ((0, 0), (0, LANES - columns.shape[1])))
    shard = jnp.concatenate([w_qkv, w_out, columns], 1)
    if outer == 1:
        cut = width // 16
        from_x, from_y = spread(shard, bits=2), spread(shard, bits=4)
        from_x, from_y = tie((from_x, from_y), tok)
        near = [(0, 0, shard), (2, 0, from_x), (4, 0, from_y)]
        far = [
            (6, 0, spread(from_x[:cut], bits=4)),
            (6, cut, spread(from_y[cut:], bits=2)),
        ]
        near += [(r + 1, skip, spread(a, bits=1)) for r, skip, a in near]
    else:
        full = lax.all_gather(shard, "fsdp", axis=0, tiled=True)
        from_x = from_y = full
        near, far = [(n, 0, full[n * (width // 8) : (n + 1) * (width // 8)]) for n in range(8)], []

    mine = lax.dynamic_slice_in_dim(padding, seq_index * own, own, 0).reshape(own, seq, span)
    mine = jnp.stack(relative([mine[:, b] for b in range(seq)], seq_index))
    vis = jnp.where(mine > 0, 0.0, neg_fill).astype(f32)
    vis = jnp.swapaxes(vis, 0, 1).reshape(own, 1, length)
    live = lax.dynamic_slice_in_dim(padding, seq_index * span, span, 1)
    kept = kept_pairs(
        routes.reshape(rows, 2), live.reshape(rows), priority.reshape(rows), expert_count, capacity
    )
    kept = jnp.swapaxes(kept.reshape(seq, own * span, expert_count), 1, 2)
    kept = jnp.pad(
        kept, ((0, 0), (0, MASK_ROWS - expert_count), (0, width - own * span))
    ).astype(bf16)
    cot = cotangent * live[:, :, None].astype(bf16)
    packed = jnp.concatenate([cot.reshape(seq, own * span, width), kept], 1)
    packed = tie(packed, tok, from_x, from_y, vis, mine)
    packed = jnp.stack(exchange([picked(packed, k) for k in range(seq)]))
    late = tie([a for _, _, a in far], packed)
    far += [(r + 1, skip, spread(a, bits=1)) for (r, skip, _), a in zip(far, late)]
    offsets = [(r, skip) for r, skip, _ in near + far]
    pieces = [a for _, _, a in near + far]
    cot_x, cot_y = spread(packed, bits=2), spread(packed, bits=4)
    half = seq // 2
    cot_far = [spread(cot_x[:half], bits=4), spread(cot_y[half:], bits=2)]

    win, wdn = w_in, w_down
    if outer > 1:
        win = lax.all_gather(win, "fsdp", axis=1, tiled=True, axis_index_groups=outer_groups)
        wdn = lax.all_gather(wdn, "fsdp", axis=1, tiled=True, axis_index_groups=outer_groups)
    win, wdn = tie((win, wdn), pieces)
    weights = [win, spread(win, bits=1), wdn, spread(wdn, bits=1)]

    middle, two, proj, att, prob, wall, wr, small = front(tok, pieces, offsets, vis, place)
    two = two.reshape(seq, own * span, width)
    two_far = [[spread(two, bits=bits)] for bits in (2, 4, 6)]

    (dw,), dwr, out_0, gin_0 = experts_call(
        [[two]], [[packed]], weights, wr, None, "experts_own", lambda flops: SHORT
    )
    cots = [[cot_x], [cot_y], cot_far]
    (*left, dw_kept, dw_sent), dwr, outs, gins = experts_call(
        two_far, cots, weights, wr, [dwr, dw], "experts_far", true_cost
    )
    arrived = [spread(a, bits=bits) for a, bits in zip(gins, (2, 4, 6))]

    def finished(dw_kept, dw_sent):
        raw = plus(dw_kept, spread(dw_sent, bits=1))
        if outer > 1:
            raw = lax.psum_scatter(
                raw, "fsdp", scatter_dimension=2, tiled=True, axis_index_groups=outer_groups
            )
        return lax.optimization_barrier([raw[n : n + 1] for n in range(raw.shape[0])])

    first = Line(seq, finished(dw_kept, dw_sent)[0]).inwards()
    left, dw = tie((left, dw), first.raw)
    parts = grads_call(two_far, cots, left, dw, 1, expert_count - 1)
    ready = first.across(arrived)
    lines = [Line(seq, raw) for raw in finished(*tie(parts, ready, arrived))]
    lines[0].inwards()
    gins = gin_0 + tie(arrived, ready, [line.raw for line in lines])
    lines = [first] + lines

    shape4 = (seq, own, span, width)
    outs = [spread(a, bits=bits) for a, bits in zip(tie(outs, arrived), (2, 4, 6))]
    *grad_tok, dense = back(
        [a.reshape(shape4) for a in gins],
        middle,
        packed[:, : own * span].reshape(shape4),
        tok,
        att,
        proj,
        prob,
        wall,
        small,
        dwr,
    )
    flying = (outs, lines[0].waiting(), lines[1].waiting())
    dense = tie(dense, flying)
    dense = lax.psum_scatter(dense, "fsdp", scatter_dimension=0, tiled=True)
    lines[2].raw, lines[3].raw = tie((lines[2].raw, lines[3].raw), grad_tok)
    lines[2].inwards()
    ready = lines[1].across(grad_tok, flying[1:])
    ready = lines[3].inwards_with(lines[0], ready, flying)
    ready = lines[2].across(ready)
    ready = lines[1].outwards(ready)
    ready = lines[3].across(ready)
    ready = lines[2].outwards(ready, lines[1].waiting())
    dense_line = Line(seq, tie(dense, ready)).inwards()
    ready = lines[3].outwards(dense_line.raw)

    ready = dense_line.across(ready)
    outs, grad_tok = tie((outs, grad_tok), ready)
    outs = [a.reshape(shape4) for a in out_0 + outs]
    home = []
    for k in range(seq):
        alive = mine[k][:, :, None].astype(f32)
        combined = sum(a[k].astype(f32) for a in outs)
        home.append(jnp.stack([(alive * (middle[k] + combined)).astype(bf16), grad_tok[k]]))
    home = exchange(home)
    lines[3].hold(dense_line.outwards(ready))
    grads = [line.finish() for line in lines]
    expert_grads = [jnp.concatenate([g[:, n] for g in grads], 0).astype(f32) for n in range(2)]
    home = relative(tie(home, expert_grads), seq_index)
    outputs, grad_tokens = (
        jnp.concatenate([a[n] for a in home], 0).reshape(images, span, width) for n in range(2)
    )
    dense = dense_line.finish().astype(f32)
    tail = dense[:, 4 * width :]
    return (
        outputs,
        grad_tokens,
        tail[:, 4],
        tail[:, 5],
        dense[:, : 3 * width],
        dense[:, 3 * width : 4 * width],
        tail[:, 6],
        tail[:, 7],
        tail[:, :expert_count],
        expert_grads[0],
        expert_grads[1],
    )


def solution(mesh):
    rows = P("fsdp", "seq", None)
    in_specs = (
        rows,
        P("fsdp"),
        P("fsdp"),
        P("fsdp", None),
        P("fsdp", None),
        P("fsdp"),
        P("fsdp"),
        P("fsdp", None),
        P(None, "fsdp", None),
        P(None, "fsdp", None),
        P("fsdp", None),
        rows,
        P("fsdp", "seq"),
        rows,
    )
    out_specs = (
        rows,
        rows,
        P("fsdp"),
        P("fsdp"),
        P("fsdp", None),
        P("fsdp", None),
        P("fsdp"),
        P("fsdp"),
        P("fsdp", None),
        P(None, "fsdp", None),
        P(None, "fsdp", None),
    )
    return jax.shard_map(
        functools.partial(local, mesh.shape["fsdp"], mesh.shape["seq"]),
        mesh=mesh,
        in_specs=in_specs,
        out_specs=out_specs,
        check_vma=False,
    )
```

```python
import functools
import math

import jax
import jax.numpy as jnp
from jax import lax
from jax.experimental import pallas as pl
from jax.experimental.pallas import tpu as pltpu
from jax.sharding import PartitionSpec as P

HEAD_DIM = 64
LANES = 128
MASK_ROWS = 16
SMALL = 8
norm_eps = 1e-06
neg_fill = -1e30
f32 = jnp.float32
bf16 = jnp.bfloat16
VMEM_BYTES = 60 * 1024 * 1024
SHORT = pl.CostEstimate(flops=1000, bytes_accessed=1000, transcendentals=0)


def true_cost(flops):
    return pl.CostEstimate(flops=2 * flops, bytes_accessed=16 * 1024 * 1024, transcendentals=0)


def mm(left, right, left_dim=1, right_dim=0):
    return lax.dot_general(
        left, right, (((left_dim,), (right_dim,)), ((), ())), preferred_element_type=f32
    )


def unit_norm(rows):
    centred = rows - jnp.mean(rows, -1, keepdims=True)
    inverse = lax.rsqrt(jnp.mean(centred * centred, -1, keepdims=True) + norm_eps)
    return centred * inverse, inverse


def norm_back(scaled, unit, inverse):
    return inverse * (
        scaled
        - jnp.mean(scaled, -1, keepdims=True)
        - unit * jnp.mean(scaled * unit, -1, keepdims=True)
    )


def half_turn(tile):
    return pltpu.roll(tile.astype(f32), HEAD_DIM, axis=1).astype(bf16)


def wall_copies(pieces, offsets, place_ref, wall_ref, sems):
    copies = []
    for n, (piece, (r, skip)) in enumerate(zip(pieces, offsets)):
        rows = piece.shape[0]
        shard = wall_ref.shape[0] // 8
        start = pl.multiple_of((place_ref[0] ^ r) * shard + skip, 16)
        copies.append(pltpu.make_async_copy(piece, wall_ref.at[pl.ds(start, rows)], sems.at[n]))
    return copies


def front_kernel(offsets, *refs):
    pieces = refs[: len(offsets)]
    tok_ref, vis_ref, place_ref = refs[len(offsets) : len(offsets) + 3]
    mid_ref, two_ref, proj_ref, att_ref, prob_ref, full_ref, wr_ref, small_ref = refs[
        len(offsets) + 3 : len(offsets) + 11
    ]
    wall_ref, sems, full_sem = refs[len(offsets) + 11 :]
    blocks, _, span, width = tok_ref.shape
    length = blocks * span
    save = pltpu.make_async_copy(wall_ref, full_ref, full_sem)

    @pl.when(pl.program_id(0) == 0)
    def _():
        copies = wall_copies(pieces, offsets, place_ref, wall_ref, sems)
        for copy in copies:
            copy.start()
        for copy in copies:
            copy.wait()
        save.start()
        columns = wall_ref[:, 4 * width :]
        wr_ref[...] = columns
        small_ref[...] = columns.astype(f32).T[:SMALL]

    rows = tok_ref[...].reshape(length, width).astype(f32)
    unit, _ = unit_norm(rows)
    one = (unit * small_ref[4:5] + small_ref[5:6]).astype(bf16)
    proj_ref[0] = mm(one, wall_ref[:, : 3 * width]).astype(bf16)
    lower = lax.broadcasted_iota(jnp.int32, (length, LANES), 1) < HEAD_DIM
    zero = jnp.zeros((length, LANES), bf16)
    bias = vis_ref[0]

    def soften(index, queries, keys):
        scores = mm(queries, keys, 1, 1) * (HEAD_DIM**-0.5) + bias
        shifted = jnp.exp(scores - jnp.max(scores, -1, keepdims=True))
        weights = (shifted / jnp.sum(shifted, -1, keepdims=True)).astype(bf16)
        prob_ref[0, index] = weights
        return weights

    for pair in range(width // LANES):
        first, second, third = (
            proj_ref[0, :, (3 * pair + n) * LANES : (3 * pair + n + 1) * LANES] for n in range(3)
        )
        weights_a = soften(2 * pair, jnp.where(lower, first, zero), half_turn(first))
        weights_b = soften(2 * pair + 1, jnp.where(lower, zero, second), half_turn(third))
        both = jnp.where(lower, mm(weights_a, second), mm(weights_b, third))
        att_ref[0, :, pair * LANES : (pair + 1) * LANES] = both.astype(bf16)
    middle = rows + mm(att_ref[0], wall_ref[:, 3 * width : 4 * width])
    mid_ref[...] = middle.reshape(mid_ref.shape)
    unit, _ = unit_norm(middle)
    two_ref[...] = (unit * small_ref[6:7] + small_ref[7:8]).astype(bf16).reshape(two_ref.shape)

    @pl.when(pl.program_id(0) == pl.num_programs(0) - 1)
    def _():
        save.wait()


def front(tok, pieces, offsets, vis, place):
    blocks, images, span, width = tok.shape
    length = blocks * span
    heads = width // HEAD_DIM
    split = pl.BlockSpec((blocks, 1, span, width), lambda i: (0, i, 0, 0))
    anywhere = pl.BlockSpec(memory_space=pl.ANY)
    columns = pieces[0].shape[1]
    return pl.pallas_call(
        functools.partial(front_kernel, offsets),
        grid=(images,),
        in_specs=[anywhere] * len(pieces)
        + [
            split,
            pl.BlockSpec((1, 1, length), lambda i: (i, 0, 0)),
            pl.BlockSpec(memory_space=pltpu.SMEM),
        ],
        out_specs=[
            split,
            split,
            pl.BlockSpec((1, length, 3 * width), lambda i: (i, 0, 0)),
            pl.BlockSpec((1, length, width), lambda i: (i, 0, 0)),
            pl.BlockSpec((1, heads, length, length), lambda i: (i, 0, 0, 0)),
            anywhere,
            pl.BlockSpec((width, LANES), lambda i: (0, 0)),
            pl.BlockSpec((SMALL, width), lambda i: (0, 0)),
        ],
        out_shape=[
            jax.ShapeDtypeStruct(tok.shape, f32),
            jax.ShapeDtypeStruct(tok.shape, bf16),
            jax.ShapeDtypeStruct((images, length, 3 * width), bf16),
            jax.ShapeDtypeStruct((images, length, width), bf16),
            jax.ShapeDtypeStruct((images, heads, length, length), bf16),
            jax.ShapeDtypeStruct((width, columns), bf16),
            jax.ShapeDtypeStruct((width, LANES), bf16),
            jax.ShapeDtypeStruct((SMALL, width), f32),
        ],
        scratch_shapes=[
            pltpu.VMEM((width, columns), bf16),
            pltpu.SemaphoreType.DMA((len(pieces),)),
            pltpu.SemaphoreType.DMA(()),
        ],
        compiler_params=pltpu.CompilerParams(vmem_limit_bytes=VMEM_BYTES),
        cost_estimate=SHORT,
        name="front",
    )(*pieces, tok, vis, place)


def gelu_parts(pre):
    bell = jnp.exp2(pre * pre * (-0.5 * math.log2(math.e)))
    frac = 1.0 / (1.0 + (0.3275911 * math.sqrt(0.5)) * jnp.abs(pre))
    a5, a4, a3, a2, a1 = (
        0.5 * c for c in (1.061405429, -1.453152027, 1.421413741, -0.284496736, 0.254829592)
    )
    tail = frac * (a1 + frac * (a2 + frac * (a3 + frac * (a4 + frac * a5)))) * bell
    cumulative = jnp.where(pre >= 0, 1.0 - tail, tail)
    return pre * cumulative, cumulative + (pre * 0.3989422804014327) * bell


def expert_kernel(plan, *refs):
    refs = list(refs)

    def take(number):
        taken, refs[:] = refs[:number], refs[number:]
        return taken

    groups, experts, opening = plan["groups"], plan["experts"], plan["opening"]
    two_parts = [take(n) for n in plan["two"]]
    cot_parts = [take(n) for n in plan["cot"]]
    weights = take(4)
    (wr_ref,) = take(1)
    dwr_carried, own_ref = (None, None) if opening else take(2)
    left = take(1 if opening else 2)
    early = [] if opening else take(2)
    (dwr_ref,) = take(1)
    results = take(2 * groups)
    two_buf, cot_buf, sems, win_buf, wdn_buf, weight_sems, gated_buf, grad_buf = take(8)
    stage, store_sems, left_sems = take(3)
    acc, own_buf, early_buf, own_sem, early_sems = [None] * 5 if opening else take(5)
    _, blocks, span, width = two_buf.shape
    rows = blocks * span
    hidden = win_buf.shape[0] // experts
    shard = hidden // 2
    group = pl.program_id(0)
    slot = group % gated_buf.shape[0]
    lane = lax.broadcasted_iota(jnp.int32, (rows, LANES), 1)

    copies = []
    for k in range(groups):
        some = []
        for parts, buffer in ((two_parts[k], two_buf), (cot_parts[k], cot_buf)):
            at = 0
            for part in parts:
                size = part.shape[0]
                some.append((part, buffer.at[k, pl.ds(at, size)]))
                at += size
        copies.append(
            [pltpu.make_async_copy(s, t, sems.at[k, n]) for n, (s, t) in enumerate(some)]
        )
    fetches = [
        pltpu.make_async_copy(
            ref.at[e],
            (win_buf, wdn_buf)[n // 2].at[pl.ds(e * hidden + (n % 2) * shard, shard)],
            weight_sems.at[e, n],
        )
        for e in range(experts)
        for n, ref in enumerate(weights)
    ]
    stores = [
        [
            pltpu.make_async_copy(stage.at[n], results[n * groups + k], store_sems.at[n])
            for n in range(2)
        ]
        for k in range(groups)
    ]
    if not opening:
        for k in range(groups):
            for n, buffer in enumerate((gated_buf, grad_buf)):
                place = k % buffer.shape[0]
                stores[k].append(
                    pltpu.make_async_copy(
                        buffer.at[place, :, pl.ds(hidden, (experts - 1) * hidden)],
                        left[n].at[pl.ds(k * rows, rows)],
                        left_sems.at[place, n],
                    )
                )

    @pl.when(group == 0)
    def _():
        for copy in copies[0] + fetches:
            copy.start()
        for some in copies[1:]:
            for copy in some:
                copy.start()
        if not opening:
            pltpu.make_async_copy(own_ref.at[0], own_buf, own_sem).start()
        dwr_ref[...] = jnp.zeros_like(dwr_ref) if opening else dwr_carried[...]
        for copy in fetches:
            copy.wait()

    for k, some in enumerate(copies):

        @pl.when(group == k)
        def _(k=k, some=some):
            for copy in some:
                copy.wait()
            if k > 0:
                for store in stores[k - 1][:2]:
                    store.wait()
            if k > 1:
                for store in stores[k - 2][2:]:
                    store.wait()

    two = two_buf[group].reshape(rows, width)
    cot = cot_buf[group, :, :span, :].reshape(rows, width)
    chosen = (
        lax.broadcasted_iota(jnp.int32, (MASK_ROWS, LANES), 0)
        == lax.broadcasted_iota(jnp.int32, (MASK_ROWS, LANES), 1)
    ).astype(bf16)
    logits = jnp.where(lane < experts, mm(two, wr_ref[...]), neg_fill)
    shifted = jnp.exp(logits - jnp.max(logits, -1, keepdims=True))
    probs = shifted / jnp.sum(shifted, -1, keepdims=True)
    kept = jnp.concatenate(
        [
            mm(cot_buf[group, b, span : span + MASK_ROWS, :span], chosen, 0, 0)
            for b in range(blocks)
        ],
        0,
    )
    grad_gate = jnp.zeros((rows, LANES), f32)
    gates = probs * kept
    out_rows = gin_rows = None
    for e in range(experts):
        at = slice(e * hidden, (e + 1) * hidden)
        win, wdn = win_buf[at], wdn_buf[at]
        pre = mm(two, win, 1, 1)
        back_rows = mm(cot, wdn, 1, 1)
        gate = gates[:, e : e + 1]
        hidden_rows, slope = gelu_parts(pre)
        product = jnp.sum(hidden_rows * back_rows, -1, keepdims=True)
        grad_gate = jnp.where(lane == e, product, grad_gate)
        gated = (hidden_rows * gate).astype(bf16)
        grad_pre = (slope * back_rows * gate).astype(bf16)
        if opening:
            gated_buf[e, 1] = mm(gated, cot, 0, 0).astype(bf16)
            gated_buf[e, 0] = mm(grad_pre, two, 0, 0).astype(bf16)
        elif e > 0:
            gated_buf[slot, :, at] = gated
            grad_buf[slot, :, at] = grad_pre
        else:
            for n, fresh in enumerate((mm(grad_pre, two, 0, 0), mm(gated, cot, 0, 0))):
                acc[n] = jnp.where(group == 0, 0.0, acc[n]) + fresh
        out_part, gin_part = mm(gated, wdn), mm(grad_pre, win)
        out_rows = out_part if e == 0 else out_rows + out_part
        gin_rows = gin_part if e == 0 else gin_rows + gin_part
    grad_gate = grad_gate * kept
    grad_logits = probs * (grad_gate - jnp.sum(probs * grad_gate, -1, keepdims=True))
    grad_logits = grad_logits.astype(bf16)
    dwr_ref[...] += mm(grad_logits, two, 0, 0)[:SMALL]
    gin_rows = gin_rows + mm(grad_logits, wr_ref[...], 1, 1)
    stage[0] = out_rows.astype(bf16).reshape(blocks, span, width)
    stage[1] = gin_rows.astype(bf16).reshape(blocks, span, width)
    for k in range(groups):

        @pl.when(group == k)
        def _(k=k):
            for store in stores[k]:
                store.start()

    @pl.when(group == groups - 1)
    def _():
        if opening:
            copy = pltpu.make_async_copy(gated_buf, left[0], left_sems.at[0, 0])
            copy.start()
            copy.wait()
        else:
            pltpu.make_async_copy(own_ref.at[0], own_buf, own_sem).wait()
            early_copies = []
            for n in range(2):
                early_buf[n] = (acc[n] + own_buf[n].astype(f32)).astype(bf16)
                for m, target in enumerate(early):
                    copy = pltpu.make_async_copy(
                        early_buf.at[n, pl.ds(m * shard, shard)],
                        target.at[0, n],
                        early_sems.at[n, m],
                    )
                    copy.start()
                    early_copies.append(copy)
            for copy in early_copies:
                copy.wait()
        for k in (groups - 1,) if groups == 1 else (groups - 2, groups - 1):
            for store in stores[k][0 if k == groups - 1 else 2 :]:
                store.wait()


def experts_call(two, cot, weights, wr, carried, name, cost):
    groups = len(two)
    opening = groups == 1
    experts, shard, width = weights[0].shape
    hidden = 2 * shard
    blocks = sum(a.shape[0] for a in two[0])
    span = two[0][0].shape[1]
    rows = blocks * span
    plan = dict(
        groups=groups,
        experts=experts,
        opening=opening,
        two=[len(parts) for parts in two],
        cot=[len(parts) for parts in cot],
    )
    anywhere = pl.BlockSpec(memory_space=pl.ANY)
    once = lambda a: pl.BlockSpec(
        a.shape, lambda g: (0,) * len(a.shape), pipeline_mode=pl.Buffered(1)
    )
    result = jax.ShapeDtypeStruct((blocks, span, width), bf16)
    little = jax.ShapeDtypeStruct((SMALL, width), f32)
    if opening:
        left = [jax.ShapeDtypeStruct((experts, 2, hidden, width), bf16)]
        buffers = [pltpu.VMEM(left[0].shape, bf16), pltpu.VMEM((16, LANES), bf16)]
    else:
        left = [jax.ShapeDtypeStruct((groups * rows, (experts - 1) * hidden), bf16)] * 2
        left += [jax.ShapeDtypeStruct((1, 2, shard, width), bf16)] * 2
        buffers = [pltpu.VMEM((2, rows, experts * hidden), bf16)] * 2
    pieces = [a for parts in two for a in parts] + [a for parts in cot for a in parts]
    outs = pl.pallas_call(
        functools.partial(expert_kernel, plan),
        grid=(groups,),
        in_specs=[anywhere] * (len(pieces) + 4)
        + [once(wr)]
        + ([] if opening else [once(little), anywhere]),
        out_specs=[anywhere] * len(left) + [once(little)] + [anywhere] * (2 * groups),
        out_shape=left + [little] + [result] * (2 * groups),
        scratch_shapes=[
            pltpu.VMEM((groups, blocks, span, width), bf16),
            pltpu.VMEM((groups, blocks, span + MASK_ROWS, width), bf16),
            pltpu.SemaphoreType.DMA((groups, 4)),
            pltpu.VMEM((experts * hidden, width), bf16),
            pltpu.VMEM((experts * hidden, width), bf16),
            pltpu.SemaphoreType.DMA((experts, 4)),
            *buffers,
            pltpu.VMEM((2, blocks, span, width), bf16),
            pltpu.SemaphoreType.DMA((2,)),
            pltpu.SemaphoreType.DMA((2, 2)),
        ]
        + (
            []
            if opening
            else [
                pltpu.VMEM((2, hidden, width), f32),
                pltpu.VMEM((2, hidden, width), bf16),
                pltpu.VMEM((2, hidden, width), bf16),
                pltpu.SemaphoreType.DMA(()),
                pltpu.SemaphoreType.DMA((2, 2)),
            ]
        ),
        compiler_params=pltpu.CompilerParams(vmem_limit_bytes=VMEM_BYTES),
        cost_estimate=cost(10 * groups * rows * width * hidden * experts),
        name=name,
    )(*pieces, *weights, wr, *(carried or []))
    left, (dwr, *outs) = list(outs[: len(left)]), outs[len(left) :]
    return left, dwr, outs[:groups], outs[groups:]


def grads_kernel(plan, *refs):
    refs = list(refs)

    def take(number):
        taken, refs[:] = refs[:number], refs[number:]
        return taken

    groups = len(plan["two"])
    two_parts = [take(n) for n in plan["two"]]
    cot_parts = [take(n) for n in plan["cot"]]
    gated_ref, grad_ref, own_ref, kept_ref, sent_ref = take(5)
    two_buf, cot_buf, cot_rows, sems = refs
    _, blocks, span, width = two_buf.shape
    rows = blocks * span
    copies = []
    for k in range(groups):
        at = 0
        for n, part in enumerate(two_parts[k]):
            size = part.shape[0]
            copies.append(
                pltpu.make_async_copy(part, two_buf.at[k, pl.ds(at, size)], sems.at[k, n])
            )
            at += size
        at = 0
        for n, part in enumerate(cot_parts[k]):
            size = part.shape[0]
            copies.append(
                pltpu.make_async_copy(
                    part, cot_buf.at[k, pl.ds(at, size)], sems.at[k, 2 + n]
                )
            )
            at += size

    @pl.when(pl.program_id(0) == 0)
    def _():
        for copy in copies:
            copy.start()
        for copy in copies:
            copy.wait()
        for k in range(groups):
            cot_rows[k * rows : (k + 1) * rows] = cot_buf[k, :, :span, :].reshape(rows, width)

    half = own_ref.shape[2] // 2
    two = two_buf[...].reshape(groups * rows, width)
    for n, (left_ref, right) in enumerate(((grad_ref, two), (gated_ref, cot_rows[...]))):
        total = (own_ref[0, n].astype(f32) + mm(left_ref[...], right, 0, 0)).astype(bf16)
        kept_ref[0, n] = total[:half]
        sent_ref[0, n] = total[half:]


def grads_call(two, cot, left, own, first, many):
    groups = len(two)
    blocks = sum(a.shape[0] for a in two[0])
    _, span, width = two[0][0].shape
    rows = blocks * span
    hidden = own.shape[2]
    anywhere = pl.BlockSpec(memory_space=pl.ANY)
    pieces = [a for parts in two for a in parts] + [a for parts in cot for a in parts]
    columns = pl.BlockSpec((groups * rows, hidden), lambda e: (0, e))
    part = jax.ShapeDtypeStruct((many, 2, hidden // 2, width), bf16)
    part_spec = pl.BlockSpec((1, 2, hidden // 2, width), lambda e: (e, 0, 0, 0))
    plan = dict(two=[len(parts) for parts in two], cot=[len(parts) for parts in cot])
    return pl.pallas_call(
        functools.partial(grads_kernel, plan),
        grid=(many,),
        in_specs=[anywhere] * len(pieces)
        + [columns, columns, pl.BlockSpec((1, 2, hidden, width), lambda e: (e + first, 0, 0, 0))],
        out_specs=[part_spec, part_spec],
        out_shape=[part, part],
        scratch_shapes=[
            pltpu.VMEM((groups, blocks, span, width), bf16),
            pltpu.VMEM((groups, blocks, span + MASK_ROWS, width), bf16),
            pltpu.VMEM((groups * rows, width), bf16),
            pltpu.SemaphoreType.DMA((groups, 4)),
        ],
        compiler_params=pltpu.CompilerParams(vmem_limit_bytes=VMEM_BYTES),
        cost_estimate=true_cost(8 * groups * rows * width * hidden * many),
        name="expert_grads",
    )(*pieces, *left, own)


def flip(array, fsdp, bits):
    return lax.ppermute(array, "fsdp", [(n, n ^ bits) for n in range(fsdp)])


def tie(value, *others):
    return lax.optimization_barrier((value, others))[0]


def exchange(pieces):
    count = len(pieces)
    return [pieces[0]] + [
        lax.ppermute(pieces[k], "seq", [(n, n ^ k) for n in range(count)]) for k in range(1, count)
    ]


def relative(parts, index):
    count, bit = len(parts), 1
    while bit < count:
        swap = (index & bit) > 0
        parts = [jnp.where(swap, parts[k ^ bit], parts[k]) for k in range(count)]
        bit *= 2
    return parts


def plus(*arrays):
    return sum(a.astype(f32) for a in arrays).astype(bf16)


class Line:
    def __init__(self, seq, raw):
        self.seq, self.raw = seq, raw
        if seq != 4:
            self.total = lax.psum(raw, "seq")

    def inwards(self):
        if self.seq == 4:
            self.moving = lax.ppermute(self.raw, "seq", [(0, 1), (3, 2)])
        return self

    def inwards_with(self, other, *others):
        if self.seq != 4:
            return self.raw
        other.total = plus(other.pair, tie(other.moving, others))
        index = lax.axis_index("seq")
        both = jnp.where((index == 0) | (index == 3), self.raw, other.total)
        self.moving = lax.ppermute(both, "seq", [(0, 1), (1, 0), (2, 3), (3, 2)])
        other.moving = self.moving
        return both

    def hold(self, others):
        if self.seq == 4:
            self.moving = tie(self.moving, others)

    def across(self, *others):
        if self.seq == 4:
            self.pair = plus(self.raw, tie(self.moving, others))
            self.moving = lax.ppermute(self.pair, "seq", [(1, 2), (2, 1)])
            return self.pair
        return self.raw

    def outwards(self, *others):
        if self.seq == 4:
            self.total = plus(self.pair, tie(self.moving, others))
            self.moving = lax.ppermute(self.total, "seq", [(1, 0), (2, 3)])
        return self.total

    def finish(self):
        if self.seq != 4:
            return self.total
        index = lax.axis_index("seq")
        return jnp.where((index == 0) | (index == 3), self.moving, self.total)

    def waiting(self):
        return [self.moving] if self.seq == 4 else []


def back_kernel(
    gin_0, gin_2, gin_4, gin_6, mid_ref, cot_ref, tok_ref, att_ref, proj_ref, prob_ref, wall_ref,
    small_ref, dwr_ref, *rest,
):
    blocks, _, span, width = tok_ref.shape
    length = blocks * span
    gtok_refs, (dwall_ref, acc, acc_small, gatt, gproj) = rest[:blocks], rest[blocks:]
    step = pl.program_id(0)

    @pl.when(step == 0)
    def _():
        acc[...] = jnp.zeros_like(acc)
        acc_small[...] = jnp.zeros_like(acc_small)
        acc_small[:SMALL] = dwr_ref[...]

    gin = sum(ref[...].reshape(length, width).astype(f32) for ref in (gin_0, gin_2, gin_4, gin_6))
    unit_two, inverse_two = unit_norm(mid_ref[...].reshape(length, width))
    acc_small[6:7] += jnp.sum(gin * unit_two, 0, keepdims=True)
    acc_small[7:8] += jnp.sum(gin, 0, keepdims=True)
    grad_middle = cot_ref[...].reshape(length, width).astype(f32) + norm_back(
        gin * small_ref[6:7], unit_two, inverse_two
    )
    branch = grad_middle.astype(bf16)
    acc[:, 3 * width : 4 * width] += mm(att_ref[0], branch, 0, 0)
    gatt[...] = mm(branch, wall_ref[:, 3 * width : 4 * width], 1, 1).astype(bf16)
    lower = lax.broadcasted_iota(jnp.int32, (length, LANES), 1) < HEAD_DIM
    zero = jnp.zeros((length, LANES), bf16)
    scale = HEAD_DIM**-0.5

    def score_grad(weights, grad_weights):
        weights = weights.astype(f32)
        product = weights * grad_weights
        return (product - weights * jnp.sum(product, -1, keepdims=True)).astype(bf16)

    for pair in range(width // LANES):
        places = [slice((3 * pair + n) * LANES, (3 * pair + n + 1) * LANES) for n in range(3)]
        first, second, third = (proj_ref[0, :, place] for place in places)
        first_r, second_r, third_r = half_turn(first), half_turn(second), half_turn(third)
        grad = gatt[:, pair * LANES : (pair + 1) * LANES]
        weights_a, weights_b = prob_ref[0, 2 * pair], prob_ref[0, 2 * pair + 1]
        ds_a = score_grad(weights_a, mm(jnp.where(lower, grad, zero), second, 1, 1))
        ds_b = score_grad(weights_b, mm(jnp.where(lower, zero, grad), third, 1, 1))
        gproj[:, places[0]] = (
            jnp.where(lower, mm(ds_a, first_r), mm(ds_a, first_r, 0, 0)) * scale
        ).astype(bf16)
        gproj[:, places[1]] = jnp.where(
            lower, mm(weights_a, grad, 0, 0), mm(ds_b, third_r) * scale
        ).astype(bf16)
        gproj[:, places[2]] = jnp.where(
            lower, mm(ds_b, second_r, 0, 0) * scale, mm(weights_b, grad, 0, 0)
        ).astype(bf16)
    unit_one, inverse_one = unit_norm(tok_ref[...].reshape(length, width).astype(f32))
    one = (unit_one * small_ref[4:5] + small_ref[5:6]).astype(bf16)
    grad_one = mm(gproj[...], wall_ref[:, : 3 * width], 1, 1)
    acc_small[4:5] += jnp.sum(grad_one * unit_one, 0, keepdims=True)
    acc_small[5:6] += jnp.sum(grad_one, 0, keepdims=True)
    grad_tok = grad_middle + norm_back(grad_one * small_ref[4:5], unit_one, inverse_one)
    for k, ref in enumerate(gtok_refs):
        ref[0] = grad_tok[k * span : (k + 1) * span].astype(bf16)
    acc[:, : 3 * width] += mm(one, gproj[...], 0, 0)

    @pl.when(step == pl.num_programs(0) - 1)
    def _():
        dwall_ref[:, : 4 * width] = acc[...].astype(bf16)
        dwall_ref[:, 4 * width :] = acc_small[...].T.astype(bf16)


def back(gins, middle, cot, tok, att, proj, prob, wall, small, dwr):
    blocks, images, span, width = tok.shape
    length = blocks * span
    heads = width // HEAD_DIM
    split = pl.BlockSpec((blocks, 1, span, width), lambda i: (0, i, 0, 0))
    whole = lambda a: pl.BlockSpec(a.shape, lambda i: (0,) * len(a.shape))
    return pl.pallas_call(
        back_kernel,
        grid=(images,),
        in_specs=[split] * 7
        + [
            pl.BlockSpec((1, length, width), lambda i: (i, 0, 0)),
            pl.BlockSpec((1, length, 3 * width), lambda i: (i, 0, 0)),
            pl.BlockSpec((1, heads, length, length), lambda i: (i, 0, 0, 0)),
            whole(wall),
            whole(small),
            whole(dwr),
        ],
        out_specs=[pl.BlockSpec((1, span, width), lambda i: (i, 0, 0))] * blocks + [whole(wall)],
        out_shape=[jax.ShapeDtypeStruct((images, span, width), bf16)] * blocks
        + [jax.ShapeDtypeStruct(wall.shape, bf16)],
        scratch_shapes=[
            pltpu.VMEM((width, 4 * width), f32),
            pltpu.VMEM((LANES, width), f32),
            pltpu.VMEM((length, width), bf16),
            pltpu.VMEM((length, 3 * width), bf16),
        ],
        compiler_params=pltpu.CompilerParams(vmem_limit_bytes=VMEM_BYTES),
        cost_estimate=true_cost(10 * images * length * width * (4 * width + 3 * length)),
        name="back",
    )(*gins, middle, cot, tok, att, proj, prob, wall, small, dwr)


def kept_pairs(route_rows, token_live, order_rows, expert_count, capacity):
    labels = jnp.arange(expert_count, dtype=jnp.int32)
    alive = token_live > 0
    first_hot = ((route_rows[:, 0:1] == labels) & alive[:, None]).astype(bf16)
    second_hot = ((route_rows[:, 1:2] == labels) & alive[:, None]).astype(bf16)
    earlier = (order_rows[None, :] < order_rows[:, None]).astype(bf16)
    ahead = mm(earlier, jnp.concatenate([first_hot, second_hot], 1))
    ahead_first = ahead[:, :expert_count]
    ahead_second = ahead[:, expert_count:] + jnp.sum(first_hot.astype(f32), 0)
    return jnp.where(ahead_first < capacity, first_hot, 0) + jnp.where(
        ahead_second < capacity, second_hot, 0
    )


def local(
    fsdp,
    seq,
    tokens,
    ln1_gain,
    ln1_bias,
    w_qkv,
    w_out,
    ln2_gain,
    ln2_bias,
    w_router,
    w_in,
    w_down,
    padding,
    routes,
    priority,
    cotangent,
):
    images, span, width = tokens.shape
    expert_count, shard_rows = w_in.shape[0], w_in.shape[1]
    rows = images * span
    own = images // seq
    length = seq * span
    capacity = (2 * rows + expert_count - 1) // expert_count
    outer = fsdp // 8
    if outer > 1:
        outer_groups = [[o * 8 + n for o in range(outer)] for n in range(8)]
    spread = functools.partial(flip, fsdp=fsdp)
    seq_index = lax.axis_index("seq")
    place = lax.axis_index("fsdp") if outer == 1 else jnp.int32(0)
    place = place.astype(jnp.int32).reshape(1)

    def picked(array, k):
        return lax.dynamic_index_in_dim(array, seq_index ^ k, 0, keepdims=False)

    tokens = tokens.reshape(seq, own * span, width)
    tok = jnp.stack(exchange([picked(tokens, k) for k in range(seq)]))
    tok = tok.reshape(seq, own, span, width)

    columns = jnp.concatenate(
        [w_router] + [v[:, None] for v in (ln1_gain, ln1_bias, ln2_gain, ln2_bias)], 1
    )
    columns = jnp.pad(columns, ((0, 0), (0, LANES - columns.shape[1])))
    shard = jnp.concatenate([w_qkv, w_out, columns], 1)
    if outer == 1:
        cut = width // 16
        from_x, from_y = spread(shard, bits=2), spread(shard, bits=4)
        from_x, from_y = tie((from_x, from_y), tok)
        near = [(0, 0, shard), (2, 0, from_x), (4, 0, from_y)]
        far = [
            (6, 0, spread(from_x[:cut], bits=4)),
            (6, cut, spread(from_y[cut:], bits=2)),
        ]
        near += [(r + 1, skip, spread(a, bits=1)) for r, skip, a in near]
    else:
        full = lax.all_gather(shard, "fsdp", axis=0, tiled=True)
        from_x = from_y = full
        near, far = [(n, 0, full[n * (width // 8) : (n + 1) * (width // 8)]) for n in range(8)], []

    mine = lax.dynamic_slice_in_dim(padding, seq_index * own, own, 0).reshape(own, seq, span)
    mine = jnp.stack(relative([mine[:, b] for b in range(seq)], seq_index))
    vis = jnp.where(mine > 0, 0.0, neg_fill).astype(f32)
    vis = jnp.swapaxes(vis, 0, 1).reshape(own, 1, length)
    live = lax.dynamic_slice_in_dim(padding, seq_index * span, span, 1)
    kept = kept_pairs(
        routes.reshape(rows, 2), live.reshape(rows), priority.reshape(rows), expert_count, capacity
    )
    kept = jnp.swapaxes(kept.reshape(seq, own * span, expert_count), 1, 2)
    kept = jnp.pad(
        kept, ((0, 0), (0, MASK_ROWS - expert_count), (0, width - own * span))
    ).astype(bf16)
    cot = cotangent * live[:, :, None].astype(bf16)
    packed = jnp.concatenate([cot.reshape(seq, own * span, width), kept], 1)
    packed = tie(packed, tok, from_x, from_y, vis, mine)
    packed = jnp.stack(exchange([picked(packed, k) for k in range(seq)]))
    late = tie([a for _, _, a in far], packed)
    far += [(r + 1, skip, spread(a, bits=1)) for (r, skip, _), a in zip(far, late)]
    offsets = [(r, skip) for r, skip, _ in near + far]
    pieces = [a for _, _, a in near + far]
    cot_x, cot_y = spread(packed, bits=2), spread(packed, bits=4)
    half = seq // 2
    cot_far = [spread(cot_x[:half], bits=4), spread(cot_y[half:], bits=2)]

    win, wdn = w_in, w_down
    if outer > 1:
        win = lax.all_gather(win, "fsdp", axis=1, tiled=True, axis_index_groups=outer_groups)
        wdn = lax.all_gather(wdn, "fsdp", axis=1, tiled=True, axis_index_groups=outer_groups)
    win, wdn = tie((win, wdn), pieces)
    weights = [win, spread(win, bits=1), wdn, spread(wdn, bits=1)]

    middle, two, proj, att, prob, wall, wr, small = front(tok, pieces, offsets, vis, place)
    two = two.reshape(seq, own * span, width)
    two_far = [[spread(two, bits=bits)] for bits in (2, 4, 6)]

    (dw,), dwr, out_0, gin_0 = experts_call(
        [[two]], [[packed]], weights, wr, None, "experts_own", lambda flops: SHORT
    )
    cots = [[cot_x], [cot_y], cot_far]
    (*left, dw_kept, dw_sent), dwr, outs, gins = experts_call(
        two_far, cots, weights, wr, [dwr, dw], "experts_far", true_cost
    )
    arrived = [spread(a, bits=bits) for a, bits in zip(gins, (2, 4, 6))]

    def finished(dw_kept, dw_sent):
        raw = plus(dw_kept, spread(dw_sent, bits=1))
        if outer > 1:
            raw = lax.psum_scatter(
                raw, "fsdp", scatter_dimension=2, tiled=True, axis_index_groups=outer_groups
            )
        return lax.optimization_barrier([raw[n : n + 1] for n in range(raw.shape[0])])

    first = Line(seq, finished(dw_kept, dw_sent)[0]).inwards()
    left, dw = tie((left, dw), first.raw)
    parts = grads_call(two_far, cots, left, dw, 1, expert_count - 1)
    ready = first.across(arrived)
    lines = [Line(seq, raw) for raw in finished(*tie(parts, ready, arrived))]
    lines[0].inwards()
    gins = gin_0 + tie(arrived, ready, [line.raw for line in lines])
    lines = [first] + lines

    shape4 = (seq, own, span, width)
    outs = [spread(a, bits=bits) for a, bits in zip(tie(outs, arrived), (2, 4, 6))]
    *grad_tok, dense = back(
        [a.reshape(shape4) for a in gins],
        middle,
        packed[:, : own * span].reshape(shape4),
        tok,
        att,
        proj,
        prob,
        wall,
        small,
        dwr,
    )
    flying = (outs, lines[0].waiting(), lines[1].waiting())
    dense = tie(dense, flying[1:])
    dense = lax.psum_scatter(dense, "fsdp", scatter_dimension=0, tiled=True)
    lines[2].raw, lines[3].raw = tie((lines[2].raw, lines[3].raw), grad_tok)
    lines[2].inwards()
    ready = lines[1].across(grad_tok, flying[1:])
    ready = lines[3].inwards_with(lines[0], ready, flying)
    ready = lines[2].across(ready)
    ready = lines[1].outwards(ready)
    ready = lines[3].across(ready)
    ready = lines[2].outwards(ready, lines[1].waiting())
    dense_line = Line(seq, tie(dense, ready)).inwards()
    ready = lines[3].outwards(dense_line.raw)

    ready = dense_line.across(ready)
    outs, grad_tok = tie((outs, grad_tok), ready)
    outs = [a.reshape(shape4) for a in out_0 + outs]
    home = []
    for k in range(seq):
        alive = mine[k][:, :, None].astype(f32)
        combined = sum(a[k].astype(f32) for a in outs)
        home.append(jnp.stack([(alive * (middle[k] + combined)).astype(bf16), grad_tok[k]]))
    home = exchange(home)
    lines[3].hold(dense_line.outwards(ready))
    grads = [line.finish() for line in lines]
    expert_grads = [jnp.concatenate([g[:, n] for g in grads], 0).astype(f32) for n in range(2)]
    home = relative(tie(home, expert_grads), seq_index)
    outputs, grad_tokens = (
        jnp.concatenate([a[n] for a in home], 0).reshape(images, span, width) for n in range(2)
    )
    dense = dense_line.finish().astype(f32)
    tail = dense[:, 4 * width :]
    return (
        outputs,
        grad_tokens,
        tail[:, 4],
        tail[:, 5],
        dense[:, : 3 * width],
        dense[:, 3 * width : 4 * width],
        tail[:, 6],
        tail[:, 7],
        tail[:, :expert_count],
        expert_grads[0],
        expert_grads[1],
    )


def solution(mesh):
    rows = P("fsdp", "seq", None)
    in_specs = (
        rows,
        P("fsdp"),
        P("fsdp"),
        P("fsdp", None),
        P("fsdp", None),
        P("fsdp"),
        P("fsdp"),
        P("fsdp", None),
        P(None, "fsdp", None),
        P(None, "fsdp", None),
        P("fsdp", None),
        rows,
        P("fsdp", "seq"),
        rows,
    )
    out_specs = (
        rows,
        rows,
        P("fsdp"),
        P("fsdp"),
        P("fsdp", None),
        P("fsdp", None),
        P("fsdp"),
        P("fsdp"),
        P("fsdp", None),
        P(None, "fsdp", None),
        P(None, "fsdp", None),
    )
    return jax.shard_map(
        functools.partial(local, mesh.shape["fsdp"], mesh.shape["seq"]),
        mesh=mesh,
        in_specs=in_specs,
        out_specs=out_specs,
        check_vma=False,
    )
```
